32 devices in a mesh: dp: 8 (over z, x), tensor: 4 (over y, core).
Axes of the slice: x: 2, y: 2, z: 4, core: 2. Of those that a mesh axis runs over, the one named last changes fastest.
Arguments:
- tokens: bfloat16 [12608, 768], P(('dp', 'tensor')), may hold values from -6 to 6
- ln1_gain: bfloat16 [768], P(('dp', 'tensor')), may hold values from 0.5 to 1.5
- ln1_shift: bfloat16 [768], P(('dp', 'tensor')), may hold values from -1.5 to 1.5
- qkv_weight: bfloat16 [768, 3, 768], P('dp', None, 'tensor'), may hold values from -0.3125 to 0.3125
- qv_bias: bfloat16 [2, 768], P(None, ('dp', 'tensor')), may hold values from -1.5 to 1.5
- out_weight: bfloat16 [768, 768], P('tensor', 'dp'), may hold values from -0.875 to 0.875
- out_bias: bfloat16 [768], P(('dp', 'tensor')), may hold values from -1.5 to 1.5
- ln2_gain: bfloat16 [768], P(('dp', 'tensor')), may hold values from 0.5 to 1.5
- ln2_shift: bfloat16 [768], P(('dp', 'tensor')), may hold values from -1.5 to 1.5
- router_weight: bfloat16 [768, 8], P(('dp', 'tensor')), may hold values from -0.15625 to 0.15625
- expert_in: bfloat16 [8, 768, 3072], P(None, 'dp', 'tensor'), may hold values from -0.21875 to 0.21875
- expert_in_bias: bfloat16 [8, 3072], P(None, ('dp', 'tensor')), may hold values from -1.5 to 1.5
- expert_out: bfloat16 [8, 3072, 768], P(None, 'tensor', 'dp'), may hold values from -0.625 to 0.625
- expert_out_bias: bfloat16 [8, 768], P(None, ('dp', 'tensor')), may hold values from -1 to 1
- expert_ids: int32 [12608, 2], P('dp'), may hold values from 0 to 7, as said below
- expert_slots: int32 [12608, 2], P('dp'), may hold values from -1 to 629, as said below
- cotangent: bfloat16 [12608, 768], P(('dp', 'tensor')), may hold values from -6 to 6
Outputs:
- output: bfloat16 [12608, 768], P(('dp', 'tensor'))
- tokens_grad: float32 [12608, 768], P(('dp', 'tensor'))
- ln1_gain_grad: float32 [768], P(('dp', 'tensor'))
- ln1_shift_grad: float32 [768], P(('dp', 'tensor'))
- qkv_weight_grad: float32 [768, 3, 768], P('dp', None, 'tensor')
- qv_bias_grad: float32 [2, 768], P(None, ('dp', 'tensor'))
- out_weight_grad: float32 [768, 768], P('tensor', 'dp')
- out_bias_grad: float32 [768], P(('dp', 'tensor'))
- ln2_gain_grad: float32 [768], P(('dp', 'tensor'))
- ln2_shift_grad: float32 [768], P(('dp', 'tensor'))
- router_weight_grad: float32 [768, 8], P(('dp', 'tensor'))
- expert_in_grad: float32 [8, 768, 3072], P(None, 'dp', 'tensor')
- expert_in_bias_grad: float32 [8, 3072], P(None, ('dp', 'tensor'))
- expert_out_grad: float32 [8, 3072, 768], P(None, 'tensor', 'dp')
- expert_out_bias_grad: float32 [8, 768], P(None, ('dp', 'tensor'))
The draws below stay inside these ranges and needn't reach their ends.
Inputs may be any that keep to these rules, and one draw needn't show every extreme that they name: `expert_ids`: each token names two different experts. `expert_slots`: within each group of 1576 tokens an expert's slots are taken from 0 upward, first by the first choices in token order, then by the second choices in token order; a choice that finds all 630 slots taken is dropped (-1).
All inputs are finite; a program needn't handle non-finite values.
Results may differ from the reference program's by a relative error of at most 0.02.
Values may be sent and summed in bfloat16 or wider, within the bound.
A program may use at most 256 MiB of HBM per device.

```python
import jax
import jax.numpy as jnp
import numpy as np
from jax import lax

D = 768
HEADS = 12
HEAD_DIM = 64
FF = 3072
EXPERTS = 8
TOP = 2
SEQ = 197
IMGS = 8
GROUP = 1576
CAP = 630
TOKENS = 12608
N_DP = 8


def routing(key):
    base = jax.random.fold_in(key, 11)
    key_order, key_first, key_second = jax.random.split(base, 3)
    expert_order = jax.random.permutation(key_order, EXPERTS).astype(jnp.int32)
    shares = [max(1, 6 // (rank + 1)) for rank in range(EXPERTS)]
    bounds = jnp.asarray(np.cumsum(shares), dtype=jnp.int32)
    ticket = jax.random.randint(key_first, (TOKENS,), 0, int(np.sum(shares)), dtype=jnp.int32)
    first_rank = jnp.sum((ticket[:, None] >= bounds[None, :]).astype(jnp.int32), axis=1)
    offset = jax.random.randint(key_second, (TOKENS,), 1, EXPERTS, dtype=jnp.int32)
    second_rank = (first_rank + offset) % EXPERTS
    chosen = jnp.stack([expert_order[first_rank], expert_order[second_rank]], axis=1).astype(jnp.int32)
    groups = TOKENS // GROUP
    matches = (chosen.reshape(groups, GROUP, TOP)[..., None] == jnp.arange(EXPERTS, dtype=jnp.int32)).astype(jnp.int32)
    ordered = jnp.transpose(matches, (0, 2, 1, 3)).reshape(groups, TOP * GROUP, EXPERTS)
    before = jnp.cumsum(ordered, axis=1) - ordered
    position = jnp.sum(before * ordered, axis=-1).reshape(groups, TOP, GROUP)
    position = jnp.transpose(position, (0, 2, 1)).reshape(TOKENS, TOP)
    slot_pos = jnp.where(position < CAP, position, -1).astype(jnp.int32)
    return (chosen, slot_pos)


def draw_expert_ids(key, part):
    return routing(key)[0]


def draw_expert_slots(key, part):
    return routing(key)[1]


def steps_of(stream_key, shape, cuts, smallest, high):
    def one(dim, parts):
        draws = jax.random.uniform(jax.random.fold_in(jax.random.fold_in(stream_key, 6), dim), (parts,), jnp.float32, smallest / len(cuts), high / len(cuts))
        return jnp.repeat(jnp.exp(draws), shape[dim] // parts).reshape((-1,) + (1,) * (len(shape) - dim - 1))

    loudness = one(*cuts[0])
    for cut in cuts[1:]:
        loudness = loudness * one(*cut)
    return loudness


def gaussian(own_key, shape, scale, limit, cuts=(), kind=jnp.bfloat16):
    gain = steps_of(own_key, shape, cuts, -0.22, 0.18) if cuts else 1.0
    result = jax.random.normal(own_key, shape, jnp.float32) * scale * gain
    return jnp.minimum(jnp.maximum(result, -limit), limit).astype(kind)


def setup_inputs(seed: int = 0) -> dict:
    seeds = jax.random.split(jax.random.key(seed), 18)
    tokens = gaussian(seeds[0], (TOKENS, D), 1.0, 6.0, ((0, 32),))
    ln1_gain = jnp.clip(1.0 + 0.1 * jax.random.normal(seeds[1], (D,), jnp.float32), 0.5, 1.5).astype(jnp.bfloat16)
    ln1_shift = gaussian(seeds[2], (D,), 0.3, 1.5, ((0, 32),))
    qkv_weight = gaussian(seeds[3], (D, 3, D), (D // 2) ** -0.5, 0.3125, ((0, 8), (2, 4)))
    qv_bias = gaussian(seeds[4], (2, D), 0.3, 1.5, ((1, 32),))
    out_weight = gaussian(seeds[5], (D, D), (D // 16) ** -0.5, 0.875, ((0, 4), (1, 8)))
    out_bias = gaussian(seeds[6], (D,), 0.3, 1.5, ((0, 32),))
    ln2_gain = jnp.clip(1.0 + 0.1 * jax.random.normal(seeds[7], (D,), jnp.float32), 0.5, 1.5).astype(jnp.bfloat16)
    ln2_shift = gaussian(seeds[8], (D,), 0.3, 1.5, ((0, 32),))
    router_weight = gaussian(seeds[9], (D, EXPERTS), (16 * D // 9) ** -0.5, 0.15625, ((0, 32),))
    expert_in = gaussian(seeds[10], (EXPERTS, D, FF), D ** -0.5, 0.21875, ((1, 8), (2, 4)))
    expert_in_bias = gaussian(seeds[11], (EXPERTS, FF), 0.3, 1.5, ((1, 32),))
    expert_out = gaussian(seeds[12], (EXPERTS, FF, D), (FF // 32) ** -0.5, 0.625, ((1, 4), (2, 8)))
    expert_out_bias = gaussian(seeds[13], (EXPERTS, D), 0.2, 1.0, ((1, 32),))
    expert_ids = draw_expert_ids(jax.random.fold_in(seeds[17], 71), 0)
    expert_slots = draw_expert_slots(jax.random.fold_in(seeds[17], 71), 0)
    cotangent = gaussian(seeds[16], (TOKENS, D), 1.0, 6.0, ((0, 32),))
    return dict(tokens=tokens, ln1_gain=ln1_gain, ln1_shift=ln1_shift, qkv_weight=qkv_weight, qv_bias=qv_bias, out_weight=out_weight, out_bias=out_bias, ln2_gain=ln2_gain, ln2_shift=ln2_shift, router_weight=router_weight, expert_in=expert_in, expert_in_bias=expert_in_bias, expert_out=expert_out, expert_out_bias=expert_out_bias, expert_ids=expert_ids, expert_slots=expert_slots, cotangent=cotangent)


@jax.custom_vjp
def low(v):
    return lax.optimization_barrier(v.astype(jnp.bfloat16)).astype(jnp.float32)

@jax.custom_vjp
def low_back(v):
    return v

def low_keep(v):
    return (low(v), None)

def low_pass(kept, grad):
    return (grad,)

def back_keep(v):
    return (v, None)

def back_low(kept, grad):
    return (low(grad),)
low.defvjp(low_keep, low_pass)
low_back.defvjp(back_keep, back_low)
eps_norm = 1e-06
highest = lax.Precision.HIGHEST

def layer_norm(row_data, gain_vec, shift_vec):
    row_mean = lax.optimization_barrier(jnp.mean(row_data, axis=-1, keepdims=True))
    centred = row_data - row_mean
    spread = lax.optimization_barrier(jnp.mean(centred * centred, axis=-1, keepdims=True))
    return centred * lax.rsqrt(spread + eps_norm) * gain_vec + shift_vec

def group_layer(params, item):
    gain_first, shift_first, qkv_full, bias_pair, proj_out, bias_out, gain_second, shift_second, router_full, expert_up, up_bias, expert_down, down_bias = params
    row_data, route_ids, route_slots = item
    first_norm = low(layer_norm(row_data, gain_first, shift_first))
    projected = jnp.dot(first_norm, qkv_full.reshape(D, 3 * D), precision=highest).reshape(GROUP, 3, D)
    queries = low(low_back(projected[:, 0] + bias_pair[0]))
    keys_all = low(low_back(projected[:, 1]))
    values_all = low(low_back(projected[:, 2] + bias_pair[1]))
    shape_four = (IMGS, SEQ, HEADS, HEAD_DIM)
    scores = jnp.einsum('bqhd,bkhd->bhqk', queries.reshape(shape_four), keys_all.reshape(shape_four), precision=highest)
    scores = low_back(scores * HEAD_DIM ** (-0.5))
    attn_weights = low(jax.nn.softmax(scores, axis=-1))
    mixed_rows = jnp.einsum('bhqk,bkhd->bqhd', attn_weights, values_all.reshape(shape_four), precision=highest)
    mixed_rows = low(low_back(mixed_rows.reshape(GROUP, D)))
    branch = low_back(jnp.dot(mixed_rows, proj_out, precision=highest) + bias_out)
    hidden_rows = row_data + branch
    second_norm = low(layer_norm(hidden_rows, gain_second, shift_second))
    router_logits = jnp.dot(second_norm, router_full, precision=highest)
    router_probs = jax.nn.softmax(router_logits, axis=-1)
    labels = jnp.arange(EXPERTS, dtype=jnp.int32)
    onehot = (route_ids[:, :, None] == labels).astype(jnp.float32)
    kept_mask = route_slots >= 0
    gate_vals = lax.optimization_barrier(jnp.sum(onehot * router_probs[:, None, :], axis=-1)) * kept_mask.astype(jnp.float32)
    slot_index = jnp.where(kept_mask, route_ids * CAP + route_slots, EXPERTS * CAP).astype(jnp.int32)
    buffer_rows = jnp.zeros((EXPERTS * CAP + 1, D), jnp.float32).at[slot_index.reshape(-1)].add(jnp.repeat(second_norm, TOP, axis=0))
    dispatched = buffer_rows[:EXPERTS * CAP].reshape(EXPERTS, CAP, D)
    preact = jnp.einsum('ecd,edf->ecf', dispatched, expert_up, precision=highest) + up_bias[:, None, :]
    activated = low(jax.nn.gelu(low_back(preact), approximate=False))
    expert_rows = jnp.einsum('ecf,efd->ecd', activated, expert_down, precision=highest) + down_bias[:, None, :]
    expert_rows = low_back(expert_rows)
    padded = jnp.concatenate([expert_rows.reshape(EXPERTS * CAP, D), jnp.zeros((1, D), jnp.float32)], axis=0)
    combined = lax.optimization_barrier(jnp.sum(gate_vals[:, :, None] * padded[slot_index], axis=1))
    return hidden_rows + combined

def reference(tokens, ln1_gain, ln1_shift, qkv_weight, qv_bias, out_weight, out_bias, ln2_gain, ln2_shift, router_weight, expert_in, expert_in_bias, expert_out, expert_out_bias, expert_ids, expert_slots, cotangent):
    weights = tuple((entry.astype(jnp.float32) for entry in (ln1_gain, ln1_shift, qkv_weight, qv_bias, out_weight, out_bias, ln2_gain, ln2_shift, router_weight, expert_in, expert_in_bias, expert_out, expert_out_bias)))
    id_groups = expert_ids.reshape(N_DP, GROUP, TOP)
    slot_groups = expert_slots.reshape(N_DP, GROUP, TOP)
    checked = jax.checkpoint(group_layer)

    def forward(inputs_f, *params):
        outcome = lax.map(lambda item: checked(params, item), (inputs_f.reshape(N_DP, GROUP, D), id_groups, slot_groups))
        return outcome.reshape(TOKENS, D)
    final_rows, pull = jax.vjp(forward, tokens.astype(jnp.float32), *weights)
    grads = pull(cotangent.astype(jnp.float32))
    return (final_rows.astype(jnp.bfloat16), grads[0], grads[1], grads[2], grads[3], grads[4], grads[5], grads[6], grads[7], grads[8], grads[9], grads[10], grads[11], grads[12], grads[13])
```

```python
import functools

import jax
import jax.numpy as jnp
from jax import lax
from jax.experimental import pallas as pl
from jax.experimental.pallas import tpu as pltpu
from jax.sharding import PartitionSpec as P

HEAD_DIM = 64
SEQ = 197
SEQ_PAD = 208
CAP = 630
CAP_PAD = 640
EPS = 1e-6
BF = jnp.bfloat16
F32 = jnp.float32
MESH = pl.DeviceIdType.MESH
VMEM_LIMIT = 56 * 1024 * 1024
VM = pl.BlockSpec(memory_space=pltpu.VMEM)
HB = pl.BlockSpec(memory_space=pl.ANY)


def nn(a, b):
    return lax.dot_general(a, b, (((1,), (0,)), ((), ())), preferred_element_type=F32)


def nt(a, b):
    return lax.dot_general(a, b, (((1,), (1,)), ((), ())), preferred_element_type=F32)


def tn(a, b):
    return lax.dot_general(a, b, (((0,), (0,)), ((), ())), preferred_element_type=F32)


def unit_norm(rows):
    centred = rows - jnp.mean(rows, axis=-1, keepdims=True)
    inv = lax.rsqrt(jnp.mean(centred * centred, axis=-1, keepdims=True) + EPS)
    return centred * inv, inv


def place(cells):
    index = lax.axis_index("dp")
    return lax.div(index, cells), lax.rem(index, cells), lax.axis_index("tensor")


def tensor_peers(t):
    core = t + 1 - 2 * lax.rem(t, 2)
    side = lax.rem(t + 2, 4)
    return core, side, lax.rem(core + 2, 4)


def remote(src, dst, send, recv, device):
    return pltpu.make_async_remote_copy(
        src_ref=src, dst_ref=dst, send_sem=send, recv_sem=recv, device_id=device, device_id_type=MESH
    )


def signal(barrier, device):
    pl.semaphore_signal(barrier, inc=1, device_id=device, device_id_type=MESH)


def gather_kernel(cells, n_shared, *refs):
    n_arr = n_shared + 1
    srcs, cot = refs[:n_arr], refs[n_arr]
    dsts, cot_all = refs[n_arr + 1 : 2 * n_arr + 1], refs[2 * n_arr + 1]
    (dp_s, dp_r, y_s, y_r, c_s, c_r, f_s, f_r, own, cot_s, cot_r) = refs[2 * n_arr + 2 :]
    d, cell, t = place(cells)
    core, side, far = tensor_peers(t)
    here = d * cells + cell

    def at_dp(k):
        return (lax.rem(d + k, 8) * cells + cell, t)

    barrier = pltpu.get_barrier_semaphore()
    for k in range(1, 8):
        signal(barrier, at_dp(k))
    signal(barrier, (here, core))
    signal(barrier, (here, side))
    pl.semaphore_wait(barrier, 9)

    waits = []
    locals_ = []
    for a in range(n_arr):
        shared = a < n_shared
        mine = pltpu.make_async_copy(srcs[a] if shared else srcs[a].at[d], dsts[a].at[t, d], own.at[a])
        mine.start()
        locals_.append(mine)
    dp_copies = []
    for a in range(n_arr):
        shared = a < n_shared
        row = []
        for k in range(1, 8):
            p = lax.rem(d + k, 8)
            copy = remote(
                srcs[a] if shared else srcs[a].at[p],
                dsts[a].at[t, d],
                dp_s.at[a, k],
                dp_r.at[a, k],
                at_dp(k),
            )
            copy.start()
            row.append(copy)
        dp_copies.append(row)
    cot_y = remote(cot, cot_all.at[t], cot_s.at[0], cot_r.at[0], (here, side))
    cot_c = remote(cot, cot_all.at[t], cot_s.at[1], cot_r.at[1], (here, core))
    cot_own = pltpu.make_async_copy(cot, cot_all.at[t], own.at[n_arr])
    cot_y.start()
    cot_c.start()
    cot_own.start()

    side_copies = [[None] * 8 for _ in range(n_arr)]

    def spread(a):
        for k in range(8):
            s = lax.rem(d + 8 - k, 8)
            block = dsts[a].at[t, s]
            if k == 0:
                locals_[a].wait()
            else:
                dp_copies[a][k - 1].wait_recv()
            over = remote(block, block, y_s.at[a, k], y_r.at[a, k], (here, side))
            over.start()
            side_copies[a][k] = over
            near = remote(block, block, c_s.at[a, k], c_r.at[a, k], (here, core))
            near.start()
            waits.append(near)

    def forward(a):
        for k in range(8):
            s = lax.rem(d + 8 - k, 8)
            block = dsts[a].at[side, s]
            side_copies[a][k].wait_recv()
            near = remote(block, block, f_s.at[a, k], f_r.at[a, k], (here, core))
            near.start()
            waits.append(near)

    for a in range(n_arr):
        spread(a)
        if a:
            forward(a - 1)
        if a == n_arr - 1:
            cot_y.wait_recv()
            cot_f = remote(cot_all.at[side], cot_all.at[side], cot_s.at[2], cot_r.at[2], (here, core))
            cot_f.start()
    forward(n_arr - 1)
    for copy in waits:
        copy.wait()
    for a in range(n_arr):
        for copy in dp_copies[a]:
            copy.wait_send()
        for copy in side_copies[a]:
            copy.wait_send()
    cot_y.wait_send()
    cot_c.wait()
    cot_f.wait()
    cot_own.wait()


def gather_weights(cells, shared, expert, cot):
    arrays = list(shared) + [expert]
    n_arr = len(arrays)
    shapes = [jax.ShapeDtypeStruct((4, 8) + a.shape, a.dtype) for a in shared]
    shapes.append(jax.ShapeDtypeStruct((4,) + expert.shape, expert.dtype))
    shapes.append(jax.ShapeDtypeStruct((4,) + cot.shape, cot.dtype))
    dma = pltpu.SemaphoreType.DMA
    return pl.pallas_call(
        functools.partial(gather_kernel, cells, len(shared)),
        out_shape=shapes,
        in_specs=[HB] * (n_arr + 1),
        out_specs=[HB] * (n_arr + 1),
        scratch_shapes=[dma((n_arr, 8))] * 8 + [dma((n_arr + 1,)), dma((3,)), dma((3,))],
        compiler_params=pltpu.CompilerParams(collective_id=0, has_side_effects=True),
        name="gather_weights",
    )(*arrays, cot)


def softmax_rows(q, k):
    scores = nt(q, k) * (HEAD_DIM**-0.5)
    lane = lax.broadcasted_iota(jnp.int32, scores.shape, 1)
    scores = jnp.where(lane < SEQ, scores, -1e30)
    raised = jnp.exp(scores - jnp.max(scores, axis=-1, keepdims=True))
    return raised / jnp.sum(raised, axis=-1, keepdims=True)


def attention_kernel(tok, vec, qkv_bias, router, wall, second_out, hidden_out, probs_out, qkv_out, mixed_out, acc):
    rows = tok.shape[0]
    heads = qkv_out.shape[2] // 3
    inputs = tok[...].astype(F32)
    unit, _ = unit_norm(inputs)
    first = (unit * vec[0:1] + vec[1:2]).astype(BF)
    acc[...] = inputs + vec[4:5]

    def step(t, carry):
        weights = wall[t]
        qkv = (nn(first, weights[:, : 3 * heads]) + qkv_bias[t][0:1]).astype(BF)
        qkv_out[t] = qkv
        mixed = []
        for i in range(rows // SEQ_PAD):
            part = qkv[i * SEQ_PAD : (i + 1) * SEQ_PAD]
            sides = []
            for h in range(heads // HEAD_DIM):
                q, k, v = (part[:, j * heads + h * HEAD_DIM : j * heads + (h + 1) * HEAD_DIM] for j in range(3))
                sides.append(nn(softmax_rows(q, k).astype(BF), v).astype(BF))
            mixed.append(jnp.concatenate(sides, axis=1))
        mixed = jnp.concatenate(mixed, axis=0)
        mixed_out[t] = mixed
        acc[...] += nt(mixed, weights[:, 3 * heads :])
        return carry

    lax.fori_loop(0, 4, step, 0)
    hidden = acc[...]
    hidden_out[...] = hidden
    unit, _ = unit_norm(hidden)
    second = (unit * vec[2:3] + vec[3:4]).astype(BF)
    second_out[...] = second
    logits = nt(router[...], second)
    raised = jnp.exp(logits - jnp.max(logits, axis=0, keepdims=True))
    probs_out[...] = raised / jnp.sum(raised, axis=0, keepdims=True)


def dispatch_kernel(
    cells, second, probs, slots, cot_all, x_out, g_out, probs_all, sec_all, x_buf, g_buf, raw,
    ag_s, ag_r, x_s, x_r, own,
):
    d, cell, t = place(cells)
    core, side, far = tensor_peers(t)
    here = d * cells + cell
    line = lax.rem(d, 4)
    mine = lax.div(d, 4)
    loop = line == t

    def partner(j):
        return ((t + 4 * j) * cells + cell, line)

    def is_self(j):
        return jnp.logical_and(loop, mine == j)

    barrier = pltpu.get_barrier_semaphore()
    signal(barrier, (here, core))
    signal(barrier, (here, side))
    for j in range(2):

        @pl.when(jnp.logical_not(is_self(j)))
        def _():
            signal(barrier, partner(j))

    pl.semaphore_wait(barrier, jnp.where(loop, 3, 4))

    pairs = []
    for n, (src, dst) in enumerate(((second, sec_all), (probs, probs_all))):
        over = remote(src, dst.at[t], ag_s.at[n, 0], ag_r.at[n, 0], (here, side))
        near = remote(src, dst.at[t], ag_s.at[n, 1], ag_r.at[n, 1], (here, core))
        over.start()
        near.start()
        pairs.append((over, near))
    sec_all[t] = second[...]
    probs_all[t] = probs[...]

    def onehot(tt, e):
        slot = slots[tt, pl.ds(e, 1), :]
        return lax.broadcasted_iota(jnp.int32, (CAP_PAD, slot.shape[1]), 0) == slot

    def pick(e, rows):
        total = None
        for tt in range(4):
            part = nn(onehot(tt, e).astype(F32).astype(BF), rows[tt])
            total = part if total is None else total + part
        return total

    for j in range(2):
        raw[j] = pick(t + 4 * j, cot_all).astype(BF)

    forwards = []
    for n, dst in enumerate((sec_all, probs_all)):
        pairs[n][0].wait_recv()
        along = remote(dst.at[side], dst.at[side], ag_s.at[n, 2], ag_r.at[n, 2], (here, core))
        along.start()
        forwards.append(along)
    for n in range(2):
        pairs[n][1].wait_recv()
        forwards[n].wait_recv()

    def send(j, n, buf, out):
        copy = remote(buf.at[j], out.at[mine], x_s.at[n, j], x_r.at[n, mine], partner(j))

        @pl.when(is_self(j))
        def _():
            pltpu.make_async_copy(buf.at[j], out.at[mine], own.at[n]).start()

        @pl.when(jnp.logical_not(is_self(j)))
        def _():
            copy.start()

        return copy

    sent = []
    for j in range(2):
        x_buf[j] = pick(t + 4 * j, sec_all).astype(BF)
        sent.append((j, 0, x_buf, x_out, send(j, 0, x_buf, x_out)))
    for j in range(2):
        e = t + 4 * j
        gate = None
        for tt in range(4):
            part = jnp.sum(
                jnp.where(onehot(tt, e), probs_all[tt, pl.ds(e, 1), :], 0.0), axis=1, keepdims=True
            )
            gate = part if gate is None else gate + part
        g_buf[j] = (gate * raw[j].astype(F32)).astype(BF)
        sent.append((j, 1, g_buf, g_out, send(j, 1, g_buf, g_out)))

    for j, n, buf, out, copy in sent:

        @pl.when(is_self(j))
        def _():
            pltpu.make_async_copy(buf.at[j], out.at[mine], own.at[n]).wait()

        @pl.when(jnp.logical_not(is_self(j)))
        def _():
            copy.wait_send()
            remote(buf.at[j], out.at[j], x_s.at[n, j], x_r.at[n, j], partner(j)).wait_recv()

    for n in range(2):
        for copy in pairs[n]:
            copy.wait_send()
        forwards[n].wait_send()


def gelu_both(x):
    phi = 0.5 * (1.0 + lax.erf(x * (0.5**0.5)))
    slope = phi + x * (jnp.exp(-0.5 * x * x) * 0.3989422804014327)
    return x * phi, slope


def expert_kernel(
    x_ref, g_ref, w_ref, up_bias, down_bias, y_out, b_out, q_out, dw_out, dup_out, ddown_out,
    y_acc, b_acc, x_turned, g_turned, act_buf, pre_buf,
):
    step = pl.program_id(0)
    slots, width = y_acc.shape
    tile = 256
    w_in = w_ref[0, :, 0].reshape(width, -1)
    w_out = w_ref[0, :, 1].reshape(width, -1)

    @pl.when(step == 0)
    def _():
        y_acc[...] = jnp.broadcast_to(down_bias[...], y_acc.shape)
        b_acc[...] = jnp.zeros_like(b_acc)
        x_turned[...] = x_ref[...].T
        g_turned[...] = g_ref[...].T
        ddown_out[...] = jnp.sum(g_ref[...].astype(F32), axis=0, keepdims=True)

    def rows_step(m, bias_sum):
        here = pl.ds(pl.multiple_of(m * tile, tile), tile)
        x, g = x_ref[here, :], g_ref[here, :]
        pre = nn(x, w_in) + up_bias[0]
        act, slope = gelu_both(pre)
        act = act.astype(BF)
        act_buf[here, :] = act
        pre_grad = (nn(g, w_out) * slope).astype(BF)
        pre_buf[here, :] = pre_grad
        y_acc[here, :] += nt(act, w_out)
        b_acc[here, :] += nt(pre_grad, w_in)
        return bias_sum + jnp.sum(pre_grad.astype(F32), axis=0, keepdims=True)

    ff = w_in.shape[1]
    dup_out[0] = lax.fori_loop(0, slots // tile, rows_step, jnp.zeros((1, ff), F32))

    def grad_step(n, carry):
        here = pl.ds(pl.multiple_of(n * 192, 192), 192)
        d_in = nn(x_turned[here, :], pre_buf[...]).astype(BF)
        d_out = nn(g_turned[here, :], act_buf[...]).astype(BF)
        pair = pl.ds(2 * n, 2)
        dw_out[0, pair, 0] = d_in.reshape(2, 96, ff)
        dw_out[0, pair, 1] = d_out.reshape(2, 96, ff)
        return carry

    lax.fori_loop(0, width // 192, grad_step, 0)

    @pl.when(step == pl.num_programs(0) - 1)
    def _():
        ones = jnp.ones((8, width), BF)
        for m in range(slots // 128):
            here = slice(m * 128, (m + 1) * 128)
            y = y_acc[here, :]
            y_out[here, :] = y.astype(BF)
            b_out[here, :] = b_acc[here, :].astype(BF)
            z = y * g_ref[here, :].astype(F32)
            high = z.astype(BF)
            low = (z - high.astype(F32)).astype(BF)
            half, place_ = divmod(m * 128, slots // 2)
            q_out[half, :, place_ : place_ + 128] = nt(ones, high) + nt(ones, low)


def combine_kernel(
    cells, b_src, y_src, q_src, slots, probs, r_out, m_out, q_all, b_in, y_in, blocks, core_in, side_buf, side_in,
    a_s, a_r, q_s, q_r, c_s, c_r, y_s, y_r, own,
):
    d, cell, t = place(cells)
    core, side, far = tensor_peers(t)
    here = d * cells + cell
    line = lax.rem(d, 4)
    mine = lax.div(d, 4)
    loop = line == t

    def partner(j):
        return ((t + 4 * j) * cells + cell, line)

    def is_self(j):
        return jnp.logical_and(loop, mine == j)

    barrier = pltpu.get_barrier_semaphore()
    signal(barrier, (here, core))
    signal(barrier, (here, side))
    for e in range(8):

        @pl.when(jnp.logical_not(jnp.logical_and(loop, d == e)))
        def _():
            signal(barrier, (e * cells + cell, line))

    pl.semaphore_wait(barrier, jnp.where(loop, 9, 10))

    for n, (src, dst) in enumerate(((b_src, b_in), (y_src, y_in))):
        for j in range(2):

            @pl.when(is_self(j))
            def _():
                pltpu.make_async_copy(src.at[j], dst.at[mine], own.at[n]).start()

            @pl.when(jnp.logical_not(is_self(j)))
            def _():
                remote(src.at[j], dst.at[mine], a_s.at[n, j], a_r.at[n, mine], partner(j)).start()

        if n == 0:
            for j in range(2):
                for tt in range(4):
                    itself = jnp.logical_and(t + 4 * j == d, t == tt)

                    @pl.when(itself)
                    def _():
                        pltpu.make_async_copy(q_src.at[j], q_all.at[d], own.at[2]).start()

                    @pl.when(jnp.logical_not(itself))
                    def _():
                        remote(
                            q_src.at[j], q_all.at[d], q_s.at[j, tt], q_r.at[d], ((t + 4 * j) * cells + cell, tt)
                        ).start()

    for n, (src, dst) in enumerate(((b_src, b_in), (y_src, y_in))):
        for j in range(2):

            @pl.when(is_self(j))
            def _():
                pltpu.make_async_copy(src.at[j], dst.at[mine], own.at[n]).wait()

            @pl.when(jnp.logical_not(is_self(j)))
            def _():
                remote(src.at[j], dst.at[j], a_s.at[n, j], a_r.at[n, j], partner(j)).wait_recv()

    def block(tt):
        total_b = total_y = None
        table, gates = slots[tt], probs[tt]
        lane = lax.broadcasted_iota(jnp.int32, table.shape, 1)
        for j in range(2):
            e = t + 4 * j
            slot = jnp.sum(jnp.where(lane == e, table, 0.0), axis=1, keepdims=True)
            gate = jnp.sum(jnp.where(lane == e, gates, 0.0), axis=1, keepdims=True)
            at = lax.broadcasted_iota(jnp.int32, (table.shape[0], CAP_PAD), 1)
            hot = (at == slot.astype(jnp.int32)).astype(F32).astype(BF)
            part_b = nn(hot, b_in[j])
            part_y = nn(hot, y_in[j]) * gate
            total_b = part_b if j == 0 else total_b + part_b
            total_y = part_y if j == 0 else total_y + part_y
        return total_b, total_y

    core_copies = []
    for i, tt in enumerate((far, core)):
        total_b, total_y = block(tt)
        blocks[i, 0] = total_b.astype(BF)
        blocks[i, 1] = total_y.astype(BF)
        copy = remote(blocks.at[i], core_in.at[i], c_s.at[i], c_r.at[i], (here, core))
        copy.start()
        core_copies.append(copy)
    total_b, total_y = block(side)
    core_copies[0].wait_recv()
    side_buf[0] = (total_b + core_in[0, 0].astype(F32)).astype(BF)
    side_buf[1] = (total_y + core_in[0, 1].astype(F32)).astype(BF)
    side_copy = remote(side_buf, side_in, y_s.at[0], y_r.at[0], (here, side))
    side_copy.start()
    total_b, total_y = block(t)
    core_copies[1].wait_recv()
    total_b = total_b + core_in[1, 0].astype(F32)
    total_y = total_y + core_in[1, 1].astype(F32)
    side_copy.wait_recv()
    r_out[...] = total_b + side_in[0].astype(F32)
    m_out[...] = total_y + side_in[1].astype(F32)

    for copy in core_copies:
        copy.wait_send()
    side_copy.wait_send()
    for n, (src, dst) in enumerate(((b_src, b_in), (y_src, y_in))):
        for j in range(2):

            @pl.when(jnp.logical_not(is_self(j)))
            def _():
                remote(src.at[j], dst.at[mine], a_s.at[n, j], a_r.at[n, mine], partner(j)).wait_send()

    for j in range(2):
        for tt in range(4):
            itself = jnp.logical_and(t + 4 * j == d, t == tt)

            @pl.when(itself)
            def _():
                pltpu.make_async_copy(q_src.at[j], q_all.at[d], own.at[2]).wait()

            @pl.when(jnp.logical_not(itself))
            def _():
                remote(
                    q_src.at[j], q_all.at[d], q_s.at[j, tt], q_r.at[d], ((t + 4 * j) * cells + cell, tt)
                ).wait_send()

    for e in range(8):

        @pl.when(jnp.logical_not(jnp.logical_and(loop, d == e)))
        def _():
            remote(q_src.at[0], q_all.at[e], q_s.at[0, 0], q_r.at[e], (e * cells + cell, line)).wait_recv()


def backward_kernel(
    tok, hid, r_ref, m_ref, cot, probs, q_all, slots, router, vec, wall, qkv_ref, mixed_ref,
    out, token_grad, dw_out, vec_out, bias_out, n1,
):
    heads = qkv_ref.shape[2] // 3
    rows = tok.shape[0]
    hidden = hid[...]
    out[...] = (hidden + m_ref[...]).astype(BF)
    picked = jnp.zeros(probs.shape, F32)
    sub = lax.broadcasted_iota(jnp.int32, probs.shape, 0)
    for e in range(8):
        hot = (lax.broadcasted_iota(jnp.int32, (CAP_PAD, rows), 0) == slots[e : e + 1, :]).astype(F32).astype(BF)
        q = q_all[e]
        high = q.astype(BF)
        low = (q - high.astype(F32)).astype(BF)
        picked = jnp.where(sub == e, nn(high, hot) + nn(low, hot), picked)
    logit = picked - probs[...] * jnp.sum(picked, axis=0, keepdims=True)
    high = logit.astype(BF)
    both = jnp.concatenate([high, (logit - high.astype(F32)).astype(BF)], axis=0)
    unit, inv = unit_norm(hidden)
    gain = vec[2:3]
    second = (unit * gain + vec[3:4]).astype(BF)
    router_grad = nn(both, second)
    vec_out[8:16] = router_grad[0:8] + router_grad[8:16]
    table = router[...]
    n2 = r_ref[...] + tn(both, jnp.concatenate([table, table], axis=0))
    vec_out[2:3] = jnp.sum(n2 * unit, axis=0, keepdims=True)
    vec_out[3:4] = jnp.sum(n2, axis=0, keepdims=True)
    scaled = n2 * gain
    back = inv * (
        scaled
        - jnp.mean(scaled, axis=-1, keepdims=True)
        - unit * jnp.mean(scaled * unit, axis=-1, keepdims=True)
    )
    hidden_grad = cot[...].astype(F32) + back
    token_grad[...] = hidden_grad
    branch = hidden_grad.astype(BF)
    vec_out[4:5] = jnp.sum(branch.astype(F32), axis=0, keepdims=True)
    vec_out[5:8] = jnp.zeros((3, vec_out.shape[1]), F32)
    unit1, inv1 = unit_norm(tok[...].astype(F32))
    first = (unit1 * vec[0:1] + vec[1:2]).astype(BF)
    n1[...] = jnp.zeros_like(n1)

    def step(t, carry):
        weights = wall[t]
        qkv = qkv_ref[t]
        mixed_grad = nn(branch, weights[:, 3 * heads :]).astype(BF)
        triple = []
        for i in range(rows // SEQ_PAD):
            here = slice(i * SEQ_PAD, (i + 1) * SEQ_PAD)
            part, grad = qkv[here], mixed_grad[here]
            sides = [[], [], []]
            for h in range(heads // HEAD_DIM):
                q, k, v = (part[:, j * heads + h * HEAD_DIM : j * heads + (h + 1) * HEAD_DIM] for j in range(3))
                g = grad[:, h * HEAD_DIM : (h + 1) * HEAD_DIM]
                w = softmax_rows(q, k)
                w_grad = nt(g, v)
                s_grad = (w * (w_grad - jnp.sum(w * w_grad, axis=-1, keepdims=True))).astype(BF)
                sides[0].append((nn(s_grad, k) * (HEAD_DIM**-0.5)).astype(BF))
                sides[1].append((tn(s_grad, q) * (HEAD_DIM**-0.5)).astype(BF))
                sides[2].append(tn(w.astype(BF), g).astype(BF))
            triple.append(jnp.concatenate(sides[0] + sides[1] + sides[2], axis=1))
        triple = jnp.concatenate(triple, axis=0)
        dw_out[t] = jnp.concatenate([tn(first, triple), tn(branch, mixed_ref[t])], axis=1).astype(BF)
        n1[...] += nt(triple, weights[:, : 3 * heads])
        sums = jnp.sum(triple.astype(F32), axis=0, keepdims=True)
        bias_out[t] = jnp.broadcast_to(sums, (8, 3 * heads))
        return carry

    lax.fori_loop(0, 4, step, 0)
    grad = n1[...]
    vec_out[0:1] = jnp.sum(grad * unit1, axis=0, keepdims=True)
    vec_out[1:2] = jnp.sum(grad, axis=0, keepdims=True)
    scaled = grad * vec[0:1]
    token_grad[...] += inv1 * (
        scaled
        - jnp.mean(scaled, axis=-1, keepdims=True)
        - unit1 * jnp.mean(scaled * unit1, axis=-1, keepdims=True)
    )


def reduce_kernel(cells, with_small, *refs):
    if with_small:
        e_src, a_src, small, e_out, a_out, small_all, *refs = refs
    else:
        e_src, a_src, e_out, a_out, *refs = refs
    (e_core, a_core, e_own, a_own, e_mid, a_mid, e_side, a_side, e_fin, a_fin, a_in,
     c_s, c_r, y_s, y_r, z_s, z_r, own, *small_sems) = refs
    d, cell, t = place(cells)
    core, side, far = tensor_peers(t)
    here = d * cells + cell

    def at_dp(k):
        return (lax.rem(d + k, 8) * cells + cell, t)

    barrier = pltpu.get_barrier_semaphore()
    if with_small:
        others = [
            (lax.rem(d + k, 8), lax.rem(t + m, 4)) for k in range(8) for m in range(4) if k or m
        ]
        for other in others:
            signal(barrier, other)
        pl.semaphore_wait(barrier, 31)
    else:
        for k in range(1, 8):
            signal(barrier, at_dp(k))
        signal(barrier, (here, core))
        signal(barrier, (here, side))
        pl.semaphore_wait(barrier, 9)

    waits = []
    if with_small:
        s_s, s_r = small_sems
        row = d * 4 + t
        for n, other in enumerate(others):
            copy = remote(small.at[other[0] * 4 + other[1]], small_all.at[row], s_s.at[n], s_r.at[n], other)
            copy.start()
            waits.append(copy)
        small_own = pltpu.make_async_copy(small.at[row], small_all.at[row], own.at[4])
        small_own.start()

    sets = ((e_src, e_core, e_own, e_mid, e_side, e_fin), (a_src, a_core, a_own, a_mid, a_side, a_fin))
    first = {}
    for a, (src, inbox, kept, _, _, _) in enumerate(sets):
        for i, tt in enumerate((far, core)):
            copy = remote(src.at[tt], inbox.at[i], c_s.at[a, i], c_r.at[a, i], (here, core))
            copy.start()
            first[a, i] = copy
        for i, tt in enumerate((side, t)):
            copy = pltpu.make_async_copy(src.at[tt], kept.at[i], own.at[2 * a + i])
            copy.start()
            first[a, 2 + i] = copy
    second = {}
    for a, (_, inbox, kept, mid, arrived, _) in enumerate(sets):
        first[a, 2].wait()
        first[a, 0].wait_recv()
        for k in range(1, 9):
            p = lax.rem(d + k, 8)
            mid[p] = (kept[0, p].astype(F32) + inbox[0, p].astype(F32)).astype(BF)
            copy = remote(mid.at[p], arrived.at[p], y_s.at[a, k - 1], y_r.at[a, k - 1], (here, side))
            copy.start()
            second[a, k] = copy
    for a, (_, inbox, kept, _, arrived, final) in enumerate(sets):
        first[a, 3].wait()
        first[a, 1].wait_recv()
        for k in range(1, 9):
            p = lax.rem(d + k, 8)
            second[a, k].wait_recv()
            total = kept[1, p].astype(F32) + inbox[1, p].astype(F32) + arrived[p].astype(F32)
            final[p] = total.astype(BF)
            target = e_out if a == 0 else a_in
            if k < 8:
                copy = remote(final.at[p], target.at[d], z_s.at[a, k], z_r.at[a, k], at_dp(k))
                copy.start()
                waits.append(copy)
            elif a == 0:
                e_keep = pltpu.make_async_copy(final.at[p], target.at[d], own.at[5])
                e_keep.start()
            else:
                a_in[d] = final[p]
    for copy in waits:
        copy.wait()
    e_keep.wait()
    total = a_in[0].astype(F32)
    for p in range(1, 8):
        total = total + a_in[p].astype(F32)
    a_out[...] = total
    if with_small:
        small_own.wait()
    for a in range(2):
        for i in range(2):
            first[a, i].wait_send()
        for k in range(1, 9):
            second[a, k].wait_send()


def reduce_grads(cells, expert, attn, small):
    with_small = small is not None
    dma = pltpu.SemaphoreType.DMA
    e_block, a_block = expert.shape[1:], attn.shape[1:]
    scratch = []
    for lead in ((2,), (2,), (), (), ()):
        scratch.append(pltpu.VMEM(lead + e_block, BF))
        scratch.append(pltpu.VMEM(lead + a_block, BF))
    scratch.append(pltpu.VMEM(a_block, BF))
    scratch += [dma((2, 2)), dma((2, 2)), dma((2, 8)), dma((2, 8)), dma((2, 8)), dma((2, 8)), dma((6,))]
    shapes = [jax.ShapeDtypeStruct(e_block, BF), jax.ShapeDtypeStruct(a_block[1:], F32)]
    ins, in_specs, out_specs = [expert, attn], [HB, HB], [HB, VM]
    if with_small:
        scratch += [dma((31,)), dma((31,))]
        ins.append(small)
        in_specs.append(HB)
        out_specs.append(HB)
        shapes.append(jax.ShapeDtypeStruct(small.shape, F32))
    return pl.pallas_call(
        functools.partial(reduce_kernel, cells, with_small),
        out_shape=shapes,
        in_specs=in_specs,
        out_specs=out_specs,
        scratch_shapes=scratch,
        compiler_params=pltpu.CompilerParams(
            collective_id=3, has_side_effects=True, vmem_limit_bytes=VMEM_LIMIT
        ),
        name="reduce_grads",
    )(*ins)


def pad_images(rows, fill=0):
    images = rows.reshape((-1, SEQ) + rows.shape[1:])
    spare = [(0, 0), (0, SEQ_PAD - SEQ)] + [(0, 0)] * (rows.ndim - 1)
    return jnp.pad(images, spare, constant_values=fill).reshape((-1,) + rows.shape[1:])


def drop_pad(rows):
    return rows.reshape((-1, SEQ_PAD) + rows.shape[1:])[:, :SEQ].reshape((-1,) + rows.shape[1:])


def body(
    tokens, ln1_gain, ln1_shift, qkv_weight, qv_bias, out_weight, out_bias, ln2_gain, ln2_shift,
    router_weight, expert_in, expert_in_bias, expert_out, expert_out_bias, expert_ids, expert_slots,
    cotangent,
):
    n_dp = lax.axis_size("dp")
    cells = n_dp // 8
    n_all = n_dp * 4
    width = tokens.shape[1]
    experts = expert_in.shape[0]
    piece = ln1_gain.shape[0]
    head_cols = qkv_weight.shape[2]
    ff_slice = expert_in.shape[2]
    ff_piece = expert_in_bias.shape[1]
    index = lax.axis_index("dp")
    d = index // cells
    cell = index % cells
    groups = [[row * cells + c for row in range(8)] for c in range(cells)]
    peers = [[row * cells + c for c in range(cells)] for row in range(8)]

    packed = jnp.concatenate([qkv_weight.reshape(-1, 3 * head_cols), out_weight.T], axis=1)
    expert_pack = jnp.stack([expert_in, jnp.swapaxes(expert_out, 1, 2)], axis=1)
    if cells > 1:
        packed = lax.all_gather(packed, "dp", axis=0, tiled=True, axis_index_groups=peers)
        expert_pack = lax.all_gather(expert_pack, "dp", axis=2, tiled=True, axis_index_groups=peers)
    low_rows = [ln1_gain, ln1_shift, ln2_gain, ln2_shift, out_bias, qv_bias[0], qv_bias[1]]
    small = jnp.concatenate(
        [row.reshape(-1) for row in low_rows]
        + [router_weight.T.reshape(-1), expert_out_bias.reshape(-1), expert_in_bias.reshape(-1)]
    )
    count = small.shape[0]
    tok = pad_images(tokens)
    cot = pad_images(cotangent)
    if cells > 1:
        small_all = lax.all_gather(small, ("dp", "tensor"), axis=0, tiled=False)
        wall, expert_all, cot_all = gather_weights(cells, [packed], expert_pack, cot)
    else:
        block = jnp.pad(small, (0, 2048 - count)).reshape(16, 128)
        wall, small_all, expert_all, cot_all = gather_weights(cells, [packed, block], expert_pack, cot)
        small_all = jnp.swapaxes(small_all, 0, 1).reshape(n_all, 2048)[:, :count]
    lines = 7 + 2 * experts
    lined = small_all[:, : lines * piece].reshape(n_all, lines, piece)
    lined = jnp.swapaxes(lined, 0, 1).reshape(lines, width)
    vec = lined[:8].astype(F32)
    router = lined[7 : 7 + experts]
    down_bias = lax.dynamic_slice_in_dim(lined, 7 + experts + d, 1, 0).astype(F32)
    up_bias = small_all[:, lines * piece :].reshape(n_all, experts, ff_piece)
    up_bias = lax.dynamic_index_in_dim(up_bias, d, 1, keepdims=False).astype(F32)
    up_bias = up_bias.reshape(4, 1, ff_slice)
    biases = vec[5:7].reshape(2, 4, head_cols)
    qkv_bias = jnp.concatenate([biases[0], jnp.zeros_like(biases[0]), biases[1]], axis=1)[:, None, :]
    wall = wall.reshape(4, width, -1)

    ids, places = expert_ids, expert_slots
    labels = jnp.arange(experts, dtype=jnp.int32)
    table = jnp.where(
        ids[:, 0:1] == labels, places[:, 0:1], jnp.where(ids[:, 1:2] == labels, places[:, 1:2], -1)
    )
    table = pad_images(table, -1)
    rows = tok.shape[0]
    table = table.reshape(4, rows, experts)
    table_t = jnp.swapaxes(table, 1, 2)
    t = lax.axis_index("tensor")
    table_own = lax.dynamic_index_in_dim(table_t, t, 0, keepdims=False)

    limit = pltpu.CompilerParams(vmem_limit_bytes=VMEM_LIMIT)
    second, hidden, probs, qkv, mixed = pl.pallas_call(
        attention_kernel,
        out_shape=[
            jax.ShapeDtypeStruct((rows, width), BF),
            jax.ShapeDtypeStruct((rows, width), F32),
            jax.ShapeDtypeStruct((experts, rows), F32),
            jax.ShapeDtypeStruct((4, rows, 3 * head_cols), BF),
            jax.ShapeDtypeStruct((4, rows, head_cols), BF),
        ],
        in_specs=[VM] * 5,
        out_specs=[VM] * 5,
        scratch_shapes=[pltpu.VMEM((rows, width), F32)],
        compiler_params=limit,
        name="attention",
    )(tok, vec, qkv_bias, router, wall)

    dma = pltpu.SemaphoreType.DMA
    slot_shape = jax.ShapeDtypeStruct((2, CAP_PAD, width), BF)
    x_rows, g_rows, probs_all = pl.pallas_call(
        functools.partial(dispatch_kernel, cells),
        out_shape=[slot_shape, slot_shape, jax.ShapeDtypeStruct((4, experts, rows), F32)],
        in_specs=[VM] * 4,
        out_specs=[HB, HB, VM],
        scratch_shapes=[
            pltpu.VMEM((4, rows, width), BF),
            pltpu.VMEM((2, CAP_PAD, width), BF),
            pltpu.VMEM((2, CAP_PAD, width), BF),
            pltpu.VMEM((2, CAP_PAD, width), BF),
            dma((2, 3)), dma((2, 3)), dma((2, 2)), dma((2, 2)), dma((2,)),
        ],
        compiler_params=pltpu.CompilerParams(
            collective_id=1, has_side_effects=True, vmem_limit_bytes=VMEM_LIMIT
        ),
        name="dispatch",
    )(second, probs, table_t, cot_all)

    slots = 2 * CAP_PAD
    fixed = pl.BlockSpec((slots, width), lambda i: (0, 0))
    y_rows, b_rows, q_rows, expert_grad, up_grad, down_grad = pl.pallas_call(
        expert_kernel,
        out_shape=[
            jax.ShapeDtypeStruct((slots, width), BF),
            jax.ShapeDtypeStruct((slots, width), BF),
            jax.ShapeDtypeStruct((2, 8, CAP_PAD), F32),
            jax.ShapeDtypeStruct(expert_all.shape, BF),
            jax.ShapeDtypeStruct((4, 1, ff_slice), F32),
            jax.ShapeDtypeStruct((1, width), F32),
        ],
        grid=(4,),
        in_specs=[
            fixed,
            fixed,
            pl.BlockSpec((1,) + expert_all.shape[1:], lambda i: (i, 0, 0, 0, 0)),
            pl.BlockSpec((1, 1, ff_slice), lambda i: (i, 0, 0)),
            pl.BlockSpec((1, width), lambda i: (0, 0)),
        ],
        out_specs=[
            fixed,
            fixed,
            pl.BlockSpec((2, 8, CAP_PAD), lambda i: (0, 0, 0)),
            pl.BlockSpec((1,) + expert_all.shape[1:], lambda i: (i, 0, 0, 0, 0)),
            pl.BlockSpec((1, 1, ff_slice), lambda i: (i, 0, 0)),
            pl.BlockSpec((1, width), lambda i: (0, 0)),
        ],
        scratch_shapes=[
            pltpu.VMEM((slots, width), F32),
            pltpu.VMEM((slots, width), F32),
            pltpu.VMEM((width, slots), BF),
            pltpu.VMEM((width, slots), BF),
            pltpu.VMEM((slots, ff_slice), BF),
            pltpu.VMEM((slots, ff_slice), BF),
        ],
        compiler_params=limit,
        name="experts",
    )(x_rows.reshape(slots, width), g_rows.reshape(slots, width), expert_all, up_bias, down_bias)

    r_rows, m_rows, q_all = pl.pallas_call(
        functools.partial(combine_kernel, cells),
        out_shape=[
            jax.ShapeDtypeStruct((rows, width), F32),
            jax.ShapeDtypeStruct((rows, width), F32),
            jax.ShapeDtypeStruct((8, 8, CAP_PAD), F32),
        ],
        in_specs=[HB, HB, HB, VM, VM],
        out_specs=[VM, VM, VM],
        scratch_shapes=[
            pltpu.VMEM((2, CAP_PAD, width), BF),
            pltpu.VMEM((2, CAP_PAD, width), BF),
            pltpu.VMEM((2, 2, rows, width), BF),
            pltpu.VMEM((2, 2, rows, width), BF),
            pltpu.VMEM((2, rows, width), BF),
            pltpu.VMEM((2, rows, width), BF),
            dma((2, 2)), dma((2, 2)), dma((2, 4)), dma((8,)), dma((2,)), dma((2,)), dma((1,)), dma((1,)), dma((3,)),
        ],
        compiler_params=pltpu.CompilerParams(
            collective_id=2, has_side_effects=True, vmem_limit_bytes=VMEM_LIMIT
        ),
        name="combine",
    )(
        b_rows.reshape(2, CAP_PAD, width),
        y_rows.reshape(2, CAP_PAD, width),
        q_rows,
        table.astype(F32),
        jnp.swapaxes(probs_all, 1, 2),
    )

    out, token_grad, attn_grad, vec_grad, bias_grad = pl.pallas_call(
        backward_kernel,
        out_shape=[
            jax.ShapeDtypeStruct((rows, width), BF),
            jax.ShapeDtypeStruct((rows, width), F32),
            jax.ShapeDtypeStruct(wall.shape, BF),
            jax.ShapeDtypeStruct((16, width), F32),
            jax.ShapeDtypeStruct((4, 8, 3 * head_cols), F32),
        ],
        in_specs=[VM] * 13,
        out_specs=[VM] * 5,
        scratch_shapes=[pltpu.VMEM((rows, width), F32)],
        compiler_params=limit,
        name="backward",
    )(tok, hidden, r_rows, m_rows, cot, probs, q_all, table_own, router, vec, wall, qkv, mixed)

    bias_grad = bias_grad[:, 0].reshape(4, 3, head_cols)
    pair = jnp.stack([bias_grad[:, 0].reshape(-1), bias_grad[:, 2].reshape(-1)], axis=0)
    small_grad = jnp.concatenate([vec_grad[:5], pair, vec_grad[8:16]], axis=0)
    lines = small_grad.shape[0]
    attn_grad = attn_grad.reshape((4, 8, width // 8) + attn_grad.shape[2:])
    if cells > 1:
        expert_out_grad, attn_part = reduce_grads(cells, expert_grad, attn_grad, None)
        expert_sum = lax.psum_scatter(
            expert_out_grad.astype(F32), "dp", scatter_dimension=2, tiled=True, axis_index_groups=peers
        )
        attn_sum = lax.psum_scatter(attn_part, "dp", scatter_dimension=0, tiled=True, axis_index_groups=peers)
        hot = (labels == d).astype(F32)
        whole = lax.psum(
            (small_grad, hot[:, None] * up_grad.reshape(1, -1), hot[:, None] * down_grad), ("dp", "tensor")
        )
        spot = index * 4 + t
        params = lax.dynamic_slice_in_dim(whole[0], spot * piece, piece, 1)
        up_sum = lax.dynamic_slice_in_dim(whole[1], spot * ff_piece, ff_piece, 1)
        down_sum = lax.dynamic_slice_in_dim(whole[2], spot * piece, piece, 1)
    else:
        message = jnp.concatenate(
            [
                jnp.swapaxes(small_grad.reshape(lines, n_all, piece), 0, 1).reshape(n_all, -1),
                up_grad.reshape(n_all, ff_piece),
                down_grad.reshape(n_all, piece),
            ],
            axis=1,
        )
        message = jnp.pad(message, ((0, 0), (0, 1024 - message.shape[1]))).reshape(n_all, 8, 128)
        expert_sum, attn_sum, small_in = reduce_grads(cells, expert_grad, attn_grad, message)
        small_in = jnp.sum(small_in.reshape(8, 4, 1024), axis=1)
        params = jnp.sum(small_in, axis=0)[: lines * piece].reshape(lines, piece)
        up_sum = small_in[:, lines * piece : lines * piece + ff_piece]
        down_sum = small_in[:, lines * piece + ff_piece : lines * piece + ff_piece + piece]
    return (
        drop_pad(out),
        drop_pad(token_grad),
        params[0],
        params[1],
        attn_sum[:, : 3 * head_cols].reshape(-1, 3, head_cols),
        params[5:7],
        attn_sum[:, 3 * head_cols :].T,
        params[4],
        params[2],
        params[3],
        params[7:15].T,
        expert_sum[:, 0].astype(F32),
        up_sum,
        jnp.swapaxes(expert_sum[:, 1], 1, 2).astype(F32),
        down_sum,
    )


def solution(mesh):
    both = ("dp", "tensor")
    return jax.shard_map(
        body,
        mesh=mesh,
        in_specs=(
            P(both, None),
            P(both),
            P(both),
            P("dp", None, "tensor"),
            P(None, both),
            P("tensor", "dp"),
            P(both),
            P(both),
            P(both),
            P(both, None),
            P(None, "dp", "tensor"),
            P(None, both),
            P(None, "tensor", "dp"),
            P(None, both),
            P("dp", None),
            P("dp", None),
            P(both, None),
        ),
        out_specs=(
            P(both, None),
            P(both, None),
            P(both),
            P(both),
            P("dp", None, "tensor"),
            P(None, both),
            P("tensor", "dp"),
            P(both),
            P(both),
            P(both),
            P(both, None),
            P(None, "dp", "tensor"),
            P(None, both),
            P(None, "tensor", "dp"),
            P(None, both),
        ),
        check_vma=False,
    )
```

```python
import functools

import jax
import jax.numpy as jnp
from jax import lax
from jax.experimental import pallas as pl
from jax.experimental.pallas import tpu as pltpu
from jax.sharding import PartitionSpec as P

HEAD_DIM = 64
SEQ = 197
SEQ_PAD = 208
TOP = 2
QUARTER = 160
SLOTS = 8 * QUARTER
EPS = 1e-6
BF = jnp.bfloat16
F32 = jnp.float32
MESH = pl.DeviceIdType.MESH
VMEM_LIMIT = 60 * 1024 * 1024
VM = pl.BlockSpec(memory_space=pltpu.VMEM)
HB = pl.BlockSpec(memory_space=pl.ANY)


def nn(a, b):
    return lax.dot_general(a, b, (((1,), (0,)), ((), ())), preferred_element_type=F32)


def nt(a, b):
    return lax.dot_general(a, b, (((1,), (1,)), ((), ())), preferred_element_type=F32)


def tn(a, b):
    return lax.dot_general(a, b, (((0,), (0,)), ((), ())), preferred_element_type=F32)


def unit_norm(rows):
    centred = rows - jnp.mean(rows, axis=-1, keepdims=True)
    inv = lax.rsqrt(jnp.mean(centred * centred, axis=-1, keepdims=True) + EPS)
    return centred * inv, inv


def place(cells):
    index = lax.axis_index("dp")
    return lax.div(index, cells), lax.rem(index, cells), lax.axis_index("tensor")


def tensor_peers(t):
    core = t + 1 - 2 * lax.rem(t, 2)
    side = lax.rem(t + 2, 4)
    return core, side, lax.rem(core + 2, 4)


def remote(src, dst, send, recv, device):
    return pltpu.make_async_remote_copy(
        src_ref=src, dst_ref=dst, send_sem=send, recv_sem=recv, device_id=device, device_id_type=MESH
    )


def signal(barrier, device):
    pl.semaphore_signal(barrier, inc=1, device_id=device, device_id_type=MESH)


def softmax_rows(q, k):
    scores = nt(q, k) * (HEAD_DIM**-0.5)
    lane = lax.broadcasted_iota(jnp.int32, scores.shape, 1)
    scores = jnp.where(lane < SEQ, scores, -1e30)
    raised = jnp.exp(scores - jnp.max(scores, axis=-1, keepdims=True))
    return raised / jnp.sum(raised, axis=-1, keepdims=True)


def front_kernel(
    cells,
    packed, small_a, small_b, expert, tok, cot, cols, ids,
    hidden_out, probs_out, gates_all, qkv_out, mixed_out, vec_out, wall, b_all, expert_all, x_out, g_out,
    small_all, cot_all, sec_all, x_buf, g_buf, raw, acc, gates, qkv_bias,
    dp_s, dp_r, y_s, y_r, c_s, c_r, f_s, f_r, own, ag_s, ag_r, x_s, x_r,
):
    d, cell, t = place(cells)
    core, side, far = tensor_peers(t)
    here = d * cells + cell
    rows = tok.shape[0]
    srcs = (small_a, packed, small_b, expert)

    def at_dp(k):
        return (lax.rem(d + k, 8) * cells + cell, t)

    def spot(a, tt, s):
        return small_all.at[s, tt] if a == 0 else (None, wall, b_all, expert_all)[a].at[tt, s]

    barrier = pltpu.get_barrier_semaphore()
    for k in range(1, 8):
        signal(barrier, at_dp(k))
    signal(barrier, (here, core))
    signal(barrier, (here, side))
    pl.semaphore_wait(barrier, 9)

    mine = [
        pltpu.make_async_copy(srcs[a].at[d] if a == 3 else srcs[a], spot(a, t, d), own.at[a]) for a in range(4)
    ]
    dp_copies = [
        [
            remote(
                srcs[a].at[lax.rem(d + k, 8)] if a == 3 else srcs[a],
                spot(a, t, d),
                dp_s.at[a, k],
                dp_r.at[a, k],
                at_dp(k),
            )
            for k in range(1, 8)
        ]
        for a in range(4)
    ]
    side_copies = [[None] * 8 for _ in range(4)]
    near_copies = [[None] * 8 for _ in range(4)]
    far_copies = [[None] * 8 for _ in range(4)]

    def launch(a):
        mine[a].start()
        for copy in dp_copies[a]:
            copy.start()

    def spread(a):
        for k in range(8):
            s = lax.rem(d + 8 - k, 8)
            block = spot(a, t, s)
            if k == 0:
                mine[a].wait()
            else:
                dp_copies[a][k - 1].wait_recv()
            side_copies[a][k] = remote(block, block, y_s.at[a, k], y_r.at[a, k], (here, side))
            side_copies[a][k].start()
            near_copies[a][k] = remote(block, block, c_s.at[a, k], c_r.at[a, k], (here, core))
            near_copies[a][k].start()

    def forward(a):
        for k in range(8):
            block = spot(a, side, lax.rem(d + 8 - k, 8))
            side_copies[a][k].wait_recv()
            far_copies[a][k] = remote(block, block, f_s.at[a, k], f_r.at[a, k], (here, core))
            far_copies[a][k].start()

    def arrive(copies):
        for copy in copies:
            copy.wait_recv()

    def exchange(n, src, dst):
        over = remote(src, dst.at[t], ag_s.at[n, 0], ag_r.at[n, 0], (here, side))
        near = remote(src, dst.at[t], ag_s.at[n, 1], ag_r.at[n, 1], (here, core))
        over.start()
        near.start()
        return over, near

    def pass_on(n, pair, dst):
        pair[0].wait_recv()
        along = remote(dst.at[side], dst.at[side], ag_s.at[n, 2], ag_r.at[n, 2], (here, core))
        along.start()
        return pair + (along,)

    launch(0)
    launch(1)
    cot_pair = exchange(0, cot, cot_all)
    cot_all[t] = cot[...]
    spread(0)
    forward(0)
    arrive(near_copies[0])
    arrive(far_copies[0])
    columns = small_all[...].reshape(-1, 128)
    vec = columns.T[:32]
    vec_out[...] = vec
    heads = qkv_out.shape[2] // 3
    for tt in range(4):
        cut = slice(tt * heads, (tt + 1) * heads)
        qkv_bias[tt] = jnp.concatenate([vec[5:6, cut], jnp.zeros((1, heads), F32), vec[6:7, cut]], axis=1)
    inputs = tok[...].astype(F32)
    unit, _ = unit_norm(inputs)
    first = (unit * vec[0:1] + vec[1:2]).astype(BF)
    acc[...] = inputs + vec[4:5]

    def attend(tt):
        weights = wall[tt].reshape(8 * packed.shape[0], -1)
        qkv = (nn(first, weights[:, : 3 * heads]) + qkv_bias[tt]).astype(BF)
        qkv_out[tt] = qkv
        mixed = []
        for i in range(rows // SEQ_PAD):
            part = qkv[i * SEQ_PAD : (i + 1) * SEQ_PAD]
            sides = []
            for h in range(heads // HEAD_DIM):
                q, k, v = (part[:, j * heads + h * HEAD_DIM : j * heads + (h + 1) * HEAD_DIM] for j in range(3))
                sides.append(nn(softmax_rows(q, k).astype(BF), v).astype(BF))
            mixed.append(jnp.concatenate(sides, axis=1))
        mixed = jnp.concatenate(mixed, axis=0)
        mixed_out[tt] = mixed
        acc[...] += nt(mixed, weights[:, 3 * heads :])

    spread(1)
    launch(3)
    launch(2)
    cot_pair = pass_on(0, cot_pair, cot_all)
    attend(t)
    forward(1)
    attend(side)
    arrive(near_copies[1])
    attend(core)
    arrive(far_copies[1])
    attend(far)

    hidden = acc[...]
    hidden_out[...] = hidden
    unit, _ = unit_norm(hidden)
    second = (unit * vec[2:3] + vec[3:4]).astype(BF)
    sec_all[t] = second
    sec_pair = exchange(1, sec_all.at[t], sec_all)
    logits = nt(vec[7:15].astype(BF), second)
    raised = jnp.exp(logits - jnp.max(logits, axis=0, keepdims=True))
    probs = raised / jnp.sum(raised, axis=0, keepdims=True)
    probs_out[...] = probs
    lane = lax.broadcasted_iota(jnp.int32, probs.shape, 0)
    picked = [jnp.sum(jnp.where(lane == ids[k : k + 1], probs, 0.0), axis=0, keepdims=True) for k in range(2)]
    gates[...] = jnp.concatenate(picked + [jnp.zeros((6, rows), F32)], axis=0)
    gates_all[t] = gates[...]
    gate_pair = exchange(2, gates, gates_all)

    pair_rows = 2 * QUARTER

    def onehots(tt, base):
        at = lax.broadcasted_iota(jnp.int32, (pair_rows, rows), 0) + base
        return at == cols[tt, 0:1], at == cols[tt, 1:2]

    def pick(base, source):
        total = None
        for tt in range(4):
            one, two = onehots(tt, base)
            part = nn(jnp.logical_or(one, two).astype(F32).astype(BF), source[tt])
            total = part if total is None else total + part
        return total.astype(BF)

    def chunk(i):
        c = lax.rem(lax.div(d, 2) + 1 + i, 4)
        return c, pl.multiple_of(c * pair_rows, pair_rows)

    arrive([cot_pair[1], cot_pair[2]])
    for i in range(4):
        c, base = chunk(i)
        raw[pl.ds(base, pair_rows)] = pick(base, cot_all)
    sec_pair = pass_on(1, sec_pair, sec_all)
    gate_pair = pass_on(2, gate_pair, gates_all)
    arrive([sec_pair[1], sec_pair[2], gate_pair[1], gate_pair[2]])

    sent = []

    def post(n, i, buf, out):
        c, base = chunk(i)
        for h in range(2):
            e = 2 * c + h
            block = buf.at[pl.ds(pl.multiple_of(base + h * QUARTER, QUARTER), QUARTER)]
            copy = remote(block, out.at[d], x_s.at[n, e], x_r.at[n, d], (e * cells + cell, t))
            keep = pltpu.make_async_copy(block, out.at[d], own.at[4 + n])
            sent.append((e, copy, keep))

            @pl.when(e == d)
            def _():
                keep.start()

            @pl.when(e != d)
            def _():
                copy.start()

    for i in range(4):
        c, base = chunk(i)
        x_buf[pl.ds(base, pair_rows)] = pick(base, sec_all)
        post(0, i, x_buf, x_out)
    for i in range(4):
        c, base = chunk(i)
        gate = None
        for tt in range(4):
            one, two = onehots(tt, base)
            part = jnp.where(one, gates_all[tt, 0:1], jnp.where(two, gates_all[tt, 1:2], 0.0))
            part = jnp.sum(part, axis=1, keepdims=True)
            gate = part if gate is None else gate + part
        here_rows = pl.ds(base, pair_rows)
        g_buf[here_rows] = (gate * raw[here_rows].astype(F32)).astype(BF)
        post(1, i, g_buf, g_out)

    spread(3)
    spread(2)
    forward(3)
    forward(2)
    for a in (2, 3):
        arrive(near_copies[a])
        arrive(far_copies[a])
    for n, (buf, out) in enumerate(((x_buf, x_out), (g_buf, g_out))):
        for k in range(1, 8):
            g = lax.rem(d + 8 - k, 8)
            remote(buf.at[pl.ds(0, QUARTER)], out.at[g], x_s.at[n, g], x_r.at[n, g], at_dp(8 - k)).wait_recv()
    for e, copy, keep in sent:

        @pl.when(e == d)
        def _():
            keep.wait()

        @pl.when(e != d)
        def _():
            copy.wait_send()

    for a in range(4):
        for copy in dp_copies[a] + side_copies[a] + near_copies[a] + far_copies[a]:
            copy.wait_send()
    for trio in (cot_pair, sec_pair, gate_pair):
        for copy in trio:
            copy.wait_send()


def gelu_both(x):
    phi = 0.5 * (1.0 + lax.erf(x * (0.5**0.5)))
    slope = phi + x * (jnp.exp(-0.5 * x * x) * 0.3989422804014327)
    return x * phi, slope


def middle_kernel(
    cells,
    x_ref, g_ref, expert_all, up_bias, vec, cols, gates,
    r_out, m_out, q_out, grad_out, dup_out, ddown_out,
    w_buf, act_buf, pre_buf, x_turned, g_turned, y_acc, b_acc, y_buf, b_buf, q_buf, y_in, b_in, q_in,
    blocks, core_in, side_buf, side_in, q_blocks, q_core, q_side, q_mid,
    load, store, a_s, a_r, q_s, q_r, c_s, c_r, y_s, y_r, own,
):
    d, cell, t = place(cells)
    core, side, far = tensor_peers(t)
    here = d * cells + cell
    width = x_ref.shape[1]
    ff = act_buf.shape[2]
    pair_rows = 2 * QUARTER

    def at_dp(k):
        return (lax.rem(d + k, 8) * cells + cell, t)

    loads = [pltpu.make_async_copy(expert_all.at[tt], w_buf.at[tt], load.at[tt]) for tt in range(4)]
    for copy in loads:
        copy.start()
    barrier = pltpu.get_barrier_semaphore()
    for k in range(1, 8):
        signal(barrier, at_dp(k))
    signal(barrier, (here, core))
    signal(barrier, (here, side))
    pl.semaphore_wait(barrier, 9)

    x_turned[...] = x_ref[...].T
    g_turned[...] = g_ref[...].T
    ddown_out[...] = jnp.sum(g_ref[...].astype(F32), axis=0, keepdims=True)
    dup_out[...] = jnp.zeros_like(dup_out)
    for copy in loads:
        copy.wait()

    def weights(tt):
        return w_buf[tt, :, 0].reshape(width, ff), w_buf[tt, :, 1].reshape(width, ff)

    sent = []

    def post(n, c, buf, out):
        for h in range(2):
            g = 2 * c + h
            block = buf.at[g]
            copy = remote(block, out.at[d], a_s.at[n, g], a_r.at[n, d], (g * cells + cell, t))
            keep = pltpu.make_async_copy(block, out.at[d], own.at[n])
            sent.append((g, copy, keep))

            @pl.when(g == d)
            def _():
                keep.start()

            @pl.when(g != d)
            def _():
                copy.start()

    ones = jnp.ones((8, width), BF)
    for i in range(4):
        c = lax.rem(lax.div(d, 2) + 1 + i, 4)
        rows = pl.ds(pl.multiple_of(c * pair_rows, pair_rows), pair_rows)
        y_acc[...] = jnp.broadcast_to(vec[pl.ds(15 + d, 1)], y_acc.shape)
        b_acc[...] = jnp.zeros_like(b_acc)

        def slice_step(tt, carry):
            w_in, w_out = weights(tt)
            pre = nn(x_ref[rows], w_in) + up_bias[tt]
            act, slope = gelu_both(pre)
            act = act.astype(BF)
            act_buf[tt, rows] = act
            pre_grad = (nn(g_ref[rows], w_out) * slope).astype(BF)
            pre_buf[tt, rows] = pre_grad
            y_acc[...] += nt(act, w_out)
            b_acc[...] += nt(pre_grad, w_in)
            dup_out[tt] += jnp.sum(pre_grad.astype(F32), axis=0, keepdims=True)
            return carry

        lax.fori_loop(0, 4, slice_step, 0)
        y = y_acc[...]
        pair = pl.ds(2 * c, 2)
        b_buf[pair] = b_acc[...].astype(BF).reshape(2, QUARTER, width)
        y_buf[pair] = y.astype(BF).reshape(2, QUARTER, width)
        post(0, c, b_buf, b_in)
        z = y * g_ref[rows].astype(F32)
        high = z.astype(BF)
        low = (z - high.astype(F32)).astype(BF)
        for h in range(2):
            part = slice(h * QUARTER, (h + 1) * QUARTER)
            q_buf[2 * c + h] = nt(ones, high[part]) + nt(ones, low[part])
        post(2, c, q_buf, q_in)
    for i in range(4):
        post(1, lax.rem(lax.div(d, 2) + 1 + i, 4), y_buf, y_in)

    def grad_slice(tt, carry):
        def grad_rows(n, inner):
            span = pl.ds(pl.multiple_of(n * 192, 192), 192)
            pair = pl.ds(2 * n, 2)
            w_buf[tt, pair, 0] = nn(x_turned[span], pre_buf[tt]).astype(BF).reshape(2, width // 8, ff)
            w_buf[tt, pair, 1] = nn(g_turned[span], act_buf[tt]).astype(BF).reshape(2, width // 8, ff)
            return inner

        lax.fori_loop(0, width // 192, grad_rows, 0)
        return carry

    lax.fori_loop(0, 4, grad_slice, 0)
    stores = [pltpu.make_async_copy(w_buf.at[tt], grad_out.at[tt], store.at[tt]) for tt in range(4)]
    for copy in stores:
        copy.start()

    def landed(n, buf, out):
        for k in range(1, 8):
            e = lax.rem(d + 8 - k, 8)
            remote(buf.at[0], out.at[e], a_s.at[n, e], a_r.at[n, e], at_dp(8 - k)).wait_recv()

    def own_landed(n, buf, out):
        pltpu.make_async_copy(buf.at[d], out.at[d], own.at[n]).wait()

    def onehots(tt):
        at = lax.broadcasted_iota(jnp.int32, (cols.shape[1], SLOTS), 1)
        return at == cols[tt, :, 0:1], at == cols[tt, :, 1:2]

    landed(0, b_buf, b_in)
    own_landed(0, b_buf, b_in)
    landed(2, q_buf, q_in)
    own_landed(2, q_buf, q_in)
    q_line = jnp.concatenate([q_in[e] for e in range(8)], axis=1)
    owner = jnp.concatenate([jnp.full((8, QUARTER), e, jnp.int32) for e in range(8)], axis=1)
    q_line = jnp.where(lax.broadcasted_iota(jnp.int32, q_line.shape, 0) == owner, q_line, 0.0)
    q_high = q_line.astype(BF)
    q_both = jnp.concatenate([q_high, (q_line - q_high.astype(F32)).astype(BF)], axis=0)
    b_rows = b_in[...].reshape(SLOTS, width)

    def back_block(tt):
        one, two = onehots(tt)
        hot = jnp.logical_or(one, two).astype(F32).astype(BF)
        q = nt(q_both, hot)
        return nn(hot, b_rows), q[0:8] + q[8:16]

    def out_block(tt):
        one, two = onehots(tt)
        hot = jnp.where(one, gates[tt, :, 0:1], jnp.where(two, gates[tt, :, 1:2], 0.0)).astype(BF)
        return nn(hot, y_in[...].reshape(SLOTS, width))

    def core_send(n, i, src, dst):
        copy = remote(src.at[i], dst.at[i], c_s.at[n, i], c_r.at[n, i], (here, core))
        copy.start()
        return copy

    def side_send(n, src, dst):
        copy = remote(src, dst, y_s.at[n], y_r.at[n], (here, side))
        copy.start()
        return copy

    core_b, core_q = [], []
    for i, tt in enumerate((far, core)):
        total, q = back_block(tt)
        blocks[i] = total.astype(BF)
        q_blocks[i] = q
        core_b.append(core_send(0, i, blocks, core_in.at[0]))
        core_q.append(core_send(2, i, q_blocks, q_core))
    total, q = back_block(side)
    core_b[0].wait_recv()
    core_q[0].wait_recv()
    side_buf[...] = (total + core_in[0, 0].astype(F32)).astype(BF)
    q_mid[...] = q + q_core[0]
    side_b = side_send(0, side_buf, side_in.at[0])
    side_q = side_send(2, q_mid, q_side)
    total, q = back_block(t)
    core_b[1].wait_recv()
    core_q[1].wait_recv()
    r_out[...] = total + core_in[0, 1].astype(F32)
    q_out[...] = q + q_core[1]

    landed(1, y_buf, y_in)
    own_landed(1, y_buf, y_in)
    core_y = []
    for i, tt in enumerate((far, core)):
        core_b[i].wait_send()
        blocks[i] = out_block(tt).astype(BF)
        core_y.append(core_send(1, i, blocks, core_in.at[1]))
    total = out_block(side)
    core_y[0].wait_recv()
    side_b.wait_send()
    side_buf[...] = (total + core_in[1, 0].astype(F32)).astype(BF)
    side_y = side_send(1, side_buf, side_in.at[1])
    total = out_block(t)
    core_y[1].wait_recv()
    total = total + core_in[1, 1].astype(F32)
    side_b.wait_recv()
    side_q.wait_recv()
    r_out[...] += side_in[0].astype(F32)
    q_out[...] += q_side[...]
    side_y.wait_recv()
    m_out[...] = total + side_in[1].astype(F32)

    for copy in core_q + core_y + [side_q, side_y]:
        copy.wait_send()
    for g, copy, keep in sent:

        @pl.when(g != d)
        def _():
            copy.wait_send()

    for copy in stores:
        copy.wait()


def back_kernel(
    cells,
    tok, hid, r_ref, m_ref, cot, probs, picked_ref, vec, wall, qkv_ref, mixed_ref, e_src, bias_msg,
    out, token_grad, e_out, a_out, msg_all, vec_all,
    n1, vec_grad, vec_msg, a_grad, qv_grad,
    e_core, a_core, e_own, e_mid, a_mid, e_side, a_side, e_fin, a_fin, a_in,
    c_s, c_r, y_s, y_r, z_s, z_r, own, m_s, m_r, v_s, v_r,
):
    d, cell, t = place(cells)
    core, side, far = tensor_peers(t)
    here = d * cells + cell
    heads = qkv_ref.shape[2] // 3
    rows = tok.shape[0]
    width = tok.shape[1]
    spot = d * 4 + t

    def at_dp(k):
        return (lax.rem(d + k, 8) * cells + cell, t)

    others = [(k, m) for k in range(8) for m in range(4) if k or m]

    def other(k, m):
        return lax.rem(d + k, 8), lax.rem(t + m, 4)

    barrier = pltpu.get_barrier_semaphore()
    for k, m in others:
        dd, tt = other(k, m)
        signal(barrier, (dd * cells + cell, tt))
    pl.semaphore_wait(barrier, 31)

    waits = []
    first = []
    for i, tt in enumerate((far, core)):
        copy = remote(e_src.at[tt], e_core.at[i], c_s.at[0, i], c_r.at[0, i], (here, core))
        copy.start()
        first.append(copy)
    keeps = []
    for i, tt in enumerate((side, t)):
        copy = pltpu.make_async_copy(e_src.at[tt], e_own.at[i], own.at[i])
        copy.start()
        keeps.append(copy)
    for n, (k, m) in enumerate(others):
        dd, tt = other(k, m)
        copy = remote(bias_msg.at[dd * 4 + tt], msg_all.at[spot], m_s.at[n], m_r.at[n], (dd * cells + cell, tt))
        copy.start()
        waits.append(copy)
    msg_own = pltpu.make_async_copy(bias_msg.at[spot], msg_all.at[spot], own.at[2])
    msg_own.start()

    hidden = hid[...]
    out[...] = (hidden + m_ref[...]).astype(BF)
    picked = picked_ref[...]
    logit = picked - probs[...] * jnp.sum(picked, axis=0, keepdims=True)
    high = logit.astype(BF)
    both = jnp.concatenate([high, (logit - high.astype(F32)).astype(BF)], axis=0)
    unit, inv = unit_norm(hidden)
    gain = vec[2:3]
    second = (unit * gain + vec[3:4]).astype(BF)
    router_grad = nn(both, second)
    vec_grad[...] = jnp.zeros_like(vec_grad)
    vec_grad[8:16] = router_grad[0:8] + router_grad[8:16]
    table = vec[7:15].astype(BF)
    n2 = r_ref[...] + tn(both, jnp.concatenate([table, table], axis=0))
    vec_grad[2:3] = jnp.sum(n2 * unit, axis=0, keepdims=True)
    vec_grad[3:4] = jnp.sum(n2, axis=0, keepdims=True)
    scaled = n2 * gain
    back = inv * (
        scaled
        - jnp.mean(scaled, axis=-1, keepdims=True)
        - unit * jnp.mean(scaled * unit, axis=-1, keepdims=True)
    )
    hidden_grad = cot[...].astype(F32) + back
    token_grad[...] = hidden_grad
    branch = hidden_grad.astype(BF)
    vec_grad[4:5] = jnp.sum(branch.astype(F32), axis=0, keepdims=True)
    unit1, inv1 = unit_norm(tok[...].astype(F32))
    first_norm = (unit1 * vec[0:1] + vec[1:2]).astype(BF)
    n1[...] = jnp.zeros_like(n1)

    second_e = {}
    keeps[0].wait()
    first[0].wait_recv()
    for k in range(1, 9):
        p = lax.rem(d + k, 8)
        e_mid[p] = (e_own[0, p].astype(F32) + e_core[0, p].astype(F32)).astype(BF)
        copy = remote(e_mid.at[p], e_side.at[p], y_s.at[0, k - 1], y_r.at[0, k - 1], (here, side))
        copy.start()
        second_e[k] = copy
    keeps[1].wait()
    first[1].wait_recv()

    def finish_expert(k):
        p = lax.rem(d + k, 8)
        second_e[k].wait_recv()
        total = e_own[1, p].astype(F32) + e_core[1, p].astype(F32) + e_side[p].astype(F32)
        e_fin[p] = total.astype(BF)
        if k < 8:
            copy = remote(e_fin.at[p], e_out.at[d], z_s.at[0, k], z_r.at[0, k], at_dp(k))
            copy.start()
            waits.append(copy)

    def attend_back(tt):
        weights = wall[tt].reshape(width, -1)
        qkv = qkv_ref[tt]
        mixed_grad = nn(branch, weights[:, 3 * heads :]).astype(BF)
        triple = []
        for i in range(rows // SEQ_PAD):
            span = slice(i * SEQ_PAD, (i + 1) * SEQ_PAD)
            part, grad = qkv[span], mixed_grad[span]
            sides = [[], [], []]
            for h in range(heads // HEAD_DIM):
                q, k, v = (part[:, j * heads + h * HEAD_DIM : j * heads + (h + 1) * HEAD_DIM] for j in range(3))
                g = grad[:, h * HEAD_DIM : (h + 1) * HEAD_DIM]
                w = softmax_rows(q, k)
                w_grad = nt(g, v)
                s_grad = (w * (w_grad - jnp.sum(w * w_grad, axis=-1, keepdims=True))).astype(BF)
                sides[0].append((nn(s_grad, k) * (HEAD_DIM**-0.5)).astype(BF))
                sides[1].append((tn(s_grad, q) * (HEAD_DIM**-0.5)).astype(BF))
                sides[2].append(tn(w.astype(BF), g).astype(BF))
            triple.append(jnp.concatenate(sides[0] + sides[1] + sides[2], axis=1))
        triple = jnp.concatenate(triple, axis=0)
        grad = jnp.concatenate([tn(first_norm, triple), tn(branch, mixed_ref[tt])], axis=1).astype(BF)
        a_grad[tt] = grad.reshape(8, width // 8, -1)
        n1[...] += nt(triple, weights[:, : 3 * heads])
        sums = jnp.sum(triple.astype(F32), axis=0, keepdims=True)
        qv_grad[tt] = sums

    core_a = []
    for i, tt in enumerate((far, core)):
        attend_back(tt)
        copy = remote(a_grad.at[tt], a_core.at[i], c_s.at[1, i], c_r.at[1, i], (here, core))
        copy.start()
        core_a.append(copy)
        finish_expert(2 * i + 1)
        finish_expert(2 * i + 2)
    attend_back(side)
    core_a[0].wait_recv()
    second_a = {}
    for k in range(1, 9):
        p = lax.rem(d + k, 8)
        a_mid[p] = (a_grad[side, p].astype(F32) + a_core[0, p].astype(F32)).astype(BF)
        copy = remote(a_mid.at[p], a_side.at[p], y_s.at[1, k - 1], y_r.at[1, k - 1], (here, side))
        copy.start()
        second_a[k] = copy
    finish_expert(5)
    finish_expert(6)
    attend_back(t)
    finish_expert(7)
    finish_expert(8)
    e_keep = pltpu.make_async_copy(e_fin.at[d], e_out.at[d], own.at[3])
    e_keep.start()
    core_a[1].wait_recv()
    for k in range(1, 9):
        p = lax.rem(d + k, 8)
        second_a[k].wait_recv()
        total = a_grad[t, p].astype(F32) + a_core[1, p].astype(F32) + a_side[p].astype(F32)
        if k < 8:
            a_fin[p] = total.astype(BF)
            copy = remote(a_fin.at[p], a_in.at[d], z_s.at[1, k], z_r.at[1, k], at_dp(k))
            copy.start()
            waits.append(copy)
        else:
            a_out[...] = total

    grad = n1[...]
    vec_grad[0:1] = jnp.sum(grad * unit1, axis=0, keepdims=True)
    vec_grad[1:2] = jnp.sum(grad, axis=0, keepdims=True)
    for j, row in ((0, 5), (2, 6)):
        parts = [qv_grad[tt][:, j * heads : (j + 1) * heads] for tt in range(4)]
        vec_grad[row : row + 1] = jnp.concatenate(parts, axis=1)
    turned = vec_grad[...].T
    vec_msg[...] = turned.reshape(vec_msg.shape)
    for n, (k, m) in enumerate(others):
        dd, tt = other(k, m)
        copy = remote(vec_msg.at[dd * 4 + tt], vec_all.at[spot], v_s.at[n], v_r.at[n], (dd * cells + cell, tt))
        copy.start()
        waits.append(copy)
    vec_all[spot] = vec_msg[spot]
    scaled = grad * vec[0:1]
    token_grad[...] += inv1 * (
        scaled
        - jnp.mean(scaled, axis=-1, keepdims=True)
        - unit1 * jnp.mean(scaled * unit1, axis=-1, keepdims=True)
    )
    for copy in waits:
        copy.wait()
    for k in range(1, 8):
        a_out[...] += a_in[lax.rem(d + k, 8)].astype(F32)
    e_keep.wait()
    msg_own.wait()
    for copy in first + core_a:
        copy.wait_send()
    for k in range(1, 9):
        second_e[k].wait_send()
        second_a[k].wait_send()


def pad_images(rows, fill=0):
    images = rows.reshape((-1, SEQ) + rows.shape[1:])
    spare = [(0, 0), (0, SEQ_PAD - SEQ)] + [(0, 0)] * (rows.ndim - 1)
    return jnp.pad(images, spare, constant_values=fill).reshape((-1,) + rows.shape[1:])


def drop_pad(rows):
    return rows.reshape((-1, SEQ_PAD) + rows.shape[1:])[:, :SEQ].reshape((-1,) + rows.shape[1:])


def body(
    tokens, ln1_gain, ln1_shift, qkv_weight, qv_bias, out_weight, out_bias, ln2_gain, ln2_shift,
    router_weight, expert_in, expert_in_bias, expert_out, expert_out_bias, expert_ids, expert_slots,
    cotangent,
):
    n_dp = lax.axis_size("dp")
    cells = n_dp // 8
    width = tokens.shape[1]
    experts = expert_in.shape[0]
    head_cols = qkv_weight.shape[2]
    ff_slice = expert_in.shape[2]
    index = lax.axis_index("dp")
    t = lax.axis_index("tensor")
    d, cell = index // cells, index % cells
    peers = [[row * cells + c for c in range(cells)] for row in range(8)]

    packed = jnp.concatenate([qkv_weight.reshape(-1, 3 * head_cols), out_weight.T], axis=1)
    expert_pack = jnp.stack([expert_in, jnp.swapaxes(expert_out, 1, 2)], axis=1)
    lines = [ln1_gain, ln1_shift, ln2_gain, ln2_shift, out_bias, qv_bias[0], qv_bias[1]]
    small_a = jnp.concatenate([jnp.stack(lines, axis=1), router_weight, expert_out_bias.T], axis=1)
    small_b = expert_in_bias
    if cells > 1:
        packed = lax.all_gather(packed, "dp", axis=0, tiled=True, axis_index_groups=peers)
        expert_pack = lax.all_gather(expert_pack, "dp", axis=2, tiled=True, axis_index_groups=peers)

        def quarter(piece, axis):
            piece = lax.all_gather(piece, "tensor", axis=axis, tiled=True)
            piece = lax.all_gather(piece, "dp", axis=axis, tiled=True, axis_index_groups=peers)
            size = piece.shape[axis] // 4
            return lax.dynamic_slice_in_dim(piece, t * size, size, axis)

        small_a, small_b = quarter(small_a, 0), quarter(small_b, 1)
    piece, ff_piece = small_a.shape[0], small_b.shape[1]
    small_a = jnp.pad(small_a.astype(F32), ((0, 0), (0, 128 - small_a.shape[1])))
    small_b = jnp.pad(small_b, ((0, 16 - experts), (0, 128 - ff_piece)))
    tok = pad_images(tokens)
    cot = pad_images(cotangent)
    rows = tok.shape[0]

    wanted = expert_slots - QUARTER * t
    inside = jnp.logical_and(expert_slots >= 0, jnp.logical_and(wanted >= 0, wanted < QUARTER))
    cols = jnp.where(inside, expert_ids * QUARTER + wanted, -1)
    cols = jnp.pad(pad_images(cols, -1).reshape(4, rows, TOP), ((0, 0), (0, 0), (0, 8 - TOP)), constant_values=-1)
    cols_t = jnp.swapaxes(cols, 1, 2)
    own_ids = lax.dynamic_slice_in_dim(expert_ids, t * tokens.shape[0], tokens.shape[0], 0)
    ids = jnp.pad(pad_images(own_ids, -1).T, ((0, 8 - TOP), (0, 0)), constant_values=-1)

    dma = pltpu.SemaphoreType.DMA

    def params(identity):
        return pltpu.CompilerParams(
            collective_id=identity, has_side_effects=True, vmem_limit_bytes=VMEM_LIMIT
        )

    def like(shape, dtype=BF):
        return jax.ShapeDtypeStruct(shape, dtype)

    slot_shape = (8, QUARTER, width)
    hidden, probs, gates, qkv, mixed, vec, wall, bias_all, expert_all, x_rows, g_rows = pl.pallas_call(
        functools.partial(front_kernel, cells),
        out_shape=[
            like((rows, width), F32),
            like((experts, rows), F32),
            like((4, 8, rows), F32),
            like((4, rows, 3 * head_cols)),
            like((4, rows, head_cols)),
            like((32, width), F32),
            like((4, 8) + packed.shape),
            like((4, 8) + small_b.shape),
            like((4,) + expert_pack.shape),
            like(slot_shape),
            like(slot_shape),
        ],
        in_specs=[HB] * 4 + [VM] * 4,
        out_specs=[VM] * 7 + [HB] * 4,
        scratch_shapes=[
            pltpu.VMEM((8, 4) + small_a.shape, F32),
            pltpu.VMEM((4, rows, width), BF),
            pltpu.VMEM((4, rows, width), BF),
            pltpu.VMEM((SLOTS, width), BF),
            pltpu.VMEM((SLOTS, width), BF),
            pltpu.VMEM((SLOTS, width), BF),
            pltpu.VMEM((rows, width), F32),
            pltpu.VMEM((8, rows), F32),
            pltpu.VMEM((4, 1, 3 * head_cols), F32),
        ]
        + [dma((4, 8))] * 8
        + [dma((6,)), dma((3, 3)), dma((3, 3)), dma((2, 8)), dma((2, 8))],
        compiler_params=params(0),
        name="front",
    )(packed, small_a, small_b, expert_pack, tok, cot, cols_t, ids)

    bias_all = jnp.swapaxes(bias_all, 0, 1)
    up_bias = lax.dynamic_index_in_dim(bias_all, d, 2, keepdims=False)[:, :, :ff_piece]
    up_bias = up_bias.astype(F32).reshape(4, 1, ff_slice)
    r_rows, m_rows, picked, expert_grad, up_grad, down_grad = pl.pallas_call(
        functools.partial(middle_kernel, cells),
        out_shape=[
            like((rows, width), F32),
            like((rows, width), F32),
            like((8, rows), F32),
            like(expert_all.shape),
            like((4, 1, ff_slice), F32),
            like((1, width), F32),
        ],
        in_specs=[VM, VM, HB, VM, VM, VM, VM],
        out_specs=[VM, VM, VM, HB, VM, VM],
        scratch_shapes=[
            pltpu.VMEM(expert_all.shape, BF),
            pltpu.VMEM((4, SLOTS, ff_slice), BF),
            pltpu.VMEM((4, SLOTS, ff_slice), BF),
            pltpu.VMEM((width, SLOTS), BF),
            pltpu.VMEM((width, SLOTS), BF),
            pltpu.VMEM((2 * QUARTER, width), F32),
            pltpu.VMEM((2 * QUARTER, width), F32),
            pltpu.VMEM(slot_shape, BF),
            pltpu.VMEM(slot_shape, BF),
            pltpu.VMEM((8, 8, QUARTER), F32),
            pltpu.VMEM(slot_shape, BF),
            pltpu.VMEM(slot_shape, BF),
            pltpu.VMEM((8, 8, QUARTER), F32),
            pltpu.VMEM((2, rows, width), BF),
            pltpu.VMEM((2, 2, rows, width), BF),
            pltpu.VMEM((rows, width), BF),
            pltpu.VMEM((2, rows, width), BF),
            pltpu.VMEM((2, 8, rows), F32),
            pltpu.VMEM((2, 8, rows), F32),
            pltpu.VMEM((8, rows), F32),
            pltpu.VMEM((8, rows), F32),
            dma((4,)), dma((4,)), dma((3, 8)), dma((3, 8)), dma((1,)), dma((1,)), dma((3, 2)), dma((3, 2)),
            dma((3,)), dma((3,)), dma((3,)),
        ],
        compiler_params=params(1),
        name="middle",
    )(
        x_rows.reshape(SLOTS, width), g_rows.reshape(SLOTS, width), expert_all, up_bias, vec, cols,
        jnp.swapaxes(gates, 1, 2),
    )

    message = jnp.pad(
        jnp.stack(
            [
                jnp.pad(up_grad.reshape(32, ff_piece), ((0, 0), (0, 128 - ff_piece))),
                jnp.pad(down_grad.reshape(32, piece), ((0, 0), (0, 128 - piece))),
            ],
            axis=1,
        ),
        ((0, 0), (0, 6), (0, 0)),
    )
    e_block, a_block = expert_grad.shape[1:], wall.shape[1:]
    out, token_grad, expert_sum, attn_sum, messages, vec_all = pl.pallas_call(
        functools.partial(back_kernel, cells),
        out_shape=[
            like((rows, width)),
            like((rows, width), F32),
            like(e_block),
            like(a_block[1:], F32),
            like(message.shape, F32),
            like((32, piece, 128), F32),
        ],
        in_specs=[VM] * 11 + [HB, HB],
        out_specs=[VM, VM, HB, VM, HB, VM],
        scratch_shapes=[
            pltpu.VMEM((rows, width), F32),
            pltpu.VMEM((128, width), F32),
            pltpu.VMEM((32, piece, 128), F32),
            pltpu.VMEM(wall.shape, BF),
            pltpu.VMEM((4, 1, 3 * head_cols), F32),
            pltpu.VMEM((2,) + e_block, BF),
            pltpu.VMEM((2,) + a_block, BF),
            pltpu.VMEM((2,) + e_block, BF),
            pltpu.VMEM(e_block, BF),
            pltpu.VMEM(a_block, BF),
            pltpu.VMEM(e_block, BF),
            pltpu.VMEM(a_block, BF),
            pltpu.VMEM(e_block, BF),
            pltpu.VMEM(a_block, BF),
            pltpu.VMEM(a_block, BF),
            dma((2, 2)), dma((2, 2)), dma((2, 8)), dma((2, 8)), dma((2, 8)), dma((2, 8)), dma((4,)),
            dma((31,)), dma((31,)), dma((31,)), dma((31,)),
        ],
        compiler_params=params(2),
        name="back",
    )(tok, hidden, r_rows, m_rows, cot, probs, picked, vec, wall, qkv, mixed, expert_grad, message)

    grads = jnp.sum(vec_all, axis=0).T
    messages = jnp.sum(messages.reshape(8, 4, 8, 128), axis=1)
    up_sum, down_sum = messages[:, 0, :ff_piece], messages[:, 1, :piece]
    if cells > 1:
        expert_sum = lax.psum_scatter(
            expert_sum.astype(F32), "dp", scatter_dimension=2, tiled=True, axis_index_groups=peers
        )
        attn_sum = lax.psum_scatter(attn_sum, "dp", scatter_dimension=0, tiled=True, axis_index_groups=peers)

        def share(part):
            part = lax.psum(part, "dp", axis_index_groups=peers)
            part = lax.all_gather(part, "tensor", axis=1, tiled=True)
            size = part.shape[1] // (4 * cells)
            return lax.dynamic_slice_in_dim(part, (cell * 4 + t) * size, size, 1)

        grads, up_sum, down_sum = share(grads), share(up_sum), share(down_sum)
    return (
        drop_pad(out),
        drop_pad(token_grad),
        grads[0],
        grads[1],
        attn_sum[:, : 3 * head_cols].reshape(-1, 3, head_cols),
        grads[5:7],
        attn_sum[:, 3 * head_cols :].T,
        grads[4],
        grads[2],
        grads[3],
        grads[8:16].T,
        expert_sum[:, 0].astype(F32),
        up_sum,
        jnp.swapaxes(expert_sum[:, 1], 1, 2).astype(F32),
        down_sum,
    )


def solution(mesh):
    both = ("dp", "tensor")
    return jax.shard_map(
        body,
        mesh=mesh,
        in_specs=(
            P(both, None),
            P(both),
            P(both),
            P("dp", None, "tensor"),
            P(None, both),
            P("tensor", "dp"),
            P(both),
            P(both),
            P(both),
            P(both, None),
            P(None, "dp", "tensor"),
            P(None, both),
            P(None, "tensor", "dp"),
            P(None, both),
            P("dp", None),
            P("dp", None),
            P(both, None),
        ),
        out_specs=(
            P(both, None),
            P(both, None),
            P(both),
            P(both),
            P("dp", None, "tensor"),
            P(None, both),
            P("tensor", "dp"),
            P(both),
            P(both),
            P(both),
            P(both, None),
            P(None, "dp", "tensor"),
            P(None, both),
            P(None, "tensor", "dp"),
            P(None, both),
        ),
        check_vma=False,
    )
```

```python
import functools

import jax
import jax.numpy as jnp
from jax import lax
from jax.experimental import pallas as pl
from jax.experimental.pallas import tpu as pltpu
from jax.sharding import PartitionSpec as P

HEAD_DIM = 64
SEQ = 197
SEQ_PAD = 208
TOP = 2
QUARTER = 160
SLOTS = 8 * QUARTER
EARLY = 4
EPS = 1e-6
BF = jnp.bfloat16
F32 = jnp.float32
MESH = pl.DeviceIdType.MESH
VMEM_LIMIT = 60 * 1024 * 1024
VM = pl.BlockSpec(memory_space=pltpu.VMEM)
HB = pl.BlockSpec(memory_space=pl.ANY)


def nn(a, b):
    return lax.dot_general(a, b, (((1,), (0,)), ((), ())), preferred_element_type=F32)


def nt(a, b):
    return lax.dot_general(a, b, (((1,), (1,)), ((), ())), preferred_element_type=F32)


def tn(a, b):
    return lax.dot_general(a, b, (((0,), (0,)), ((), ())), preferred_element_type=F32)


def unit_norm(rows):
    centred = rows - jnp.mean(rows, axis=-1, keepdims=True)
    inv = lax.rsqrt(jnp.mean(centred * centred, axis=-1, keepdims=True) + EPS)
    return centred * inv, inv


def place(cells):
    index = lax.axis_index("dp")
    return lax.div(index, cells), lax.rem(index, cells), lax.axis_index("tensor")


def tensor_peers(t):
    core = t + 1 - 2 * lax.rem(t, 2)
    side = lax.rem(t + 2, 4)
    return core, side, lax.rem(core + 2, 4)


def remote(src, dst, send, recv, device):
    return pltpu.make_async_remote_copy(
        src_ref=src, dst_ref=dst, send_sem=send, recv_sem=recv, device_id=device, device_id_type=MESH
    )


def signal(barrier, device):
    pl.semaphore_signal(barrier, inc=1, device_id=device, device_id_type=MESH)


def softmax_rows(q, k):
    scores = nt(q, k) * (HEAD_DIM**-0.5)
    lane = lax.broadcasted_iota(jnp.int32, scores.shape, 1)
    scores = jnp.where(lane < SEQ, scores, -1e30)
    raised = jnp.exp(scores - jnp.max(scores, axis=-1, keepdims=True))
    return raised / jnp.sum(raised, axis=-1, keepdims=True)


def front_kernel(
    cells,
    packed, small_a, small_b, expert, tok, cot, cols, ids,
    hidden_out, probs_out, gates_all, qkv_out, mixed_out, vec_out, wall, b_all, expert_all, x_out, g_out,
    small_all, cot_all, sec_all, x_buf, raw, acc, gates, qkv_bias,
    dp_s, dp_r, y_s, y_r, c_s, c_r, f_s, f_r, own, ag_s, ag_r, x_s, x_r, w_s, w_r,
):
    d, cell, t = place(cells)
    core, side, far = tensor_peers(t)
    here = d * cells + cell
    twin = d + 1 - 2 * lax.rem(d, 2)
    rows = tok.shape[0]
    srcs = (small_a, packed, small_b, expert)

    def at_dp(k):
        return (lax.rem(d + k, 8) * cells + cell, t)

    def spot(a, tt, s):
        return small_all.at[s, tt] if a == 0 else (None, wall, b_all, expert_all)[a].at[tt, s]

    barrier = pltpu.get_barrier_semaphore()
    for k in range(1, 8):
        signal(barrier, at_dp(k))
    signal(barrier, (here, core))
    signal(barrier, (here, side))
    pl.semaphore_wait(barrier, 9)

    mine = [
        pltpu.make_async_copy(srcs[a].at[d] if a == 3 else srcs[a], spot(a, t, d), own.at[a]) for a in range(4)
    ]
    dp_copies = [
        [
            remote(
                srcs[a].at[lax.rem(d + k, 8)] if a == 3 else srcs[a],
                spot(a, t, d),
                dp_s.at[a, k],
                dp_r.at[a, d if a == 3 else k],
                at_dp(k),
            )
            for k in ((2, 4, 6) if a == 1 else range(1, 8))
        ]
        for a in range(4)
    ]
    side_copies = [[None] * 8 for _ in range(4)]
    near_copies = [[None] * 8 for _ in range(4)]
    far_copies = [[None] * 8 for _ in range(4)]

    cross = [remote(packed, wall.at[t, d], w_s.at[0], w_r.at[0], (twin * cells + cell, t))]

    def launch(a):
        mine[a].start()
        for copy in dp_copies[a]:
            copy.start()
        if a == 1:
            cross[0].start()

    near_z = d + 2 - 4 * lax.rem(lax.div(d, 2), 2)
    near_twin = twin + near_z - d
    by_distance = [d, twin, near_z, near_twin] + [lax.rem(s + 4, 8) for s in (d, twin, near_z, near_twin)]

    def source(a, k):
        if a == 3:
            return by_distance[k]
        if a != 1:
            return lax.rem(d + 8 - k, 8)
        return lax.rem((d if k < 4 else twin) + 8 - 2 * (k % 4), 8)

    def spread(a, first, last):
        for k in range(first, last):
            block = spot(a, t, source(a, k))
            if k == 0:
                mine[a].wait()
            elif a == 3:
                remote(block, block, dp_s.at[a, k], dp_r.at[a, source(a, k)], at_dp(k)).wait_recv()
            elif a != 1 or k < 4:
                dp_copies[a][k - 1].wait_recv()
            else:
                cross[k - 4].wait_recv()
            if a == 1 and 0 < k < 4:
                cross.append(remote(block, block, w_s.at[k], w_r.at[k], (twin * cells + cell, t)))
                cross[k].start()
            side_copies[a][k] = remote(block, block, y_s.at[a, k], y_r.at[a, k], (here, side))
            side_copies[a][k].start()
            near_copies[a][k] = remote(block, block, c_s.at[a, k], c_r.at[a, k], (here, core))
            near_copies[a][k].start()

    def forward(a):
        for k in range(8):
            block = spot(a, side, source(a, k))
            side_copies[a][k].wait_recv()
            far_copies[a][k] = remote(block, block, f_s.at[a, k], f_r.at[a, k], (here, core))
            far_copies[a][k].start()

    def arrive(copies):
        for copy in copies:
            copy.wait_recv()

    def exchange(n, src, dst):
        over = remote(src, dst.at[t], ag_s.at[n, 0], ag_r.at[n, 0], (here, side))
        near = remote(src, dst.at[t], ag_s.at[n, 1], ag_r.at[n, 1], (here, core))
        over.start()
        near.start()
        return over, near

    def pass_on(n, pair, dst):
        pair[0].wait_recv()
        along = remote(dst.at[side], dst.at[side], ag_s.at[n, 2], ag_r.at[n, 2], (here, core))
        along.start()
        return pair + (along,)

    launch(0)
    launch(1)
    cot_pair = exchange(0, cot, cot_all)
    cot_all[t] = cot[...]
    spread(0, 0, 8)
    forward(0)
    arrive(near_copies[0])
    arrive(far_copies[0])
    columns = small_all[...].reshape(-1, 128)
    vec = columns.T[:32]
    vec_out[...] = vec
    heads = qkv_out.shape[2] // 3
    for tt in range(4):
        cut = slice(tt * heads, (tt + 1) * heads)
        qkv_bias[tt] = jnp.concatenate([vec[5:6, cut], jnp.zeros((1, heads), F32), vec[6:7, cut]], axis=1)
    inputs = tok[...].astype(F32)
    unit, _ = unit_norm(inputs)
    first = (unit * vec[0:1] + vec[1:2]).astype(BF)
    acc[...] = inputs + vec[4:5]

    def attend(tt):
        weights = wall[tt].reshape(8 * packed.shape[0], -1)
        qkv = (nn(first, weights[:, : 3 * heads]) + qkv_bias[tt]).astype(BF)
        qkv_out[tt] = qkv
        mixed = []
        for i in range(rows // SEQ_PAD):
            part = qkv[i * SEQ_PAD : (i + 1) * SEQ_PAD]
            sides = []
            for h in range(heads // HEAD_DIM):
                q, k, v = (part[:, j * heads + h * HEAD_DIM : j * heads + (h + 1) * HEAD_DIM] for j in range(3))
                sides.append(nn(softmax_rows(q, k).astype(BF), v).astype(BF))
            mixed.append(jnp.concatenate(sides, axis=1))
        mixed = jnp.concatenate(mixed, axis=0)
        mixed_out[tt] = mixed
        acc[...] += nt(mixed, weights[:, 3 * heads :])

    spread(1, 0, 4)
    launch(3)
    launch(2)
    spread(1, 4, 8)
    cot_pair = pass_on(0, cot_pair, cot_all)
    attend(t)
    forward(1)
    attend(side)
    arrive(near_copies[1])
    attend(core)
    spread(3, 0, 2)
    arrive(far_copies[1])
    attend(far)

    hidden = acc[...]
    hidden_out[...] = hidden
    unit, _ = unit_norm(hidden)
    second = (unit * vec[2:3] + vec[3:4]).astype(BF)
    sec_all[t] = second
    sec_pair = exchange(1, sec_all.at[t], sec_all)
    logits = nt(vec[7:15].astype(BF), second)
    raised = jnp.exp(logits - jnp.max(logits, axis=0, keepdims=True))
    probs = raised / jnp.sum(raised, axis=0, keepdims=True)
    probs_out[...] = probs
    lane = lax.broadcasted_iota(jnp.int32, probs.shape, 0)
    picked = [jnp.sum(jnp.where(lane == ids[k : k + 1], probs, 0.0), axis=0, keepdims=True) for k in range(2)]
    gates[...] = jnp.concatenate(picked + [jnp.zeros((6, rows), F32)], axis=0)
    gates_all[t] = gates[...]
    gate_pair = exchange(2, gates, gates_all)

    pair_rows = 2 * QUARTER

    def onehots(tt, base):
        at = lax.broadcasted_iota(jnp.int32, (pair_rows, rows), 0) + base
        return at == cols[tt, 0:1], at == cols[tt, 1:2]

    def pick(base, source):
        total = None
        for tt in range(4):
            one, two = onehots(tt, base)
            part = nn(jnp.logical_or(one, two).astype(F32).astype(BF), source[tt])
            total = part if total is None else total + part
        return total.astype(BF)

    def chunk(i):
        c = lax.rem(lax.div(d, 2) + 1 + i, 4)
        return c, pl.multiple_of(c * pair_rows, pair_rows)

    arrive([cot_pair[1], cot_pair[2]])
    for i in range(4):
        c, base = chunk(i)
        raw[pl.ds(base, pair_rows)] = pick(base, cot_all)
    sec_pair = pass_on(1, sec_pair, sec_all)
    gate_pair = pass_on(2, gate_pair, gates_all)
    arrive([sec_pair[1], sec_pair[2], gate_pair[1], gate_pair[2]])

    sent = []

    for i in range(4):
        c, base = chunk(i)
        x_buf[pl.ds(base, pair_rows)] = pick(base, sec_all)
        for h in range(2):
            e = 2 * c + h
            block = x_buf.at[pl.ds(pl.multiple_of(base + h * QUARTER, QUARTER), QUARTER)]
            copy = remote(block, x_out.at[d], x_s.at[e], x_r.at[d], (e * cells + cell, t))
            keep = pltpu.make_async_copy(block, x_out.at[d], own.at[4])
            sent.append((e, copy, keep))

            @pl.when(e == d)
            def _():
                keep.start()

            @pl.when(e != d)
            def _():
                copy.start()

    spread(3, 2, 4)
    for i in range(4):
        c, base = chunk(i)
        gate = None
        for tt in range(4):
            one, two = onehots(tt, base)
            part = jnp.where(one, gates_all[tt, 0:1], jnp.where(two, gates_all[tt, 1:2], 0.0))
            part = jnp.sum(part, axis=1, keepdims=True)
            gate = part if gate is None else gate + part
        kept = (gate * raw[pl.ds(base, pair_rows)].astype(F32)).astype(BF)
        g_out[pl.ds(2 * c, 2)] = kept.reshape(2, QUARTER, kept.shape[1])

    spread(3, 4, 8)
    spread(2, 0, 8)
    forward(3)
    forward(2)
    for a in (2, 3):
        arrive(near_copies[a])
        arrive(far_copies[a])
    for k in range(1, 8):
        g = lax.rem(d + 8 - k, 8)
        remote(x_buf.at[pl.ds(0, QUARTER)], x_out.at[g], x_s.at[g], x_r.at[g], at_dp(8 - k)).wait_recv()
    for e, copy, keep in sent:

        @pl.when(e == d)
        def _():
            keep.wait()

        @pl.when(e != d)
        def _():
            copy.wait_send()

    for copy in cross:
        copy.wait_send()
    for a in range(4):
        for copy in dp_copies[a] + side_copies[a] + near_copies[a] + far_copies[a]:
            copy.wait_send()
    for trio in (cot_pair, sec_pair, gate_pair):
        for copy in trio:
            copy.wait_send()


def gelu_both(x):
    phi = 0.5 * (1.0 + lax.erf(x * (0.5**0.5)))
    slope = phi + x * (jnp.exp(-0.5 * x * x) * 0.3989422804014327)
    return x * phi, slope


def middle_kernel(
    cells,
    x_ref, g_src, expert_all, up_bias, vec, cols,
    r_out, q_out, y_out, e_out, e_side_out, dup_out, ddown_out,
    w_buf, act_buf, pre_buf, x_turned, g_turned, acc, y_buf, b_buf, q_buf, g_in, b_in, q_in,
    blocks, core_in, side_buf, side_in, q_blocks, q_core, q_side, q_mid,
    load, store, g_s, g_r, a_s, a_r, c_s, c_r, y_s, y_r, e_s, e_r, f_s, f_r, own, core_free, side_free,
):
    d, cell, t = place(cells)
    core, side, far = tensor_peers(t)
    here = d * cells + cell
    width = x_ref.shape[1]
    ff = act_buf.shape[1]
    half = width // 8
    pair_rows = 2 * QUARTER

    def at_dp(k):
        return (lax.rem(d + k, 8) * cells + cell, t)

    loads = [pltpu.make_async_copy(expert_all.at[tt], w_buf.at[tt], load.at[tt]) for tt in range(4)]
    for copy in loads:
        copy.start()
    barrier = pltpu.get_barrier_semaphore()
    for k in range(1, 8):
        signal(barrier, at_dp(k))
    signal(barrier, (here, core))
    signal(barrier, (here, side))
    pl.semaphore_wait(barrier, 9)

    sent = []

    def post(c, src, out, send, recv, keep_sem):
        for h in range(2):
            g = 2 * c + h
            copy = remote(src.at[g], out.at[d], send.at[g], recv.at[d], (g * cells + cell, t))
            keep = pltpu.make_async_copy(src.at[g], out.at[d], keep_sem)
            sent.append((g, copy))

            @pl.when(g == d)
            def _():
                keep.start()

            @pl.when(g != d)
            def _():
                copy.start()

    def landed(g, src, out, send, recv, keep_sem):
        @pl.when(g == d)
        def _():
            pltpu.make_async_copy(src.at[g], out.at[g], keep_sem).wait()

        @pl.when(g != d)
        def _():
            remote(src.at[g], out.at[g], send.at[g], recv.at[g], (g * cells + cell, t)).wait_recv()

    for i in range(4):
        post(lax.rem(lax.div(d, 2) + 1 + i, 4), g_src, g_in, g_s, g_r, own.at[3])
    x_turned[...] = x_ref[...].T
    dup_out[...] = jnp.zeros_like(dup_out)
    for copy in loads:
        copy.wait()

    def w_in(tt):
        return w_buf[tt, :, 0:half].reshape(width, ff)

    def w_out(tt):
        return w_buf[tt, :, half : 2 * half].reshape(width, ff)

    def held(tt, base):
        return pl.ds(pl.multiple_of(tt * SLOTS + base, pair_rows), pair_rows)

    def ahead(i, carry):
        base = pl.multiple_of(i * pair_rows, pair_rows)
        acc[...] = jnp.broadcast_to(vec[pl.ds(15 + d, 1)], acc.shape)

        def slice_step(tt, inner):
            pre = nn(x_ref[pl.ds(base, pair_rows)], w_in(tt)) + up_bias[tt]
            act, slope = gelu_both(pre)
            act = act.astype(BF)
            act_buf[held(tt, base)] = act
            pre_buf[held(tt, base)] = slope.astype(BF)
            acc[...] += nt(act, w_out(tt))
            return inner

        lax.fori_loop(0, 4, slice_step, 0)
        y_buf[pl.ds(2 * i, 2)] = acc[...].astype(BF).reshape(2, QUARTER, width)
        return carry

    lax.fori_loop(0, 4, ahead, 0)
    ones = jnp.ones((8, width), BF)
    for i in range(4):
        c = lax.rem(lax.div(d, 2) + 3 - i, 4)
        base = pl.multiple_of(c * pair_rows, pair_rows)
        pair = pl.ds(2 * c, 2)
        for h in range(2):
            landed(2 * c + h, g_src, g_in, g_s, g_r, own.at[3])
        acc[...] = jnp.zeros_like(acc)

        def slice_back(tt, carry):
            grad = nn(g_in[pair].reshape(pair_rows, width), w_out(tt)) * pre_buf[held(tt, base)].astype(F32)
            grad = grad.astype(BF)
            pre_buf[held(tt, base)] = grad
            acc[...] += nt(grad, w_in(tt))
            dup_out[tt] += jnp.sum(grad.astype(F32), axis=0, keepdims=True)
            return carry

        lax.fori_loop(0, 4, slice_back, 0)
        b_buf[pair] = acc[...].astype(BF).reshape(2, QUARTER, width)
        post(c, b_buf, b_in, a_s.at[0], a_r.at[0], own.at[0])
        for h in range(2):
            g = 2 * c + h
            z = y_buf[g].astype(F32) * g_in[g].astype(F32)
            high = z.astype(BF)
            q_buf[g] = nt(ones, high) + nt(ones, (z - high.astype(F32)).astype(BF))
        post(c, q_buf, q_in, a_s.at[2], a_r.at[2], own.at[2])
    for i in range(4):
        post(lax.rem(lax.div(d, 2) + 3 - i + 4, 4), y_buf, y_out, a_s.at[1], a_r.at[1], own.at[1])
    g_rows = g_in[...].reshape(SLOTS, width)
    g_turned[...] = g_rows.T
    ddown_out[...] = jnp.sum(g_rows.astype(F32), axis=0, keepdims=True)

    def grad_slice(tt, carry):
        def grad_rows(n, inner):
            span = pl.ds(pl.multiple_of(n * 2 * half, 2 * half), 2 * half)
            pair = pl.ds(2 * n, 2)
            at = pl.ds(pl.multiple_of(tt * SLOTS, SLOTS), SLOTS)
            w_buf[tt, pair, 0:half] = nn(x_turned[span], pre_buf[at]).astype(BF).reshape(2, half, ff)
            w_buf[tt, pair, half : 2 * half] = nn(g_turned[span], act_buf[at]).astype(BF).reshape(2, half, ff)
            return inner

        lax.fori_loop(0, 4, grad_rows, 0)
        return carry

    lax.fori_loop(0, 4, grad_slice, 0)

    pl.semaphore_signal(core_free, inc=1, device_id=(here, core), device_id_type=MESH)
    pl.semaphore_signal(side_free, inc=1, device_id=(here, side), device_id_type=MESH)
    pl.semaphore_wait(core_free, 1)

    def inbox(i, p):
        return pl.ds(pl.multiple_of((i * 8 + p) * 2 * half, 2 * half), 2 * half)

    near = {}
    for i, tt in enumerate((far, core)):
        for k in range(1, 9):
            p = lax.rem(d + k, 8)
            near[i, k] = remote(
                w_buf.at[tt, p], act_buf.at[inbox(i, p)], e_s.at[i, k - 1], e_r.at[i, k - 1], (here, core)
            )
            near[i, k].start()
    pl.semaphore_wait(side_free, 1)
    over = {}
    for k in range(1, 9):
        p = lax.rem(d + k, 8)
        near[0, k].wait_recv()
        total = w_buf[side, p].astype(F32) + act_buf[inbox(0, p)].astype(F32)
        w_buf[side, p] = total.astype(BF)
        if k <= EARLY:
            over[k] = remote(
                w_buf.at[side, p], pre_buf.at[inbox(0, p)], f_s.at[k - 1], f_r.at[k - 1], (here, side)
            )
            over[k].start()
    keep_side = pltpu.make_async_copy(w_buf.at[side], e_side_out, store.at[1])
    keep_side.start()

    def onehots(tt):
        at = lax.broadcasted_iota(jnp.int32, (cols.shape[1], SLOTS), 1)
        return at == cols[tt, :, 0:1], at == cols[tt, :, 1:2]

    for k in range(1, 9):
        e = lax.rem(d + k, 8)
        landed(e, b_buf, b_in, a_s.at[0], a_r.at[0], own.at[0])
        landed(e, q_buf, q_in, a_s.at[2], a_r.at[2], own.at[2])
    q_line = jnp.concatenate([q_in[e] for e in range(8)], axis=1)
    owner = jnp.concatenate([jnp.full((8, QUARTER), e, jnp.int32) for e in range(8)], axis=1)
    q_line = jnp.where(lax.broadcasted_iota(jnp.int32, q_line.shape, 0) == owner, q_line, 0.0)
    q_high = q_line.astype(BF)
    q_both = jnp.concatenate([q_high, (q_line - q_high.astype(F32)).astype(BF)], axis=0)
    b_rows = b_in[...].reshape(SLOTS, width)

    def back_block(tt):
        one, two = onehots(tt)
        hot = jnp.logical_or(one, two).astype(F32).astype(BF)
        q = nt(q_both, hot)
        return nn(hot, b_rows), q[0:8] + q[8:16]

    def core_send(n, i, src, dst):
        copy = remote(src.at[i], dst.at[i], c_s.at[n, i], c_r.at[n, i], (here, core))
        copy.start()
        return copy

    def side_send(n, src, dst):
        copy = remote(src, dst, y_s.at[n], y_r.at[n], (here, side))
        copy.start()
        return copy

    core_b, core_q = [], []
    for i, tt in enumerate((far, core)):
        total, q = back_block(tt)
        blocks[i] = total.astype(BF)
        q_blocks[i] = q
        core_b.append(core_send(0, i, blocks, core_in))
        core_q.append(core_send(1, i, q_blocks, q_core))
    total, q = back_block(side)
    core_b[0].wait_recv()
    core_q[0].wait_recv()
    side_buf[...] = (total + core_in[0].astype(F32)).astype(BF)
    q_mid[...] = q + q_core[0]
    side_b = side_send(0, side_buf, side_in)
    side_q = side_send(1, q_mid, q_side)
    total, q = back_block(t)
    core_b[1].wait_recv()
    core_q[1].wait_recv()
    r_out[...] = total + core_in[1].astype(F32)
    q_out[...] = q + q_core[1]

    for k in range(1, 9):
        p = lax.rem(d + k, 8)
        near[1, k].wait_recv()
        total = w_buf[t, p].astype(F32) + act_buf[inbox(1, p)].astype(F32)
        if k <= EARLY:
            over[k].wait_recv()
            total = total + pre_buf[inbox(0, p)].astype(F32)
        w_buf[t, p] = total.astype(BF)
    keep_e = pltpu.make_async_copy(w_buf.at[t], e_out, store.at[0])
    keep_e.start()
    side_b.wait_recv()
    side_q.wait_recv()
    r_out[...] += side_in[...].astype(F32)
    q_out[...] += q_side[...]

    for k in range(1, 9):
        landed(lax.rem(d + k, 8), y_buf, y_out, a_s.at[1], a_r.at[1], own.at[1])
    for copy in core_b + core_q + [side_b, side_q] + list(near.values()) + list(over.values()):
        copy.wait_send()
    for g, copy in sent:

        @pl.when(g != d)
        def _():
            copy.wait_send()

    keep_e.wait()
    keep_side.wait()


def back_kernel(
    cells,
    tok, hid, r_ref, y_rows, cols, gates, cot, probs, picked_ref, vec, wall, qkv_ref, mixed_ref, e_src, e_side_src,
    bias_msg, out, token_grad, e_out, a_out, msg_all, vec_all,
    n1, vec_grad, vec_msg, a_grad, qv_grad, a_core, a_mid, a_side, a_fin, a_cross, a_in,
    blocks, core_in, side_buf, side_in, e_own, e_in,
    c_s, c_r, y_s, y_r, e_s, e_r, f_s, f_r, x_s, x_r, z_s, z_r, o_s, o_r, own, m_s, m_r, v_s, v_r,
):
    d, cell, t = place(cells)
    core, side, far = tensor_peers(t)
    here = d * cells + cell
    heads = qkv_ref.shape[2] // 3
    rows = tok.shape[0]
    width = tok.shape[1]
    spot = d * 4 + t
    twin = d + 1 - 2 * lax.rem(d, 2)

    def at_dp(k):
        return (lax.rem(d + k, 8) * cells + cell, t)

    others = [(k, m) for k in range(8) for m in range(4) if k or m]

    def other(k, m):
        return lax.rem(d + k, 8), lax.rem(t + m, 4)

    barrier = pltpu.get_barrier_semaphore()
    for k, m in others:
        dd, tt = other(k, m)
        signal(barrier, (dd * cells + cell, tt))
    pl.semaphore_wait(barrier, 31)

    waits = []
    late = range(EARLY + 1, 9)
    over_e, load_e = {}, {}
    for k in range(1, EARLY + 1):
        copy = remote(e_src.at[lax.rem(d + k, 8)], e_out.at[d], e_s.at[k], e_r.at[k], at_dp(k))
        copy.start()
        waits.append(copy)
    for k in late:
        p = lax.rem(d + k, 8)
        over_e[k] = remote(e_side_src.at[p], e_in.at[p], f_s.at[k - 1], f_r.at[k - 1], (here, side))
        over_e[k].start()
        load_e[k] = pltpu.make_async_copy(e_src.at[p], e_own.at[p], own.at[k])
        load_e[k].start()

    def finish_expert(k):
        p = lax.rem(d + k, 8)
        load_e[k].wait()
        over_e[k].wait_recv()
        e_own[p] = (e_own[p].astype(F32) + e_in[p].astype(F32)).astype(BF)
        if k < 8:
            copy = remote(e_own.at[p], e_out.at[d], e_s.at[k], e_r.at[k], at_dp(k))
            waits.append(copy)
        else:
            copy = pltpu.make_async_copy(e_own.at[p], e_out.at[d], own.at[0])
            load_e[0] = copy
        copy.start()
    for n, (k, m) in enumerate(others):
        dd, tt = other(k, m)
        copy = remote(bias_msg.at[dd * 4 + tt], msg_all.at[spot], m_s.at[n], m_r.at[n], (dd * cells + cell, tt))
        copy.start()
        waits.append(copy)
    msg_own = pltpu.make_async_copy(bias_msg.at[spot], msg_all.at[spot], own.at[1])
    msg_own.start()

    hidden = hid[...]
    picked = picked_ref[...]
    logit = picked - probs[...] * jnp.sum(picked, axis=0, keepdims=True)
    high = logit.astype(BF)
    both = jnp.concatenate([high, (logit - high.astype(F32)).astype(BF)], axis=0)
    unit, inv = unit_norm(hidden)
    gain = vec[2:3]
    second = (unit * gain + vec[3:4]).astype(BF)
    router_grad = nn(both, second)
    vec_grad[...] = jnp.zeros_like(vec_grad)
    vec_grad[8:16] = router_grad[0:8] + router_grad[8:16]
    table = vec[7:15].astype(BF)
    n2 = r_ref[...] + tn(both, jnp.concatenate([table, table], axis=0))
    vec_grad[2:3] = jnp.sum(n2 * unit, axis=0, keepdims=True)
    vec_grad[3:4] = jnp.sum(n2, axis=0, keepdims=True)
    scaled = n2 * gain
    back = inv * (
        scaled
        - jnp.mean(scaled, axis=-1, keepdims=True)
        - unit * jnp.mean(scaled * unit, axis=-1, keepdims=True)
    )
    hidden_grad = cot[...].astype(F32) + back
    token_grad[...] = hidden_grad
    branch = hidden_grad.astype(BF)
    vec_grad[4:5] = jnp.sum(branch.astype(F32), axis=0, keepdims=True)
    unit1, inv1 = unit_norm(tok[...].astype(F32))
    first_norm = (unit1 * vec[0:1] + vec[1:2]).astype(BF)
    n1[...] = jnp.zeros_like(n1)

    def attend_back(tt):
        weights = wall[tt].reshape(width, -1)
        qkv = qkv_ref[tt]
        mixed_grad = nn(branch, weights[:, 3 * heads :]).astype(BF)
        triple = []
        for i in range(rows // SEQ_PAD):
            span = slice(i * SEQ_PAD, (i + 1) * SEQ_PAD)
            part, grad = qkv[span], mixed_grad[span]
            sides = [[], [], []]
            for h in range(heads // HEAD_DIM):
                q, k, v = (part[:, j * heads + h * HEAD_DIM : j * heads + (h + 1) * HEAD_DIM] for j in range(3))
                g = grad[:, h * HEAD_DIM : (h + 1) * HEAD_DIM]
                w = softmax_rows(q, k)
                w_grad = nt(g, v)
                s_grad = (w * (w_grad - jnp.sum(w * w_grad, axis=-1, keepdims=True))).astype(BF)
                sides[0].append((nn(s_grad, k) * (HEAD_DIM**-0.5)).astype(BF))
                sides[1].append((tn(s_grad, q) * (HEAD_DIM**-0.5)).astype(BF))
                sides[2].append(tn(w.astype(BF), g).astype(BF))
            triple.append(jnp.concatenate(sides[0] + sides[1] + sides[2], axis=1))
        triple = jnp.concatenate(triple, axis=0)
        grad = jnp.concatenate([tn(first_norm, triple), tn(branch, mixed_ref[tt])], axis=1).astype(BF)
        a_grad[tt] = grad.reshape(8, width // 8, -1)
        n1[...] += nt(triple, weights[:, : 3 * heads])
        sums = jnp.sum(triple.astype(F32), axis=0, keepdims=True)
        qv_grad[tt] = sums

    def core_a(i, tt):
        copy = remote(a_grad.at[tt], a_core.at[i], c_s.at[i], c_r.at[i], (here, core))
        copy.start()
        return copy

    order = [lax.rem(twin + 2 * m, 8) for m in range(4)] + [lax.rem(d + 2 * m, 8) for m in (1, 2, 3, 0)]
    attend_back(far)
    near_a = core_a(0, far)
    finish_expert(EARLY + 1)
    attend_back(side)
    near_a.wait_recv()
    over_a = []
    for n, p in enumerate(order):
        a_mid[p] = (a_grad[side, p].astype(F32) + a_core[0, p].astype(F32)).astype(BF)
        copy = remote(a_mid.at[p], a_side.at[p], y_s.at[n], y_r.at[n], (here, side))
        copy.start()
        over_a.append(copy)
    finish_expert(EARLY + 2)
    attend_back(core)
    far_a = core_a(1, core)
    for k in list(late)[2:-1]:
        finish_expert(k)
    attend_back(t)
    finish_expert(8)

    def out_block(tt):
        at = lax.broadcasted_iota(jnp.int32, (rows, SLOTS), 1)
        one, two = at == cols[tt, :, 0:1], at == cols[tt, :, 1:2]
        hot = jnp.where(one, gates[tt, :, 0:1], jnp.where(two, gates[tt, :, 1:2], 0.0)).astype(BF)
        return nn(hot, y_rows[...])

    out_copies = []
    for i, tt in enumerate((far, core)):
        blocks[i] = out_block(tt).astype(BF)
        copy = remote(blocks.at[i], core_in.at[i], o_s.at[i], o_r.at[i], (here, core))
        copy.start()
        out_copies.append(copy)
    total = out_block(side)
    out_copies[0].wait_recv()
    side_buf[...] = (total + core_in[0].astype(F32)).astype(BF)
    side_out = remote(side_buf, side_in, o_s.at[2], o_r.at[2], (here, side))
    side_out.start()

    far_a.wait_recv()
    cross = []
    for n, p in enumerate(order):
        over_a[n].wait_recv()
        total = a_grad[t, p].astype(F32) + a_core[1, p].astype(F32) + a_side[p].astype(F32)
        if n < 4:
            a_fin[p] = total.astype(BF)
            copy = remote(a_fin.at[p], a_cross.at[n], x_s.at[n], x_r.at[n], (twin * cells + cell, t))
            copy.start()
            cross.append(copy)
        else:
            m = (n - 3) % 4
            cross[m].wait_recv()
            total = total + a_cross[m].astype(F32)
            if m:
                a_fin[p] = total.astype(BF)
                copy = remote(a_fin.at[p], a_in.at[m], z_s.at[m], z_r.at[m], at_dp(2 * m))
                copy.start()
                waits.append(copy)
            else:
                a_out[...] = total

    grad = n1[...]
    vec_grad[0:1] = jnp.sum(grad * unit1, axis=0, keepdims=True)
    vec_grad[1:2] = jnp.sum(grad, axis=0, keepdims=True)
    for j, row in ((0, 5), (2, 6)):
        parts = [qv_grad[tt][:, j * heads : (j + 1) * heads] for tt in range(4)]
        vec_grad[row : row + 1] = jnp.concatenate(parts, axis=1)
    turned = vec_grad[...].T
    vec_msg[...] = turned.reshape(vec_msg.shape)
    for n, (k, m) in enumerate(others):
        dd, tt = other(k, m)
        copy = remote(vec_msg.at[dd * 4 + tt], vec_all.at[spot], v_s.at[n], v_r.at[n], (dd * cells + cell, tt))
        copy.start()
        waits.append(copy)
    vec_all[spot] = vec_msg[spot]
    scaled = grad * vec[0:1]
    token_grad[...] += inv1 * (
        scaled
        - jnp.mean(scaled, axis=-1, keepdims=True)
        - unit1 * jnp.mean(scaled * unit1, axis=-1, keepdims=True)
    )
    total = out_block(t)
    out_copies[1].wait_recv()
    total = total + core_in[1].astype(F32)
    side_out.wait_recv()
    out[...] = (hid[...] + (total + side_in[...].astype(F32))).astype(BF)
    for copy in waits:
        copy.wait()
    for m in range(1, 4):
        a_out[...] += a_in[m].astype(F32)
    load_e[0].wait()
    msg_own.wait()
    for copy in [near_a, far_a, side_out] + out_copies + over_a + cross + list(over_e.values()):
        copy.wait_send()


def pad_images(rows, fill=0):
    images = rows.reshape((-1, SEQ) + rows.shape[1:])
    spare = [(0, 0), (0, SEQ_PAD - SEQ)] + [(0, 0)] * (rows.ndim - 1)
    return jnp.pad(images, spare, constant_values=fill).reshape((-1,) + rows.shape[1:])


def drop_pad(rows):
    return rows.reshape((-1, SEQ_PAD) + rows.shape[1:])[:, :SEQ].reshape((-1,) + rows.shape[1:])


def body(
    tokens, ln1_gain, ln1_shift, qkv_weight, qv_bias, out_weight, out_bias, ln2_gain, ln2_shift,
    router_weight, expert_in, expert_in_bias, expert_out, expert_out_bias, expert_ids, expert_slots,
    cotangent,
):
    n_dp = lax.axis_size("dp")
    cells = n_dp // 8
    width = tokens.shape[1]
    experts = expert_in.shape[0]
    head_cols = qkv_weight.shape[2]
    ff_slice = expert_in.shape[2]
    index = lax.axis_index("dp")
    t = lax.axis_index("tensor")
    d, cell = index // cells, index % cells
    peers = [[row * cells + c for c in range(cells)] for row in range(8)]

    packed = jnp.concatenate([qkv_weight.reshape(-1, 3 * head_cols), out_weight.T], axis=1)
    expert_pack = [expert_in, jnp.swapaxes(expert_out, 1, 2)]
    lines = [ln1_gain, ln1_shift, ln2_gain, ln2_shift, out_bias, qv_bias[0], qv_bias[1]]
    small_a = jnp.concatenate([jnp.stack(lines, axis=1), router_weight, expert_out_bias.T], axis=1)
    small_b = expert_in_bias
    if cells > 1:
        packed = lax.all_gather(packed, "dp", axis=0, tiled=True, axis_index_groups=peers)
        expert_pack = [
            lax.all_gather(part, "dp", axis=1, tiled=True, axis_index_groups=peers) for part in expert_pack
        ]

        def quarter(piece, axis):
            piece = lax.all_gather(piece, "tensor", axis=axis, tiled=True)
            piece = lax.all_gather(piece, "dp", axis=axis, tiled=True, axis_index_groups=peers)
            size = piece.shape[axis] // 4
            return lax.dynamic_slice_in_dim(piece, t * size, size, axis)

        small_a, small_b = quarter(small_a, 0), quarter(small_b, 1)
    expert_pack = jnp.concatenate(expert_pack, axis=1)
    piece, ff_piece = small_a.shape[0], small_b.shape[1]
    small_a = jnp.pad(small_a.astype(F32), ((0, 0), (0, 128 - small_a.shape[1])))
    small_b = jnp.pad(small_b, ((0, 16 - experts), (0, 128 - ff_piece)))
    tok = pad_images(tokens)
    cot = pad_images(cotangent)
    rows = tok.shape[0]

    wanted = expert_slots - QUARTER * t
    inside = jnp.logical_and(expert_slots >= 0, jnp.logical_and(wanted >= 0, wanted < QUARTER))
    cols = jnp.where(inside, expert_ids * QUARTER + wanted, -1)
    cols = jnp.pad(pad_images(cols, -1).reshape(4, rows, TOP), ((0, 0), (0, 0), (0, 8 - TOP)), constant_values=-1)
    cols_t = jnp.swapaxes(cols, 1, 2)
    own_ids = lax.dynamic_slice_in_dim(expert_ids, t * tokens.shape[0], tokens.shape[0], 0)
    ids = jnp.pad(pad_images(own_ids, -1).T, ((0, 8 - TOP), (0, 0)), constant_values=-1)

    dma = pltpu.SemaphoreType.DMA

    def params(identity):
        return pltpu.CompilerParams(
            collective_id=identity, has_side_effects=True, vmem_limit_bytes=VMEM_LIMIT
        )

    def like(shape, dtype=BF):
        return jax.ShapeDtypeStruct(shape, dtype)

    slot_shape = (8, QUARTER, width)
    hidden, probs, gates, qkv, mixed, vec, wall, bias_all, expert_all, x_rows, g_rows = pl.pallas_call(
        functools.partial(front_kernel, cells),
        out_shape=[
            like((rows, width), F32),
            like((experts, rows), F32),
            like((4, 8, rows), F32),
            like((4, rows, 3 * head_cols)),
            like((4, rows, head_cols)),
            like((32, width), F32),
            like((4, 8) + packed.shape),
            like((4, 8) + small_b.shape),
            like((4,) + expert_pack.shape),
            like(slot_shape),
            like(slot_shape),
        ],
        in_specs=[HB] * 4 + [VM] * 4,
        out_specs=[VM] * 7 + [HB] * 3 + [VM],
        scratch_shapes=[
            pltpu.VMEM((8, 4) + small_a.shape, F32),
            pltpu.VMEM((4, rows, width), BF),
            pltpu.VMEM((4, rows, width), BF),
            pltpu.VMEM((SLOTS, width), BF),
            pltpu.VMEM((SLOTS, width), BF),
            pltpu.VMEM((rows, width), F32),
            pltpu.VMEM((8, rows), F32),
            pltpu.VMEM((4, 1, 3 * head_cols), F32),
        ]
        + [dma((4, 8))] * 8
        + [dma((5,)), dma((3, 3)), dma((3, 3)), dma((8,)), dma((8,)), dma((4,)), dma((4,))],
        compiler_params=params(0),
        name="front",
    )(packed, small_a, small_b, expert_pack, tok, cot, cols_t, ids)

    bias_all = jnp.swapaxes(bias_all, 0, 1)
    up_bias = lax.dynamic_index_in_dim(bias_all, d, 2, keepdims=False)[:, :, :ff_piece]
    up_bias = up_bias.astype(F32).reshape(4, 1, ff_slice)
    e_block = expert_pack.shape
    r_rows, picked, y_rows, expert_grad, side_grad, up_grad, down_grad = pl.pallas_call(
        functools.partial(middle_kernel, cells),
        out_shape=[
            like((rows, width), F32),
            like((8, rows), F32),
            like(slot_shape),
            like(e_block),
            like(e_block),
            like((4, 1, ff_slice), F32),
            like((1, width), F32),
        ],
        in_specs=[VM, HB, HB, VM, VM, VM],
        out_specs=[VM, VM, HB, HB, HB, VM, VM],
        scratch_shapes=[
            pltpu.VMEM(expert_all.shape, BF),
            pltpu.VMEM((4 * SLOTS, ff_slice), BF),
            pltpu.VMEM((4 * SLOTS, ff_slice), BF),
            pltpu.VMEM((width, SLOTS), BF),
            pltpu.VMEM((width, SLOTS), BF),
            pltpu.VMEM((2 * QUARTER, width), F32),
            pltpu.VMEM(slot_shape, BF),
            pltpu.VMEM(slot_shape, BF),
            pltpu.VMEM((8, 8, QUARTER), F32),
            pltpu.VMEM(slot_shape, BF),
            pltpu.VMEM(slot_shape, BF),
            pltpu.VMEM((8, 8, QUARTER), F32),
            pltpu.VMEM((2, rows, width), BF),
            pltpu.VMEM((2, rows, width), BF),
            pltpu.VMEM((rows, width), BF),
            pltpu.VMEM((rows, width), BF),
            pltpu.VMEM((2, 8, rows), F32),
            pltpu.VMEM((2, 8, rows), F32),
            pltpu.VMEM((8, rows), F32),
            pltpu.VMEM((8, rows), F32),
            dma((4,)), dma((2,)), dma((8,)), dma((8,)), dma((3, 8)), dma((3, 8)), dma((2, 2)), dma((2, 2)),
            dma((2,)), dma((2,)), dma((2, 8)), dma((2, 8)), dma((8,)), dma((8,)), dma((4,)),
            pltpu.SemaphoreType.REGULAR, pltpu.SemaphoreType.REGULAR,
        ],
        compiler_params=params(1),
        name="middle",
    )(x_rows.reshape(SLOTS, width), g_rows, expert_all, up_bias, vec, cols)

    message = jnp.pad(
        jnp.stack(
            [
                jnp.pad(up_grad.reshape(32, ff_piece), ((0, 0), (0, 128 - ff_piece))),
                jnp.pad(down_grad.reshape(32, piece), ((0, 0), (0, 128 - piece))),
            ],
            axis=1,
        ),
        ((0, 0), (0, 6), (0, 0)),
    )
    a_block = wall.shape[1:]
    out, token_grad, expert_sum, attn_sum, messages, vec_all = pl.pallas_call(
        functools.partial(back_kernel, cells),
        out_shape=[
            like((rows, width)),
            like((rows, width), F32),
            like(e_block),
            like(a_block[1:], F32),
            like(message.shape, F32),
            like((32, piece, 128), F32),
        ],
        in_specs=[VM] * 13 + [HB, HB, HB],
        out_specs=[VM, VM, HB, VM, HB, VM],
        scratch_shapes=[
            pltpu.VMEM((rows, width), F32),
            pltpu.VMEM((128, width), F32),
            pltpu.VMEM((32, piece, 128), F32),
            pltpu.VMEM(wall.shape, BF),
            pltpu.VMEM((4, 1, 3 * head_cols), F32),
            pltpu.VMEM((2,) + a_block, BF),
            pltpu.VMEM(a_block, BF),
            pltpu.VMEM(a_block, BF),
            pltpu.VMEM(a_block, BF),
            pltpu.VMEM((4,) + a_block[1:], BF),
            pltpu.VMEM((4,) + a_block[1:], BF),
            pltpu.VMEM((2, rows, width), BF),
            pltpu.VMEM((2, rows, width), BF),
            pltpu.VMEM((rows, width), BF),
            pltpu.VMEM((rows, width), BF),
            pltpu.VMEM(e_block, BF),
            pltpu.VMEM(e_block, BF),
            dma((2,)), dma((2,)), dma((8,)), dma((8,)), dma((8,)), dma((8,)), dma((8,)), dma((8,)),
            dma((4,)), dma((4,)), dma((4,)), dma((4,)), dma((3,)), dma((3,)), dma((9,)), dma((31,)), dma((31,)), dma((31,)), dma((31,)),
        ],
        compiler_params=params(2),
        name="back",
    )(
        tok, hidden, r_rows, y_rows.reshape(SLOTS, width), cols, jnp.swapaxes(gates, 1, 2), cot, probs, picked, vec,
        wall, qkv, mixed, expert_grad, side_grad, message,
    )

    grads = jnp.sum(vec_all, axis=0).T
    messages = jnp.sum(messages.reshape(8, 4, 8, 128), axis=1)
    up_sum, down_sum = messages[:, 0, :ff_piece], messages[:, 1, :piece]
    if cells > 1:
        expert_sum = lax.psum_scatter(
            expert_sum.astype(F32).reshape(8, 2, width // 8, -1), "dp", scatter_dimension=2, tiled=True,
            axis_index_groups=peers,
        )
        expert_sum = expert_sum.reshape(8, -1, expert_sum.shape[3])
        attn_sum = lax.psum_scatter(attn_sum, "dp", scatter_dimension=0, tiled=True, axis_index_groups=peers)

        def share(part):
            part = lax.psum(part, "dp", axis_index_groups=peers)
            part = lax.all_gather(part, "tensor", axis=1, tiled=True)
            size = part.shape[1] // (4 * cells)
            return lax.dynamic_slice_in_dim(part, (cell * 4 + t) * size, size, 1)

        grads, up_sum, down_sum = share(grads), share(up_sum), share(down_sum)
    own_rows = expert_in.shape[1]
    return (
        drop_pad(out),
        drop_pad(token_grad),
        grads[0],
        grads[1],
        attn_sum[:, : 3 * head_cols].reshape(-1, 3, head_cols),
        grads[5:7],
        attn_sum[:, 3 * head_cols :].T,
        grads[4],
        grads[2],
        grads[3],
        grads[8:16].T,
        expert_sum[:, :own_rows].astype(F32),
        up_sum,
        jnp.swapaxes(expert_sum[:, own_rows:], 1, 2).astype(F32),
        down_sum,
    )


def solution(mesh):
    both = ("dp", "tensor")
    return jax.shard_map(
        body,
        mesh=mesh,
        in_specs=(
            P(both, None),
            P(both),
            P(both),
            P("dp", None, "tensor"),
            P(None, both),
            P("tensor", "dp"),
            P(both),
            P(both),
            P(both),
            P(both, None),
            P(None, "dp", "tensor"),
            P(None, both),
            P(None, "tensor", "dp"),
            P(None, both),
            P("dp", None),
            P("dp", None),
            P(both, None),
        ),
        out_specs=(
            P(both, None),
            P(both, None),
            P(both),
            P(both),
            P("dp", None, "tensor"),
            P(None, both),
            P("tensor", "dp"),
            P(both),
            P(both),
            P(both),
            P(both, None),
            P(None, "dp", "tensor"),
            P(None, both),
            P(None, "tensor", "dp"),
            P(None, both),
        ),
        check_vma=False,
    )
```

```python
import functools

import jax
import jax.numpy as jnp
from jax import lax
from jax.experimental import pallas as pl
from jax.experimental.pallas import tpu as pltpu
from jax.sharding import PartitionSpec as P

HEAD_DIM = 64
SEQ = 197
SEQ_PAD = 208
TOP = 2
QUARTER = 160
SLOTS = 8 * QUARTER
EARLY = 5
EPS = 1e-6
BF = jnp.bfloat16
F32 = jnp.float32
MESH = pl.DeviceIdType.MESH
VMEM_LIMIT = 60 * 1024 * 1024
VM = pl.BlockSpec(memory_space=pltpu.VMEM)
HB = pl.BlockSpec(memory_space=pl.ANY)


def nn(a, b):
    return lax.dot_general(a, b, (((1,), (0,)), ((), ())), preferred_element_type=F32)


def nt(a, b):
    return lax.dot_general(a, b, (((1,), (1,)), ((), ())), preferred_element_type=F32)


def tn(a, b):
    return lax.dot_general(a, b, (((0,), (0,)), ((), ())), preferred_element_type=F32)


def unit_norm(rows):
    centred = rows - jnp.mean(rows, axis=-1, keepdims=True)
    inv = lax.rsqrt(jnp.mean(centred * centred, axis=-1, keepdims=True) + EPS)
    return centred * inv, inv


def place(cells):
    index = lax.axis_index("dp")
    return lax.div(index, cells), lax.rem(index, cells), lax.axis_index("tensor")


def tensor_peers(t):
    core = t + 1 - 2 * lax.rem(t, 2)
    side = lax.rem(t + 2, 4)
    return core, side, lax.rem(core + 2, 4)


def remote(src, dst, send, recv, device):
    return pltpu.make_async_remote_copy(
        src_ref=src, dst_ref=dst, send_sem=send, recv_sem=recv, device_id=device, device_id_type=MESH
    )


def signal(barrier, device):
    pl.semaphore_signal(barrier, inc=1, device_id=device, device_id_type=MESH)


def softmax_rows(q, k):
    scores = nt(q, k) * (HEAD_DIM**-0.5)
    lane = lax.broadcasted_iota(jnp.int32, scores.shape, 1)
    scores = jnp.where(lane < SEQ, scores, -1e30)
    raised = jnp.exp(scores - jnp.max(scores, axis=-1, keepdims=True))
    return raised / jnp.sum(raised, axis=-1, keepdims=True)


def front_kernel(
    cells,
    packed, small_a, small_b, expert, tok, cot, cols, ids,
    probs_out, gates_all, vec_out, hidden_hbm, qkv_hbm, mixed_hbm, wall_hbm, b_all, expert_all, x_out, g_hbm,
    hidden_out, qkv_out, mixed_out, wall, g_out, small_all, cot_all, sec_all, x_buf, raw, acc, gates, qkv_bias,
    dp_s, dp_r, y_s, y_r, c_s, c_r, f_s, f_r, own, ag_s, ag_r, x_s, x_r, w_s, w_r, save_s,
):
    d, cell, t = place(cells)
    core, side, far = tensor_peers(t)
    here = d * cells + cell
    twin = d + 1 - 2 * lax.rem(d, 2)
    rows = tok.shape[0]
    srcs = (small_a, packed, small_b, expert)

    def at_dp(k):
        return (lax.rem(d + k, 8) * cells + cell, t)

    def spot(a, tt, s):
        return small_all.at[s, tt] if a == 0 else (None, wall, b_all, expert_all)[a].at[tt, s]

    barrier = pltpu.get_barrier_semaphore()
    for k in range(1, 8):
        signal(barrier, at_dp(k))
    signal(barrier, (here, core))
    signal(barrier, (here, side))
    pl.semaphore_wait(barrier, 9)

    mine = [
        pltpu.make_async_copy(srcs[a].at[d] if a == 3 else srcs[a], spot(a, t, d), own.at[a]) for a in range(4)
    ]
    dp_copies = [
        [
            remote(
                srcs[a].at[lax.rem(d + k, 8)] if a == 3 else srcs[a],
                spot(a, t, d),
                dp_s.at[a, k],
                dp_r.at[a, d if a == 3 else k],
                at_dp(k),
            )
            for k in ((2, 4, 6) if a == 1 else range(1, 8))
        ]
        for a in range(4)
    ]
    side_copies = [[None] * (4 if a == 3 else 8) for a in range(4)]
    near_copies = [[None] * (4 if a == 3 else 8) for a in range(4)]
    far_copies = [[None] * (4 if a == 3 else 8) for a in range(4)]

    cross = [remote(packed, wall.at[t, d], w_s.at[0], w_r.at[0], (twin * cells + cell, t))]

    def launch(a, part=slice(0, 7)):
        if part.start == 0:
            mine[a].start()
        for copy in dp_copies[a][part]:
            copy.start()
        if a == 1:
            cross[0].start()

    near_z = d + 2 - 4 * lax.rem(lax.div(d, 2), 2)
    near_twin = twin + near_z - d
    by_distance = [d, twin, near_z, near_twin] + [lax.rem(s + 4, 8) for s in (d, twin, near_z, near_twin)]

    def source(a, k):
        if a == 3:
            return by_distance[k]
        if a != 1:
            return lax.rem(d + 8 - k, 8)
        return lax.rem((d if k < 4 else twin) + 8 - 2 * (k % 4), 8)

    def spread(a, first, last):
        for k in range(first, last):
            block = spot(a, t, source(a, k))
            if k == 0:
                mine[a].wait()
            elif a == 3:
                remote(block, block, dp_s.at[a, k], dp_r.at[a, source(a, k)], at_dp(k)).wait_recv()
            elif a != 1 or k < 4:
                dp_copies[a][k - 1].wait_recv()
            else:
                cross[k - 4].wait_recv()
            if a == 1 and 0 < k < 4:
                cross.append(remote(block, block, w_s.at[k], w_r.at[k], (twin * cells + cell, t)))
                cross[k].start()
            side_copies[a][k] = remote(block, block, y_s.at[a, k], y_r.at[a, k], (here, side))
            side_copies[a][k].start()
            near_copies[a][k] = remote(block, block, c_s.at[a, k], c_r.at[a, k], (here, core))
            near_copies[a][k].start()

    def forward(a, count=8):
        for k in range(count):
            block = spot(a, side, source(a, k))
            side_copies[a][k].wait_recv()
            far_copies[a][k] = remote(block, block, f_s.at[a, k], f_r.at[a, k], (here, core))
            far_copies[a][k].start()

    def arrive(copies):
        for copy in copies:
            copy.wait_recv()

    def exchange(n, src, dst):
        over = remote(src, dst.at[t], ag_s.at[n, 0], ag_r.at[n, 0], (here, side))
        near = remote(src, dst.at[t], ag_s.at[n, 1], ag_r.at[n, 1], (here, core))
        over.start()
        near.start()
        return over, near

    def pass_on(n, pair, dst):
        pair[0].wait_recv()
        along = remote(dst.at[side], dst.at[side], ag_s.at[n, 2], ag_r.at[n, 2], (here, core))
        along.start()
        return pair + (along,)

    launch(0)
    launch(1)
    cot_pair = exchange(0, cot, cot_all)
    cot_all[t] = cot[...]
    spread(0, 0, 8)
    forward(0)
    arrive(near_copies[0])
    arrive(far_copies[0])
    columns = small_all[...].reshape(-1, 128)
    vec = columns.T[:32]
    vec_out[...] = vec
    heads = qkv_out.shape[2] // 3
    for tt in range(4):
        cut = slice(tt * heads, (tt + 1) * heads)
        qkv_bias[tt] = jnp.concatenate([vec[5:6, cut], jnp.zeros((1, heads), F32), vec[6:7, cut]], axis=1)
    inputs = tok[...].astype(F32)
    unit, _ = unit_norm(inputs)
    first = (unit * vec[0:1] + vec[1:2]).astype(BF)
    acc[...] = inputs + vec[4:5]

    def attend(tt):
        weights = wall[tt].reshape(8 * packed.shape[0], -1)
        qkv = (nn(first, weights[:, : 3 * heads]) + qkv_bias[tt]).astype(BF)
        qkv_out[tt] = qkv
        mixed = []
        for i in range(rows // SEQ_PAD):
            part = qkv[i * SEQ_PAD : (i + 1) * SEQ_PAD]
            sides = []
            for h in range(heads // HEAD_DIM):
                q, k, v = (part[:, j * heads + h * HEAD_DIM : j * heads + (h + 1) * HEAD_DIM] for j in range(3))
                sides.append(nn(softmax_rows(q, k).astype(BF), v).astype(BF))
            mixed.append(jnp.concatenate(sides, axis=1))
        mixed = jnp.concatenate(mixed, axis=0)
        mixed_out[tt] = mixed
        acc[...] += nt(mixed, weights[:, 3 * heads :])

    spread(1, 0, 4)
    launch(3, slice(1, 7, 2))
    spread(1, 4, 8)
    launch(3, slice(0, 7, 2))
    launch(2)
    cot_pair = pass_on(0, cot_pair, cot_all)
    attend(t)
    forward(1)
    attend(side)
    arrive(near_copies[1])
    attend(core)
    arrive(far_copies[1])
    attend(far)

    kept_copies = []

    def save(n, src, dst):
        copy = pltpu.make_async_copy(src, dst, save_s.at[n])
        copy.start()
        kept_copies.append(copy)

    hidden = acc[...]
    hidden_out[...] = hidden
    unit, _ = unit_norm(hidden)
    second = (unit * vec[2:3] + vec[3:4]).astype(BF)
    sec_all[t] = second
    sec_pair = exchange(1, sec_all.at[t], sec_all)
    logits = nt(vec[7:15].astype(BF), second)
    raised = jnp.exp(logits - jnp.max(logits, axis=0, keepdims=True))
    probs = raised / jnp.sum(raised, axis=0, keepdims=True)
    probs_out[...] = probs
    lane = lax.broadcasted_iota(jnp.int32, probs.shape, 0)
    picked = [jnp.sum(jnp.where(lane == ids[k : k + 1], probs, 0.0), axis=0, keepdims=True) for k in range(2)]
    gates[...] = jnp.concatenate(picked + [jnp.zeros((6, rows), F32)], axis=0)
    gates_all[t] = gates[...]
    gate_pair = exchange(2, gates, gates_all)

    pair_rows = 2 * QUARTER

    def onehots(tt, base):
        at = lax.broadcasted_iota(jnp.int32, (pair_rows, rows), 0) + base
        return at == cols[tt, 0:1], at == cols[tt, 1:2]

    def pick(base, source):
        total = None
        for tt in range(4):
            one, two = onehots(tt, base)
            part = nn(jnp.logical_or(one, two).astype(F32).astype(BF), source[tt])
            total = part if total is None else total + part
        return total.astype(BF)

    def chunk(i):
        c = lax.rem(lax.div(d, 2) + 1 + i, 4)
        return c, pl.multiple_of(c * pair_rows, pair_rows)

    save(0, hidden_out, hidden_hbm)
    save(1, qkv_out, qkv_hbm)
    save(2, mixed_out, mixed_hbm)
    save(3, wall, wall_hbm)
    arrive([cot_pair[1], cot_pair[2]])
    for i in range(4):
        c, base = chunk(i)
        raw[pl.ds(base, pair_rows)] = pick(base, cot_all)
    sec_pair = pass_on(1, sec_pair, sec_all)
    gate_pair = pass_on(2, gate_pair, gates_all)
    arrive([sec_pair[1], sec_pair[2], gate_pair[1], gate_pair[2]])

    sent = []

    for i in range(4):
        c, base = chunk(i)
        x_buf[pl.ds(base, pair_rows)] = pick(base, sec_all)
        for h in range(2):
            e = 2 * c + h
            block = x_buf.at[pl.ds(pl.multiple_of(base + h * QUARTER, QUARTER), QUARTER)]
            copy = remote(block, x_out.at[d], x_s.at[e], x_r.at[d], (e * cells + cell, t))
            keep = pltpu.make_async_copy(block, x_out.at[d], own.at[4])
            sent.append((e, copy, keep))

            @pl.when(e == d)
            def _():
                keep.start()

            @pl.when(e != d)
            def _():
                copy.start()

    spread(2, 0, 8)
    spread(3, 0, 4)
    forward(2)
    for i in range(4):
        c, base = chunk(i)
        gate = None
        for tt in range(4):
            one, two = onehots(tt, base)
            part = jnp.where(one, gates_all[tt, 0:1], jnp.where(two, gates_all[tt, 1:2], 0.0))
            part = jnp.sum(part, axis=1, keepdims=True)
            gate = part if gate is None else gate + part
        kept = (gate * raw[pl.ds(base, pair_rows)].astype(F32)).astype(BF)
        g_out[pl.ds(2 * c, 2)] = kept.reshape(2, QUARTER, kept.shape[1])
    save(4, g_out, g_hbm)

    forward(3, 4)
    for a in (2, 3):
        arrive(near_copies[a])
        arrive(far_copies[a])
    for k in range(4, 8):
        block = spot(3, t, source(3, k))
        remote(block, block, dp_s.at[3, k], dp_r.at[3, source(3, k)], at_dp(k)).wait_recv()
    for k in range(1, 8):
        g = lax.rem(d + 8 - k, 8)
        remote(x_buf.at[pl.ds(0, QUARTER)], x_out.at[g], x_s.at[g], x_r.at[g], at_dp(8 - k)).wait_recv()
    for e, copy, keep in sent:

        @pl.when(e == d)
        def _():
            keep.wait()

        @pl.when(e != d)
        def _():
            copy.wait_send()

    for copy in kept_copies:
        copy.wait()
    for copy in cross:
        copy.wait_send()
    for a in range(4):
        for copy in dp_copies[a] + side_copies[a] + near_copies[a] + far_copies[a]:
            copy.wait_send()
    for trio in (cot_pair, sec_pair, gate_pair):
        for copy in trio:
            copy.wait_send()


def gelu_both(x):
    phi = 0.5 * (1.0 + lax.erf(x * (0.5**0.5)))
    slope = phi + x * (jnp.exp(-0.5 * x * x) * 0.3989422804014327)
    return x * phi, slope


def middle_kernel(
    cells,
    x_ref, g_src, expert_all, up_bias, vec, cols,
    r_out, q_out, y_out, e_out, e_side_out, dup_out, ddown_out,
    w_buf, act_buf, pre_buf, x_turned, g_turned, acc, y_acc, y_buf, b_buf, q_buf, g_in, b_in, q_in,
    blocks, core_in, side_buf, side_in, q_blocks, q_core, q_side, q_mid,
    load, store, w_s, w_r, g_s, g_r, a_s, a_r, c_s, c_r, y_s, y_r, e_s, e_r, f_s, f_r, own, core_free, side_free,
):
    d, cell, t = place(cells)
    core, side, far = tensor_peers(t)
    here = d * cells + cell
    width = x_ref.shape[1]
    ff = act_buf.shape[1]
    half = width // 8
    pair_rows = 2 * QUARTER

    def at_dp(k):
        return (lax.rem(d + k, 8) * cells + cell, t)

    twin = d + 1 - 2 * lax.rem(d, 2)
    near_z = d + 2 - 4 * lax.rem(lax.div(d, 2), 2)
    early = (d, twin, near_z, twin + near_z - d)
    late = tuple(lax.rem(p + 4, 8) for p in early)
    loads = [[pltpu.make_async_copy(expert_all.at[t], w_buf.at[t], load.at[0, 0])]]
    for i, tt in enumerate((core, side, far)):
        loads.append(
            [pltpu.make_async_copy(expert_all.at[tt, p], w_buf.at[tt, p], load.at[i + 1, k]) for k, p in enumerate(early)]
        )
    for copy in sum(loads, []):
        copy.start()
    barrier = pltpu.get_barrier_semaphore()
    for k in range(1, 8):
        signal(barrier, at_dp(k))
    signal(barrier, (here, core))
    signal(barrier, (here, side))
    pl.semaphore_wait(barrier, 9)

    sent = []

    def post(c, src, out, send, recv, keep_sem):
        for h in range(2):
            g = 2 * c + h
            copy = remote(src.at[g], out.at[d], send.at[g], recv.at[d], (g * cells + cell, t))
            keep = pltpu.make_async_copy(src.at[g], out.at[d], keep_sem)
            sent.append((g, copy))

            @pl.when(g == d)
            def _():
                keep.start()

            @pl.when(g != d)
            def _():
                copy.start()

    def landed(g, src, out, send, recv, keep_sem):
        @pl.when(g == d)
        def _():
            pltpu.make_async_copy(src.at[g], out.at[g], keep_sem).wait()

        @pl.when(g != d)
        def _():
            remote(src.at[g], out.at[g], send.at[g], recv.at[g], (g * cells + cell, t)).wait_recv()

    for i in range(4):
        post(lax.rem(lax.div(d, 2) + 1 + i, 4), g_src, g_in, g_s, g_r, own.at[3])
    w_side, w_near, w_far = [], [], []
    for k, p in enumerate(late):
        block = expert_all.at[t, p]
        w_side.append(remote(block, w_buf.at[t, p], w_s.at[0, k], w_r.at[0, k], (here, side)))
        w_near.append(remote(block, w_buf.at[t, p], w_s.at[1, k], w_r.at[1, k], (here, core)))
        w_far.append(remote(w_buf.at[side, p], w_buf.at[side, p], w_s.at[2, k], w_r.at[2, k], (here, core)))
    for copy in w_side + w_near:
        copy.start()
    x_turned[...] = x_ref[...].T
    dup_out[...] = jnp.zeros_like(dup_out)

    def w_in(tt):
        return w_buf[tt, :, 0:half].reshape(width, ff)

    def w_out(tt):
        return w_buf[tt, :, half : 2 * half].reshape(width, ff)

    def held(tt, base):
        return pl.ds(pl.multiple_of(tt * SLOTS + base, pair_rows), pair_rows)

    y_acc[...] = jnp.broadcast_to(vec[pl.ds(15 + d, 1)], y_acc.shape)

    def ahead(tt):
        def rows_step(i, carry):
            base = pl.multiple_of(i * pair_rows, pair_rows)
            span = pl.ds(base, pair_rows)
            pre = nn(x_ref[span], w_in(tt)) + up_bias[tt]
            act, slope = gelu_both(pre)
            act = act.astype(BF)
            act_buf[held(tt, base)] = act
            pre_buf[held(tt, base)] = slope.astype(BF)
            y_acc[span] += nt(act, w_out(tt))
            return carry

        lax.fori_loop(0, 4, rows_step, 0)

    loads[0][0].wait()
    ahead(t)
    for copy in loads[1]:
        copy.wait()
    for copy in w_near:
        copy.wait_recv()
    ahead(core)
    for i in range(4):
        w_side[i].wait_recv()
        w_far[i].start()
    for copy in loads[2]:
        copy.wait()
    ahead(side)
    for copy in loads[3]:
        copy.wait()
    for copy in w_far:
        copy.wait_recv()
    ahead(far)
    for copy in w_far:
        copy.wait_send()
    y_buf[...] = y_acc[...].astype(BF).reshape(y_buf.shape)
    ones = jnp.ones((8, width), BF)
    for i in range(4):
        c = lax.rem(lax.div(d, 2) + 3 - i, 4)
        base = pl.multiple_of(c * pair_rows, pair_rows)
        pair = pl.ds(2 * c, 2)
        for h in range(2):
            landed(2 * c + h, g_src, g_in, g_s, g_r, own.at[3])
        acc[...] = jnp.zeros_like(acc)

        def slice_back(tt, carry):
            grad = nn(g_in[pair].reshape(pair_rows, width), w_out(tt)) * pre_buf[held(tt, base)].astype(F32)
            grad = grad.astype(BF)
            pre_buf[held(tt, base)] = grad
            acc[...] += nt(grad, w_in(tt))
            dup_out[tt] += jnp.sum(grad.astype(F32), axis=0, keepdims=True)
            return carry

        lax.fori_loop(0, 4, slice_back, 0)
        b_buf[pair] = acc[...].astype(BF).reshape(2, QUARTER, width)
        post(c, b_buf, b_in, a_s.at[0], a_r.at[0], own.at[0])
        for h in range(2):
            g = 2 * c + h
            z = y_buf[g].astype(F32) * g_in[g].astype(F32)
            high = z.astype(BF)
            q_buf[g] = nt(ones, high) + nt(ones, (z - high.astype(F32)).astype(BF))
        post(c, q_buf, q_in, a_s.at[2], a_r.at[2], own.at[2])
    for i in range(4):
        post(lax.rem(lax.div(d, 2) + 3 - i + 4, 4), y_buf, y_out, a_s.at[1], a_r.at[1], own.at[1])
    g_rows = g_in[...].reshape(SLOTS, width)
    g_turned[...] = g_rows.T
    ddown_out[...] = jnp.sum(g_rows.astype(F32), axis=0, keepdims=True)

    def grad_slice(tt, carry):
        def grad_rows(n, inner):
            span = pl.ds(pl.multiple_of(n * 2 * half, 2 * half), 2 * half)
            pair = pl.ds(2 * n, 2)
            at = pl.ds(pl.multiple_of(tt * SLOTS, SLOTS), SLOTS)
            w_buf[tt, pair, 0:half] = nn(x_turned[span], pre_buf[at]).astype(BF).reshape(2, half, ff)
            w_buf[tt, pair, half : 2 * half] = nn(g_turned[span], act_buf[at]).astype(BF).reshape(2, half, ff)
            return inner

        lax.fori_loop(0, 4, grad_rows, 0)
        return carry

    lax.fori_loop(0, 4, grad_slice, 0)

    pl.semaphore_signal(core_free, inc=1, device_id=(here, core), device_id_type=MESH)
    pl.semaphore_signal(side_free, inc=1, device_id=(here, side), device_id_type=MESH)
    pl.semaphore_wait(core_free, 1)

    def inbox(i, p):
        return pl.ds(pl.multiple_of((i * 8 + p) * 2 * half, 2 * half), 2 * half)

    near = {}
    for i, tt in enumerate((far, core)):
        for k in range(1, 9):
            p = lax.rem(d + k, 8)
            near[i, k] = remote(
                w_buf.at[tt, p], act_buf.at[inbox(i, p)], e_s.at[i, k - 1], e_r.at[i, k - 1], (here, core)
            )
            near[i, k].start()
    pl.semaphore_wait(side_free, 1)
    over = {}
    for k in range(1, 9):
        p = lax.rem(d + k, 8)
        near[0, k].wait_recv()
        total = w_buf[side, p].astype(F32) + act_buf[inbox(0, p)].astype(F32)
        w_buf[side, p] = total.astype(BF)
        if k <= EARLY:
            over[k] = remote(
                w_buf.at[side, p], pre_buf.at[inbox(0, p)], f_s.at[k - 1], f_r.at[k - 1], (here, side)
            )
            over[k].start()
    keep_side = pltpu.make_async_copy(w_buf.at[side], e_side_out, store.at[1])
    keep_side.start()

    def onehots(tt):
        at = lax.broadcasted_iota(jnp.int32, (cols.shape[1], SLOTS), 1)
        return at == cols[tt, :, 0:1], at == cols[tt, :, 1:2]

    for k in range(1, 9):
        e = lax.rem(d + k, 8)
        landed(e, b_buf, b_in, a_s.at[0], a_r.at[0], own.at[0])
        landed(e, q_buf, q_in, a_s.at[2], a_r.at[2], own.at[2])
    q_line = jnp.concatenate([q_in[e] for e in range(8)], axis=1)
    owner = jnp.concatenate([jnp.full((8, QUARTER), e, jnp.int32) for e in range(8)], axis=1)
    q_line = jnp.where(lax.broadcasted_iota(jnp.int32, q_line.shape, 0) == owner, q_line, 0.0)
    q_high = q_line.astype(BF)
    q_both = jnp.concatenate([q_high, (q_line - q_high.astype(F32)).astype(BF)], axis=0)
    b_rows = b_in[...].reshape(SLOTS, width)

    def back_block(tt):
        one, two = onehots(tt)
        hot = jnp.logical_or(one, two).astype(F32).astype(BF)
        q = nt(q_both, hot)
        return nn(hot, b_rows), q[0:8] + q[8:16]

    def core_send(n, i, src, dst):
        copy = remote(src.at[i], dst.at[i], c_s.at[n, i], c_r.at[n, i], (here, core))
        copy.start()
        return copy

    def side_send(n, src, dst):
        copy = remote(src, dst, y_s.at[n], y_r.at[n], (here, side))
        copy.start()
        return copy

    core_b, core_q = [], []
    for i, tt in enumerate((far, core)):
        total, q = back_block(tt)
        blocks[i] = total.astype(BF)
        q_blocks[i] = q
        core_b.append(core_send(0, i, blocks, core_in))
        core_q.append(core_send(1, i, q_blocks, q_core))
    total, q = back_block(side)
    core_b[0].wait_recv()
    core_q[0].wait_recv()
    side_buf[...] = (total + core_in[0].astype(F32)).astype(BF)
    q_mid[...] = q + q_core[0]
    side_b = side_send(0, side_buf, side_in)
    side_q = side_send(1, q_mid, q_side)
    total, q = back_block(t)
    core_b[1].wait_recv()
    core_q[1].wait_recv()
    r_out[...] = total + core_in[1].astype(F32)
    q_out[...] = q + q_core[1]

    for k in range(1, 9):
        p = lax.rem(d + k, 8)
        near[1, k].wait_recv()
        total = w_buf[t, p].astype(F32) + act_buf[inbox(1, p)].astype(F32)
        if k <= EARLY:
            over[k].wait_recv()
            total = total + pre_buf[inbox(0, p)].astype(F32)
        w_buf[t, p] = total.astype(BF)
    keep_e = pltpu.make_async_copy(w_buf.at[t], e_out, store.at[0])
    keep_e.start()
    side_b.wait_recv()
    side_q.wait_recv()
    r_out[...] += side_in[...].astype(F32)
    q_out[...] += q_side[...]

    for k in range(1, 9):
        landed(lax.rem(d + k, 8), y_buf, y_out, a_s.at[1], a_r.at[1], own.at[1])
    for copy in core_b + core_q + [side_b, side_q] + list(near.values()) + list(over.values()) + w_near:
        copy.wait_send()
    for copy in w_side:
        copy.wait_send()
    for g, copy in sent:

        @pl.when(g != d)
        def _():
            copy.wait_send()

    keep_e.wait()
    keep_side.wait()


def back_kernel(
    cells,
    tok, hid, r_ref, cols, gates, cot, probs, picked_ref, vec, y_hbm, wall_hbm, qkv_hbm, mixed_hbm, e_src, e_side_src,
    bias_msg, out, token_grad, e_out, a_out, msg_all, vec_all,
    n1, vec_grad, vec_msg, a_grad, qv_grad, a_core, a_mid, a_side, a_fin, a_cross, a_in,
    blocks, core_in, side_buf, side_in, e_own, e_in, y_rows, wall, qkv_ref, mixed_ref, fetch,
    c_s, c_r, y_s, y_r, e_s, e_r, f_s, f_r, x_s, x_r, z_s, z_r, o_s, o_r, own, m_s, m_r, v_s, v_r,
):
    d, cell, t = place(cells)
    core, side, far = tensor_peers(t)
    here = d * cells + cell
    fetches = []
    for n, (src, dst) in enumerate(((wall_hbm, wall), (qkv_hbm, qkv_ref), (mixed_hbm, mixed_ref), (y_hbm, y_rows))):
        copy = pltpu.make_async_copy(src, dst, fetch.at[n])
        copy.start()
        fetches.append(copy)
    heads = qkv_ref.shape[2] // 3
    rows = tok.shape[0]
    width = tok.shape[1]
    spot = d * 4 + t
    twin = d + 1 - 2 * lax.rem(d, 2)

    def at_dp(k):
        return (lax.rem(d + k, 8) * cells + cell, t)

    others = [(k, m) for k in range(8) for m in range(4) if k or m]

    def other(k, m):
        return lax.rem(d + k, 8), lax.rem(t + m, 4)

    barrier = pltpu.get_barrier_semaphore()
    for k, m in others:
        dd, tt = other(k, m)
        signal(barrier, (dd * cells + cell, tt))
    pl.semaphore_wait(barrier, 31)

    waits = []
    late = range(EARLY + 1, 9)
    over_e, load_e = {}, {}
    for k in range(1, EARLY + 1):
        copy = remote(e_src.at[lax.rem(d + k, 8)], e_out.at[d], e_s.at[k], e_r.at[k], at_dp(k))
        copy.start()
        waits.append(copy)
    for k in late:
        p = lax.rem(d + k, 8)
        over_e[k] = remote(e_side_src.at[p], e_in.at[p], f_s.at[k - 1], f_r.at[k - 1], (here, side))
        over_e[k].start()
        load_e[k] = pltpu.make_async_copy(e_src.at[p], e_own.at[p], own.at[k])
        load_e[k].start()

    def finish_expert(k):
        p = lax.rem(d + k, 8)
        load_e[k].wait()
        over_e[k].wait_recv()
        e_own[p] = (e_own[p].astype(F32) + e_in[p].astype(F32)).astype(BF)
        if k < 8:
            copy = remote(e_own.at[p], e_out.at[d], e_s.at[k], e_r.at[k], at_dp(k))
            waits.append(copy)
        else:
            copy = pltpu.make_async_copy(e_own.at[p], e_out.at[d], own.at[0])
            load_e[0] = copy
        copy.start()
    for n, (k, m) in enumerate(others):
        dd, tt = other(k, m)
        copy = remote(bias_msg.at[dd * 4 + tt], msg_all.at[spot], m_s.at[n], m_r.at[n], (dd * cells + cell, tt))
        copy.start()
        waits.append(copy)
    msg_own = pltpu.make_async_copy(bias_msg.at[spot], msg_all.at[spot], own.at[1])
    msg_own.start()

    hidden = hid[...]
    picked = picked_ref[...]
    logit = picked - probs[...] * jnp.sum(picked, axis=0, keepdims=True)
    high = logit.astype(BF)
    both = jnp.concatenate([high, (logit - high.astype(F32)).astype(BF)], axis=0)
    unit, inv = unit_norm(hidden)
    gain = vec[2:3]
    second = (unit * gain + vec[3:4]).astype(BF)
    router_grad = nn(both, second)
    vec_grad[...] = jnp.zeros_like(vec_grad)
    vec_grad[8:16] = router_grad[0:8] + router_grad[8:16]
    table = vec[7:15].astype(BF)
    n2 = r_ref[...] + tn(both, jnp.concatenate([table, table], axis=0))
    vec_grad[2:3] = jnp.sum(n2 * unit, axis=0, keepdims=True)
    vec_grad[3:4] = jnp.sum(n2, axis=0, keepdims=True)
    scaled = n2 * gain
    back = inv * (
        scaled
        - jnp.mean(scaled, axis=-1, keepdims=True)
        - unit * jnp.mean(scaled * unit, axis=-1, keepdims=True)
    )
    hidden_grad = cot[...].astype(F32) + back
    token_grad[...] = hidden_grad
    branch = hidden_grad.astype(BF)
    vec_grad[4:5] = jnp.sum(branch.astype(F32), axis=0, keepdims=True)
    unit1, inv1 = unit_norm(tok[...].astype(F32))
    first_norm = (unit1 * vec[0:1] + vec[1:2]).astype(BF)
    n1[...] = jnp.zeros_like(n1)

    def attend_back(tt):
        weights = wall[tt].reshape(width, -1)
        qkv = qkv_ref[tt]
        mixed_grad = nn(branch, weights[:, 3 * heads :]).astype(BF)
        triple = []
        for i in range(rows // SEQ_PAD):
            span = slice(i * SEQ_PAD, (i + 1) * SEQ_PAD)
            part, grad = qkv[span], mixed_grad[span]
            sides = [[], [], []]
            for h in range(heads // HEAD_DIM):
                q, k, v = (part[:, j * heads + h * HEAD_DIM : j * heads + (h + 1) * HEAD_DIM] for j in range(3))
                g = grad[:, h * HEAD_DIM : (h + 1) * HEAD_DIM]
                w = softmax_rows(q, k)
                w_grad = nt(g, v)
                s_grad = (w * (w_grad - jnp.sum(w * w_grad, axis=-1, keepdims=True))).astype(BF)
                sides[0].append((nn(s_grad, k) * (HEAD_DIM**-0.5)).astype(BF))
                sides[1].append((tn(s_grad, q) * (HEAD_DIM**-0.5)).astype(BF))
                sides[2].append(tn(w.astype(BF), g).astype(BF))
            triple.append(jnp.concatenate(sides[0] + sides[1] + sides[2], axis=1))
        triple = jnp.concatenate(triple, axis=0)
        grad = jnp.concatenate([tn(first_norm, triple), tn(branch, mixed_ref[tt])], axis=1).astype(BF)
        a_grad[tt] = grad.reshape(8, width // 8, -1)
        n1[...] += nt(triple, weights[:, : 3 * heads])
        sums = jnp.sum(triple.astype(F32), axis=0, keepdims=True)
        qv_grad[tt] = sums

    def core_a(i, tt):
        copy = remote(a_grad.at[tt], a_core.at[i], c_s.at[i], c_r.at[i], (here, core))
        copy.start()
        return copy

    order = [lax.rem(twin + 2 * m, 8) for m in range(4)] + [lax.rem(d + 2 * m, 8) for m in (1, 2, 3, 0)]
    for copy in fetches:
        copy.wait()
    attend_back(far)
    near_a = core_a(0, far)
    finish_expert(EARLY + 1)
    attend_back(side)
    near_a.wait_recv()
    over_a = []
    for n, p in enumerate(order):
        a_mid[p] = (a_grad[side, p].astype(F32) + a_core[0, p].astype(F32)).astype(BF)
        copy = remote(a_mid.at[p], a_side.at[p], y_s.at[n], y_r.at[n], (here, side))
        copy.start()
        over_a.append(copy)
    finish_expert(EARLY + 2)
    attend_back(core)
    far_a = core_a(1, core)
    for k in list(late)[2:-1]:
        finish_expert(k)
    attend_back(t)
    finish_expert(8)

    def out_block(tt):
        at = lax.broadcasted_iota(jnp.int32, (rows, SLOTS), 1)
        one, two = at == cols[tt, :, 0:1], at == cols[tt, :, 1:2]
        hot = jnp.where(one, gates[tt, :, 0:1], jnp.where(two, gates[tt, :, 1:2], 0.0)).astype(BF)
        return nn(hot, y_rows[...])

    out_copies = []
    for i, tt in enumerate((far, core)):
        blocks[i] = out_block(tt).astype(BF)
        copy = remote(blocks.at[i], core_in.at[i], o_s.at[i], o_r.at[i], (here, core))
        copy.start()
        out_copies.append(copy)
    total = out_block(side)
    out_copies[0].wait_recv()
    side_buf[...] = (total + core_in[0].astype(F32)).astype(BF)
    side_out = remote(side_buf, side_in, o_s.at[2], o_r.at[2], (here, side))
    side_out.start()

    far_a.wait_recv()
    cross = []
    for n, p in enumerate(order):
        over_a[n].wait_recv()
        total = a_grad[t, p].astype(F32) + a_core[1, p].astype(F32) + a_side[p].astype(F32)
        if n < 4:
            a_fin[p] = total.astype(BF)
            copy = remote(a_fin.at[p], a_cross.at[n], x_s.at[n], x_r.at[n], (twin * cells + cell, t))
            copy.start()
            cross.append(copy)
        else:
            m = (n - 3) % 4
            cross[m].wait_recv()
            total = total + a_cross[m].astype(F32)
            if m:
                a_fin[p] = total.astype(BF)
                copy = remote(a_fin.at[p], a_in.at[m], z_s.at[m], z_r.at[m], at_dp(2 * m))
                copy.start()
                waits.append(copy)
            else:
                a_out[...] = total

    grad = n1[...]
    vec_grad[0:1] = jnp.sum(grad * unit1, axis=0, keepdims=True)
    vec_grad[1:2] = jnp.sum(grad, axis=0, keepdims=True)
    for j, row in ((0, 5), (2, 6)):
        parts = [qv_grad[tt][:, j * heads : (j + 1) * heads] for tt in range(4)]
        vec_grad[row : row + 1] = jnp.concatenate(parts, axis=1)
    turned = vec_grad[...].T
    vec_msg[...] = turned.reshape(vec_msg.shape)
    for n, (k, m) in enumerate(others):
        dd, tt = other(k, m)
        copy = remote(vec_msg.at[dd * 4 + tt], vec_all.at[spot], v_s.at[n], v_r.at[n], (dd * cells + cell, tt))
        copy.start()
        waits.append(copy)
    vec_all[spot] = vec_msg[spot]
    scaled = grad * vec[0:1]
    token_grad[...] += inv1 * (
        scaled
        - jnp.mean(scaled, axis=-1, keepdims=True)
        - unit1 * jnp.mean(scaled * unit1, axis=-1, keepdims=True)
    )
    total = out_block(t)
    out_copies[1].wait_recv()
    total = total + core_in[1].astype(F32)
    side_out.wait_recv()
    out[...] = (hid[...] + (total + side_in[...].astype(F32))).astype(BF)
    for copy in waits:
        copy.wait()
    for m in range(1, 4):
        a_out[...] += a_in[m].astype(F32)
    load_e[0].wait()
    msg_own.wait()
    for copy in [near_a, far_a, side_out] + out_copies + over_a + cross + list(over_e.values()):
        copy.wait_send()


def pad_images(rows, fill=0):
    images = rows.reshape((-1, SEQ) + rows.shape[1:])
    spare = [(0, 0), (0, SEQ_PAD - SEQ)] + [(0, 0)] * (rows.ndim - 1)
    return jnp.pad(images, spare, constant_values=fill).reshape((-1,) + rows.shape[1:])


def drop_pad(rows):
    return rows.reshape((-1, SEQ_PAD) + rows.shape[1:])[:, :SEQ].reshape((-1,) + rows.shape[1:])


def body(
    tokens, ln1_gain, ln1_shift, qkv_weight, qv_bias, out_weight, out_bias, ln2_gain, ln2_shift,
    router_weight, expert_in, expert_in_bias, expert_out, expert_out_bias, expert_ids, expert_slots,
    cotangent,
):
    n_dp = lax.axis_size("dp")
    cells = n_dp // 8
    width = tokens.shape[1]
    experts = expert_in.shape[0]
    head_cols = qkv_weight.shape[2]
    ff_slice = expert_in.shape[2]
    index = lax.axis_index("dp")
    t = lax.axis_index("tensor")
    d, cell = index // cells, index % cells
    peers = [[row * cells + c for c in range(cells)] for row in range(8)]

    packed = jnp.concatenate([qkv_weight.reshape(-1, 3 * head_cols), out_weight.T], axis=1)
    expert_pack = [expert_in, jnp.swapaxes(expert_out, 1, 2)]
    lines = [ln1_gain, ln1_shift, ln2_gain, ln2_shift, out_bias, qv_bias[0], qv_bias[1]]
    small_a = jnp.concatenate([jnp.stack(lines, axis=1), router_weight, expert_out_bias.T], axis=1)
    small_b = expert_in_bias
    if cells > 1:
        packed = lax.all_gather(packed, "dp", axis=0, tiled=True, axis_index_groups=peers)
        expert_pack = [
            lax.all_gather(part, "dp", axis=1, tiled=True, axis_index_groups=peers) for part in expert_pack
        ]

        def quarter(piece, axis):
            piece = lax.all_gather(piece, "tensor", axis=axis, tiled=True)
            piece = lax.all_gather(piece, "dp", axis=axis, tiled=True, axis_index_groups=peers)
            size = piece.shape[axis] // 4
            return lax.dynamic_slice_in_dim(piece, t * size, size, axis)

        small_a, small_b = quarter(small_a, 0), quarter(small_b, 1)
    expert_pack = jnp.concatenate(expert_pack, axis=1)
    piece, ff_piece = small_a.shape[0], small_b.shape[1]
    small_a = jnp.pad(small_a.astype(F32), ((0, 0), (0, 128 - small_a.shape[1])))
    small_b = jnp.pad(small_b, ((0, 16 - experts), (0, 128 - ff_piece)))
    tok = pad_images(tokens)
    cot = pad_images(cotangent)
    rows = tok.shape[0]

    wanted = expert_slots - QUARTER * t
    inside = jnp.logical_and(expert_slots >= 0, jnp.logical_and(wanted >= 0, wanted < QUARTER))
    cols = jnp.where(inside, expert_ids * QUARTER + wanted, -1)
    cols = jnp.pad(pad_images(cols, -1).reshape(4, rows, TOP), ((0, 0), (0, 0), (0, 8 - TOP)), constant_values=-1)
    cols_t = jnp.swapaxes(cols, 1, 2)
    own_ids = lax.dynamic_slice_in_dim(expert_ids, t * tokens.shape[0], tokens.shape[0], 0)
    ids = jnp.pad(pad_images(own_ids, -1).T, ((0, 8 - TOP), (0, 0)), constant_values=-1)

    dma = pltpu.SemaphoreType.DMA

    def params(identity):
        return pltpu.CompilerParams(
            collective_id=identity, has_side_effects=True, vmem_limit_bytes=VMEM_LIMIT
        )

    def like(shape, dtype=BF):
        return jax.ShapeDtypeStruct(shape, dtype)

    slot_shape = (8, QUARTER, width)
    probs, gates, vec, hidden, qkv, mixed, wall, bias_all, expert_all, x_rows, g_rows = pl.pallas_call(
        functools.partial(front_kernel, cells),
        out_shape=[
            like((experts, rows), F32),
            like((4, 8, rows), F32),
            like((32, width), F32),
            like((rows, width), F32),
            like((4, rows, 3 * head_cols)),
            like((4, rows, head_cols)),
            like((4, 8) + packed.shape),
            like((4, 8) + small_b.shape),
            like((4,) + expert_pack.shape),
            like(slot_shape),
            like(slot_shape),
        ],
        in_specs=[HB] * 4 + [VM] * 4,
        out_specs=[VM] * 3 + [HB] * 8,
        scratch_shapes=[
            pltpu.VMEM((rows, width), F32),
            pltpu.VMEM((4, rows, 3 * head_cols), BF),
            pltpu.VMEM((4, rows, head_cols), BF),
            pltpu.VMEM((4, 8) + packed.shape, BF),
            pltpu.VMEM(slot_shape, BF),
            pltpu.VMEM((8, 4) + small_a.shape, F32),
            pltpu.VMEM((4, rows, width), BF),
            pltpu.VMEM((4, rows, width), BF),
            pltpu.VMEM((SLOTS, width), BF),
            pltpu.VMEM((SLOTS, width), BF),
            pltpu.VMEM((rows, width), F32),
            pltpu.VMEM((8, rows), F32),
            pltpu.VMEM((4, 1, 3 * head_cols), F32),
        ]
        + [dma((4, 8))] * 8
        + [dma((5,)), dma((3, 3)), dma((3, 3)), dma((8,)), dma((8,)), dma((4,)), dma((4,)), dma((5,))],
        compiler_params=params(0),
        name="front",
    )(packed, small_a, small_b, expert_pack, tok, cot, cols_t, ids)

    bias_all = jnp.swapaxes(bias_all, 0, 1)
    up_bias = lax.dynamic_index_in_dim(bias_all, d, 2, keepdims=False)[:, :, :ff_piece]
    up_bias = up_bias.astype(F32).reshape(4, 1, ff_slice)
    e_block = expert_pack.shape
    r_rows, picked, y_rows, expert_grad, side_grad, up_grad, down_grad = pl.pallas_call(
        functools.partial(middle_kernel, cells),
        out_shape=[
            like((rows, width), F32),
            like((8, rows), F32),
            like(slot_shape),
            like(e_block),
            like(e_block),
            like((4, 1, ff_slice), F32),
            like((1, width), F32),
        ],
        in_specs=[VM, HB, HB, VM, VM, VM],
        out_specs=[VM, VM, HB, HB, HB, VM, VM],
        scratch_shapes=[
            pltpu.VMEM(expert_all.shape, BF),
            pltpu.VMEM((4 * SLOTS, ff_slice), BF),
            pltpu.VMEM((4 * SLOTS, ff_slice), BF),
            pltpu.VMEM((width, SLOTS), BF),
            pltpu.VMEM((width, SLOTS), BF),
            pltpu.VMEM((2 * QUARTER, width), F32),
            pltpu.VMEM((SLOTS, width), F32),
            pltpu.VMEM(slot_shape, BF),
            pltpu.VMEM(slot_shape, BF),
            pltpu.VMEM((8, 8, QUARTER), F32),
            pltpu.VMEM(slot_shape, BF),
            pltpu.VMEM(slot_shape, BF),
            pltpu.VMEM((8, 8, QUARTER), F32),
            pltpu.VMEM((2, rows, width), BF),
            pltpu.VMEM((2, rows, width), BF),
            pltpu.VMEM((rows, width), BF),
            pltpu.VMEM((rows, width), BF),
            pltpu.VMEM((2, 8, rows), F32),
            pltpu.VMEM((2, 8, rows), F32),
            pltpu.VMEM((8, rows), F32),
            pltpu.VMEM((8, rows), F32),
            dma((4, 4)), dma((2,)), dma((3, 4)), dma((3, 4)), dma((8,)), dma((8,)), dma((3, 8)), dma((3, 8)), dma((2, 2)), dma((2, 2)),
            dma((2,)), dma((2,)), dma((2, 8)), dma((2, 8)), dma((8,)), dma((8,)), dma((4,)),
            pltpu.SemaphoreType.REGULAR, pltpu.SemaphoreType.REGULAR,
        ],
        compiler_params=params(1),
        name="middle",
    )(x_rows.reshape(SLOTS, width), g_rows, expert_all, up_bias, vec, cols)

    message = jnp.pad(
        jnp.stack(
            [
                jnp.pad(up_grad.reshape(32, ff_piece), ((0, 0), (0, 128 - ff_piece))),
                jnp.pad(down_grad.reshape(32, piece), ((0, 0), (0, 128 - piece))),
            ],
            axis=1,
        ),
        ((0, 0), (0, 6), (0, 0)),
    )
    a_block = wall.shape[1:]
    out, token_grad, expert_sum, attn_sum, messages, vec_all = pl.pallas_call(
        functools.partial(back_kernel, cells),
        out_shape=[
            like((rows, width)),
            like((rows, width), F32),
            like(e_block),
            like(a_block[1:], F32),
            like(message.shape, F32),
            like((32, piece, 128), F32),
        ],
        in_specs=[VM] * 9 + [HB] * 7,
        out_specs=[VM, VM, HB, VM, HB, VM],
        scratch_shapes=[
            pltpu.VMEM((rows, width), F32),
            pltpu.VMEM((128, width), F32),
            pltpu.VMEM((32, piece, 128), F32),
            pltpu.VMEM(wall.shape, BF),
            pltpu.VMEM((4, 1, 3 * head_cols), F32),
            pltpu.VMEM((2,) + a_block, BF),
            pltpu.VMEM(a_block, BF),
            pltpu.VMEM(a_block, BF),
            pltpu.VMEM(a_block, BF),
            pltpu.VMEM((4,) + a_block[1:], BF),
            pltpu.VMEM((4,) + a_block[1:], BF),
            pltpu.VMEM((2, rows, width), BF),
            pltpu.VMEM((2, rows, width), BF),
            pltpu.VMEM((rows, width), BF),
            pltpu.VMEM((rows, width), BF),
            pltpu.VMEM(e_block, BF),
            pltpu.VMEM(e_block, BF),
            pltpu.VMEM((SLOTS, width), BF),
            pltpu.VMEM(wall.shape, BF),
            pltpu.VMEM(qkv.shape, BF),
            pltpu.VMEM(mixed.shape, BF),
            dma((4,)),
            dma((2,)), dma((2,)), dma((8,)), dma((8,)), dma((8,)), dma((8,)), dma((8,)), dma((8,)),
            dma((4,)), dma((4,)), dma((4,)), dma((4,)), dma((3,)), dma((3,)), dma((9,)), dma((31,)), dma((31,)), dma((31,)), dma((31,)),
        ],
        compiler_params=params(2),
        name="back",
    )(
        tok, hidden, r_rows, cols, jnp.swapaxes(gates, 1, 2), cot, probs, picked, vec,
        y_rows.reshape(SLOTS, width), wall, qkv, mixed, expert_grad, side_grad, message,
    )

    grads = jnp.sum(vec_all, axis=0).T
    messages = jnp.sum(messages.reshape(8, 4, 8, 128), axis=1)
    up_sum, down_sum = messages[:, 0, :ff_piece], messages[:, 1, :piece]
    if cells > 1:
        expert_sum = lax.psum_scatter(
            expert_sum.astype(F32).reshape(8, 2, width // 8, -1), "dp", scatter_dimension=2, tiled=True,
            axis_index_groups=peers,
        )
        expert_sum = expert_sum.reshape(8, -1, expert_sum.shape[3])
        attn_sum = lax.psum_scatter(attn_sum, "dp", scatter_dimension=0, tiled=True, axis_index_groups=peers)

        def share(part):
            part = lax.psum(part, "dp", axis_index_groups=peers)
            part = lax.all_gather(part, "tensor", axis=1, tiled=True)
            size = part.shape[1] // (4 * cells)
            return lax.dynamic_slice_in_dim(part, (cell * 4 + t) * size, size, 1)

        grads, up_sum, down_sum = share(grads), share(up_sum), share(down_sum)
    own_rows = expert_in.shape[1]
    return (
        drop_pad(out),
        drop_pad(token_grad),
        grads[0],
        grads[1],
        attn_sum[:, : 3 * head_cols].reshape(-1, 3, head_cols),
        grads[5:7],
        attn_sum[:, 3 * head_cols :].T,
        grads[4],
        grads[2],
        grads[3],
        grads[8:16].T,
        expert_sum[:, :own_rows].astype(F32),
        up_sum,
        jnp.swapaxes(expert_sum[:, own_rows:], 1, 2).astype(F32),
        down_sum,
    )


def solution(mesh):
    both = ("dp", "tensor")
    return jax.shard_map(
        body,
        mesh=mesh,
        in_specs=(
            P(both, None),
            P(both),
            P(both),
            P("dp", None, "tensor"),
            P(None, both),
            P("tensor", "dp"),
            P(both),
            P(both),
            P(both),
            P(both, None),
            P(None, "dp", "tensor"),
            P(None, both),
            P(None, "tensor", "dp"),
            P(None, both),
            P("dp", None),
            P("dp", None),
            P(both, None),
        ),
        out_specs=(
            P(both, None),
            P(both, None),
            P(both),
            P(both),
            P("dp", None, "tensor"),
            P(None, both),
            P("tensor", "dp"),
            P(both),
            P(both),
            P(both),
            P(both, None),
            P(None, "dp", "tensor"),
            P(None, both),
            P(None, "tensor", "dp"),
            P(None, both),
        ),
        check_vma=False,
    )
```

```python
import functools

import jax
import jax.numpy as jnp
from jax import lax
from jax.experimental import pallas as pl
from jax.experimental.pallas import tpu as pltpu
from jax.sharding import PartitionSpec as P

HEAD_DIM = 64
SEQ = 197
SEQ_PAD = 208
TOP = 2
QUARTER = 160
SLOTS = 8 * QUARTER
EARLY = 5
EPS = 1e-6
BF = jnp.bfloat16
F32 = jnp.float32
MESH = pl.DeviceIdType.MESH
VMEM_LIMIT = 60 * 1024 * 1024
VM = pl.BlockSpec(memory_space=pltpu.VMEM)
HB = pl.BlockSpec(memory_space=pl.ANY)


def nn(a, b):
    return lax.dot_general(a, b, (((1,), (0,)), ((), ())), preferred_element_type=F32)


def nt(a, b):
    return lax.dot_general(a, b, (((1,), (1,)), ((), ())), preferred_element_type=F32)


def tn(a, b):
    return lax.dot_general(a, b, (((0,), (0,)), ((), ())), preferred_element_type=F32)


def unit_norm(rows):
    centred = rows - jnp.mean(rows, axis=-1, keepdims=True)
    inv = lax.rsqrt(jnp.mean(centred * centred, axis=-1, keepdims=True) + EPS)
    return centred * inv, inv


def place(cells):
    index = lax.axis_index("dp")
    return lax.div(index, cells), lax.rem(index, cells), lax.axis_index("tensor")


def tensor_peers(t):
    core = t + 1 - 2 * lax.rem(t, 2)
    side = lax.rem(t + 2, 4)
    return core, side, lax.rem(core + 2, 4)


def remote(src, dst, send, recv, device):
    return pltpu.make_async_remote_copy(
        src_ref=src, dst_ref=dst, send_sem=send, recv_sem=recv, device_id=device, device_id_type=MESH
    )


def signal(barrier, device):
    pl.semaphore_signal(barrier, inc=1, device_id=device, device_id_type=MESH)


def softmax_rows(q, k):
    scores = nt(q, k) * (HEAD_DIM**-0.5)
    lane = lax.broadcasted_iota(jnp.int32, scores.shape, 1)
    scores = jnp.where(lane < SEQ, scores, -1e30)
    raised = jnp.exp(scores - jnp.max(scores, axis=-1, keepdims=True))
    return raised / jnp.sum(raised, axis=-1, keepdims=True)


def front_kernel(
    cells,
    qkv_w, out_w, lines, pair_bias, router_w, down_b, up_b, expert, tokens, cotangent, routes,
    probs_out, cols_out, gates_out, vec_out, tok_hbm, cot_hbm, hidden_hbm, qkv_hbm, mixed_hbm, wall_hbm, b_all,
    expert_all, x_out, g_hbm,
    packed, small_a, small_b, small_rows, tok, cols, gates_all, hidden_out, qkv_out, mixed_out, wall, g_out, small_all, cot_all, sec_all, x_buf, raw, acc, gates, qkv_bias,
    dp_s, dp_r, y_s, y_r, c_s, c_r, f_s, f_r, own, ag_s, ag_r, x_s, x_r, w_s, w_r, save_s,
):
    d, cell, t = place(cells)
    core, side, far = tensor_peers(t)
    here = d * cells + cell
    twin = d + 1 - 2 * lax.rem(d, 2)
    rows = tok.shape[0]
    srcs = (small_a, packed, small_b, expert)

    def at_dp(k):
        return (lax.rem(d + k, 8) * cells + cell, t)

    def spot(a, tt, s):
        return small_all.at[s, tt] if a == 0 else (None, wall, b_all, expert_all)[a].at[tt, s]

    barrier = pltpu.get_barrier_semaphore()
    for k in range(1, 8):
        signal(barrier, at_dp(k))
    signal(barrier, (here, core))
    signal(barrier, (here, side))
    joined = 3 * qkv_w.shape[2]
    for j in range(3):
        packed[:, j * qkv_w.shape[2] : (j + 1) * qkv_w.shape[2]] = qkv_w[:, j, :]
    packed[:, joined : joined + out_w.shape[0]] = out_w[...].astype(F32).T.astype(BF)
    small_rows[...] = jnp.zeros_like(small_rows)
    piece = lines.shape[1]
    small_rows[0:5, 0:piece] = lines[...].astype(F32)
    small_rows[5:7, 0:piece] = pair_bias[...].astype(F32)
    small_rows[7:15, 0:piece] = router_w[...].astype(F32).T
    small_rows[15:23, 0:piece] = down_b[...].astype(F32)
    small_a[...] = small_rows[...].T[0:piece]
    small_b[...] = jnp.zeros_like(small_b)
    small_b[:, 0 : up_b.shape[1]] = up_b[...].astype(F32)
    tok[...] = jnp.zeros_like(tok)
    for i in range(rows // SEQ_PAD):
        tok[i * SEQ_PAD : i * SEQ_PAD + SEQ] = tokens[i * SEQ : (i + 1) * SEQ]
    cot_all[t] = jnp.zeros_like(tok)
    for i in range(rows // SEQ_PAD):
        cot_all[t, i * SEQ_PAD : i * SEQ_PAD + SEQ] = cotangent[i * SEQ : (i + 1) * SEQ]
    pl.semaphore_wait(barrier, 9)

    mine = [
        pltpu.make_async_copy(srcs[a].at[d] if a == 3 else srcs[a], spot(a, t, d), own.at[a]) for a in range(4)
    ]
    dp_copies = [
        [
            remote(
                srcs[a].at[lax.rem(d + k, 8)] if a == 3 else srcs[a],
                spot(a, t, d),
                dp_s.at[a, k],
                dp_r.at[a, d if a == 3 else k],
                at_dp(k),
            )
            for k in ((2, 4, 6) if a == 1 else range(1, 8))
        ]
        for a in range(4)
    ]
    side_copies = [[None] * (4 if a == 3 else 8) for a in range(4)]
    near_copies = [[None] * (4 if a == 3 else 8) for a in range(4)]
    far_copies = [[None] * (4 if a == 3 else 8) for a in range(4)]

    cross = [remote(packed, wall.at[t, d], w_s.at[0], w_r.at[0], (twin * cells + cell, t))]

    def launch(a, part=slice(0, 7)):
        if part.start == 0:
            mine[a].start()
        for copy in dp_copies[a][part]:
            copy.start()
        if a == 1:
            cross[0].start()

    near_z = d + 2 - 4 * lax.rem(lax.div(d, 2), 2)
    near_twin = twin + near_z - d
    by_distance = [d, twin, near_z, near_twin] + [lax.rem(s + 4, 8) for s in (d, twin, near_z, near_twin)]

    def source(a, k):
        if a == 3:
            return by_distance[k]
        if a != 1:
            return lax.rem(d + 8 - k, 8)
        return lax.rem((d if k < 4 else twin) + 8 - 2 * (k % 4), 8)

    def spread(a, first, last):
        for k in range(first, last):
            block = spot(a, t, source(a, k))
            if k == 0:
                mine[a].wait()
            elif a == 3:
                remote(block, block, dp_s.at[a, k], dp_r.at[a, source(a, k)], at_dp(k)).wait_recv()
            elif a != 1 or k < 4:
                dp_copies[a][k - 1].wait_recv()
            else:
                cross[k - 4].wait_recv()
            if a == 1 and 0 < k < 4:
                cross.append(remote(block, block, w_s.at[k], w_r.at[k], (twin * cells + cell, t)))
                cross[k].start()
            side_copies[a][k] = remote(block, block, y_s.at[a, k], y_r.at[a, k], (here, side))
            side_copies[a][k].start()
            near_copies[a][k] = remote(block, block, c_s.at[a, k], c_r.at[a, k], (here, core))
            near_copies[a][k].start()

    def forward(a, count=8):
        for k in range(count):
            block = spot(a, side, source(a, k))
            side_copies[a][k].wait_recv()
            far_copies[a][k] = remote(block, block, f_s.at[a, k], f_r.at[a, k], (here, core))
            far_copies[a][k].start()

    def arrive(copies):
        for copy in copies:
            copy.wait_recv()

    def exchange(n, src, dst):
        over = remote(src, dst.at[t], ag_s.at[n, 0], ag_r.at[n, 0], (here, side))
        near = remote(src, dst.at[t], ag_s.at[n, 1], ag_r.at[n, 1], (here, core))
        over.start()
        near.start()
        return over, near

    def pass_on(n, pair, dst):
        pair[0].wait_recv()
        along = remote(dst.at[side], dst.at[side], ag_s.at[n, 2], ag_r.at[n, 2], (here, core))
        along.start()
        return pair + (along,)

    launch(0)
    launch(1)
    cot_pair = exchange(0, cot_all.at[t], cot_all)
    for tt in range(4):
        route = routes[tt]
        wanted = route[2:4] - QUARTER * t
        inside = jnp.logical_and(route[2:4] >= 0, jnp.logical_and(wanted >= 0, wanted < QUARTER))
        col = jnp.where(inside, route[0:2] * QUARTER + wanted, -1)
        cols[tt] = jnp.concatenate([col, jnp.full((6, rows), -1, jnp.int32)], axis=0)
        cols_out[tt] = cols[tt].astype(F32).T
    ids = routes[t, 0:2]
    spread(0, 0, 8)
    forward(0)
    arrive(near_copies[0])
    arrive(far_copies[0])
    columns = small_all[...].reshape(-1, 128)
    vec = columns.T[:32]
    vec_out[...] = vec
    heads = qkv_out.shape[2] // 3
    for tt in range(4):
        cut = slice(tt * heads, (tt + 1) * heads)
        qkv_bias[tt] = jnp.concatenate([vec[5:6, cut], jnp.zeros((1, heads), F32), vec[6:7, cut]], axis=1)
    inputs = tok[...].astype(F32)
    unit, _ = unit_norm(inputs)
    first = (unit * vec[0:1] + vec[1:2]).astype(BF)
    acc[...] = inputs + vec[4:5]

    def attend(tt):
        weights = wall[tt].reshape(8 * packed.shape[0], -1)
        qkv = (nn(first, weights[:, : 3 * heads]) + qkv_bias[tt]).astype(BF)
        qkv_out[tt] = qkv
        mixed = []
        for i in range(rows // SEQ_PAD):
            part = qkv[i * SEQ_PAD : (i + 1) * SEQ_PAD]
            sides = []
            for h in range(heads // HEAD_DIM):
                q, k, v = (part[:, j * heads + h * HEAD_DIM : j * heads + (h + 1) * HEAD_DIM] for j in range(3))
                sides.append(nn(softmax_rows(q, k).astype(BF), v).astype(BF))
            mixed.append(jnp.concatenate(sides, axis=1))
        mixed = jnp.concatenate(mixed, axis=0)
        mixed_out[tt] = mixed
        acc[...] += nt(mixed, weights[:, 3 * heads :])

    spread(1, 0, 4)
    launch(3, slice(1, 7, 2))
    spread(1, 4, 8)
    launch(3, slice(0, 7, 2))
    launch(2)
    cot_pair = pass_on(0, cot_pair, cot_all)
    attend(t)
    forward(1)
    attend(side)
    arrive(near_copies[1])
    attend(core)
    arrive(far_copies[1])
    attend(far)

    kept_copies = []

    def save(n, src, dst):
        copy = pltpu.make_async_copy(src, dst, save_s.at[n])
        copy.start()
        kept_copies.append(copy)

    hidden = acc[...]
    hidden_out[...] = hidden
    unit, _ = unit_norm(hidden)
    second = (unit * vec[2:3] + vec[3:4]).astype(BF)
    sec_all[t] = second
    sec_pair = exchange(1, sec_all.at[t], sec_all)
    logits = nt(vec[7:15].astype(BF), second)
    raised = jnp.exp(logits - jnp.max(logits, axis=0, keepdims=True))
    probs = raised / jnp.sum(raised, axis=0, keepdims=True)
    probs_out[...] = probs
    lane = lax.broadcasted_iota(jnp.int32, probs.shape, 0)
    picked = [jnp.sum(jnp.where(lane == ids[k : k + 1], probs, 0.0), axis=0, keepdims=True) for k in range(2)]
    gates[...] = jnp.concatenate(picked + [jnp.zeros((6, rows), F32)], axis=0)
    gates_all[t] = gates[...]
    gate_pair = exchange(2, gates, gates_all)

    pair_rows = 2 * QUARTER

    def onehots(tt, base):
        at = lax.broadcasted_iota(jnp.int32, (pair_rows, rows), 0) + base
        return at == cols[tt, 0:1], at == cols[tt, 1:2]

    def pick(base, source):
        total = None
        for tt in range(4):
            one, two = onehots(tt, base)
            part = nn(jnp.logical_or(one, two).astype(F32).astype(BF), source[tt])
            total = part if total is None else total + part
        return total.astype(BF)

    def chunk(i):
        c = lax.rem(lax.div(d, 2) + 1 + i, 4)
        return c, pl.multiple_of(c * pair_rows, pair_rows)

    save(0, hidden_out, hidden_hbm)
    save(1, qkv_out, qkv_hbm)
    save(2, mixed_out, mixed_hbm)
    save(3, wall, wall_hbm)
    save(5, tok, tok_hbm)
    save(6, cot_all.at[t], cot_hbm)
    arrive([cot_pair[1], cot_pair[2]])
    for i in range(4):
        c, base = chunk(i)
        raw[pl.ds(base, pair_rows)] = pick(base, cot_all)
    sec_pair = pass_on(1, sec_pair, sec_all)
    gate_pair = pass_on(2, gate_pair, gates_all)
    arrive([sec_pair[1], sec_pair[2], gate_pair[1], gate_pair[2]])

    for tt in range(4):
        gates_out[tt] = gates_all[tt].T
    sent = []

    for i in range(4):
        c, base = chunk(i)
        x_buf[pl.ds(base, pair_rows)] = pick(base, sec_all)
        for h in range(2):
            half = lax.rem(d + h, 2)
            e = 2 * c + half
            block = x_buf.at[pl.ds(pl.multiple_of(base + half * QUARTER, QUARTER), QUARTER)]
            copy = remote(block, x_out.at[d], x_s.at[e], x_r.at[d], (e * cells + cell, t))
            keep = pltpu.make_async_copy(block, x_out.at[d], own.at[4])
            sent.append((e, copy, keep))

            @pl.when(e == d)
            def _():
                keep.start()

            @pl.when(e != d)
            def _():
                copy.start()

    spread(2, 0, 8)
    spread(3, 0, 4)
    forward(2)
    for i in range(4):
        c, base = chunk(i)
        gate = None
        for tt in range(4):
            one, two = onehots(tt, base)
            part = jnp.where(one, gates_all[tt, 0:1], jnp.where(two, gates_all[tt, 1:2], 0.0))
            part = jnp.sum(part, axis=1, keepdims=True)
            gate = part if gate is None else gate + part
        kept = (gate * raw[pl.ds(base, pair_rows)].astype(F32)).astype(BF)
        g_out[pl.ds(2 * c, 2)] = kept.reshape(2, QUARTER, kept.shape[1])
    save(4, g_out, g_hbm)

    forward(3, 4)
    for a in (2, 3):
        arrive(near_copies[a])
        arrive(far_copies[a])
    for k in range(4, 8):
        block = spot(3, t, source(3, k))
        remote(block, block, dp_s.at[3, k], dp_r.at[3, source(3, k)], at_dp(k)).wait_recv()
    for k in range(1, 8):
        g = lax.rem(d + 8 - k, 8)
        remote(x_buf.at[pl.ds(0, QUARTER)], x_out.at[g], x_s.at[g], x_r.at[g], at_dp(8 - k)).wait_recv()
    for e, copy, keep in sent:

        @pl.when(e == d)
        def _():
            keep.wait()

        @pl.when(e != d)
        def _():
            copy.wait_send()

    for copy in kept_copies:
        copy.wait()
    for copy in cross:
        copy.wait_send()
    for a in range(4):
        for copy in dp_copies[a] + side_copies[a] + near_copies[a] + far_copies[a]:
            copy.wait_send()
    for trio in (cot_pair, sec_pair, gate_pair):
        for copy in trio:
            copy.wait_send()


def gelu_both(x):
    phi = 0.5 * (1.0 + lax.erf(x * (0.5**0.5)))
    slope = phi + x * (jnp.exp(-0.5 * x * x) * 0.3989422804014327)
    return x * phi, slope


def middle_kernel(
    cells,
    x_ref, g_src, expert_all, b_all, vec, cols,
    r_out, q_out, y_out, e_out, e_side_out, msg_out,
    up_bias, dup_out, ddown_out, w_buf, act_buf, pre_buf, x_turned, g_turned, acc, y_acc, y_buf, b_buf, q_buf, g_in, b_in, q_in,
    blocks, core_in, side_buf, side_in, q_blocks, q_core, q_side, q_mid,
    load, store, w_s, w_r, g_s, g_r, a_s, a_r, c_s, c_r, y_s, y_r, e_s, e_r, f_s, f_r, own, core_free, side_free,
):
    d, cell, t = place(cells)
    core, side, far = tensor_peers(t)
    here = d * cells + cell
    width = x_ref.shape[1]
    ff = act_buf.shape[1]
    half = width // 8
    pair_rows = 2 * QUARTER

    def at_dp(k):
        return (lax.rem(d + k, 8) * cells + cell, t)

    twin = d + 1 - 2 * lax.rem(d, 2)
    near_z = d + 2 - 4 * lax.rem(lax.div(d, 2), 2)
    early = (d, twin, near_z, twin + near_z - d)
    late = tuple(lax.rem(p + 4, 8) for p in early)
    loads = [[pltpu.make_async_copy(expert_all.at[t], w_buf.at[t], load.at[0, 0])]]
    for i, tt in enumerate((core, side, far)):
        loads.append(
            [pltpu.make_async_copy(expert_all.at[tt, p], w_buf.at[tt, p], load.at[i + 1, k]) for k, p in enumerate(early)]
        )
    for copy in sum(loads, []):
        copy.start()
    barrier = pltpu.get_barrier_semaphore()
    for k in range(1, 8):
        signal(barrier, at_dp(k))
    signal(barrier, (here, core))
    signal(barrier, (here, side))
    pl.semaphore_wait(barrier, 9)

    sent = []

    def post(c, src, out, send, recv, keep_sem):
        for h in range(2):
            g = 2 * c + lax.rem(d + h, 2)
            copy = remote(src.at[g], out.at[d], send.at[g], recv.at[d], (g * cells + cell, t))
            keep = pltpu.make_async_copy(src.at[g], out.at[d], keep_sem)
            sent.append((g, copy))

            @pl.when(g == d)
            def _():
                keep.start()

            @pl.when(g != d)
            def _():
                copy.start()

    def landed(g, src, out, send, recv, keep_sem):
        @pl.when(g == d)
        def _():
            pltpu.make_async_copy(src.at[g], out.at[g], keep_sem).wait()

        @pl.when(g != d)
        def _():
            remote(src.at[g], out.at[g], send.at[g], recv.at[g], (g * cells + cell, t)).wait_recv()

    for i in range(4):
        post(lax.rem(lax.div(d, 2) + 1 + i, 4), g_src, g_in, g_s, g_r, own.at[3])
    w_side, w_near, w_far = [], [], []
    for k, p in enumerate(late):
        block = expert_all.at[t, p]
        w_side.append(remote(block, w_buf.at[t, p], w_s.at[0, k], w_r.at[0, k], (here, side)))
        w_near.append(remote(block, w_buf.at[t, p], w_s.at[1, k], w_r.at[1, k], (here, core)))
        w_far.append(remote(w_buf.at[side, p], w_buf.at[side, p], w_s.at[2, k], w_r.at[2, k], (here, core)))
    for copy in w_side + w_near:
        copy.start()
    ff_piece = ff // 8
    for p in range(8):
        for tt in range(4):
            at = (p % 2) * 4 + tt
            up_bias[p // 2, :, at * ff_piece : (at + 1) * ff_piece] = b_all[tt, p, pl.ds(d, 1), 0:ff_piece]
    x_turned[...] = x_ref[...].T
    dup_out[...] = jnp.zeros_like(dup_out)

    def w_in(tt):
        return w_buf[tt, :, 0:half].reshape(width, ff)

    def w_out(tt):
        return w_buf[tt, :, half : 2 * half].reshape(width, ff)

    def held(tt, base):
        return pl.ds(pl.multiple_of(tt * SLOTS + base, pair_rows), pair_rows)

    y_acc[...] = jnp.broadcast_to(vec[pl.ds(15 + d, 1)], y_acc.shape)

    def ahead(tt):
        def rows_step(i, carry):
            base = pl.multiple_of(i * pair_rows, pair_rows)
            span = pl.ds(base, pair_rows)
            pre = nn(x_ref[span], w_in(tt)) + up_bias[tt]
            act, slope = gelu_both(pre)
            act = act.astype(BF)
            act_buf[held(tt, base)] = act
            pre_buf[held(tt, base)] = slope.astype(BF)
            y_acc[span] += nt(act, w_out(tt))
            return carry

        lax.fori_loop(0, 4, rows_step, 0)

    loads[0][0].wait()
    ahead(t)
    for copy in loads[1]:
        copy.wait()
    for copy in w_near:
        copy.wait_recv()
    ahead(core)
    for i in range(4):
        w_side[i].wait_recv()
        w_far[i].start()
    for copy in loads[2]:
        copy.wait()
    ahead(side)
    for copy in loads[3]:
        copy.wait()
    for copy in w_far:
        copy.wait_recv()
    ahead(far)
    for copy in w_far:
        copy.wait_send()
    y_buf[...] = y_acc[...].astype(BF).reshape(y_buf.shape)
    ones = jnp.ones((8, width), BF)
    for i in range(4):
        c = lax.rem(lax.div(d, 2) + 3 - i, 4)
        base = pl.multiple_of(c * pair_rows, pair_rows)
        pair = pl.ds(2 * c, 2)
        for h in range(2):
            landed(2 * c + h, g_src, g_in, g_s, g_r, own.at[3])
        acc[...] = jnp.zeros_like(acc)

        def slice_back(tt, carry):
            grad = nn(g_in[pair].reshape(pair_rows, width), w_out(tt)) * pre_buf[held(tt, base)].astype(F32)
            grad = grad.astype(BF)
            pre_buf[held(tt, base)] = grad
            acc[...] += nt(grad, w_in(tt))
            dup_out[tt] += jnp.sum(grad.astype(F32), axis=0, keepdims=True)
            return carry

        lax.fori_loop(0, 4, slice_back, 0)
        b_buf[pair] = acc[...].astype(BF).reshape(2, QUARTER, width)
        post(c, b_buf, b_in, a_s.at[0], a_r.at[0], own.at[0])
        for h in range(2):
            g = 2 * c + h
            z = y_buf[g].astype(F32) * g_in[g].astype(F32)
            high = z.astype(BF)
            q_buf[g] = nt(ones, high) + nt(ones, (z - high.astype(F32)).astype(BF))
        post(c, q_buf, q_in, a_s.at[2], a_r.at[2], own.at[2])
    for i in range(4):
        post(lax.rem(lax.div(d, 2) + 3 - i + 4, 4), y_buf, y_out, a_s.at[1], a_r.at[1], own.at[1])
    g_rows = g_in[...].reshape(SLOTS, width)
    g_turned[...] = g_rows.T
    ddown_out[...] = jnp.sum(g_rows.astype(F32), axis=0, keepdims=True)

    def grad_slice(tt, carry):
        def grad_rows(n, inner):
            span = pl.ds(pl.multiple_of(n * 2 * half, 2 * half), 2 * half)
            pair = pl.ds(2 * n, 2)
            at = pl.ds(pl.multiple_of(tt * SLOTS, SLOTS), SLOTS)
            w_buf[tt, pair, 0:half] = nn(x_turned[span], pre_buf[at]).astype(BF).reshape(2, half, ff)
            w_buf[tt, pair, half : 2 * half] = nn(g_turned[span], act_buf[at]).astype(BF).reshape(2, half, ff)
            return inner

        lax.fori_loop(0, 4, grad_rows, 0)
        return carry

    lax.fori_loop(0, 4, grad_slice, 0)

    msg_out[...] = jnp.zeros_like(msg_out)
    piece = width // 32
    for n in range(32):
        at = (n % 8) * ff_piece
        msg_out[n, 0:1, 0:ff_piece] = dup_out[n // 8, :, at : at + ff_piece]
        msg_out[n, 1:2, 0:piece] = ddown_out[:, n * piece : (n + 1) * piece]

    pl.semaphore_signal(core_free, inc=1, device_id=(here, core), device_id_type=MESH)
    pl.semaphore_signal(side_free, inc=1, device_id=(here, side), device_id_type=MESH)
    pl.semaphore_wait(core_free, 1)

    def inbox(i, p):
        return pl.ds(pl.multiple_of((i * 8 + p) * 2 * half, 2 * half), 2 * half)

    near = {}
    for i, tt in enumerate((far, core)):
        for k in range(1, 9):
            p = lax.rem(d + k, 8)
            near[i, k] = remote(
                w_buf.at[tt, p], act_buf.at[inbox(i, p)], e_s.at[i, k - 1], e_r.at[i, k - 1], (here, core)
            )
            near[i, k].start()
    pl.semaphore_wait(side_free, 1)
    over = {}
    for k in range(1, 9):
        p = lax.rem(d + k, 8)
        near[0, k].wait_recv()
        total = w_buf[side, p].astype(F32) + act_buf[inbox(0, p)].astype(F32)
        w_buf[side, p] = total.astype(BF)
        if k <= EARLY:
            over[k] = remote(
                w_buf.at[side, p], pre_buf.at[inbox(0, p)], f_s.at[k - 1], f_r.at[k - 1], (here, side)
            )
            over[k].start()
    keep_side = pltpu.make_async_copy(w_buf.at[side], e_side_out, store.at[1])
    keep_side.start()

    def onehots(tt):
        at = lax.broadcasted_iota(jnp.int32, (cols.shape[1], SLOTS), 1)
        col = cols[tt, :, 0:2].astype(jnp.int32)
        return at == col[:, 0:1], at == col[:, 1:2]

    for k in range(1, 9):
        e = lax.rem(d + k, 8)
        landed(e, b_buf, b_in, a_s.at[0], a_r.at[0], own.at[0])
        landed(e, q_buf, q_in, a_s.at[2], a_r.at[2], own.at[2])
    q_line = jnp.concatenate([q_in[e] for e in range(8)], axis=1)
    owner = jnp.concatenate([jnp.full((8, QUARTER), e, jnp.int32) for e in range(8)], axis=1)
    q_line = jnp.where(lax.broadcasted_iota(jnp.int32, q_line.shape, 0) == owner, q_line, 0.0)
    q_high = q_line.astype(BF)
    q_both = jnp.concatenate([q_high, (q_line - q_high.astype(F32)).astype(BF)], axis=0)
    b_rows = b_in[...].reshape(SLOTS, width)

    def back_block(tt):
        one, two = onehots(tt)
        hot = jnp.logical_or(one, two).astype(F32).astype(BF)
        q = nt(q_both, hot)
        return nn(hot, b_rows), q[0:8] + q[8:16]

    def core_send(n, i, src, dst):
        copy = remote(src.at[i], dst.at[i], c_s.at[n, i], c_r.at[n, i], (here, core))
        copy.start()
        return copy

    def side_send(n, src, dst):
        copy = remote(src, dst, y_s.at[n], y_r.at[n], (here, side))
        copy.start()
        return copy

    core_b, core_q = [], []
    for i, tt in enumerate((far, core)):
        total, q = back_block(tt)
        blocks[i] = total.astype(BF)
        q_blocks[i] = q
        core_b.append(core_send(0, i, blocks, core_in))
        core_q.append(core_send(1, i, q_blocks, q_core))
    total, q = back_block(side)
    core_b[0].wait_recv()
    core_q[0].wait_recv()
    side_buf[...] = (total + core_in[0].astype(F32)).astype(BF)
    q_mid[...] = q + q_core[0]
    side_b = side_send(0, side_buf, side_in)
    side_q = side_send(1, q_mid, q_side)
    total, q = back_block(t)
    core_b[1].wait_recv()
    core_q[1].wait_recv()
    r_out[...] = total + core_in[1].astype(F32)
    q_out[...] = q + q_core[1]

    for k in range(1, 9):
        p = lax.rem(d + k, 8)
        near[1, k].wait_recv()
        total = w_buf[t, p].astype(F32) + act_buf[inbox(1, p)].astype(F32)
        if k <= EARLY:
            over[k].wait_recv()
            total = total + pre_buf[inbox(0, p)].astype(F32)
        w_buf[t, p] = total.astype(BF)
    keep_e = pltpu.make_async_copy(w_buf.at[t], e_out, store.at[0])
    keep_e.start()
    side_b.wait_recv()
    side_q.wait_recv()
    r_out[...] += side_in[...].astype(F32)
    q_out[...] += q_side[...]

    for k in range(1, 9):
        landed(lax.rem(d + k, 8), y_buf, y_out, a_s.at[1], a_r.at[1], own.at[1])
    for copy in core_b + core_q + [side_b, side_q] + list(near.values()) + list(over.values()) + w_near:
        copy.wait_send()
    for copy in w_side:
        copy.wait_send()
    for g, copy in sent:

        @pl.when(g != d)
        def _():
            copy.wait_send()

    keep_e.wait()
    keep_side.wait()


def back_kernel(
    cells,
    tok, hid, r_ref, cols, gates, cot, probs, picked_ref, vec, y_hbm, wall_hbm, qkv_hbm, mixed_hbm, e_src, e_side_src,
    bias_msg, out, token_out, e_out, qkv_out, proj_out, line_out, pair_out, router_out, up_out, down_out,
    token_grad, a_out, msg_all, vec_all, n1, vec_grad, vec_msg, a_grad, qv_grad, a_core, a_mid, a_side, a_fin, a_cross, a_in,
    blocks, core_in, side_buf, side_in, e_own, e_in, y_rows, wall, qkv_ref, mixed_ref, fetch,
    c_s, c_r, y_s, y_r, e_s, e_r, f_s, f_r, x_s, x_r, z_s, z_r, o_s, o_r, own, m_s, m_r, v_s, v_r,
):
    d, cell, t = place(cells)
    core, side, far = tensor_peers(t)
    here = d * cells + cell
    fetches = []
    for n, (src, dst) in enumerate(((wall_hbm, wall), (qkv_hbm, qkv_ref), (mixed_hbm, mixed_ref), (y_hbm, y_rows))):
        copy = pltpu.make_async_copy(src, dst, fetch.at[n])
        copy.start()
        fetches.append(copy)
    heads = qkv_ref.shape[2] // 3
    rows = tok.shape[0]
    width = tok.shape[1]
    spot = d * 4 + t
    twin = d + 1 - 2 * lax.rem(d, 2)

    def at_dp(k):
        return (lax.rem(d + k, 8) * cells + cell, t)

    others = [(k, m) for k in range(8) for m in range(4) if k or m]

    def other(k, m):
        return lax.rem(d + k, 8), lax.rem(t + m, 4)

    barrier = pltpu.get_barrier_semaphore()
    for k, m in others:
        dd, tt = other(k, m)
        signal(barrier, (dd * cells + cell, tt))
    pl.semaphore_wait(barrier, 31)

    waits = []
    late = range(EARLY + 1, 9)
    over_e, load_e = {}, {}
    for k in range(1, EARLY + 1):
        copy = remote(e_src.at[lax.rem(d + k, 8)], e_out.at[d], e_s.at[k], e_r.at[k], at_dp(k))
        copy.start()
        waits.append(copy)
    for k in late:
        p = lax.rem(d + k, 8)
        over_e[k] = remote(e_side_src.at[p], e_in.at[p], f_s.at[k - 1], f_r.at[k - 1], (here, side))
        over_e[k].start()
        load_e[k] = pltpu.make_async_copy(e_src.at[p], e_own.at[p], own.at[k])
        load_e[k].start()

    def finish_expert(k):
        p = lax.rem(d + k, 8)
        load_e[k].wait()
        over_e[k].wait_recv()
        e_own[p] = (e_own[p].astype(F32) + e_in[p].astype(F32)).astype(BF)
        if k < 8:
            copy = remote(e_own.at[p], e_out.at[d], e_s.at[k], e_r.at[k], at_dp(k))
            waits.append(copy)
        else:
            copy = pltpu.make_async_copy(e_own.at[p], e_out.at[d], own.at[0])
            load_e[0] = copy
        copy.start()
    for n, (k, m) in enumerate(others):
        dd, tt = other(k, m)
        copy = remote(bias_msg.at[dd * 4 + tt], msg_all.at[spot], m_s.at[n], m_r.at[n], (dd * cells + cell, tt))
        copy.start()
        waits.append(copy)
    msg_own = pltpu.make_async_copy(bias_msg.at[spot], msg_all.at[spot], own.at[1])
    msg_own.start()

    hidden = hid[...]
    picked = picked_ref[...]
    logit = picked - probs[...] * jnp.sum(picked, axis=0, keepdims=True)
    high = logit.astype(BF)
    both = jnp.concatenate([high, (logit - high.astype(F32)).astype(BF)], axis=0)
    unit, inv = unit_norm(hidden)
    gain = vec[2:3]
    second = (unit * gain + vec[3:4]).astype(BF)
    router_grad = nn(both, second)
    vec_grad[...] = jnp.zeros_like(vec_grad)
    vec_grad[8:16] = router_grad[0:8] + router_grad[8:16]
    table = vec[7:15].astype(BF)
    n2 = r_ref[...] + tn(both, jnp.concatenate([table, table], axis=0))
    vec_grad[2:3] = jnp.sum(n2 * unit, axis=0, keepdims=True)
    vec_grad[3:4] = jnp.sum(n2, axis=0, keepdims=True)
    scaled = n2 * gain
    back = inv * (
        scaled
        - jnp.mean(scaled, axis=-1, keepdims=True)
        - unit * jnp.mean(scaled * unit, axis=-1, keepdims=True)
    )
    hidden_grad = cot[...].astype(F32) + back
    token_grad[...] = hidden_grad
    branch = hidden_grad.astype(BF)
    vec_grad[4:5] = jnp.sum(branch.astype(F32), axis=0, keepdims=True)
    unit1, inv1 = unit_norm(tok[...].astype(F32))
    first_norm = (unit1 * vec[0:1] + vec[1:2]).astype(BF)
    n1[...] = jnp.zeros_like(n1)

    def attend_back(tt):
        weights = wall[tt].reshape(width, -1)
        qkv = qkv_ref[tt]
        mixed_grad = nn(branch, weights[:, 3 * heads :]).astype(BF)
        triple = []
        for i in range(rows // SEQ_PAD):
            span = slice(i * SEQ_PAD, (i + 1) * SEQ_PAD)
            part, grad = qkv[span], mixed_grad[span]
            sides = [[], [], []]
            for h in range(heads // HEAD_DIM):
                q, k, v = (part[:, j * heads + h * HEAD_DIM : j * heads + (h + 1) * HEAD_DIM] for j in range(3))
                g = grad[:, h * HEAD_DIM : (h + 1) * HEAD_DIM]
                w = softmax_rows(q, k)
                w_grad = nt(g, v)
                s_grad = (w * (w_grad - jnp.sum(w * w_grad, axis=-1, keepdims=True))).astype(BF)
                sides[0].append((nn(s_grad, k) * (HEAD_DIM**-0.5)).astype(BF))
                sides[1].append((tn(s_grad, q) * (HEAD_DIM**-0.5)).astype(BF))
                sides[2].append(tn(w.astype(BF), g).astype(BF))
            triple.append(jnp.concatenate(sides[0] + sides[1] + sides[2], axis=1))
        triple = jnp.concatenate(triple, axis=0)
        grad = jnp.concatenate([tn(first_norm, triple), tn(branch, mixed_ref[tt])], axis=1).astype(BF)
        a_grad[tt] = grad.reshape(8, width // 8, -1)
        n1[...] += nt(triple, weights[:, : 3 * heads])
        sums = jnp.sum(triple.astype(F32), axis=0, keepdims=True)
        qv_grad[tt] = sums

    def core_a(i, tt):
        copy = remote(a_grad.at[tt], a_core.at[i], c_s.at[i], c_r.at[i], (here, core))
        copy.start()
        return copy

    order = [lax.rem(twin + 2 * m, 8) for m in range(4)] + [lax.rem(d + 2 * m, 8) for m in (1, 2, 3, 0)]
    for copy in fetches:
        copy.wait()
    attend_back(far)
    near_a = core_a(0, far)
    finish_expert(EARLY + 1)
    attend_back(side)
    near_a.wait_recv()
    over_a = []
    for n, p in enumerate(order):
        a_mid[p] = (a_grad[side, p].astype(F32) + a_core[0, p].astype(F32)).astype(BF)
        copy = remote(a_mid.at[p], a_side.at[p], y_s.at[n], y_r.at[n], (here, side))
        copy.start()
        over_a.append(copy)
    finish_expert(EARLY + 2)
    attend_back(core)
    far_a = core_a(1, core)
    for k in list(late)[2:-1]:
        finish_expert(k)
    attend_back(t)
    finish_expert(8)

    def out_block(tt):
        at = lax.broadcasted_iota(jnp.int32, (rows, SLOTS), 1)
        col = cols[tt, :, 0:2].astype(jnp.int32)
        one, two = at == col[:, 0:1], at == col[:, 1:2]
        hot = jnp.where(one, gates[tt, :, 0:1], jnp.where(two, gates[tt, :, 1:2], 0.0)).astype(BF)
        return nn(hot, y_rows[...])

    out_copies = []
    for i, tt in enumerate((far, core)):
        blocks[i] = out_block(tt).astype(BF)
        copy = remote(blocks.at[i], core_in.at[i], o_s.at[i], o_r.at[i], (here, core))
        copy.start()
        out_copies.append(copy)
    total = out_block(side)
    out_copies[0].wait_recv()
    side_buf[...] = (total + core_in[0].astype(F32)).astype(BF)
    side_out = remote(side_buf, side_in, o_s.at[2], o_r.at[2], (here, side))
    side_out.start()

    far_a.wait_recv()
    cross = []
    for n, p in enumerate(order):
        over_a[n].wait_recv()
        total = a_grad[t, p].astype(F32) + a_core[1, p].astype(F32) + a_side[p].astype(F32)
        if n < 4:
            a_fin[p] = total.astype(BF)
            copy = remote(a_fin.at[p], a_cross.at[n], x_s.at[n], x_r.at[n], (twin * cells + cell, t))
            copy.start()
            cross.append(copy)
        else:
            m = (n - 3) % 4
            cross[m].wait_recv()
            total = total + a_cross[m].astype(F32)
            if m:
                a_fin[p] = total.astype(BF)
                copy = remote(a_fin.at[p], a_in.at[m], z_s.at[m], z_r.at[m], at_dp(2 * m))
                copy.start()
                waits.append(copy)
            else:
                a_out[...] = total

    grad = n1[...]
    vec_grad[0:1] = jnp.sum(grad * unit1, axis=0, keepdims=True)
    vec_grad[1:2] = jnp.sum(grad, axis=0, keepdims=True)
    for j, row in ((0, 5), (2, 6)):
        parts = [qv_grad[tt][:, j * heads : (j + 1) * heads] for tt in range(4)]
        vec_grad[row : row + 1] = jnp.concatenate(parts, axis=1)
    turned = vec_grad[...].T
    vec_msg[...] = turned.reshape(vec_msg.shape)
    for n, (k, m) in enumerate(others):
        dd, tt = other(k, m)
        copy = remote(vec_msg.at[dd * 4 + tt], vec_all.at[spot], v_s.at[n], v_r.at[n], (dd * cells + cell, tt))
        copy.start()
        waits.append(copy)
    vec_all[spot] = vec_msg[spot]
    scaled = grad * vec[0:1]
    token_grad[...] += inv1 * (
        scaled
        - jnp.mean(scaled, axis=-1, keepdims=True)
        - unit1 * jnp.mean(scaled * unit1, axis=-1, keepdims=True)
    )
    for i in range(rows // SEQ_PAD):
        token_out[i * SEQ : (i + 1) * SEQ] = token_grad[i * SEQ_PAD : i * SEQ_PAD + SEQ]
    total = out_block(t)
    out_copies[1].wait_recv()
    total = total + core_in[1].astype(F32)
    side_out.wait_recv()
    total = (hid[...] + (total + side_in[...].astype(F32))).astype(BF)
    for i in range(rows // SEQ_PAD):
        out[i * SEQ : (i + 1) * SEQ] = total[i * SEQ_PAD : i * SEQ_PAD + SEQ]
    for copy in waits:
        copy.wait()
    for m in range(1, 4):
        a_out[...] += a_in[m].astype(F32)
    for j in range(3):
        qkv_out[:, j, :] = a_out[:, j * heads : (j + 1) * heads]
    proj_out[...] = a_out[:, 3 * heads : 4 * heads].T
    load_e[0].wait()
    msg_own.wait()
    vec_sum, msg_sum = vec_all[0], []
    for n in range(1, 32):
        vec_sum = vec_sum + vec_all[n]
    router_out[...] = vec_sum[:, 8:16]
    turned = vec_sum.T
    line_out[...] = turned[0:5]
    pair_out[...] = turned[5:7]
    for e in range(8):
        total = msg_all[4 * e] + msg_all[4 * e + 1] + msg_all[4 * e + 2] + msg_all[4 * e + 3]
        up_out[e : e + 1] = total[0:1, 0 : up_out.shape[1]]
        down_out[e : e + 1] = total[1:2, 0 : down_out.shape[1]]
    for copy in [near_a, far_a, side_out] + out_copies + over_a + cross + list(over_e.values()):
        copy.wait_send()


def pad_images(rows, fill=0):
    images = rows.reshape((-1, SEQ) + rows.shape[1:])
    spare = [(0, 0), (0, SEQ_PAD - SEQ)] + [(0, 0)] * (rows.ndim - 1)
    return jnp.pad(images, spare, constant_values=fill).reshape((-1,) + rows.shape[1:])


def body(
    tokens, ln1_gain, ln1_shift, qkv_weight, qv_bias, out_weight, out_bias, ln2_gain, ln2_shift,
    router_weight, expert_in, expert_in_bias, expert_out, expert_out_bias, expert_ids, expert_slots,
    cotangent,
):
    n_dp = lax.axis_size("dp")
    cells = n_dp // 8
    width = tokens.shape[1]
    experts = expert_in.shape[0]
    head_cols = qkv_weight.shape[2]
    ff_slice = expert_in.shape[2]
    index = lax.axis_index("dp")
    t = lax.axis_index("tensor")
    d, cell = index // cells, index % cells
    peers = [[row * cells + c for c in range(cells)] for row in range(8)]

    expert_pack = [expert_in, jnp.swapaxes(expert_out, 1, 2)]
    lines = jnp.concatenate([ln1_gain, ln1_shift, ln2_gain, ln2_shift, out_bias]).reshape(5, -1)
    vectors = [(lines, 1), (qv_bias, 1), (router_weight, 0), (expert_out_bias, 1), (expert_in_bias, 1)]
    if cells > 1:

        def gather(part, axis):
            return lax.all_gather(part, "dp", axis=axis, tiled=True, axis_index_groups=peers)

        def quarter(part, axis):
            part = gather(lax.all_gather(part, "tensor", axis=axis, tiled=True), axis)
            size = part.shape[axis] // 4
            return lax.dynamic_slice_in_dim(part, t * size, size, axis)

        qkv_weight, out_weight = gather(qkv_weight, 0), gather(out_weight, 1)
        expert_pack = [gather(part, 1) for part in expert_pack]
        vectors = [(quarter(part, axis), axis) for part, axis in vectors]
    expert_pack = jnp.concatenate(expert_pack, axis=1)
    vectors = [part for part, _ in vectors]
    piece, ff_piece = vectors[0].shape[1], vectors[4].shape[1]
    rows = tokens.shape[0] // SEQ * SEQ_PAD
    routes = pad_images(jnp.concatenate([expert_ids, expert_slots], axis=1), -1).reshape(4, rows, 2 * TOP)
    routes = jnp.swapaxes(routes, 1, 2)
    packed_shape = (width // 8, 4 * head_cols)

    dma = pltpu.SemaphoreType.DMA

    def params(identity):
        return pltpu.CompilerParams(
            collective_id=identity, has_side_effects=True, vmem_limit_bytes=VMEM_LIMIT
        )

    def like(shape, dtype=BF):
        return jax.ShapeDtypeStruct(shape, dtype)

    slot_shape = (8, QUARTER, width)
    (
        probs, cols, gates, vec, tok, cot, hidden, qkv, mixed, wall, bias_all, expert_all, x_rows, g_rows,
    ) = pl.pallas_call(
        functools.partial(front_kernel, cells),
        out_shape=[
            like((experts, rows), F32),
            like((4, rows, 8), F32),
            like((4, rows, 8), F32),
            like((32, width), F32),
            like((rows, width)),
            like((rows, width)),
            like((rows, width), F32),
            like((4, rows, 3 * head_cols)),
            like((4, rows, head_cols)),
            like((4, 8) + packed_shape),
            like((4, 8, 8, 128), F32),
            like((4,) + expert_pack.shape),
            like(slot_shape),
            like(slot_shape),
        ],
        in_specs=[VM] * 7 + [HB] + [VM] * 3,
        out_specs=[VM] * 4 + [HB] * 10,
        scratch_shapes=[
            pltpu.VMEM(packed_shape, BF),
            pltpu.VMEM((piece, 128), F32),
            pltpu.VMEM((8, 128), F32),
            pltpu.VMEM((128, 128), F32),
            pltpu.VMEM((rows, width), BF),
            pltpu.VMEM((4, 8, rows), jnp.int32),
            pltpu.VMEM((4, 8, rows), F32),
            pltpu.VMEM((rows, width), F32),
            pltpu.VMEM((4, rows, 3 * head_cols), BF),
            pltpu.VMEM((4, rows, head_cols), BF),
            pltpu.VMEM((4, 8) + packed_shape, BF),
            pltpu.VMEM(slot_shape, BF),
            pltpu.VMEM((8, 4, piece, 128), F32),
            pltpu.VMEM((4, rows, width), BF),
            pltpu.VMEM((4, rows, width), BF),
            pltpu.VMEM((SLOTS, width), BF),
            pltpu.VMEM((SLOTS, width), BF),
            pltpu.VMEM((rows, width), F32),
            pltpu.VMEM((8, rows), F32),
            pltpu.VMEM((4, 1, 3 * head_cols), F32),
        ]
        + [dma((4, 8))] * 8
        + [dma((5,)), dma((3, 3)), dma((3, 3)), dma((8,)), dma((8,)), dma((4,)), dma((4,)), dma((7,))],
        compiler_params=params(0),
        name="front",
    )(qkv_weight, out_weight, *vectors, expert_pack, tokens, cotangent, routes)

    e_block = expert_pack.shape
    r_rows, picked, y_rows, expert_grad, side_grad, message = pl.pallas_call(
        functools.partial(middle_kernel, cells),
        out_shape=[
            like((rows, width), F32),
            like((8, rows), F32),
            like(slot_shape),
            like(e_block),
            like(e_block),
            like((32, 8, 128), F32),
        ],
        in_specs=[VM, HB, HB, VM, VM, VM],
        out_specs=[VM, VM, HB, HB, HB, VM],
        scratch_shapes=[
            pltpu.VMEM((4, 1, ff_slice), F32),
            pltpu.VMEM((4, 1, ff_slice), F32),
            pltpu.VMEM((1, width), F32),
            pltpu.VMEM(expert_all.shape, BF),
            pltpu.VMEM((4 * SLOTS, ff_slice), BF),
            pltpu.VMEM((4 * SLOTS, ff_slice), BF),
            pltpu.VMEM((width, SLOTS), BF),
            pltpu.VMEM((width, SLOTS), BF),
            pltpu.VMEM((2 * QUARTER, width), F32),
            pltpu.VMEM((SLOTS, width), F32),
            pltpu.VMEM(slot_shape, BF),
            pltpu.VMEM(slot_shape, BF),
            pltpu.VMEM((8, 8, QUARTER), F32),
            pltpu.VMEM(slot_shape, BF),
            pltpu.VMEM(slot_shape, BF),
            pltpu.VMEM((8, 8, QUARTER), F32),
            pltpu.VMEM((2, rows, width), BF),
            pltpu.VMEM((2, rows, width), BF),
            pltpu.VMEM((rows, width), BF),
            pltpu.VMEM((rows, width), BF),
            pltpu.VMEM((2, 8, rows), F32),
            pltpu.VMEM((2, 8, rows), F32),
            pltpu.VMEM((8, rows), F32),
            pltpu.VMEM((8, rows), F32),
            dma((4, 4)), dma((2,)), dma((3, 4)), dma((3, 4)), dma((8,)), dma((8,)), dma((3, 8)), dma((3, 8)), dma((2, 2)), dma((2, 2)),
            dma((2,)), dma((2,)), dma((2, 8)), dma((2, 8)), dma((8,)), dma((8,)), dma((4,)),
            pltpu.SemaphoreType.REGULAR, pltpu.SemaphoreType.REGULAR,
        ],
        compiler_params=params(1),
        name="middle",
    )(x_rows.reshape(SLOTS, width), g_rows, expert_all, bias_all, vec, cols)

    a_block = wall.shape[1:]
    out, token_grad, expert_sum, qkv_sum, proj_sum, line_sum, pair_sum, router_sum, up_sum, down_sum = pl.pallas_call(
        functools.partial(back_kernel, cells),
        out_shape=[
            like(tokens.shape),
            like(tokens.shape, F32),
            like(e_block),
            like((width // 8, 3, head_cols), F32),
            like((head_cols, width // 8), F32),
            like((5, piece), F32),
            like((2, piece), F32),
            like((piece, 8), F32),
            like((8, ff_piece), F32),
            like((8, piece), F32),
        ],
        in_specs=[VM] * 9 + [HB] * 7,
        out_specs=[VM, VM, HB] + [VM] * 7,
        scratch_shapes=[
            pltpu.VMEM((rows, width), F32),
            pltpu.VMEM(a_block[1:], F32),
            pltpu.VMEM(message.shape, F32),
            pltpu.VMEM((32, piece, 128), F32),
            pltpu.VMEM((rows, width), F32),
            pltpu.VMEM((128, width), F32),
            pltpu.VMEM((32, piece, 128), F32),
            pltpu.VMEM(wall.shape, BF),
            pltpu.VMEM((4, 1, 3 * head_cols), F32),
            pltpu.VMEM((2,) + a_block, BF),
            pltpu.VMEM(a_block, BF),
            pltpu.VMEM(a_block, BF),
            pltpu.VMEM(a_block, BF),
            pltpu.VMEM((4,) + a_block[1:], BF),
            pltpu.VMEM((4,) + a_block[1:], BF),
            pltpu.VMEM((2, rows, width), BF),
            pltpu.VMEM((2, rows, width), BF),
            pltpu.VMEM((rows, width), BF),
            pltpu.VMEM((rows, width), BF),
            pltpu.VMEM(e_block, BF),
            pltpu.VMEM(e_block, BF),
            pltpu.VMEM((SLOTS, width), BF),
            pltpu.VMEM(wall.shape, BF),
            pltpu.VMEM(qkv.shape, BF),
            pltpu.VMEM(mixed.shape, BF),
            dma((4,)),
            dma((2,)), dma((2,)), dma((8,)), dma((8,)), dma((8,)), dma((8,)), dma((8,)), dma((8,)),
            dma((4,)), dma((4,)), dma((4,)), dma((4,)), dma((3,)), dma((3,)), dma((9,)), dma((31,)), dma((31,)), dma((31,)), dma((31,)),
        ],
        compiler_params=params(2),
        name="back",
    )(
        tok, hidden, r_rows, cols, gates, cot, probs, picked, vec,
        y_rows.reshape(SLOTS, width), wall, qkv, mixed, expert_grad, side_grad, message,
    )

    if cells > 1:

        def scatter(part, axis):
            return lax.psum_scatter(part, "dp", scatter_dimension=axis, tiled=True, axis_index_groups=peers)

        def share(part, axis):
            part = lax.psum(part, "dp", axis_index_groups=peers)
            part = lax.all_gather(part, "tensor", axis=axis, tiled=True)
            size = part.shape[axis] // (4 * cells)
            return lax.dynamic_slice_in_dim(part, (cell * 4 + t) * size, size, axis)

        expert_sum = scatter(expert_sum.astype(F32).reshape(8, 2, width // 8, -1), 2)
        expert_sum = expert_sum.reshape(8, -1, expert_sum.shape[3])
        qkv_sum, proj_sum = scatter(qkv_sum, 0), scatter(proj_sum, 1)
        line_sum, pair_sum, up_sum, down_sum = (share(part, 1) for part in (line_sum, pair_sum, up_sum, down_sum))
        router_sum = share(router_sum, 0)
    own_rows = expert_in.shape[1]
    return (
        out,
        token_grad,
        line_sum[0],
        line_sum[1],
        qkv_sum,
        pair_sum,
        proj_sum,
        line_sum[4],
        line_sum[2],
        line_sum[3],
        router_sum,
        expert_sum[:, :own_rows].astype(F32),
        up_sum,
        jnp.swapaxes(expert_sum[:, own_rows:], 1, 2).astype(F32),
        down_sum,
    )


def solution(mesh):
    both = ("dp", "tensor")
    return jax.shard_map(
        body,
        mesh=mesh,
        in_specs=(
            P(both, None),
            P(both),
            P(both),
            P("dp", None, "tensor"),
            P(None, both),
            P("tensor", "dp"),
            P(both),
            P(both),
            P(both),
            P(both, None),
            P(None, "dp", "tensor"),
            P(None, both),
            P(None, "tensor", "dp"),
            P(None, both),
            P("dp", None),
            P("dp", None),
            P(both, None),
        ),
        out_specs=(
            P(both, None),
            P(both, None),
            P(both),
            P(both),
            P("dp", None, "tensor"),
            P(None, both),
            P("tensor", "dp"),
            P(both),
            P(both),
            P(both),
            P(both, None),
            P(None, "dp", "tensor"),
            P(None, both),
            P(None, "tensor", "dp"),
            P(None, both),
        ),
        check_vma=False,
    )
```

```python
import functools

import jax
import jax.numpy as jnp
from jax import lax
from jax.experimental import pallas as pl
from jax.experimental.pallas import tpu as pltpu
from jax.sharding import PartitionSpec as P

HEAD_DIM = 64
SEQ = 197
SEQ_PAD = 208
TOP = 2
QUARTER = 160
SLOTS = 8 * QUARTER
EARLY = 5
EPS = 1e-6
BF = jnp.bfloat16
F32 = jnp.float32
MESH = pl.DeviceIdType.MESH
VMEM_LIMIT = 60 * 1024 * 1024
VM = pl.BlockSpec(memory_space=pltpu.VMEM)
HB = pl.BlockSpec(memory_space=pl.ANY)


def nn(a, b):
    return lax.dot_general(a, b, (((1,), (0,)), ((), ())), preferred_element_type=F32)


def nt(a, b):
    return lax.dot_general(a, b, (((1,), (1,)), ((), ())), preferred_element_type=F32)


def tn(a, b):
    return lax.dot_general(a, b, (((0,), (0,)), ((), ())), preferred_element_type=F32)


def unit_norm(rows):
    centred = rows - jnp.mean(rows, axis=-1, keepdims=True)
    inv = lax.rsqrt(jnp.mean(centred * centred, axis=-1, keepdims=True) + EPS)
    return centred * inv, inv


def place(cells):
    index = lax.axis_index("dp")
    return lax.div(index, cells), lax.rem(index, cells), lax.axis_index("tensor")


def tensor_peers(t):
    core = t + 1 - 2 * lax.rem(t, 2)
    side = lax.rem(t + 2, 4)
    return core, side, lax.rem(core + 2, 4)


def remote(src, dst, send, recv, device):
    return pltpu.make_async_remote_copy(
        src_ref=src, dst_ref=dst, send_sem=send, recv_sem=recv, device_id=device, device_id_type=MESH
    )


def signal(barrier, device):
    pl.semaphore_signal(barrier, inc=1, device_id=device, device_id_type=MESH)


def softmax_rows(q, k):
    scores = nt(q, k) * (HEAD_DIM**-0.5)
    lane = lax.broadcasted_iota(jnp.int32, scores.shape, 1)
    scores = jnp.where(lane < SEQ, scores, -1e30)
    raised = jnp.exp(scores - jnp.max(scores, axis=-1, keepdims=True))
    return raised / jnp.sum(raised, axis=-1, keepdims=True)


def front_kernel(
    cells,
    qkv_w, out_w, lines, pair_bias, router_w, down_b, up_b, expert_a, expert_b, tokens, cotangent, routes,
    probs_out, cols_out, gates_out, vec_out, tok_hbm, cot_hbm, hidden_hbm, qkv_hbm, mixed_hbm, wall_hbm, b_all,
    expert_all, x_out, g_hbm,
    packed, small_a, small_b, small_rows, tok, cols, gates_all, hidden_out, qkv_out, mixed_out, wall, g_out, small_all, cot_all, sec_all, x_buf, raw, acc, gates, qkv_bias,
    dp_s, dp_r, y_s, y_r, c_s, c_r, f_s, f_r, own, ag_s, ag_r, x_s, x_r, w_s, w_r, save_s,
):
    d, cell, t = place(cells)
    core, side, far = tensor_peers(t)
    here = d * cells + cell
    twin = d + 1 - 2 * lax.rem(d, 2)
    rows = tok.shape[0]
    srcs = (small_a, packed, small_b)

    def at_dp(k):
        return (lax.rem(d + k, 8) * cells + cell, t)

    def spot(a, tt, s):
        return small_all.at[s, tt] if a == 0 else (None, wall, b_all, expert_all)[a].at[tt, s]

    barrier = pltpu.get_barrier_semaphore()
    for k in range(1, 8):
        signal(barrier, at_dp(k))
    signal(barrier, (here, core))
    signal(barrier, (here, side))
    joined = 3 * qkv_w.shape[2]
    for j in range(3):
        packed[:, j * qkv_w.shape[2] : (j + 1) * qkv_w.shape[2]] = qkv_w[:, j, :]
    packed[:, joined : joined + out_w.shape[0]] = out_w[...].astype(F32).T.astype(BF)
    small_rows[...] = jnp.zeros_like(small_rows)
    piece = lines.shape[1]
    small_rows[0:5, 0:piece] = lines[...].astype(F32)
    small_rows[5:7, 0:piece] = pair_bias[...].astype(F32)
    small_rows[7:15, 0:piece] = router_w[...].astype(F32).T
    small_rows[15:23, 0:piece] = down_b[...].astype(F32)
    small_a[...] = small_rows[...].T[0:piece]
    small_b[...] = jnp.zeros_like(small_b)
    small_b[:, 0 : up_b.shape[1]] = up_b[...].astype(F32)
    tok[...] = jnp.zeros_like(tok)
    for i in range(rows // SEQ_PAD):
        tok[i * SEQ_PAD : i * SEQ_PAD + SEQ] = tokens[i * SEQ : (i + 1) * SEQ]
    cot_all[t] = jnp.zeros_like(tok)
    for i in range(rows // SEQ_PAD):
        cot_all[t, i * SEQ_PAD : i * SEQ_PAD + SEQ] = cotangent[i * SEQ : (i + 1) * SEQ]
    pl.semaphore_wait(barrier, 9)

    depth = expert_a.shape[1]

    def part_of(ref, h):
        return ref.at[pl.ds(h * depth, depth)]

    mine = [pltpu.make_async_copy(srcs[a], spot(a, t, d), own.at[a]) for a in range(3)]
    mine_w = [
        pltpu.make_async_copy(part.at[d], part_of(spot(3, t, d), h), own.at[3 + 2 * h])
        for h, part in enumerate((expert_a, expert_b))
    ]
    dp_copies = [
        [
            remote(srcs[a], spot(a, t, d), dp_s.at[a, k], dp_r.at[a, k], at_dp(k))
            for k in ((2, 4, 6) if a == 1 else range(1, 8))
        ]
        for a in range(3)
    ]
    dp_copies.append(
        [
            [
                remote(
                    part.at[lax.rem(d + k, 8)],
                    part_of(spot(3, t, d), h),
                    dp_s.at[3 + h, k],
                    dp_r.at[3 + h, d],
                    at_dp(k),
                )
                for h, part in enumerate((expert_a, expert_b))
            ]
            for k in range(1, 8)
        ]
    )

    def land(k):
        block = spot(3, t, source(3, k))
        for h in range(2):
            piece_of = part_of(block, h)
            remote(piece_of, piece_of, dp_s.at[3 + h, k], dp_r.at[3 + h, source(3, k)], at_dp(k)).wait_recv()

    side_copies = [[None] * (4 if a == 3 else 8) for a in range(4)]
    near_copies = [[None] * (4 if a == 3 else 8) for a in range(4)]
    far_copies = [[None] * (4 if a == 3 else 8) for a in range(4)]

    cross = [remote(packed, wall.at[t, d], w_s.at[0], w_r.at[0], (twin * cells + cell, t))]

    def launch(a, part=slice(0, 7)):
        for copy in (mine_w if a == 3 else [mine[a]]) if part.start == 0 else []:
            copy.start()
        for copy in sum(dp_copies[3][part], []) if a == 3 else dp_copies[a]:
            copy.start()
        if a == 1:
            cross[0].start()

    near_z = d + 2 - 4 * lax.rem(lax.div(d, 2), 2)
    near_twin = twin + near_z - d
    by_distance = [d, twin, near_z, near_twin] + [lax.rem(s + 4, 8) for s in (d, twin, near_z, near_twin)]

    def source(a, k):
        if a == 3:
            return by_distance[k]
        if a != 1:
            return lax.rem(d + 8 - k, 8)
        return lax.rem((d if k < 4 else twin) + 8 - 2 * (k % 4), 8)

    def spread(a, first, last):
        for k in range(first, last):
            block = spot(a, t, source(a, k))
            if k == 0:
                for copy in mine_w if a == 3 else [mine[a]]:
                    copy.wait()
            elif a == 3:
                land(k)
            elif a != 1 or k < 4:
                dp_copies[a][k - 1].wait_recv()
            else:
                cross[k - 4].wait_recv()
            if a == 1 and 0 < k < 4:
                cross.append(remote(block, block, w_s.at[k], w_r.at[k], (twin * cells + cell, t)))
                cross[k].start()
            side_copies[a][k] = remote(block, block, y_s.at[a, k], y_r.at[a, k], (here, side))
            side_copies[a][k].start()
            near_copies[a][k] = remote(block, block, c_s.at[a, k], c_r.at[a, k], (here, core))
            near_copies[a][k].start()

    def forward(a, count=8):
        for k in range(count):
            block = spot(a, side, source(a, k))
            side_copies[a][k].wait_recv()
            far_copies[a][k] = remote(block, block, f_s.at[a, k], f_r.at[a, k], (here, core))
            far_copies[a][k].start()

    def arrive(copies):
        for copy in copies:
            copy.wait_recv()

    def exchange(n, src, dst):
        over = remote(src, dst.at[t], ag_s.at[n, 0], ag_r.at[n, 0], (here, side))
        near = remote(src, dst.at[t], ag_s.at[n, 1], ag_r.at[n, 1], (here, core))
        over.start()
        near.start()
        return over, near

    def pass_on(n, pair, dst):
        pair[0].wait_recv()
        along = remote(dst.at[side], dst.at[side], ag_s.at[n, 2], ag_r.at[n, 2], (here, core))
        along.start()
        return pair + (along,)

    launch(0)
    launch(1)
    cot_pair = exchange(0, cot_all.at[t], cot_all)
    for tt in range(4):
        route = routes[tt]
        wanted = route[2:4] - QUARTER * t
        inside = jnp.logical_and(route[2:4] >= 0, jnp.logical_and(wanted >= 0, wanted < QUARTER))
        col = jnp.where(inside, route[0:2] * QUARTER + wanted, -1)
        cols[tt] = jnp.concatenate([col, jnp.full((6, rows), -1, jnp.int32)], axis=0)
        cols_out[tt] = cols[tt].astype(F32).T
    ids = routes[t, 0:2]
    spread(0, 0, 8)
    forward(0)
    arrive(near_copies[0])
    arrive(far_copies[0])
    columns = small_all[...].reshape(-1, 128)
    vec = columns.T[:32]
    vec_out[...] = vec
    heads = qkv_out.shape[2] // 3
    for tt in range(4):
        cut = slice(tt * heads, (tt + 1) * heads)
        qkv_bias[tt] = jnp.concatenate([vec[5:6, cut], jnp.zeros((1, heads), F32), vec[6:7, cut]], axis=1)
    inputs = tok[...].astype(F32)
    unit, _ = unit_norm(inputs)
    first = (unit * vec[0:1] + vec[1:2]).astype(BF)
    acc[...] = inputs + vec[4:5]

    def attend(tt):
        weights = wall[tt].reshape(8 * packed.shape[0], -1)
        qkv = (nn(first, weights[:, : 3 * heads]) + qkv_bias[tt]).astype(BF)
        qkv_out[tt] = qkv
        mixed = []
        for i in range(rows // SEQ_PAD):
            part = qkv[i * SEQ_PAD : (i + 1) * SEQ_PAD]
            sides = []
            for h in range(heads // HEAD_DIM):
                q, k, v = (part[:, j * heads + h * HEAD_DIM : j * heads + (h + 1) * HEAD_DIM] for j in range(3))
                sides.append(nn(softmax_rows(q, k).astype(BF), v).astype(BF))
            mixed.append(jnp.concatenate(sides, axis=1))
        mixed = jnp.concatenate(mixed, axis=0)
        mixed_out[tt] = mixed
        acc[...] += nt(mixed, weights[:, 3 * heads :])

    spread(1, 0, 4)
    launch(3, slice(1, 7, 2))
    spread(1, 4, 8)
    launch(3, slice(0, 7, 2))
    launch(2)
    cot_pair = pass_on(0, cot_pair, cot_all)
    attend(t)
    forward(1)
    attend(side)
    arrive(near_copies[1])
    attend(core)
    arrive(far_copies[1])
    attend(far)

    kept_copies = []

    def save(n, src, dst):
        copy = pltpu.make_async_copy(src, dst, save_s.at[n])
        copy.start()
        kept_copies.append(copy)

    hidden = acc[...]
    hidden_out[...] = hidden
    unit, _ = unit_norm(hidden)
    second = (unit * vec[2:3] + vec[3:4]).astype(BF)
    sec_all[t] = second
    sec_pair = exchange(1, sec_all.at[t], sec_all)
    logits = nt(vec[7:15].astype(BF), second)
    raised = jnp.exp(logits - jnp.max(logits, axis=0, keepdims=True))
    probs = raised / jnp.sum(raised, axis=0, keepdims=True)
    probs_out[...] = probs
    lane = lax.broadcasted_iota(jnp.int32, probs.shape, 0)
    picked = [jnp.sum(jnp.where(lane == ids[k : k + 1], probs, 0.0), axis=0, keepdims=True) for k in range(2)]
    gates[...] = jnp.concatenate(picked + [jnp.zeros((6, rows), F32)], axis=0)
    gates_all[t] = gates[...]
    gate_pair = exchange(2, gates, gates_all)

    pair_rows = 2 * QUARTER

    def onehots(tt, base):
        at = lax.broadcasted_iota(jnp.int32, (pair_rows, rows), 0) + base
        return at == cols[tt, 0:1], at == cols[tt, 1:2]

    def pick(base, source):
        total = None
        for tt in range(4):
            one, two = onehots(tt, base)
            part = nn(jnp.logical_or(one, two).astype(F32).astype(BF), source[tt])
            total = part if total is None else total + part
        return total.astype(BF)

    def chunk(i):
        c = lax.rem(lax.div(d, 2) + 1 + i, 4)
        return c, pl.multiple_of(c * pair_rows, pair_rows)

    save(0, hidden_out, hidden_hbm)
    save(1, qkv_out, qkv_hbm)
    save(2, mixed_out, mixed_hbm)
    save(3, wall, wall_hbm)
    save(5, tok, tok_hbm)
    save(6, cot_all.at[t], cot_hbm)
    arrive([cot_pair[1], cot_pair[2]])
    for i in range(4):
        c, base = chunk(i)
        raw[pl.ds(base, pair_rows)] = pick(base, cot_all)
    sec_pair = pass_on(1, sec_pair, sec_all)
    gate_pair = pass_on(2, gate_pair, gates_all)
    arrive([sec_pair[1], sec_pair[2], gate_pair[1], gate_pair[2]])

    for tt in range(4):
        gates_out[tt] = gates_all[tt].T
    sent = []

    for i in range(4):
        c, base = chunk(i)
        x_buf[pl.ds(base, pair_rows)] = pick(base, sec_all)
        for h in range(2):
            half = lax.rem(d + h, 2)
            e = 2 * c + half
            block = x_buf.at[pl.ds(pl.multiple_of(base + half * QUARTER, QUARTER), QUARTER)]
            copy = remote(block, x_out.at[d], x_s.at[e], x_r.at[d], (e * cells + cell, t))
            keep = pltpu.make_async_copy(block, x_out.at[d], own.at[4])
            sent.append((e, copy, keep))

            @pl.when(e == d)
            def _():
                keep.start()

            @pl.when(e != d)
            def _():
                copy.start()

    spread(2, 0, 8)
    spread(3, 0, 4)
    forward(2)
    for i in range(4):
        c, base = chunk(i)
        gate = None
        for tt in range(4):
            one, two = onehots(tt, base)
            part = jnp.where(one, gates_all[tt, 0:1], jnp.where(two, gates_all[tt, 1:2], 0.0))
            part = jnp.sum(part, axis=1, keepdims=True)
            gate = part if gate is None else gate + part
        kept = (gate * raw[pl.ds(base, pair_rows)].astype(F32)).astype(BF)
        g_out[pl.ds(2 * c, 2)] = kept.reshape(2, QUARTER, kept.shape[1])
    save(4, g_out, g_hbm)

    forward(3, 4)
    for a in (2, 3):
        arrive(near_copies[a])
        arrive(far_copies[a])
    for k in range(4, 8):
        land(k)
    for k in range(1, 8):
        g = lax.rem(d + 8 - k, 8)
        remote(x_buf.at[pl.ds(0, QUARTER)], x_out.at[g], x_s.at[g], x_r.at[g], at_dp(8 - k)).wait_recv()
    for e, copy, keep in sent:

        @pl.when(e == d)
        def _():
            keep.wait()

        @pl.when(e != d)
        def _():
            copy.wait_send()

    for copy in kept_copies:
        copy.wait()
    for copy in cross:
        copy.wait_send()
    for a in range(4):
        direct = sum(dp_copies[a], []) if a == 3 else dp_copies[a]
        for copy in direct + side_copies[a] + near_copies[a] + far_copies[a]:
            copy.wait_send()
    for trio in (cot_pair, sec_pair, gate_pair):
        for copy in trio:
            copy.wait_send()


def gelu_both(x):
    phi = 0.5 * (1.0 + lax.erf(x * (0.5**0.5)))
    slope = phi + x * (jnp.exp(-0.5 * x * x) * 0.3989422804014327)
    return x * phi, slope


def middle_kernel(
    cells,
    x_ref, g_src, expert_all, b_all, vec, cols,
    r_out, q_out, y_out, e_out, e_side_out, msg_out,
    up_bias, dup_out, ddown_out, w_buf, act_buf, pre_buf, x_turned, g_turned, acc, y_acc, y_buf, b_buf, q_buf, g_in, b_in, q_in,
    blocks, core_in, side_buf, side_in, q_blocks, q_core, q_side, q_mid,
    load, store, w_s, w_r, g_s, g_r, a_s, a_r, c_s, c_r, y_s, y_r, e_s, e_r, f_s, f_r, own, core_free, side_free,
):
    d, cell, t = place(cells)
    core, side, far = tensor_peers(t)
    here = d * cells + cell
    width = x_ref.shape[1]
    ff = act_buf.shape[1]
    half = width // 8
    pair_rows = 2 * QUARTER

    def at_dp(k):
        return (lax.rem(d + k, 8) * cells + cell, t)

    twin = d + 1 - 2 * lax.rem(d, 2)
    near_z = d + 2 - 4 * lax.rem(lax.div(d, 2), 2)
    early = (d, twin, near_z, twin + near_z - d)
    late = tuple(lax.rem(p + 4, 8) for p in early)
    loads = [[pltpu.make_async_copy(expert_all.at[t], w_buf.at[t], load.at[0, 0])]]
    for i, tt in enumerate((core, side, far)):
        loads.append(
            [pltpu.make_async_copy(expert_all.at[tt, p], w_buf.at[tt, p], load.at[i + 1, k]) for k, p in enumerate(early)]
        )
    for copy in sum(loads, []):
        copy.start()
    barrier = pltpu.get_barrier_semaphore()
    for k in range(1, 8):
        signal(barrier, at_dp(k))
    signal(barrier, (here, core))
    signal(barrier, (here, side))
    pl.semaphore_wait(barrier, 9)

    plane = lax.div(d, 2)
    near_plane = plane + 1 - 2 * lax.rem(plane, 2)
    planes = (plane, lax.rem(plane + 2, 4), lax.rem(near_plane + 2, 4), near_plane)
    sent = []

    def post(c, src, out, send, recv, keep_sem):
        for h in range(2):
            g = 2 * c + lax.rem(d + h, 2)
            copy = remote(src.at[g], out.at[d], send.at[g], recv.at[d], (g * cells + cell, t))
            keep = pltpu.make_async_copy(src.at[g], out.at[d], keep_sem)
            sent.append((g, copy))

            @pl.when(g == d)
            def _():
                keep.start()

            @pl.when(g != d)
            def _():
                copy.start()

    def landed(g, src, out, send, recv, keep_sem):
        @pl.when(g == d)
        def _():
            pltpu.make_async_copy(src.at[g], out.at[g], keep_sem).wait()

        @pl.when(g != d)
        def _():
            remote(src.at[g], out.at[g], send.at[g], recv.at[g], (g * cells + cell, t)).wait_recv()

    for i in range(4):
        post(planes[3 - i], g_src, g_in, g_s, g_r, own.at[3])
    w_side, w_near, w_far = [], [], []
    for k, p in enumerate(late):
        block = expert_all.at[t, p]
        w_side.append(remote(block, w_buf.at[t, p], w_s.at[0, k], w_r.at[0, k], (here, side)))
        w_near.append(remote(block, w_buf.at[t, p], w_s.at[1, k], w_r.at[1, k], (here, core)))
        w_far.append(remote(w_buf.at[side, p], w_buf.at[side, p], w_s.at[2, k], w_r.at[2, k], (here, core)))
    for copy in w_side + w_near:
        copy.start()
    ff_piece = ff // 8
    for p in range(8):
        for tt in range(4):
            at = (p % 2) * 4 + tt
            up_bias[p // 2, :, at * ff_piece : (at + 1) * ff_piece] = b_all[tt, p, pl.ds(d, 1), 0:ff_piece]
    x_turned[...] = x_ref[...].T
    dup_out[...] = jnp.zeros_like(dup_out)

    def w_in(tt):
        return w_buf[tt, :, 0:half].reshape(width, ff)

    def w_out(tt):
        return w_buf[tt, :, half : 2 * half].reshape(width, ff)

    def held(tt, base):
        return pl.ds(pl.multiple_of(tt * SLOTS + base, pair_rows), pair_rows)

    y_acc[...] = jnp.broadcast_to(vec[pl.ds(15 + d, 1)], y_acc.shape)

    def ahead(tt):
        def rows_step(i, carry):
            base = pl.multiple_of(i * pair_rows, pair_rows)
            span = pl.ds(base, pair_rows)
            pre = nn(x_ref[span], w_in(tt)) + up_bias[tt]
            act, slope = gelu_both(pre)
            act = act.astype(BF)
            act_buf[held(tt, base)] = act
            pre_buf[held(tt, base)] = slope.astype(BF)
            y_acc[span] += nt(act, w_out(tt))
            return carry

        lax.fori_loop(0, 4, rows_step, 0)

    loads[0][0].wait()
    ahead(t)
    for copy in loads[1]:
        copy.wait()
    for copy in w_near:
        copy.wait_recv()
    ahead(core)
    for i in range(4):
        w_side[i].wait_recv()
        w_far[i].start()
    for copy in loads[2]:
        copy.wait()
    ahead(side)
    for copy in loads[3]:
        copy.wait()
    for copy in w_far:
        copy.wait_recv()
    ahead(far)
    for copy in w_far:
        copy.wait_send()
    y_buf[...] = y_acc[...].astype(BF).reshape(y_buf.shape)
    ones = jnp.ones((8, width), BF)
    for i in range(4):
        c = planes[i]
        base = pl.multiple_of(c * pair_rows, pair_rows)
        pair = pl.ds(2 * c, 2)
        for h in range(2):
            landed(2 * c + h, g_src, g_in, g_s, g_r, own.at[3])
        acc[...] = jnp.zeros_like(acc)

        def slice_back(tt, carry):
            grad = nn(g_in[pair].reshape(pair_rows, width), w_out(tt)) * pre_buf[held(tt, base)].astype(F32)
            grad = grad.astype(BF)
            pre_buf[held(tt, base)] = grad
            acc[...] += nt(grad, w_in(tt))
            dup_out[tt] += jnp.sum(grad.astype(F32), axis=0, keepdims=True)
            return carry

        lax.fori_loop(0, 4, slice_back, 0)
        b_buf[pair] = acc[...].astype(BF).reshape(2, QUARTER, width)
        post(c, b_buf, b_in, a_s.at[0], a_r.at[0], own.at[0])
        for h in range(2):
            g = 2 * c + h
            z = y_buf[g].astype(F32) * g_in[g].astype(F32)
            high = z.astype(BF)
            q_buf[g] = nt(ones, high) + nt(ones, (z - high.astype(F32)).astype(BF))
        post(c, q_buf, q_in, a_s.at[2], a_r.at[2], own.at[2])
    for i in range(4):
        post(planes[3 - i], y_buf, y_out, a_s.at[1], a_r.at[1], own.at[1])
    g_rows = g_in[...].reshape(SLOTS, width)
    g_turned[...] = g_rows.T
    ddown_out[...] = jnp.sum(g_rows.astype(F32), axis=0, keepdims=True)

    def grad_slice(tt, carry):
        def grad_rows(n, inner):
            span = pl.ds(pl.multiple_of(n * 2 * half, 2 * half), 2 * half)
            pair = pl.ds(2 * n, 2)
            at = pl.ds(pl.multiple_of(tt * SLOTS, SLOTS), SLOTS)
            w_buf[tt, pair, 0:half] = nn(x_turned[span], pre_buf[at]).astype(BF).reshape(2, half, ff)
            w_buf[tt, pair, half : 2 * half] = nn(g_turned[span], act_buf[at]).astype(BF).reshape(2, half, ff)
            return inner

        lax.fori_loop(0, 4, grad_rows, 0)
        return carry

    lax.fori_loop(0, 4, grad_slice, 0)

    msg_out[...] = jnp.zeros_like(msg_out)
    piece = width // 32
    for n in range(32):
        at = (n % 8) * ff_piece
        msg_out[n, 0:1, 0:ff_piece] = dup_out[n // 8, :, at : at + ff_piece]
        msg_out[n, 1:2, 0:piece] = ddown_out[:, n * piece : (n + 1) * piece]

    pl.semaphore_signal(core_free, inc=1, device_id=(here, core), device_id_type=MESH)
    pl.semaphore_signal(side_free, inc=1, device_id=(here, side), device_id_type=MESH)
    pl.semaphore_wait(core_free, 1)

    def inbox(i, p):
        return pl.ds(pl.multiple_of((i * 8 + p) * 2 * half, 2 * half), 2 * half)

    near = {}
    for i, tt in enumerate((far, core)):
        for k in range(1, 9):
            p = lax.rem(d + k, 8)
            near[i, k] = remote(
                w_buf.at[tt, p], act_buf.at[inbox(i, p)], e_s.at[i, k - 1], e_r.at[i, k - 1], (here, core)
            )
            near[i, k].start()
    pl.semaphore_wait(side_free, 1)
    over = {}
    for k in range(1, 9):
        p = lax.rem(d + k, 8)
        near[0, k].wait_recv()
        total = w_buf[side, p].astype(F32) + act_buf[inbox(0, p)].astype(F32)
        w_buf[side, p] = total.astype(BF)
        if k <= EARLY:
            over[k] = remote(
                w_buf.at[side, p], pre_buf.at[inbox(0, p)], f_s.at[k - 1], f_r.at[k - 1], (here, side)
            )
            over[k].start()
    keep_side = pltpu.make_async_copy(w_buf.at[side], e_side_out, store.at[1])
    keep_side.start()

    def onehots(tt):
        at = lax.broadcasted_iota(jnp.int32, (cols.shape[1], SLOTS), 1)
        col = cols[tt, :, 0:2].astype(jnp.int32)
        return at == col[:, 0:1], at == col[:, 1:2]

    for k in range(1, 9):
        e = lax.rem(d + k, 8)
        landed(e, b_buf, b_in, a_s.at[0], a_r.at[0], own.at[0])
        landed(e, q_buf, q_in, a_s.at[2], a_r.at[2], own.at[2])
    q_line = jnp.concatenate([q_in[e] for e in range(8)], axis=1)
    owner = jnp.concatenate([jnp.full((8, QUARTER), e, jnp.int32) for e in range(8)], axis=1)
    q_line = jnp.where(lax.broadcasted_iota(jnp.int32, q_line.shape, 0) == owner, q_line, 0.0)
    q_high = q_line.astype(BF)
    q_both = jnp.concatenate([q_high, (q_line - q_high.astype(F32)).astype(BF)], axis=0)
    b_rows = b_in[...].reshape(SLOTS, width)

    def back_block(tt):
        one, two = onehots(tt)
        hot = jnp.logical_or(one, two).astype(F32).astype(BF)
        q = nt(q_both, hot)
        return nn(hot, b_rows), q[0:8] + q[8:16]

    def core_send(n, i, src, dst):
        copy = remote(src.at[i], dst.at[i], c_s.at[n, i], c_r.at[n, i], (here, core))
        copy.start()
        return copy

    def side_send(n, src, dst):
        copy = remote(src, dst, y_s.at[n], y_r.at[n], (here, side))
        copy.start()
        return copy

    core_b, core_q = [], []
    for i, tt in enumerate((far, core)):
        total, q = back_block(tt)
        blocks[i] = total.astype(BF)
        q_blocks[i] = q
        core_b.append(core_send(0, i, blocks, core_in))
        core_q.append(core_send(1, i, q_blocks, q_core))
    total, q = back_block(side)
    core_b[0].wait_recv()
    core_q[0].wait_recv()
    side_buf[...] = (total + core_in[0].astype(F32)).astype(BF)
    q_mid[...] = q + q_core[0]
    side_b = side_send(0, side_buf, side_in)
    side_q = side_send(1, q_mid, q_side)
    total, q = back_block(t)
    core_b[1].wait_recv()
    core_q[1].wait_recv()
    r_out[...] = total + core_in[1].astype(F32)
    q_out[...] = q + q_core[1]

    for k in range(1, 9):
        p = lax.rem(d + k, 8)
        near[1, k].wait_recv()
        total = w_buf[t, p].astype(F32) + act_buf[inbox(1, p)].astype(F32)
        if k <= EARLY:
            over[k].wait_recv()
            total = total + pre_buf[inbox(0, p)].astype(F32)
        w_buf[t, p] = total.astype(BF)
    keep_e = pltpu.make_async_copy(w_buf.at[t], e_out, store.at[0])
    keep_e.start()
    side_b.wait_recv()
    side_q.wait_recv()
    r_out[...] += side_in[...].astype(F32)
    q_out[...] += q_side[...]

    for k in range(1, 9):
        landed(lax.rem(d + k, 8), y_buf, y_out, a_s.at[1], a_r.at[1], own.at[1])
    for copy in core_b + core_q + [side_b, side_q] + list(near.values()) + list(over.values()) + w_near:
        copy.wait_send()
    for copy in w_side:
        copy.wait_send()
    for g, copy in sent:

        @pl.when(g != d)
        def _():
            copy.wait_send()

    keep_e.wait()
    keep_side.wait()


def back_kernel(
    cells,
    tok, hid, r_ref, cols, gates, cot, probs, picked_ref, vec, y_hbm, wall_hbm, qkv_hbm, mixed_hbm, e_src, e_side_src,
    bias_msg, out, token_out, up_grad_out, down_grad_out, qkv_out, proj_out, line_out, pair_out, router_out, up_out, down_out,
    token_grad, a_out, msg_all, vec_all, e_out, up_wide, down_wide, n1, vec_grad, vec_msg, a_grad, qv_grad, a_core, a_mid, a_side, a_fin, a_cross, a_in,
    blocks, core_in, side_buf, side_in, e_own, e_in, y_rows, wall, qkv_ref, mixed_ref, fetch, wide_s,
    c_s, c_r, y_s, y_r, e_s, e_r, f_s, f_r, x_s, x_r, z_s, z_r, o_s, o_r, own, m_s, m_r, v_s, v_r,
):
    d, cell, t = place(cells)
    core, side, far = tensor_peers(t)
    here = d * cells + cell
    fetches = []
    for n, (src, dst) in enumerate(((wall_hbm, wall), (qkv_hbm, qkv_ref), (mixed_hbm, mixed_ref), (y_hbm, y_rows))):
        copy = pltpu.make_async_copy(src, dst, fetch.at[n])
        copy.start()
        fetches.append(copy)
    heads = qkv_ref.shape[2] // 3
    rows = tok.shape[0]
    width = tok.shape[1]
    spot = d * 4 + t
    twin = d + 1 - 2 * lax.rem(d, 2)

    def at_dp(k):
        return (lax.rem(d + k, 8) * cells + cell, t)

    others = [(k, m) for k in range(8) for m in range(4) if k or m]

    def other(k, m):
        return lax.rem(d + k, 8), lax.rem(t + m, 4)

    barrier = pltpu.get_barrier_semaphore()
    for k, m in others:
        dd, tt = other(k, m)
        signal(barrier, (dd * cells + cell, tt))
    pl.semaphore_wait(barrier, 31)

    waits = []
    half = width // 8
    late = range(EARLY + 1, 9)
    over_e, load_e = {}, {}
    moved = {}
    for k in range(1, EARLY + 1):
        moved[k] = remote(e_src.at[lax.rem(d + k, 8)], e_out.at[d], e_s.at[k], e_r.at[k], at_dp(k))
        moved[k].start()
    for k in late:
        p = lax.rem(d + k, 8)
        over_e[k] = remote(e_side_src.at[p], e_in.at[p], f_s.at[k - 1], f_r.at[k - 1], (here, side))
        over_e[k].start()
        load_e[k] = pltpu.make_async_copy(e_src.at[p], e_own.at[p], own.at[k])
        load_e[k].start()

    def finish_expert(k):
        p = lax.rem(d + k, 8)
        load_e[k].wait()
        over_e[k].wait_recv()
        e_own[p] = (e_own[p].astype(F32) + e_in[p].astype(F32)).astype(BF)
        if k < 8:
            moved[k] = remote(e_own.at[p], e_out.at[d], e_s.at[k], e_r.at[k], at_dp(k))
            moved[k].start()
        else:
            e_out[d] = e_own[p]
            widen(8)

    wide = []

    def widen(k):
        p = lax.rem(d + 8 - k, 8)
        if k < 8:
            moved[k].wait_recv()
        for h, (buf, target) in enumerate(((up_wide, up_grad_out), (down_wide, down_grad_out))):
            buf[p] = e_out[p, h * half : (h + 1) * half].astype(F32)
            copy = pltpu.make_async_copy(buf.at[p], target.at[p], wide_s.at[h, k - 1])
            copy.start()
            wide.append(copy)
    for n, (k, m) in enumerate(others):
        dd, tt = other(k, m)
        copy = remote(bias_msg.at[dd * 4 + tt], msg_all.at[spot], m_s.at[n], m_r.at[n], (dd * cells + cell, tt))
        copy.start()
        waits.append(copy)
    msg_own = pltpu.make_async_copy(bias_msg.at[spot], msg_all.at[spot], own.at[1])
    msg_own.start()

    hidden = hid[...]
    picked = picked_ref[...]
    logit = picked - probs[...] * jnp.sum(picked, axis=0, keepdims=True)
    high = logit.astype(BF)
    both = jnp.concatenate([high, (logit - high.astype(F32)).astype(BF)], axis=0)
    unit, inv = unit_norm(hidden)
    gain = vec[2:3]
    second = (unit * gain + vec[3:4]).astype(BF)
    router_grad = nn(both, second)
    vec_grad[...] = jnp.zeros_like(vec_grad)
    vec_grad[8:16] = router_grad[0:8] + router_grad[8:16]
    table = vec[7:15].astype(BF)
    n2 = r_ref[...] + tn(both, jnp.concatenate([table, table], axis=0))
    vec_grad[2:3] = jnp.sum(n2 * unit, axis=0, keepdims=True)
    vec_grad[3:4] = jnp.sum(n2, axis=0, keepdims=True)
    scaled = n2 * gain
    back = inv * (
        scaled
        - jnp.mean(scaled, axis=-1, keepdims=True)
        - unit * jnp.mean(scaled * unit, axis=-1, keepdims=True)
    )
    hidden_grad = cot[...].astype(F32) + back
    token_grad[...] = hidden_grad
    branch = hidden_grad.astype(BF)
    vec_grad[4:5] = jnp.sum(branch.astype(F32), axis=0, keepdims=True)
    unit1, inv1 = unit_norm(tok[...].astype(F32))
    first_norm = (unit1 * vec[0:1] + vec[1:2]).astype(BF)
    n1[...] = jnp.zeros_like(n1)

    def attend_back(tt):
        weights = wall[tt].reshape(width, -1)
        qkv = qkv_ref[tt]
        mixed_grad = nn(branch, weights[:, 3 * heads :]).astype(BF)
        triple = []
        for i in range(rows // SEQ_PAD):
            span = slice(i * SEQ_PAD, (i + 1) * SEQ_PAD)
            part, grad = qkv[span], mixed_grad[span]
            sides = [[], [], []]
            for h in range(heads // HEAD_DIM):
                q, k, v = (part[:, j * heads + h * HEAD_DIM : j * heads + (h + 1) * HEAD_DIM] for j in range(3))
                g = grad[:, h * HEAD_DIM : (h + 1) * HEAD_DIM]
                w = softmax_rows(q, k)
                w_grad = nt(g, v)
                s_grad = (w * (w_grad - jnp.sum(w * w_grad, axis=-1, keepdims=True))).astype(BF)
                sides[0].append((nn(s_grad, k) * (HEAD_DIM**-0.5)).astype(BF))
                sides[1].append((tn(s_grad, q) * (HEAD_DIM**-0.5)).astype(BF))
                sides[2].append(tn(w.astype(BF), g).astype(BF))
            triple.append(jnp.concatenate(sides[0] + sides[1] + sides[2], axis=1))
        triple = jnp.concatenate(triple, axis=0)
        grad = jnp.concatenate([tn(first_norm, triple), tn(branch, mixed_ref[tt])], axis=1).astype(BF)
        a_grad[tt] = grad.reshape(8, width // 8, -1)
        n1[...] += nt(triple, weights[:, : 3 * heads])
        sums = jnp.sum(triple.astype(F32), axis=0, keepdims=True)
        qv_grad[tt] = sums

    def core_a(i, tt):
        copy = remote(a_grad.at[tt], a_core.at[i], c_s.at[i], c_r.at[i], (here, core))
        copy.start()
        return copy

    order = [lax.rem(twin + 2 * m, 8) for m in range(4)] + [lax.rem(d + 2 * m, 8) for m in (1, 2, 3, 0)]
    for copy in fetches:
        copy.wait()
    attend_back(far)
    near_a = core_a(0, far)
    for k in list(late)[:-1][:1]:
        finish_expert(k)
    attend_back(side)
    near_a.wait_recv()
    over_a = []
    for n, p in enumerate(order):
        a_mid[p] = (a_grad[side, p].astype(F32) + a_core[0, p].astype(F32)).astype(BF)
        copy = remote(a_mid.at[p], a_side.at[p], y_s.at[n], y_r.at[n], (here, side))
        copy.start()
        over_a.append(copy)
    for k in list(late)[:-1][1:2]:
        finish_expert(k)
    attend_back(core)
    far_a = core_a(1, core)
    for k in list(late)[2:-1]:
        finish_expert(k)
    attend_back(t)
    finish_expert(8)

    def out_block(tt):
        at = lax.broadcasted_iota(jnp.int32, (rows, SLOTS), 1)
        col = cols[tt, :, 0:2].astype(jnp.int32)
        one, two = at == col[:, 0:1], at == col[:, 1:2]
        hot = jnp.where(one, gates[tt, :, 0:1], jnp.where(two, gates[tt, :, 1:2], 0.0)).astype(BF)
        return nn(hot, y_rows[...])

    out_copies = []
    for i, tt in enumerate((far, core)):
        blocks[i] = out_block(tt).astype(BF)
        copy = remote(blocks.at[i], core_in.at[i], o_s.at[i], o_r.at[i], (here, core))
        copy.start()
        out_copies.append(copy)
    total = out_block(side)
    out_copies[0].wait_recv()
    side_buf[...] = (total + core_in[0].astype(F32)).astype(BF)
    side_out = remote(side_buf, side_in, o_s.at[2], o_r.at[2], (here, side))

    far_a.wait_recv()
    cross = []
    for n, p in enumerate(order):
        over_a[n].wait_recv()
        total = a_grad[t, p].astype(F32) + a_core[1, p].astype(F32) + a_side[p].astype(F32)
        if n < 4:
            a_fin[p] = total.astype(BF)
            copy = remote(a_fin.at[p], a_cross.at[n], x_s.at[n], x_r.at[n], (twin * cells + cell, t))
            copy.start()
            cross.append(copy)
        else:
            m = (n - 3) % 4
            cross[m].wait_recv()
            total = total + a_cross[m].astype(F32)
            if m:
                a_fin[p] = total.astype(BF)
                copy = remote(a_fin.at[p], a_in.at[m], z_s.at[m], z_r.at[m], at_dp(2 * m))
                copy.start()
                waits.append(copy)
            else:
                a_out[...] = total
    side_out.start()

    grad = n1[...]
    vec_grad[0:1] = jnp.sum(grad * unit1, axis=0, keepdims=True)
    vec_grad[1:2] = jnp.sum(grad, axis=0, keepdims=True)
    for j, row in ((0, 5), (2, 6)):
        parts = [qv_grad[tt][:, j * heads : (j + 1) * heads] for tt in range(4)]
        vec_grad[row : row + 1] = jnp.concatenate(parts, axis=1)
    turned = vec_grad[...].T
    vec_msg[...] = turned.reshape(vec_msg.shape)
    for n, (k, m) in enumerate(others):
        dd, tt = other(k, m)
        copy = remote(vec_msg.at[dd * 4 + tt], vec_all.at[spot], v_s.at[n], v_r.at[n], (dd * cells + cell, tt))
        copy.start()
        waits.append(copy)
    vec_all[spot] = vec_msg[spot]
    scaled = grad * vec[0:1]
    token_grad[...] += inv1 * (
        scaled
        - jnp.mean(scaled, axis=-1, keepdims=True)
        - unit1 * jnp.mean(scaled * unit1, axis=-1, keepdims=True)
    )
    for i in range(rows // SEQ_PAD):
        token_out[i * SEQ : (i + 1) * SEQ] = token_grad[i * SEQ_PAD : i * SEQ_PAD + SEQ]
    for k in range(1, 8):
        widen(k)
    total = out_block(t)
    out_copies[1].wait_recv()
    total = total + core_in[1].astype(F32)
    side_out.wait_recv()
    total = (hid[...] + (total + side_in[...].astype(F32))).astype(BF)
    for i in range(rows // SEQ_PAD):
        out[i * SEQ : (i + 1) * SEQ] = total[i * SEQ_PAD : i * SEQ_PAD + SEQ]
    for copy in waits:
        copy.wait()
    for m in range(1, 4):
        a_out[...] += a_in[m].astype(F32)
    for j in range(3):
        qkv_out[:, j, :] = a_out[:, j * heads : (j + 1) * heads]
    proj_out[...] = a_out[:, 3 * heads : 4 * heads].T
    msg_own.wait()
    for copy in wide:
        copy.wait()
    for copy in moved.values():
        copy.wait_send()
    vec_sum, msg_sum = vec_all[0], []
    for n in range(1, 32):
        vec_sum = vec_sum + vec_all[n]
    router_out[...] = vec_sum[:, 8:16]
    turned = vec_sum.T
    line_out[...] = turned[0:5]
    pair_out[...] = turned[5:7]
    for e in range(8):
        total = msg_all[4 * e] + msg_all[4 * e + 1] + msg_all[4 * e + 2] + msg_all[4 * e + 3]
        up_out[e : e + 1] = total[0:1, 0 : up_out.shape[1]]
        down_out[e : e + 1] = total[1:2, 0 : down_out.shape[1]]
    for copy in [near_a, far_a, side_out] + out_copies + over_a + cross + list(over_e.values()):
        copy.wait_send()


def pad_images(rows, fill=0):
    images = rows.reshape((-1, SEQ) + rows.shape[1:])
    spare = [(0, 0), (0, SEQ_PAD - SEQ)] + [(0, 0)] * (rows.ndim - 1)
    return jnp.pad(images, spare, constant_values=fill).reshape((-1,) + rows.shape[1:])


def body(
    tokens, ln1_gain, ln1_shift, qkv_weight, qv_bias, out_weight, out_bias, ln2_gain, ln2_shift,
    router_weight, expert_in, expert_in_bias, expert_out, expert_out_bias, expert_ids, expert_slots,
    cotangent,
):
    n_dp = lax.axis_size("dp")
    cells = n_dp // 8
    width = tokens.shape[1]
    experts = expert_in.shape[0]
    head_cols = qkv_weight.shape[2]
    ff_slice = expert_in.shape[2]
    index = lax.axis_index("dp")
    t = lax.axis_index("tensor")
    d, cell = index // cells, index % cells
    peers = [[row * cells + c for c in range(cells)] for row in range(8)]

    expert_pack = [expert_in, jnp.swapaxes(expert_out, 1, 2)]
    lines = jnp.concatenate([ln1_gain, ln1_shift, ln2_gain, ln2_shift, out_bias]).reshape(5, -1)
    vectors = [(lines, 1), (qv_bias, 1), (router_weight, 0), (expert_out_bias, 1), (expert_in_bias, 1)]
    if cells > 1:

        def gather(part, axis):
            return lax.all_gather(part, "dp", axis=axis, tiled=True, axis_index_groups=peers)

        def quarter(part, axis):
            part = gather(lax.all_gather(part, "tensor", axis=axis, tiled=True), axis)
            size = part.shape[axis] // 4
            return lax.dynamic_slice_in_dim(part, t * size, size, axis)

        qkv_weight, out_weight = gather(qkv_weight, 0), gather(out_weight, 1)
        expert_pack = [gather(part, 1) for part in expert_pack]
        vectors = [(quarter(part, axis), axis) for part, axis in vectors]
    vectors = [part for part, _ in vectors]
    piece, ff_piece = vectors[0].shape[1], vectors[4].shape[1]
    rows = tokens.shape[0] // SEQ * SEQ_PAD
    routes = pad_images(jnp.concatenate([expert_ids, expert_slots], axis=1), -1).reshape(4, rows, 2 * TOP)
    routes = jnp.swapaxes(routes, 1, 2)
    packed_shape = (width // 8, 4 * head_cols)
    e_block = (experts, 2 * (width // 8), ff_slice)

    dma = pltpu.SemaphoreType.DMA

    def params(identity):
        return pltpu.CompilerParams(
            collective_id=identity, has_side_effects=True, vmem_limit_bytes=VMEM_LIMIT
        )

    def like(shape, dtype=BF):
        return jax.ShapeDtypeStruct(shape, dtype)

    slot_shape = (8, QUARTER, width)
    (
        probs, cols, gates, vec, tok, cot, hidden, qkv, mixed, wall, bias_all, expert_all, x_rows, g_rows,
    ) = pl.pallas_call(
        functools.partial(front_kernel, cells),
        out_shape=[
            like((experts, rows), F32),
            like((4, rows, 8), F32),
            like((4, rows, 8), F32),
            like((32, width), F32),
            like((rows, width)),
            like((rows, width)),
            like((rows, width), F32),
            like((4, rows, 3 * head_cols)),
            like((4, rows, head_cols)),
            like((4, 8) + packed_shape),
            like((4, 8, 8, 128), F32),
            like((4,) + e_block),
            like(slot_shape),
            like(slot_shape),
        ],
        in_specs=[VM] * 7 + [HB] * 2 + [VM] * 3,
        out_specs=[VM] * 4 + [HB] * 10,
        scratch_shapes=[
            pltpu.VMEM(packed_shape, BF),
            pltpu.VMEM((piece, 128), F32),
            pltpu.VMEM((8, 128), F32),
            pltpu.VMEM((128, 128), F32),
            pltpu.VMEM((rows, width), BF),
            pltpu.VMEM((4, 8, rows), jnp.int32),
            pltpu.VMEM((4, 8, rows), F32),
            pltpu.VMEM((rows, width), F32),
            pltpu.VMEM((4, rows, 3 * head_cols), BF),
            pltpu.VMEM((4, rows, head_cols), BF),
            pltpu.VMEM((4, 8) + packed_shape, BF),
            pltpu.VMEM(slot_shape, BF),
            pltpu.VMEM((8, 4, piece, 128), F32),
            pltpu.VMEM((4, rows, width), BF),
            pltpu.VMEM((4, rows, width), BF),
            pltpu.VMEM((SLOTS, width), BF),
            pltpu.VMEM((SLOTS, width), BF),
            pltpu.VMEM((rows, width), F32),
            pltpu.VMEM((8, rows), F32),
            pltpu.VMEM((4, 1, 3 * head_cols), F32),
        ]
        + [dma((5, 8))] * 2
        + [dma((4, 8))] * 6
        + [dma((6,)), dma((3, 3)), dma((3, 3)), dma((8,)), dma((8,)), dma((4,)), dma((4,)), dma((7,))],
        compiler_params=params(0),
        name="front",
    )(qkv_weight, out_weight, *vectors, *expert_pack, tokens, cotangent, routes)

    r_rows, picked, y_rows, expert_grad, side_grad, message = pl.pallas_call(
        functools.partial(middle_kernel, cells),
        out_shape=[
            like((rows, width), F32),
            like((8, rows), F32),
            like(slot_shape),
            like(e_block),
            like(e_block),
            like((32, 8, 128), F32),
        ],
        in_specs=[VM, HB, HB, VM, VM, VM],
        out_specs=[VM, VM, HB, HB, HB, VM],
        scratch_shapes=[
            pltpu.VMEM((4, 1, ff_slice), F32),
            pltpu.VMEM((4, 1, ff_slice), F32),
            pltpu.VMEM((1, width), F32),
            pltpu.VMEM(expert_all.shape, BF),
            pltpu.VMEM((4 * SLOTS, ff_slice), BF),
            pltpu.VMEM((4 * SLOTS, ff_slice), BF),
            pltpu.VMEM((width, SLOTS), BF),
            pltpu.VMEM((width, SLOTS), BF),
            pltpu.VMEM((2 * QUARTER, width), F32),
            pltpu.VMEM((SLOTS, width), F32),
            pltpu.VMEM(slot_shape, BF),
            pltpu.VMEM(slot_shape, BF),
            pltpu.VMEM((8, 8, QUARTER), F32),
            pltpu.VMEM(slot_shape, BF),
            pltpu.VMEM(slot_shape, BF),
            pltpu.VMEM((8, 8, QUARTER), F32),
            pltpu.VMEM((2, rows, width), BF),
            pltpu.VMEM((2, rows, width), BF),
            pltpu.VMEM((rows, width), BF),
            pltpu.VMEM((rows, width), BF),
            pltpu.VMEM((2, 8, rows), F32),
            pltpu.VMEM((2, 8, rows), F32),
            pltpu.VMEM((8, rows), F32),
            pltpu.VMEM((8, rows), F32),
            dma((4, 4)), dma((2,)), dma((3, 4)), dma((3, 4)), dma((8,)), dma((8,)), dma((3, 8)), dma((3, 8)), dma((2, 2)), dma((2, 2)),
            dma((2,)), dma((2,)), dma((2, 8)), dma((2, 8)), dma((8,)), dma((8,)), dma((4,)),
            pltpu.SemaphoreType.REGULAR, pltpu.SemaphoreType.REGULAR,
        ],
        compiler_params=params(1),
        name="middle",
    )(x_rows.reshape(SLOTS, width), g_rows, expert_all, bias_all, vec, cols)

    a_block = wall.shape[1:]
    out, token_grad, up_grad, down_grad, qkv_sum, proj_sum, line_sum, pair_sum, router_sum, up_sum, down_sum = pl.pallas_call(
        functools.partial(back_kernel, cells),
        out_shape=[
            like(tokens.shape),
            like(tokens.shape, F32),
            like((8, width // 8, ff_slice), F32),
            like((8, width // 8, ff_slice), F32),
            like((width // 8, 3, head_cols), F32),
            like((head_cols, width // 8), F32),
            like((5, piece), F32),
            like((2, piece), F32),
            like((piece, 8), F32),
            like((8, ff_piece), F32),
            like((8, piece), F32),
        ],
        in_specs=[VM] * 9 + [HB] * 7,
        out_specs=[VM, VM, HB, HB] + [VM] * 7,
        scratch_shapes=[
            pltpu.VMEM((rows, width), F32),
            pltpu.VMEM(a_block[1:], F32),
            pltpu.VMEM(message.shape, F32),
            pltpu.VMEM((32, piece, 128), F32),
            pltpu.VMEM(e_block, BF),
            pltpu.VMEM((8, width // 8, ff_slice), F32),
            pltpu.VMEM((8, width // 8, ff_slice), F32),
            pltpu.VMEM((rows, width), F32),
            pltpu.VMEM((128, width), F32),
            pltpu.VMEM((32, piece, 128), F32),
            pltpu.VMEM(wall.shape, BF),
            pltpu.VMEM((4, 1, 3 * head_cols), F32),
            pltpu.VMEM((2,) + a_block, BF),
            pltpu.VMEM(a_block, BF),
            pltpu.VMEM(a_block, BF),
            pltpu.VMEM(a_block, BF),
            pltpu.VMEM((4,) + a_block[1:], BF),
            pltpu.VMEM((4,) + a_block[1:], BF),
            pltpu.VMEM((2, rows, width), BF),
            pltpu.VMEM((2, rows, width), BF),
            pltpu.VMEM((rows, width), BF),
            pltpu.VMEM((rows, width), BF),
            pltpu.VMEM(e_block, BF),
            pltpu.VMEM(e_block, BF),
            pltpu.VMEM((SLOTS, width), BF),
            pltpu.VMEM(wall.shape, BF),
            pltpu.VMEM(qkv.shape, BF),
            pltpu.VMEM(mixed.shape, BF),
            dma((4,)), dma((2, 8)),
            dma((2,)), dma((2,)), dma((8,)), dma((8,)), dma((8,)), dma((8,)), dma((8,)), dma((8,)),
            dma((4,)), dma((4,)), dma((4,)), dma((4,)), dma((3,)), dma((3,)), dma((9,)), dma((31,)), dma((31,)), dma((31,)), dma((31,)),
        ],
        compiler_params=params(2),
        name="back",
    )(
        tok, hidden, r_rows, cols, gates, cot, probs, picked, vec,
        y_rows.reshape(SLOTS, width), wall, qkv, mixed, expert_grad, side_grad, message,
    )

    if cells > 1:

        def scatter(part, axis):
            return lax.psum_scatter(part, "dp", scatter_dimension=axis, tiled=True, axis_index_groups=peers)

        def share(part, axis):
            part = lax.psum(part, "dp", axis_index_groups=peers)
            part = lax.all_gather(part, "tensor", axis=axis, tiled=True)
            size = part.shape[axis] // (4 * cells)
            return lax.dynamic_slice_in_dim(part, (cell * 4 + t) * size, size, axis)

        up_grad, down_grad = scatter(up_grad, 1), scatter(down_grad, 1)
        qkv_sum, proj_sum = scatter(qkv_sum, 0), scatter(proj_sum, 1)
        line_sum, pair_sum, up_sum, down_sum = (share(part, 1) for part in (line_sum, pair_sum, up_sum, down_sum))
        router_sum = share(router_sum, 0)
    return (
        out,
        token_grad,
        line_sum[0],
        line_sum[1],
        qkv_sum,
        pair_sum,
        proj_sum,
        line_sum[4],
        line_sum[2],
        line_sum[3],
        router_sum,
        up_grad,
        up_sum,
        jnp.swapaxes(down_grad, 1, 2),
        down_sum,
    )


def solution(mesh):
    both = ("dp", "tensor")
    return jax.shard_map(
        body,
        mesh=mesh,
        in_specs=(
            P(both, None),
            P(both),
            P(both),
            P("dp", None, "tensor"),
            P(None, both),
            P("tensor", "dp"),
            P(both),
            P(both),
            P(both),
            P(both, None),
            P(None, "dp", "tensor"),
            P(None, both),
            P(None, "tensor", "dp"),
            P(None, both),
            P("dp", None),
            P("dp", None),
            P(both, None),
        ),
        out_specs=(
            P(both, None),
            P(both, None),
            P(both),
            P(both),
            P("dp", None, "tensor"),
            P(None, both),
            P("tensor", "dp"),
            P(both),
            P(both),
            P(both),
            P(both, None),
            P(None, "dp", "tensor"),
            P(None, both),
            P(None, "tensor", "dp"),
            P(None, both),
        ),
        check_vma=False,
    )
```

```python
import functools

import jax
import jax.numpy as jnp
from jax import lax
from jax.experimental import pallas as pl
from jax.experimental.pallas import tpu as pltpu
from jax.sharding import PartitionSpec as P

HEAD_DIM = 64
SEQ = 197
SEQ_PAD = 208
TOP = 2
QUARTER = 160
SLOTS = 8 * QUARTER
EARLY = 5
EPS = 1e-6
BF = jnp.bfloat16
F32 = jnp.float32
MESH = pl.DeviceIdType.MESH
VMEM_LIMIT = 60 * 1024 * 1024
VM = pl.BlockSpec(memory_space=pltpu.VMEM)
HB = pl.BlockSpec(memory_space=pl.ANY)


def nn(a, b):
    return lax.dot_general(a, b, (((1,), (0,)), ((), ())), preferred_element_type=F32)


def nt(a, b):
    return lax.dot_general(a, b, (((1,), (1,)), ((), ())), preferred_element_type=F32)


def tn(a, b):
    return lax.dot_general(a, b, (((0,), (0,)), ((), ())), preferred_element_type=F32)


def unit_norm(rows):
    centred = rows - jnp.mean(rows, axis=-1, keepdims=True)
    inv = lax.rsqrt(jnp.mean(centred * centred, axis=-1, keepdims=True) + EPS)
    return centred * inv, inv


def place(cells):
    index = lax.axis_index("dp")
    return lax.div(index, cells), lax.rem(index, cells), lax.axis_index("tensor")


def tensor_peers(t):
    core = t + 1 - 2 * lax.rem(t, 2)
    side = lax.rem(t + 2, 4)
    return core, side, lax.rem(core + 2, 4)


def remote(src, dst, send, recv, device):
    return pltpu.make_async_remote_copy(
        src_ref=src, dst_ref=dst, send_sem=send, recv_sem=recv, device_id=device, device_id_type=MESH
    )


def signal(barrier, device):
    pl.semaphore_signal(barrier, inc=1, device_id=device, device_id_type=MESH)


def masked_scores(q, k):
    scores = nt(q, k) * (HEAD_DIM**-0.5)
    lane = lax.broadcasted_iota(jnp.int32, scores.shape, 1)
    return jnp.where(lane < SEQ, scores, -1e30)


def softmax_rows(q, k):
    scores = masked_scores(q, k)
    top = jnp.max(scores, axis=-1, keepdims=True)
    raised = jnp.exp(scores - top)
    total = jnp.sum(raised, axis=-1, keepdims=True)
    return raised * (1.0 / total), top + jnp.log(total)


def front_kernel(
    cells,
    qkv_w, out_w, lines, pair_bias, router_w, down_b, up_b, expert_a, expert_b, tokens, cotangent, routes,
    probs_out, cols_out, gates_out, vec_out, tok_hbm, cot_hbm, hidden_hbm, qkv_hbm, mixed_hbm, totals_hbm, wall_hbm, b_all,
    expert_all, x_out, g_hbm,
    totals, packed, small_a, small_b, small_rows, tok, cols, gates_all, hidden_out, qkv_out, mixed_out, wall, g_out, small_all, cot_all, sec_all, x_buf, raw, acc, gates, qkv_bias,
    dp_s, dp_r, y_s, y_r, c_s, c_r, f_s, f_r, own, ag_s, ag_r, x_s, x_r, w_s, w_r, save_s,
):
    d, cell, t = place(cells)
    core, side, far = tensor_peers(t)
    here = d * cells + cell
    twin = d + 1 - 2 * lax.rem(d, 2)
    rows = tok.shape[0]
    srcs = (small_a, packed, small_b)

    def at_dp(k):
        return (lax.rem(d + k, 8) * cells + cell, t)

    def spot(a, tt, s):
        return small_all.at[s, tt] if a == 0 else (None, wall, b_all, expert_all)[a].at[tt, s]

    barrier = pltpu.get_barrier_semaphore()
    for k in range(1, 8):
        signal(barrier, at_dp(k))
    signal(barrier, (here, core))
    signal(barrier, (here, side))
    joined = 3 * qkv_w.shape[2]
    for j in range(3):
        packed[:, j * qkv_w.shape[2] : (j + 1) * qkv_w.shape[2]] = qkv_w[:, j, :]
    packed[:, joined : joined + out_w.shape[0]] = out_w[...].astype(F32).T.astype(BF)
    small_rows[...] = jnp.zeros_like(small_rows)
    piece = lines.shape[1]
    small_rows[0:5, 0:piece] = lines[...].astype(F32)
    small_rows[5:7, 0:piece] = pair_bias[...].astype(F32)
    small_rows[7:15, 0:piece] = router_w[...].astype(F32).T
    small_rows[15:23, 0:piece] = down_b[...].astype(F32)
    small_a[...] = small_rows[...].T[0:piece]
    small_b[...] = jnp.zeros_like(small_b)
    small_b[:, 0 : up_b.shape[1]] = up_b[...].astype(F32)
    tok[...] = jnp.zeros_like(tok)
    for i in range(rows // SEQ_PAD):
        tok[i * SEQ_PAD : i * SEQ_PAD + SEQ] = tokens[i * SEQ : (i + 1) * SEQ]
    cot_all[t] = jnp.zeros_like(tok)
    for i in range(rows // SEQ_PAD):
        cot_all[t, i * SEQ_PAD : i * SEQ_PAD + SEQ] = cotangent[i * SEQ : (i + 1) * SEQ]
    pl.semaphore_wait(barrier, 9)

    depth = expert_a.shape[1]

    def part_of(ref, h):
        return ref.at[pl.ds(h * depth, depth)]

    mine = [pltpu.make_async_copy(srcs[a], spot(a, t, d), own.at[a]) for a in range(3)]
    mine_w = [
        pltpu.make_async_copy(part.at[d], part_of(spot(3, t, d), h), own.at[3 + 2 * h])
        for h, part in enumerate((expert_a, expert_b))
    ]
    dp_copies = [
        [
            remote(srcs[a], spot(a, t, d), dp_s.at[a, k], dp_r.at[a, k], at_dp(k))
            for k in ((2, 4, 6) if a == 1 else range(1, 8))
        ]
        for a in range(3)
    ]
    dp_copies.append(
        [
            [
                remote(
                    part.at[lax.rem(d + k, 8)],
                    part_of(spot(3, t, d), h),
                    dp_s.at[3 + h, k],
                    dp_r.at[3 + h, d],
                    at_dp(k),
                )
                for h, part in enumerate((expert_a, expert_b))
            ]
            for k in range(1, 8)
        ]
    )

    def land(k):
        block = spot(3, t, source(3, k))
        for h in range(2):
            piece_of = part_of(block, h)
            remote(piece_of, piece_of, dp_s.at[3 + h, k], dp_r.at[3 + h, source(3, k)], at_dp(k)).wait_recv()

    side_copies = [[None] * (4 if a == 3 else 8) for a in range(4)]
    near_copies = [[None] * (4 if a == 3 else 8) for a in range(4)]
    far_copies = [[None] * (4 if a == 3 else 8) for a in range(4)]

    cross = [remote(packed, wall.at[t, d], w_s.at[0], w_r.at[0], (twin * cells + cell, t))]

    def launch(a, part=slice(0, 7)):
        for copy in (mine_w if a == 3 else [mine[a]]) if part.start == 0 else []:
            copy.start()
        for copy in sum(dp_copies[3][part], []) if a == 3 else dp_copies[a]:
            copy.start()
        if a == 1:
            cross[0].start()

    near_z = d + 2 - 4 * lax.rem(lax.div(d, 2), 2)
    near_twin = twin + near_z - d
    by_distance = [d, twin, near_z, near_twin] + [lax.rem(s + 4, 8) for s in (d, twin, near_z, near_twin)]

    def source(a, k):
        if a == 3:
            return by_distance[k]
        if a != 1:
            return lax.rem(d + 8 - k, 8)
        return lax.rem((d if k < 4 else twin) + 8 - 2 * (k % 4), 8)

    def spread(a, first, last):
        for k in range(first, last):
            block = spot(a, t, source(a, k))
            if k == 0:
                for copy in mine_w if a == 3 else [mine[a]]:
                    copy.wait()
            elif a == 3:
                land(k)
            elif a != 1 or k < 4:
                dp_copies[a][k - 1].wait_recv()
            else:
                cross[k - 4].wait_recv()
            if a == 1 and 0 < k < 4:
                cross.append(remote(block, block, w_s.at[k], w_r.at[k], (twin * cells + cell, t)))
                cross[k].start()
            side_copies[a][k] = remote(block, block, y_s.at[a, k], y_r.at[a, k], (here, side))
            side_copies[a][k].start()
            near_copies[a][k] = remote(block, block, c_s.at[a, k], c_r.at[a, k], (here, core))
            near_copies[a][k].start()

    def forward(a, count=8):
        for k in range(count):
            block = spot(a, side, source(a, k))
            side_copies[a][k].wait_recv()
            far_copies[a][k] = remote(block, block, f_s.at[a, k], f_r.at[a, k], (here, core))
            far_copies[a][k].start()

    def arrive(copies):
        for copy in copies:
            copy.wait_recv()

    def exchange(n, src, dst):
        over = remote(src, dst.at[t], ag_s.at[n, 0], ag_r.at[n, 0], (here, side))
        near = remote(src, dst.at[t], ag_s.at[n, 1], ag_r.at[n, 1], (here, core))
        over.start()
        near.start()
        return over, near

    def pass_on(n, pair, dst):
        pair[0].wait_recv()
        along = remote(dst.at[side], dst.at[side], ag_s.at[n, 2], ag_r.at[n, 2], (here, core))
        along.start()
        return pair + (along,)

    launch(0)
    launch(1)
    cot_pair = exchange(0, cot_all.at[t], cot_all)
    for tt in range(4):
        route = routes[tt]
        wanted = route[2:4] - QUARTER * t
        inside = jnp.logical_and(route[2:4] >= 0, jnp.logical_and(wanted >= 0, wanted < QUARTER))
        col = jnp.where(inside, route[0:2] * QUARTER + wanted, -1)
        cols[tt] = jnp.concatenate([col, jnp.full((6, rows), -1, jnp.int32)], axis=0)
        cols_out[tt] = cols[tt].astype(F32).T
    ids = routes[t, 0:2]
    spread(0, 0, 8)
    forward(0)
    arrive(near_copies[0])
    arrive(far_copies[0])
    columns = small_all[...].reshape(-1, 128)
    vec = columns.T[:32]
    vec_out[...] = vec
    heads = qkv_out.shape[2] // 3
    for tt in range(4):
        cut = slice(tt * heads, (tt + 1) * heads)
        qkv_bias[tt] = jnp.concatenate([vec[5:6, cut], jnp.zeros((1, heads), F32), vec[6:7, cut]], axis=1)
    inputs = tok[...].astype(F32)
    unit, _ = unit_norm(inputs)
    first = (unit * vec[0:1] + vec[1:2]).astype(BF)
    acc[...] = inputs + vec[4:5]

    def attend(tt):
        weights = wall[tt].reshape(8 * packed.shape[0], -1)
        qkv = (nn(first, weights[:, : 3 * heads]) + qkv_bias[tt]).astype(BF)
        qkv_out[tt] = qkv
        mixed = []
        for i in range(rows // SEQ_PAD):
            part = qkv[i * SEQ_PAD : (i + 1) * SEQ_PAD]
            sides = []
            for h in range(heads // HEAD_DIM):
                q, k, v = (part[:, j * heads + h * HEAD_DIM : j * heads + (h + 1) * HEAD_DIM] for j in range(3))
                weight, log_total = softmax_rows(q, k)
                totals[tt, i * SEQ_PAD : (i + 1) * SEQ_PAD, h : h + 1] = log_total
                sides.append(nn(weight.astype(BF), v).astype(BF))
            mixed.append(jnp.concatenate(sides, axis=1))
        mixed = jnp.concatenate(mixed, axis=0)
        mixed_out[tt] = mixed
        acc[...] += nt(mixed, weights[:, 3 * heads :])

    spread(1, 0, 4)
    launch(3, slice(1, 7, 2))
    spread(1, 4, 8)
    launch(3, slice(0, 7, 2))
    launch(2)
    cot_pair = pass_on(0, cot_pair, cot_all)
    attend(t)
    forward(1)
    attend(side)
    arrive(near_copies[1])
    attend(core)
    arrive(far_copies[1])
    attend(far)

    kept_copies = []

    def save(n, src, dst):
        copy = pltpu.make_async_copy(src, dst, save_s.at[n])
        copy.start()
        kept_copies.append(copy)

    hidden = acc[...]
    hidden_out[...] = hidden
    unit, _ = unit_norm(hidden)
    second = (unit * vec[2:3] + vec[3:4]).astype(BF)
    sec_all[t] = second
    sec_pair = exchange(1, sec_all.at[t], sec_all)
    logits = nt(vec[7:15].astype(BF), second)
    raised = jnp.exp(logits - jnp.max(logits, axis=0, keepdims=True))
    probs = raised / jnp.sum(raised, axis=0, keepdims=True)
    probs_out[...] = probs
    lane = lax.broadcasted_iota(jnp.int32, probs.shape, 0)
    picked = [jnp.sum(jnp.where(lane == ids[k : k + 1], probs, 0.0), axis=0, keepdims=True) for k in range(2)]
    gates[...] = jnp.concatenate(picked + [jnp.zeros((6, rows), F32)], axis=0)
    gates_all[t] = gates[...]
    gate_pair = exchange(2, gates, gates_all)

    pair_rows = 2 * QUARTER

    def onehots(tt, base):
        at = lax.broadcasted_iota(jnp.int32, (pair_rows, rows), 0) + base
        return at == cols[tt, 0:1], at == cols[tt, 1:2]

    def pick(base, source):
        total = None
        for tt in range(4):
            one, two = onehots(tt, base)
            part = nn(jnp.logical_or(one, two).astype(F32).astype(BF), source[tt])
            total = part if total is None else total + part
        return total.astype(BF)

    def chunk(i):
        c = lax.rem(lax.div(d, 2) + 1 + i, 4)
        return c, pl.multiple_of(c * pair_rows, pair_rows)

    save(0, hidden_out, hidden_hbm)
    save(1, qkv_out, qkv_hbm)
    save(2, mixed_out, mixed_hbm)
    save(7, totals, totals_hbm)
    save(3, wall, wall_hbm)
    save(5, tok, tok_hbm)
    save(6, cot_all.at[t], cot_hbm)
    arrive([cot_pair[1], cot_pair[2]])
    for i in range(4):
        c, base = chunk(i)
        raw[pl.ds(base, pair_rows)] = pick(base, cot_all)
    sec_pair = pass_on(1, sec_pair, sec_all)
    gate_pair = pass_on(2, gate_pair, gates_all)
    arrive([sec_pair[1], sec_pair[2], gate_pair[1], gate_pair[2]])

    for tt in range(4):
        gates_out[tt] = gates_all[tt].T
    sent = []

    for i in range(4):
        c, base = chunk(i)
        x_buf[pl.ds(base, pair_rows)] = pick(base, sec_all)
        for h in range(2):
            half = lax.rem(d + h, 2)
            e = 2 * c + half
            block = x_buf.at[pl.ds(pl.multiple_of(base + half * QUARTER, QUARTER), QUARTER)]
            copy = remote(block, x_out.at[d], x_s.at[e], x_r.at[d], (e * cells + cell, t))
            keep = pltpu.make_async_copy(block, x_out.at[d], own.at[4])
            sent.append((e, copy, keep))

            @pl.when(e == d)
            def _():
                keep.start()

            @pl.when(e != d)
            def _():
                copy.start()

    spread(2, 0, 8)
    spread(3, 0, 4)
    forward(2)
    for i in range(4):
        c, base = chunk(i)
        gate = None
        for tt in range(4):
            one, two = onehots(tt, base)
            part = jnp.where(one, gates_all[tt, 0:1], jnp.where(two, gates_all[tt, 1:2], 0.0))
            part = jnp.sum(part, axis=1, keepdims=True)
            gate = part if gate is None else gate + part
        kept = (gate * raw[pl.ds(base, pair_rows)].astype(F32)).astype(BF)
        g_out[pl.ds(2 * c, 2)] = kept.reshape(2, QUARTER, kept.shape[1])
    save(4, g_out, g_hbm)

    forward(3, 4)
    for a in (2, 3):
        arrive(near_copies[a])
        arrive(far_copies[a])
    for k in range(4, 8):
        land(k)
    for k in range(1, 8):
        g = lax.rem(d + 8 - k, 8)
        remote(x_buf.at[pl.ds(0, QUARTER)], x_out.at[g], x_s.at[g], x_r.at[g], at_dp(8 - k)).wait_recv()
    for e, copy, keep in sent:

        @pl.when(e == d)
        def _():
            keep.wait()

        @pl.when(e != d)
        def _():
            copy.wait_send()

    for copy in kept_copies:
        copy.wait()
    for copy in cross:
        copy.wait_send()
    for a in range(4):
        direct = sum(dp_copies[a], []) if a == 3 else dp_copies[a]
        for copy in direct + side_copies[a] + near_copies[a] + far_copies[a]:
            copy.wait_send()
    for trio in (cot_pair, sec_pair, gate_pair):
        for copy in trio:
            copy.wait_send()


def gelu_both(x):
    phi = 0.5 * (1.0 + lax.erf(x * (0.5**0.5)))
    slope = phi + x * (jnp.exp(-0.5 * x * x) * 0.3989422804014327)
    return x * phi, slope


def middle_kernel(
    cells,
    x_ref, g_src, expert_all, b_all, vec, cols,
    r_out, q_out, y_out, e_out, e_side_out, msg_out,
    up_bias, dup_out, ddown_out, w_buf, act_buf, pre_buf, x_turned, g_turned, acc, y_acc, y_buf, b_buf, q_buf, g_in, b_in, q_in,
    blocks, core_in, side_buf, side_in, q_blocks, q_core, q_side, q_mid,
    load, store, w_s, w_r, g_s, g_r, a_s, a_r, c_s, c_r, y_s, y_r, e_s, e_r, f_s, f_r, own, core_free, side_free,
):
    d, cell, t = place(cells)
    core, side, far = tensor_peers(t)
    here = d * cells + cell
    width = x_ref.shape[1]
    ff = act_buf.shape[1]
    half = width // 8
    pair_rows = 2 * QUARTER

    def at_dp(k):
        return (lax.rem(d + k, 8) * cells + cell, t)

    twin = d + 1 - 2 * lax.rem(d, 2)
    near_z = d + 2 - 4 * lax.rem(lax.div(d, 2), 2)
    early = (d, twin, near_z, twin + near_z - d)
    late = tuple(lax.rem(p + 4, 8) for p in early)
    loads = [[pltpu.make_async_copy(expert_all.at[t], w_buf.at[t], load.at[0, 0])]]
    for i, tt in enumerate((core, side, far)):
        loads.append(
            [pltpu.make_async_copy(expert_all.at[tt, p], w_buf.at[tt, p], load.at[i + 1, k]) for k, p in enumerate(early)]
        )
    for copy in sum(loads, []):
        copy.start()
    barrier = pltpu.get_barrier_semaphore()
    for k in range(1, 8):
        signal(barrier, at_dp(k))
    signal(barrier, (here, core))
    signal(barrier, (here, side))
    pl.semaphore_wait(barrier, 9)

    plane = lax.div(d, 2)
    near_plane = plane + 1 - 2 * lax.rem(plane, 2)
    planes = (plane, lax.rem(plane + 2, 4), lax.rem(near_plane + 2, 4), near_plane)
    sent = []

    def post(c, src, out, send, recv, keep_sem):
        for h in range(2):
            g = 2 * c + lax.rem(d + h, 2)
            copy = remote(src.at[g], out.at[d], send.at[g], recv.at[d], (g * cells + cell, t))
            keep = pltpu.make_async_copy(src.at[g], out.at[d], keep_sem)
            sent.append((g, copy))

            @pl.when(g == d)
            def _():
                keep.start()

            @pl.when(g != d)
            def _():
                copy.start()

    def landed(g, src, out, send, recv, keep_sem):
        @pl.when(g == d)
        def _():
            pltpu.make_async_copy(src.at[g], out.at[g], keep_sem).wait()

        @pl.when(g != d)
        def _():
            remote(src.at[g], out.at[g], send.at[g], recv.at[g], (g * cells + cell, t)).wait_recv()

    for i in range(4):
        post(planes[3 - i], g_src, g_in, g_s, g_r, own.at[3])
    w_side, w_near, w_far = [], [], []
    for k, p in enumerate(late):
        block = expert_all.at[t, p]
        w_side.append(remote(block, w_buf.at[t, p], w_s.at[0, k], w_r.at[0, k], (here, side)))
        w_near.append(remote(block, w_buf.at[t, p], w_s.at[1, k], w_r.at[1, k], (here, core)))
        w_far.append(remote(w_buf.at[side, p], w_buf.at[side, p], w_s.at[2, k], w_r.at[2, k], (here, core)))
    for copy in w_side + w_near:
        copy.start()
    ff_piece = ff // 8
    for p in range(8):
        for tt in range(4):
            at = (p % 2) * 4 + tt
            up_bias[p // 2, :, at * ff_piece : (at + 1) * ff_piece] = b_all[tt, p, pl.ds(d, 1), 0:ff_piece]
    x_turned[...] = x_ref[...].T
    dup_out[...] = jnp.zeros_like(dup_out)

    def w_in(tt):
        return w_buf[tt, :, 0:half].reshape(width, ff)

    def w_out(tt):
        return w_buf[tt, :, half : 2 * half].reshape(width, ff)

    def held(tt, base):
        return pl.ds(pl.multiple_of(tt * SLOTS + base, pair_rows), pair_rows)

    y_acc[...] = jnp.broadcast_to(vec[pl.ds(15 + d, 1)], y_acc.shape)

    def ahead(tt):
        def rows_step(i, carry):
            base = pl.multiple_of(i * pair_rows, pair_rows)
            span = pl.ds(base, pair_rows)
            pre = nn(x_ref[span], w_in(tt)) + up_bias[tt]
            act, slope = gelu_both(pre)
            act = act.astype(BF)
            act_buf[held(tt, base)] = act
            pre_buf[held(tt, base)] = slope.astype(BF)
            y_acc[span] += nt(act, w_out(tt))
            return carry

        lax.fori_loop(0, 4, rows_step, 0)

    loads[0][0].wait()
    ahead(t)
    for copy in loads[1]:
        copy.wait()
    for copy in w_near:
        copy.wait_recv()
    ahead(core)
    for i in range(4):
        w_side[i].wait_recv()
        w_far[i].start()
    for copy in loads[2]:
        copy.wait()
    ahead(side)
    for copy in loads[3]:
        copy.wait()
    for copy in w_far:
        copy.wait_recv()
    ahead(far)
    for copy in w_far:
        copy.wait_send()
    y_buf[...] = y_acc[...].astype(BF).reshape(y_buf.shape)
    ones = jnp.ones((8, width), BF)
    for i in range(4):
        c = planes[i]
        base = pl.multiple_of(c * pair_rows, pair_rows)
        pair = pl.ds(2 * c, 2)
        for h in range(2):
            landed(2 * c + h, g_src, g_in, g_s, g_r, own.at[3])
        acc[...] = jnp.zeros_like(acc)

        def slice_back(tt, carry):
            grad = nn(g_in[pair].reshape(pair_rows, width), w_out(tt)) * pre_buf[held(tt, base)].astype(F32)
            grad = grad.astype(BF)
            pre_buf[held(tt, base)] = grad
            acc[...] += nt(grad, w_in(tt))
            dup_out[tt] += jnp.sum(grad.astype(F32), axis=0, keepdims=True)
            return carry

        lax.fori_loop(0, 4, slice_back, 0)
        b_buf[pair] = acc[...].astype(BF).reshape(2, QUARTER, width)
        post(c, b_buf, b_in, a_s.at[0], a_r.at[0], own.at[0])
        for h in range(2):
            g = 2 * c + h
            z = y_buf[g].astype(F32) * g_in[g].astype(F32)
            high = z.astype(BF)
            q_buf[g] = nt(ones, high) + nt(ones, (z - high.astype(F32)).astype(BF))
        post(c, q_buf, q_in, a_s.at[2], a_r.at[2], own.at[2])
    for i in range(4):
        post(planes[3 - i], y_buf, y_out, a_s.at[1], a_r.at[1], own.at[1])
    g_rows = g_in[...].reshape(SLOTS, width)
    g_turned[...] = g_rows.T
    ddown_out[...] = jnp.sum(g_rows.astype(F32), axis=0, keepdims=True)

    def grad_slice(tt, carry):
        def grad_rows(n, inner):
            span = pl.ds(pl.multiple_of(n * 2 * half, 2 * half), 2 * half)
            pair = pl.ds(2 * n, 2)
            at = pl.ds(pl.multiple_of(tt * SLOTS, SLOTS), SLOTS)
            w_buf[tt, pair, 0:half] = nn(x_turned[span], pre_buf[at]).astype(BF).reshape(2, half, ff)
            w_buf[tt, pair, half : 2 * half] = nn(g_turned[span], act_buf[at]).astype(BF).reshape(2, half, ff)
            return inner

        lax.fori_loop(0, 4, grad_rows, 0)
        return carry

    lax.fori_loop(0, 4, grad_slice, 0)

    msg_out[...] = jnp.zeros_like(msg_out)
    piece = width // 32
    for n in range(32):
        at = (n % 8) * ff_piece
        msg_out[n, 0:1, 0:ff_piece] = dup_out[n // 8, :, at : at + ff_piece]
        msg_out[n, 1:2, 0:piece] = ddown_out[:, n * piece : (n + 1) * piece]

    pl.semaphore_signal(core_free, inc=1, device_id=(here, core), device_id_type=MESH)
    pl.semaphore_signal(side_free, inc=1, device_id=(here, side), device_id_type=MESH)
    pl.semaphore_wait(core_free, 1)

    def inbox(i, p):
        return pl.ds(pl.multiple_of((i * 8 + p) * 2 * half, 2 * half), 2 * half)

    near = {}
    for i, tt in enumerate((far, core)):
        for k in range(1, 9):
            p = lax.rem(d + k, 8)
            near[i, k] = remote(
                w_buf.at[tt, p], act_buf.at[inbox(i, p)], e_s.at[i, k - 1], e_r.at[i, k - 1], (here, core)
            )
            near[i, k].start()
    pl.semaphore_wait(side_free, 1)
    over = {}
    for k in range(1, 9):
        p = lax.rem(d + k, 8)
        near[0, k].wait_recv()
        total = w_buf[side, p].astype(F32) + act_buf[inbox(0, p)].astype(F32)
        w_buf[side, p] = total.astype(BF)
        if k <= EARLY:
            over[k] = remote(
                w_buf.at[side, p], pre_buf.at[inbox(0, p)], f_s.at[k - 1], f_r.at[k - 1], (here, side)
            )
            over[k].start()
    keep_side = pltpu.make_async_copy(w_buf.at[side], e_side_out, store.at[1])
    keep_side.start()

    def onehots(tt):
        at = lax.broadcasted_iota(jnp.int32, (cols.shape[1], SLOTS), 1)
        col = cols[tt, :, 0:2].astype(jnp.int32)
        return at == col[:, 0:1], at == col[:, 1:2]

    for k in range(1, 9):
        e = lax.rem(d + k, 8)
        landed(e, b_buf, b_in, a_s.at[0], a_r.at[0], own.at[0])
        landed(e, q_buf, q_in, a_s.at[2], a_r.at[2], own.at[2])
    q_line = jnp.concatenate([q_in[e] for e in range(8)], axis=1)
    owner = jnp.concatenate([jnp.full((8, QUARTER), e, jnp.int32) for e in range(8)], axis=1)
    q_line = jnp.where(lax.broadcasted_iota(jnp.int32, q_line.shape, 0) == owner, q_line, 0.0)
    q_high = q_line.astype(BF)
    q_both = jnp.concatenate([q_high, (q_line - q_high.astype(F32)).astype(BF)], axis=0)
    b_rows = b_in[...].reshape(SLOTS, width)

    def back_block(tt):
        one, two = onehots(tt)
        hot = jnp.logical_or(one, two).astype(F32).astype(BF)
        q = nt(q_both, hot)
        return nn(hot, b_rows), q[0:8] + q[8:16]

    def core_send(n, i, src, dst):
        copy = remote(src.at[i], dst.at[i], c_s.at[n, i], c_r.at[n, i], (here, core))
        copy.start()
        return copy

    def side_send(n, src, dst):
        copy = remote(src, dst, y_s.at[n], y_r.at[n], (here, side))
        copy.start()
        return copy

    core_b, core_q = [], []
    for i, tt in enumerate((far, core)):
        total, q = back_block(tt)
        blocks[i] = total.astype(BF)
        q_blocks[i] = q
        core_b.append(core_send(0, i, blocks, core_in))
        core_q.append(core_send(1, i, q_blocks, q_core))
    total, q = back_block(side)
    core_b[0].wait_recv()
    core_q[0].wait_recv()
    side_buf[...] = (total + core_in[0].astype(F32)).astype(BF)
    q_mid[...] = q + q_core[0]
    side_b = side_send(0, side_buf, side_in)
    side_q = side_send(1, q_mid, q_side)
    total, q = back_block(t)
    core_b[1].wait_recv()
    core_q[1].wait_recv()
    r_out[...] = total + core_in[1].astype(F32)
    q_out[...] = q + q_core[1]

    for k in range(1, 9):
        p = lax.rem(d + k, 8)
        near[1, k].wait_recv()
        total = w_buf[t, p].astype(F32) + act_buf[inbox(1, p)].astype(F32)
        if k <= EARLY:
            over[k].wait_recv()
            total = total + pre_buf[inbox(0, p)].astype(F32)
        w_buf[t, p] = total.astype(BF)
    keep_e = pltpu.make_async_copy(w_buf.at[t], e_out, store.at[0])
    keep_e.start()
    side_b.wait_recv()
    side_q.wait_recv()
    r_out[...] += side_in[...].astype(F32)
    q_out[...] += q_side[...]

    for k in range(1, 9):
        landed(lax.rem(d + k, 8), y_buf, y_out, a_s.at[1], a_r.at[1], own.at[1])
    for copy in core_b + core_q + [side_b, side_q] + list(near.values()) + list(over.values()) + w_near:
        copy.wait_send()
    for copy in w_side:
        copy.wait_send()
    for g, copy in sent:

        @pl.when(g != d)
        def _():
            copy.wait_send()

    keep_e.wait()
    keep_side.wait()


def back_kernel(
    cells,
    tok, hid, r_ref, cols, gates, totals, cot, probs, picked_ref, vec, y_hbm, wall_hbm, qkv_hbm, mixed_hbm, e_src, e_side_src,
    bias_msg, out, token_out, e_out, qkv_out, proj_out, line_out, pair_out, router_out, up_out, down_out,
    token_grad, a_out, msg_all, vec_all, n1, vec_grad, vec_msg, a_grad, qv_grad, a_core, a_mid, a_side, a_fin, a_cross, a_in,
    blocks, core_in, side_buf, side_in, e_own, e_in, y_rows, wall, qkv_ref, mixed_ref, fetch,
    c_s, c_r, y_s, y_r, e_s, e_r, f_s, f_r, x_s, x_r, z_s, z_r, o_s, o_r, own, m_s, m_r, v_s, v_r,
):
    d, cell, t = place(cells)
    core, side, far = tensor_peers(t)
    here = d * cells + cell
    fetches = []
    for n, (src, dst) in enumerate(((wall_hbm, wall), (qkv_hbm, qkv_ref), (mixed_hbm, mixed_ref), (y_hbm, y_rows))):
        copy = pltpu.make_async_copy(src, dst, fetch.at[n])
        copy.start()
        fetches.append(copy)
    heads = qkv_ref.shape[2] // 3
    rows = tok.shape[0]
    width = tok.shape[1]
    spot = d * 4 + t
    twin = d + 1 - 2 * lax.rem(d, 2)

    def at_dp(k):
        return (lax.rem(d + k, 8) * cells + cell, t)

    others = [(k, m) for k in range(8) for m in range(4) if k or m]

    def other(k, m):
        return lax.rem(d + k, 8), lax.rem(t + m, 4)

    barrier = pltpu.get_barrier_semaphore()
    for k, m in others:
        dd, tt = other(k, m)
        signal(barrier, (dd * cells + cell, tt))
    pl.semaphore_wait(barrier, 31)

    waits = []
    late = range(EARLY + 1, 9)
    over_e, load_e = {}, {}
    for k in range(1, EARLY + 1):
        copy = remote(e_src.at[lax.rem(d + k, 8)], e_out.at[d], e_s.at[k], e_r.at[k], at_dp(k))
        copy.start()
        waits.append(copy)
    for k in late:
        p = lax.rem(d + k, 8)
        over_e[k] = remote(e_side_src.at[p], e_in.at[p], f_s.at[k - 1], f_r.at[k - 1], (here, side))
        over_e[k].start()
        load_e[k] = pltpu.make_async_copy(e_src.at[p], e_own.at[p], own.at[k])
        load_e[k].start()

    def finish_expert(k):
        p = lax.rem(d + k, 8)
        load_e[k].wait()
        over_e[k].wait_recv()
        e_own[p] = (e_own[p].astype(F32) + e_in[p].astype(F32)).astype(BF)
        if k < 8:
            copy = remote(e_own.at[p], e_out.at[d], e_s.at[k], e_r.at[k], at_dp(k))
            waits.append(copy)
        else:
            copy = pltpu.make_async_copy(e_own.at[p], e_out.at[d], own.at[0])
            load_e[0] = copy
        copy.start()
    for n, (k, m) in enumerate(others):
        dd, tt = other(k, m)
        copy = remote(bias_msg.at[dd * 4 + tt], msg_all.at[spot], m_s.at[n], m_r.at[n], (dd * cells + cell, tt))
        copy.start()
        waits.append(copy)
    msg_own = pltpu.make_async_copy(bias_msg.at[spot], msg_all.at[spot], own.at[1])
    msg_own.start()

    hidden = hid[...]
    picked = picked_ref[...]
    logit = picked - probs[...] * jnp.sum(picked, axis=0, keepdims=True)
    high = logit.astype(BF)
    both = jnp.concatenate([high, (logit - high.astype(F32)).astype(BF)], axis=0)
    unit, inv = unit_norm(hidden)
    gain = vec[2:3]
    second = (unit * gain + vec[3:4]).astype(BF)
    router_grad = nn(both, second)
    vec_grad[...] = jnp.zeros_like(vec_grad)
    vec_grad[8:16] = router_grad[0:8] + router_grad[8:16]
    table = vec[7:15].astype(BF)
    n2 = r_ref[...] + tn(both, jnp.concatenate([table, table], axis=0))
    vec_grad[2:3] = jnp.sum(n2 * unit, axis=0, keepdims=True)
    vec_grad[3:4] = jnp.sum(n2, axis=0, keepdims=True)
    scaled = n2 * gain
    back = inv * (
        scaled
        - jnp.mean(scaled, axis=-1, keepdims=True)
        - unit * jnp.mean(scaled * unit, axis=-1, keepdims=True)
    )
    hidden_grad = cot[...].astype(F32) + back
    token_grad[...] = hidden_grad
    branch = hidden_grad.astype(BF)
    vec_grad[4:5] = jnp.sum(branch.astype(F32), axis=0, keepdims=True)
    unit1, inv1 = unit_norm(tok[...].astype(F32))
    first_norm = (unit1 * vec[0:1] + vec[1:2]).astype(BF)
    n1[...] = jnp.zeros_like(n1)

    def attend_back(tt):
        weights = wall[tt].reshape(width, -1)
        qkv = qkv_ref[tt]
        mixed_grad = nn(branch, weights[:, 3 * heads :]).astype(BF)
        triple = []
        for i in range(rows // SEQ_PAD):
            span = slice(i * SEQ_PAD, (i + 1) * SEQ_PAD)
            part, grad = qkv[span], mixed_grad[span]
            sides = [[], [], []]
            for h in range(heads // HEAD_DIM):
                q, k, v = (part[:, j * heads + h * HEAD_DIM : j * heads + (h + 1) * HEAD_DIM] for j in range(3))
                g = grad[:, h * HEAD_DIM : (h + 1) * HEAD_DIM]
                log_total = totals[tt, i * SEQ_PAD : (i + 1) * SEQ_PAD, h : h + 1]
                w = jnp.exp(masked_scores(q, k) - log_total)
                w_grad = nt(g, v)
                s_grad = (w * (w_grad - jnp.sum(w * w_grad, axis=-1, keepdims=True))).astype(BF)
                sides[0].append((nn(s_grad, k) * (HEAD_DIM**-0.5)).astype(BF))
                sides[1].append((tn(s_grad, q) * (HEAD_DIM**-0.5)).astype(BF))
                sides[2].append(tn(w.astype(BF), g).astype(BF))
            triple.append(jnp.concatenate(sides[0] + sides[1] + sides[2], axis=1))
        triple = jnp.concatenate(triple, axis=0)
        grad = jnp.concatenate([tn(first_norm, triple), tn(branch, mixed_ref[tt])], axis=1).astype(BF)
        a_grad[tt] = grad.reshape(8, width // 8, -1)
        n1[...] += nt(triple, weights[:, : 3 * heads])
        sums = jnp.sum(triple.astype(F32), axis=0, keepdims=True)
        qv_grad[tt] = sums

    def core_a(i, tt):
        copy = remote(a_grad.at[tt], a_core.at[i], c_s.at[i], c_r.at[i], (here, core))
        copy.start()
        return copy

    order = [lax.rem(twin + 2 * m, 8) for m in range(4)] + [lax.rem(d + 2 * m, 8) for m in (1, 2, 3, 0)]
    for copy in fetches:
        copy.wait()
    attend_back(far)
    near_a = core_a(0, far)
    for k in list(late)[:-1][:1]:
        finish_expert(k)
    attend_back(side)
    near_a.wait_recv()
    over_a = []
    for n, p in enumerate(order):
        a_mid[p] = (a_grad[side, p].astype(F32) + a_core[0, p].astype(F32)).astype(BF)
        copy = remote(a_mid.at[p], a_side.at[p], y_s.at[n], y_r.at[n], (here, side))
        copy.start()
        over_a.append(copy)
    for k in list(late)[:-1][1:2]:
        finish_expert(k)
    attend_back(core)
    far_a = core_a(1, core)
    for k in list(late)[2:-1]:
        finish_expert(k)
    attend_back(t)
    finish_expert(8)

    def out_block(tt):
        at = lax.broadcasted_iota(jnp.int32, (rows, SLOTS), 1)
        col = cols[tt, :, 0:2].astype(jnp.int32)
        one, two = at == col[:, 0:1], at == col[:, 1:2]
        hot = jnp.where(one, gates[tt, :, 0:1], jnp.where(two, gates[tt, :, 1:2], 0.0)).astype(BF)
        return nn(hot, y_rows[...])

    out_copies = []
    for i, tt in enumerate((far, core)):
        blocks[i] = out_block(tt).astype(BF)
        copy = remote(blocks.at[i], core_in.at[i], o_s.at[i], o_r.at[i], (here, core))
        copy.start()
        out_copies.append(copy)
    total = out_block(side)
    out_copies[0].wait_recv()
    side_buf[...] = (total + core_in[0].astype(F32)).astype(BF)
    side_out = remote(side_buf, side_in, o_s.at[2], o_r.at[2], (here, side))

    far_a.wait_recv()
    cross = []
    for n, p in enumerate(order):
        over_a[n].wait_recv()
        total = a_grad[t, p].astype(F32) + a_core[1, p].astype(F32) + a_side[p].astype(F32)
        if n < 4:
            a_fin[p] = total.astype(BF)
            copy = remote(a_fin.at[p], a_cross.at[n], x_s.at[n], x_r.at[n], (twin * cells + cell, t))
            copy.start()
            cross.append(copy)
        else:
            m = (n - 3) % 4
            cross[m].wait_recv()
            total = total + a_cross[m].astype(F32)
            if m:
                a_fin[p] = total.astype(BF)
                copy = remote(a_fin.at[p], a_in.at[m], z_s.at[m], z_r.at[m], at_dp(2 * m))
                copy.start()
                waits.append(copy)
            else:
                a_out[...] = total
    side_out.start()

    grad = n1[...]
    vec_grad[0:1] = jnp.sum(grad * unit1, axis=0, keepdims=True)
    vec_grad[1:2] = jnp.sum(grad, axis=0, keepdims=True)
    for j, row in ((0, 5), (2, 6)):
        parts = [qv_grad[tt][:, j * heads : (j + 1) * heads] for tt in range(4)]
        vec_grad[row : row + 1] = jnp.concatenate(parts, axis=1)
    turned = vec_grad[...].T
    vec_msg[...] = turned.reshape(vec_msg.shape)
    for n, (k, m) in enumerate(others):
        dd, tt = other(k, m)
        copy = remote(vec_msg.at[dd * 4 + tt], vec_all.at[spot], v_s.at[n], v_r.at[n], (dd * cells + cell, tt))
        copy.start()
        waits.append(copy)
    vec_all[spot] = vec_msg[spot]
    scaled = grad * vec[0:1]
    token_grad[...] += inv1 * (
        scaled
        - jnp.mean(scaled, axis=-1, keepdims=True)
        - unit1 * jnp.mean(scaled * unit1, axis=-1, keepdims=True)
    )
    for i in range(rows // SEQ_PAD):
        token_out[i * SEQ : (i + 1) * SEQ] = token_grad[i * SEQ_PAD : i * SEQ_PAD + SEQ]
    total = out_block(t)
    out_copies[1].wait_recv()
    total = total + core_in[1].astype(F32)
    side_out.wait_recv()
    total = (hid[...] + (total + side_in[...].astype(F32))).astype(BF)
    for i in range(rows // SEQ_PAD):
        out[i * SEQ : (i + 1) * SEQ] = total[i * SEQ_PAD : i * SEQ_PAD + SEQ]
    for copy in waits:
        copy.wait()
    for m in range(1, 4):
        a_out[...] += a_in[m].astype(F32)
    for j in range(3):
        qkv_out[:, j, :] = a_out[:, j * heads : (j + 1) * heads]
    proj_out[...] = a_out[:, 3 * heads : 4 * heads].T
    load_e[0].wait()
    msg_own.wait()
    vec_sum, msg_sum = vec_all[0], []
    for n in range(1, 32):
        vec_sum = vec_sum + vec_all[n]
    router_out[...] = vec_sum[:, 8:16]
    turned = vec_sum.T
    line_out[...] = turned[0:5]
    pair_out[...] = turned[5:7]
    for e in range(8):
        total = msg_all[4 * e] + msg_all[4 * e + 1] + msg_all[4 * e + 2] + msg_all[4 * e + 3]
        up_out[e : e + 1] = total[0:1, 0 : up_out.shape[1]]
        down_out[e : e + 1] = total[1:2, 0 : down_out.shape[1]]
    for copy in [near_a, far_a, side_out] + out_copies + over_a + cross + list(over_e.values()):
        copy.wait_send()


def finish_kernel(
    out, token, expert, qkv, proj, line, pair, router, up_b, down_b,
    out_o, token_o, up_o, down_o, qkv_o, proj_o, line_0, line_1, line_2, line_3, line_4, pair_o, router_o, up_b_o, down_b_o,
):
    half = up_o.shape[1]
    out_o[...] = out[...]
    token_o[...] = token[...]
    up_o[...] = expert[:, 0:half].astype(F32)
    down_o[...] = expert[:, half : 2 * half].astype(F32)
    qkv_o[...] = qkv[...]
    proj_o[...] = proj[...]
    for i, target in enumerate((line_0, line_1, line_2, line_3, line_4)):
        target[...] = line[i]
    pair_o[...] = pair[...]
    router_o[...] = router[...]
    up_b_o[...] = up_b[...]
    down_b_o[...] = down_b[...]


def pad_images(rows, fill=0):
    images = rows.reshape((-1, SEQ) + rows.shape[1:])
    spare = [(0, 0), (0, SEQ_PAD - SEQ)] + [(0, 0)] * (rows.ndim - 1)
    return jnp.pad(images, spare, constant_values=fill).reshape((-1,) + rows.shape[1:])


def body(
    tokens, ln1_gain, ln1_shift, qkv_weight, qv_bias, out_weight, out_bias, ln2_gain, ln2_shift,
    router_weight, expert_in, expert_in_bias, expert_out, expert_out_bias, expert_ids, expert_slots,
    cotangent,
):
    n_dp = lax.axis_size("dp")
    cells = n_dp // 8
    width = tokens.shape[1]
    experts = expert_in.shape[0]
    head_cols = qkv_weight.shape[2]
    ff_slice = expert_in.shape[2]
    index = lax.axis_index("dp")
    t = lax.axis_index("tensor")
    d, cell = index // cells, index % cells
    peers = [[row * cells + c for c in range(cells)] for row in range(8)]

    expert_pack = [expert_in, jnp.swapaxes(expert_out, 1, 2)]
    lines = jnp.concatenate([ln1_gain, ln1_shift, ln2_gain, ln2_shift, out_bias]).reshape(5, -1)
    vectors = [(lines, 1), (qv_bias, 1), (router_weight, 0), (expert_out_bias, 1), (expert_in_bias, 1)]
    if cells > 1:

        def gather(part, axis):
            return lax.all_gather(part, "dp", axis=axis, tiled=True, axis_index_groups=peers)

        def quarter(part, axis):
            part = gather(lax.all_gather(part, "tensor", axis=axis, tiled=True), axis)
            size = part.shape[axis] // 4
            return lax.dynamic_slice_in_dim(part, t * size, size, axis)

        qkv_weight, out_weight = gather(qkv_weight, 0), gather(out_weight, 1)
        expert_pack = [gather(part, 1) for part in expert_pack]
        vectors = [(quarter(part, axis), axis) for part, axis in vectors]
    vectors = [part for part, _ in vectors]
    piece, ff_piece = vectors[0].shape[1], vectors[4].shape[1]
    rows = tokens.shape[0] // SEQ * SEQ_PAD
    routes = pad_images(jnp.concatenate([expert_ids, expert_slots], axis=1), -1).reshape(4, rows, 2 * TOP)
    routes = jnp.swapaxes(routes, 1, 2)
    packed_shape = (width // 8, 4 * head_cols)
    e_block = (experts, 2 * (width // 8), ff_slice)

    dma = pltpu.SemaphoreType.DMA

    def params(identity):
        return pltpu.CompilerParams(
            collective_id=identity, has_side_effects=True, vmem_limit_bytes=VMEM_LIMIT
        )

    def like(shape, dtype=BF):
        return jax.ShapeDtypeStruct(shape, dtype)

    slot_shape = (8, QUARTER, width)
    (
        probs, cols, gates, vec, tok, cot, hidden, qkv, mixed, totals, wall, bias_all, expert_all, x_rows, g_rows,
    ) = pl.pallas_call(
        functools.partial(front_kernel, cells),
        out_shape=[
            like((experts, rows), F32),
            like((4, rows, 8), F32),
            like((4, rows, 8), F32),
            like((32, width), F32),
            like((rows, width)),
            like((rows, width)),
            like((rows, width), F32),
            like((4, rows, 3 * head_cols)),
            like((4, rows, head_cols)),
            like((4, rows, 8), F32),
            like((4, 8) + packed_shape),
            like((4, 8, 8, 128), F32),
            like((4,) + e_block),
            like(slot_shape),
            like(slot_shape),
        ],
        in_specs=[VM] * 7 + [HB] * 2 + [VM] * 3,
        out_specs=[VM] * 4 + [HB] * 11,
        scratch_shapes=[
            pltpu.VMEM((4, rows, 8), F32),
            pltpu.VMEM(packed_shape, BF),
            pltpu.VMEM((piece, 128), F32),
            pltpu.VMEM((8, 128), F32),
            pltpu.VMEM((128, 128), F32),
            pltpu.VMEM((rows, width), BF),
            pltpu.VMEM((4, 8, rows), jnp.int32),
            pltpu.VMEM((4, 8, rows), F32),
            pltpu.VMEM((rows, width), F32),
            pltpu.VMEM((4, rows, 3 * head_cols), BF),
            pltpu.VMEM((4, rows, head_cols), BF),
            pltpu.VMEM((4, 8) + packed_shape, BF),
            pltpu.VMEM(slot_shape, BF),
            pltpu.VMEM((8, 4, piece, 128), F32),
            pltpu.VMEM((4, rows, width), BF),
            pltpu.VMEM((4, rows, width), BF),
            pltpu.VMEM((SLOTS, width), BF),
            pltpu.VMEM((SLOTS, width), BF),
            pltpu.VMEM((rows, width), F32),
            pltpu.VMEM((8, rows), F32),
            pltpu.VMEM((4, 1, 3 * head_cols), F32),
        ]
        + [dma((5, 8))] * 2
        + [dma((4, 8))] * 6
        + [dma((6,)), dma((3, 3)), dma((3, 3)), dma((8,)), dma((8,)), dma((4,)), dma((4,)), dma((8,))],
        compiler_params=params(0),
        name="front",
    )(qkv_weight, out_weight, *vectors, *expert_pack, tokens, cotangent, routes)

    r_rows, picked, y_rows, expert_grad, side_grad, message = pl.pallas_call(
        functools.partial(middle_kernel, cells),
        out_shape=[
            like((rows, width), F32),
            like((8, rows), F32),
            like(slot_shape),
            like(e_block),
            like(e_block),
            like((32, 8, 128), F32),
        ],
        in_specs=[VM, HB, HB, VM, VM, VM],
        out_specs=[VM, VM, HB, HB, HB, VM],
        scratch_shapes=[
            pltpu.VMEM((4, 1, ff_slice), F32),
            pltpu.VMEM((4, 1, ff_slice), F32),
            pltpu.VMEM((1, width), F32),
            pltpu.VMEM(expert_all.shape, BF),
            pltpu.VMEM((4 * SLOTS, ff_slice), BF),
            pltpu.VMEM((4 * SLOTS, ff_slice), BF),
            pltpu.VMEM((width, SLOTS), BF),
            pltpu.VMEM((width, SLOTS), BF),
            pltpu.VMEM((2 * QUARTER, width), F32),
            pltpu.VMEM((SLOTS, width), F32),
            pltpu.VMEM(slot_shape, BF),
            pltpu.VMEM(slot_shape, BF),
            pltpu.VMEM((8, 8, QUARTER), F32),
            pltpu.VMEM(slot_shape, BF),
            pltpu.VMEM(slot_shape, BF),
            pltpu.VMEM((8, 8, QUARTER), F32),
            pltpu.VMEM((2, rows, width), BF),
            pltpu.VMEM((2, rows, width), BF),
            pltpu.VMEM((rows, width), BF),
            pltpu.VMEM((rows, width), BF),
            pltpu.VMEM((2, 8, rows), F32),
            pltpu.VMEM((2, 8, rows), F32),
            pltpu.VMEM((8, rows), F32),
            pltpu.VMEM((8, rows), F32),
            dma((4, 4)), dma((2,)), dma((3, 4)), dma((3, 4)), dma((8,)), dma((8,)), dma((3, 8)), dma((3, 8)), dma((2, 2)), dma((2, 2)),
            dma((2,)), dma((2,)), dma((2, 8)), dma((2, 8)), dma((8,)), dma((8,)), dma((4,)),
            pltpu.SemaphoreType.REGULAR, pltpu.SemaphoreType.REGULAR,
        ],
        compiler_params=params(1),
        name="middle",
    )(x_rows.reshape(SLOTS, width), g_rows, expert_all, bias_all, vec, cols)

    a_block = wall.shape[1:]
    out, token_grad, expert_sum, qkv_sum, proj_sum, line_sum, pair_sum, router_sum, up_sum, down_sum = pl.pallas_call(
        functools.partial(back_kernel, cells),
        out_shape=[
            like(tokens.shape),
            like(tokens.shape, F32),
            like(e_block),
            like((width // 8, 3, head_cols), F32),
            like((head_cols, width // 8), F32),
            like((5, piece), F32),
            like((2, piece), F32),
            like((piece, 8), F32),
            like((8, ff_piece), F32),
            like((8, piece), F32),
        ],
        in_specs=[VM] * 10 + [HB] * 7,
        out_specs=[VM, VM, HB] + [VM] * 7,
        scratch_shapes=[
            pltpu.VMEM((rows, width), F32),
            pltpu.VMEM(a_block[1:], F32),
            pltpu.VMEM(message.shape, F32),
            pltpu.VMEM((32, piece, 128), F32),
            pltpu.VMEM((rows, width), F32),
            pltpu.VMEM((128, width), F32),
            pltpu.VMEM((32, piece, 128), F32),
            pltpu.VMEM(wall.shape, BF),
            pltpu.VMEM((4, 1, 3 * head_cols), F32),
            pltpu.VMEM((2,) + a_block, BF),
            pltpu.VMEM(a_block, BF),
            pltpu.VMEM(a_block, BF),
            pltpu.VMEM(a_block, BF),
            pltpu.VMEM((4,) + a_block[1:], BF),
            pltpu.VMEM((4,) + a_block[1:], BF),
            pltpu.VMEM((2, rows, width), BF),
            pltpu.VMEM((2, rows, width), BF),
            pltpu.VMEM((rows, width), BF),
            pltpu.VMEM((rows, width), BF),
            pltpu.VMEM(e_block, BF),
            pltpu.VMEM(e_block, BF),
            pltpu.VMEM((SLOTS, width), BF),
            pltpu.VMEM(wall.shape, BF),
            pltpu.VMEM(qkv.shape, BF),
            pltpu.VMEM(mixed.shape, BF),
            dma((4,)),
            dma((2,)), dma((2,)), dma((8,)), dma((8,)), dma((8,)), dma((8,)), dma((8,)), dma((8,)),
            dma((4,)), dma((4,)), dma((4,)), dma((4,)), dma((3,)), dma((3,)), dma((9,)), dma((31,)), dma((31,)), dma((31,)), dma((31,)),
        ],
        compiler_params=params(2),
        name="back",
    )(
        tok, hidden, r_rows, cols, gates, totals, cot, probs, picked, vec,
        y_rows.reshape(SLOTS, width), wall, qkv, mixed, expert_grad, side_grad, message,
    )

    if cells > 1:

        def scatter(part, axis):
            return lax.psum_scatter(part, "dp", scatter_dimension=axis, tiled=True, axis_index_groups=peers)

        def share(part, axis):
            part = lax.psum(part, "dp", axis_index_groups=peers)
            part = lax.all_gather(part, "tensor", axis=axis, tiled=True)
            size = part.shape[axis] // (4 * cells)
            return lax.dynamic_slice_in_dim(part, (cell * 4 + t) * size, size, axis)

        expert_sum = scatter(expert_sum.astype(F32).reshape(8, 2, width // 8, -1), 2)
        expert_sum = expert_sum.reshape(8, -1, expert_sum.shape[3])
        qkv_sum, proj_sum = scatter(qkv_sum, 0), scatter(proj_sum, 1)
        line_sum, pair_sum, up_sum, down_sum = (share(part, 1) for part in (line_sum, pair_sum, up_sum, down_sum))
        router_sum = share(router_sum, 0)
    if cells > 1:
        own_rows = expert_in.shape[1]
        up_grad, down_grad = expert_sum[:, :own_rows].astype(F32), expert_sum[:, own_rows:].astype(F32)
        line_sum = [line_sum[i] for i in range(5)]
    else:
        half_block = like((8, width // 8, ff_slice), F32)
        parts = (out, token_grad, expert_sum, qkv_sum, proj_sum, line_sum, pair_sum, router_sum, up_sum, down_sum)
        shapes = [like(part.shape, part.dtype) for part in parts]
        shapes = shapes[:2] + [half_block] * 2 + shapes[3:5] + [like((piece,), F32)] * 5 + shapes[6:]
        out, token_grad, up_grad, down_grad, qkv_sum, proj_sum, *line_sum, pair_sum, router_sum, up_sum, down_sum = (
            pl.pallas_call(
                finish_kernel,
                out_shape=shapes,
                in_specs=[VM] * 10,
                out_specs=[VM] * 15,
                compiler_params=pltpu.CompilerParams(vmem_limit_bytes=VMEM_LIMIT),
                name="finish",
            )(*parts)
        )
    return (
        out,
        token_grad,
        line_sum[0],
        line_sum[1],
        qkv_sum,
        pair_sum,
        proj_sum,
        line_sum[4],
        line_sum[2],
        line_sum[3],
        router_sum,
        up_grad,
        up_sum,
        jnp.swapaxes(down_grad, 1, 2),
        down_sum,
    )


def solution(mesh):
    both = ("dp", "tensor")
    return jax.shard_map(
        body,
        mesh=mesh,
        in_specs=(
            P(both, None),
            P(both),
            P(both),
            P("dp", None, "tensor"),
            P(None, both),
            P("tensor", "dp"),
            P(both),
            P(both),
            P(both),
            P(both, None),
            P(None, "dp", "tensor"),
            P(None, both),
            P(None, "tensor", "dp"),
            P(None, both),
            P("dp", None),
            P("dp", None),
            P(both, None),
        ),
        out_specs=(
            P(both, None),
            P(both, None),
            P(both),
            P(both),
            P("dp", None, "tensor"),
            P(None, both),
            P("tensor", "dp"),
            P(both),
            P(both),
            P(both),
            P(both, None),
            P(None, "dp", "tensor"),
            P(None, both),
            P(None, "tensor", "dp"),
            P(None, both),
        ),
        check_vma=False,
    )
```

```python
import functools

import jax
import jax.numpy as jnp
from jax import lax
from jax.experimental import pallas as pl
from jax.experimental.pallas import tpu as pltpu
from jax.sharding import PartitionSpec as P

HEAD_DIM = 64
SEQ = 197
SEQ_PAD = 208
TOP = 2
QUARTER = 160
SLOTS = 8 * QUARTER
EARLY = 5
EPS = 1e-6
BF = jnp.bfloat16
F32 = jnp.float32
MESH = pl.DeviceIdType.MESH
VMEM_LIMIT = 60 * 1024 * 1024
VM = pl.BlockSpec(memory_space=pltpu.VMEM)
HB = pl.BlockSpec(memory_space=pl.ANY)


def nn(a, b):
    return lax.dot_general(a, b, (((1,), (0,)), ((), ())), preferred_element_type=F32)


def nt(a, b):
    return lax.dot_general(a, b, (((1,), (1,)), ((), ())), preferred_element_type=F32)


def tn(a, b):
    return lax.dot_general(a, b, (((0,), (0,)), ((), ())), preferred_element_type=F32)


def unit_norm(rows):
    centred = rows - jnp.mean(rows, axis=-1, keepdims=True)
    inv = lax.rsqrt(jnp.mean(centred * centred, axis=-1, keepdims=True) + EPS)
    return centred * inv, inv


def place(cells):
    index = lax.axis_index("dp")
    return lax.div(index, cells), lax.rem(index, cells), lax.axis_index("tensor")


def tensor_peers(t):
    core = t + 1 - 2 * lax.rem(t, 2)
    side = lax.rem(t + 2, 4)
    return core, side, lax.rem(core + 2, 4)


def remote(src, dst, send, recv, device):
    return pltpu.make_async_remote_copy(
        src_ref=src, dst_ref=dst, send_sem=send, recv_sem=recv, device_id=device, device_id_type=MESH
    )


def signal(barrier, device):
    pl.semaphore_signal(barrier, inc=1, device_id=device, device_id_type=MESH)


def masked_scores(q, k):
    scores = nt(q, k) * (HEAD_DIM**-0.5)
    lane = lax.broadcasted_iota(jnp.int32, scores.shape, 1)
    return jnp.where(lane < SEQ, scores, -1e30)


def softmax_rows(q, k):
    scores = masked_scores(q, k)
    top = jnp.max(scores, axis=-1, keepdims=True)
    raised = jnp.exp(scores - top)
    total = jnp.sum(raised, axis=-1, keepdims=True)
    return raised * (1.0 / total), top + jnp.log(total)


def front_kernel(
    cells,
    qkv_w, out_w, line_0, line_1, line_2, line_3, line_4, pair_bias, router_w, down_b, up_b, expert_a, expert_b, tokens, cotangent, routes,
    probs_out, cols_out, gates_out, vec_out, tok_hbm, cot_hbm, hidden_hbm, qkv_hbm, mixed_hbm, totals_hbm, wall_hbm, b_all,
    expert_all, x_out, g_hbm,
    totals, packed, small_a, small_b, small_rows, tok, cols, gates_all, hidden_out, qkv_out, mixed_out, wall, g_out, small_all, cot_all, sec_all, x_buf, raw, acc, gates, qkv_bias,
    dp_s, dp_r, y_s, y_r, c_s, c_r, f_s, f_r, own, ag_s, ag_r, x_s, x_r, w_s, w_r, save_s,
):
    d, cell, t = place(cells)
    core, side, far = tensor_peers(t)
    here = d * cells + cell
    twin = d + 1 - 2 * lax.rem(d, 2)
    rows = tok.shape[0]
    srcs = (small_a, packed, small_b)

    def at_dp(k):
        return (lax.rem(d + k, 8) * cells + cell, t)

    def spot(a, tt, s):
        return small_all.at[s, tt] if a == 0 else (None, wall, b_all, expert_all)[a].at[tt, s]

    barrier = pltpu.get_barrier_semaphore()
    for k in range(1, 8):
        signal(barrier, at_dp(k))
    signal(barrier, (here, core))
    signal(barrier, (here, side))
    joined = 3 * qkv_w.shape[2]
    for j in range(3):
        packed[:, j * qkv_w.shape[2] : (j + 1) * qkv_w.shape[2]] = qkv_w[:, j, :]
    packed[:, joined : joined + out_w.shape[0]] = out_w[...].astype(F32).T.astype(BF)
    small_rows[...] = jnp.zeros_like(small_rows)
    piece = line_0.shape[0]
    for i, line in enumerate((line_0, line_1, line_2, line_3, line_4)):
        small_rows[i : i + 1, 0:piece] = line[...].astype(F32).reshape(1, piece)
    small_rows[5:7, 0:piece] = pair_bias[...].astype(F32)
    small_rows[7:15, 0:piece] = router_w[...].astype(F32).T
    small_rows[15:23, 0:piece] = down_b[...].astype(F32)
    small_a[...] = small_rows[...].T[0:piece]
    small_b[...] = jnp.zeros_like(small_b)
    small_b[:, 0 : up_b.shape[1]] = up_b[...].astype(F32)
    tok[...] = jnp.zeros_like(tok)
    for i in range(rows // SEQ_PAD):
        tok[i * SEQ_PAD : i * SEQ_PAD + SEQ] = tokens[i * SEQ : (i + 1) * SEQ]
    cot_all[t] = jnp.zeros_like(tok)
    for i in range(rows // SEQ_PAD):
        cot_all[t, i * SEQ_PAD : i * SEQ_PAD + SEQ] = cotangent[i * SEQ : (i + 1) * SEQ]
    pl.semaphore_wait(barrier, 9)

    depth = expert_a.shape[1]

    def part_of(ref, h):
        return ref.at[pl.ds(h * depth, depth)]

    mine = [pltpu.make_async_copy(srcs[a], spot(a, t, d), own.at[a]) for a in range(3)]
    mine_w = [
        pltpu.make_async_copy(part.at[d], part_of(spot(3, t, d), h), own.at[3 + 2 * h])
        for h, part in enumerate((expert_a, expert_b))
    ]
    dp_copies = [
        [
            remote(srcs[a], spot(a, t, d), dp_s.at[a, k], dp_r.at[a, k], at_dp(k))
            for k in ((2, 4, 6) if a == 1 else range(1, 8))
        ]
        for a in range(3)
    ]
    dp_copies.append(
        [
            [
                remote(
                    part.at[lax.rem(d + k, 8)],
                    part_of(spot(3, t, d), h),
                    dp_s.at[3 + h, k],
                    dp_r.at[3 + h, d],
                    at_dp(k),
                )
                for h, part in enumerate((expert_a, expert_b))
            ]
            for k in range(1, 8)
        ]
    )

    def land(k):
        block = spot(3, t, source(3, k))
        for h in range(2):
            piece_of = part_of(block, h)
            remote(piece_of, piece_of, dp_s.at[3 + h, k], dp_r.at[3 + h, source(3, k)], at_dp(k)).wait_recv()

    side_copies = [[None] * (4 if a == 3 else 8) for a in range(4)]
    near_copies = [[None] * (4 if a == 3 else 8) for a in range(4)]
    far_copies = [[None] * (4 if a == 3 else 8) for a in range(4)]

    cross = [remote(packed, wall.at[t, d], w_s.at[0], w_r.at[0], (twin * cells + cell, t))]

    def launch(a, part=slice(0, 7)):
        for copy in (mine_w if a == 3 else [mine[a]]) if part.start == 0 else []:
            copy.start()
        for copy in sum(dp_copies[3][part], []) if a == 3 else dp_copies[a]:
            copy.start()
        if a == 1:
            cross[0].start()

    near_z = d + 2 - 4 * lax.rem(lax.div(d, 2), 2)
    near_twin = twin + near_z - d
    by_distance = [d, twin, near_z, near_twin] + [lax.rem(s + 4, 8) for s in (d, twin, near_z, near_twin)]

    def source(a, k):
        if a == 3:
            return by_distance[k]
        if a != 1:
            return lax.rem(d + 8 - k, 8)
        return lax.rem((d if k < 4 else twin) + 8 - 2 * (k % 4), 8)

    def spread(a, first, last):
        for k in range(first, last):
            block = spot(a, t, source(a, k))
            if k == 0:
                for copy in mine_w if a == 3 else [mine[a]]:
                    copy.wait()
            elif a == 3:
                land(k)
            elif a != 1 or k < 4:
                dp_copies[a][k - 1].wait_recv()
            else:
                cross[k - 4].wait_recv()
            if a == 1 and 0 < k < 4:
                cross.append(remote(block, block, w_s.at[k], w_r.at[k], (twin * cells + cell, t)))
                cross[k].start()
            side_copies[a][k] = remote(block, block, y_s.at[a, k], y_r.at[a, k], (here, side))
            side_copies[a][k].start()
            near_copies[a][k] = remote(block, block, c_s.at[a, k], c_r.at[a, k], (here, core))
            near_copies[a][k].start()

    def forward(a, count=8):
        for k in range(count):
            block = spot(a, side, source(a, k))
            side_copies[a][k].wait_recv()
            far_copies[a][k] = remote(block, block, f_s.at[a, k], f_r.at[a, k], (here, core))
            far_copies[a][k].start()

    def arrive(copies):
        for copy in copies:
            copy.wait_recv()

    def exchange(n, src, dst):
        over = remote(src, dst.at[t], ag_s.at[n, 0], ag_r.at[n, 0], (here, side))
        near = remote(src, dst.at[t], ag_s.at[n, 1], ag_r.at[n, 1], (here, core))
        over.start()
        near.start()
        return over, near

    def pass_on(n, pair, dst):
        pair[0].wait_recv()
        along = remote(dst.at[side], dst.at[side], ag_s.at[n, 2], ag_r.at[n, 2], (here, core))
        along.start()
        return pair + (along,)

    launch(0)
    launch(1)
    cot_pair = exchange(0, cot_all.at[t], cot_all)
    for tt in range(4):
        route = routes[tt]
        wanted = route[2:4] - QUARTER * t
        inside = jnp.logical_and(route[2:4] >= 0, jnp.logical_and(wanted >= 0, wanted < QUARTER))
        col = jnp.where(inside, route[0:2] * QUARTER + wanted, -1)
        cols[tt] = jnp.concatenate([col, jnp.full((6, rows), -1, jnp.int32)], axis=0)
        cols_out[tt] = cols[tt].astype(F32).T
    ids = routes[t, 0:2]
    spread(0, 0, 8)
    forward(0)
    arrive(near_copies[0])
    arrive(far_copies[0])
    columns = small_all[...].reshape(-1, 128)
    vec = columns.T[:32]
    vec_out[...] = vec
    heads = qkv_out.shape[2] // 3
    for tt in range(4):
        cut = slice(tt * heads, (tt + 1) * heads)
        qkv_bias[tt] = jnp.concatenate([vec[5:6, cut], jnp.zeros((1, heads), F32), vec[6:7, cut]], axis=1)
    inputs = tok[...].astype(F32)
    unit, _ = unit_norm(inputs)
    first = (unit * vec[0:1] + vec[1:2]).astype(BF)
    acc[...] = inputs + vec[4:5]

    def attend(tt):
        weights = wall[tt].reshape(8 * packed.shape[0], -1)
        qkv = (nn(first, weights[:, : 3 * heads]) + qkv_bias[tt]).astype(BF)
        qkv_out[tt] = qkv
        mixed = []
        for i in range(rows // SEQ_PAD):
            part = qkv[i * SEQ_PAD : (i + 1) * SEQ_PAD]
            sides = []
            for h in range(heads // HEAD_DIM):
                q, k, v = (part[:, j * heads + h * HEAD_DIM : j * heads + (h + 1) * HEAD_DIM] for j in range(3))
                weight, log_total = softmax_rows(q, k)
                totals[tt, i * SEQ_PAD : (i + 1) * SEQ_PAD, h : h + 1] = log_total
                sides.append(nn(weight.astype(BF), v).astype(BF))
            mixed.append(jnp.concatenate(sides, axis=1))
        mixed = jnp.concatenate(mixed, axis=0)
        mixed_out[tt] = mixed
        acc[...] += nt(mixed, weights[:, 3 * heads :])

    spread(1, 0, 4)
    launch(3, slice(1, 7, 2))
    spread(1, 4, 8)
    launch(3, slice(0, 7, 2))
    launch(2)
    cot_pair = pass_on(0, cot_pair, cot_all)
    attend(t)
    forward(1)
    attend(side)
    arrive(near_copies[1])
    attend(core)
    arrive(far_copies[1])
    attend(far)

    kept_copies = []

    def save(n, src, dst):
        copy = pltpu.make_async_copy(src, dst, save_s.at[n])
        copy.start()
        kept_copies.append(copy)

    hidden = acc[...]
    hidden_out[...] = hidden
    unit, _ = unit_norm(hidden)
    second = (unit * vec[2:3] + vec[3:4]).astype(BF)
    sec_all[t] = second
    sec_pair = exchange(1, sec_all.at[t], sec_all)
    logits = nt(vec[7:15].astype(BF), second)
    raised = jnp.exp(logits - jnp.max(logits, axis=0, keepdims=True))
    probs = raised / jnp.sum(raised, axis=0, keepdims=True)
    probs_out[...] = probs
    lane = lax.broadcasted_iota(jnp.int32, probs.shape, 0)
    picked = [jnp.sum(jnp.where(lane == ids[k : k + 1], probs, 0.0), axis=0, keepdims=True) for k in range(2)]
    gates[...] = jnp.concatenate(picked + [jnp.zeros((6, rows), F32)], axis=0)
    gates_all[t] = gates[...]
    gate_pair = exchange(2, gates, gates_all)

    pair_rows = 2 * QUARTER

    def onehots(tt, base):
        at = lax.broadcasted_iota(jnp.int32, (pair_rows, rows), 0) + base
        return at == cols[tt, 0:1], at == cols[tt, 1:2]

    def pick(base, source):
        total = None
        for tt in range(4):
            one, two = onehots(tt, base)
            part = nn(jnp.logical_or(one, two).astype(F32).astype(BF), source[tt])
            total = part if total is None else total + part
        return total.astype(BF)

    def chunk(i):
        c = lax.rem(lax.div(d, 2) + 1 + i, 4)
        return c, pl.multiple_of(c * pair_rows, pair_rows)

    save(0, hidden_out, hidden_hbm)
    save(1, qkv_out, qkv_hbm)
    save(2, mixed_out, mixed_hbm)
    save(7, totals, totals_hbm)
    save(3, wall, wall_hbm)
    save(5, tok, tok_hbm)
    save(6, cot_all.at[t], cot_hbm)
    arrive([cot_pair[1], cot_pair[2]])
    for i in range(4):
        c, base = chunk(i)
        raw[pl.ds(base, pair_rows)] = pick(base, cot_all)
    sec_pair = pass_on(1, sec_pair, sec_all)
    gate_pair = pass_on(2, gate_pair, gates_all)
    arrive([sec_pair[1], sec_pair[2], gate_pair[1], gate_pair[2]])

    for tt in range(4):
        gates_out[tt] = gates_all[tt].T
    sent = []

    for i in range(4):
        c, base = chunk(i)
        x_buf[pl.ds(base, pair_rows)] = pick(base, sec_all)
        for h in range(2):
            half = lax.rem(d + h, 2)
            e = 2 * c + half
            block = x_buf.at[pl.ds(pl.multiple_of(base + half * QUARTER, QUARTER), QUARTER)]
            copy = remote(block, x_out.at[d], x_s.at[e], x_r.at[d], (e * cells + cell, t))
            keep = pltpu.make_async_copy(block, x_out.at[d], own.at[4])
            sent.append((e, copy, keep))

            @pl.when(e == d)
            def _():
                keep.start()

            @pl.when(e != d)
            def _():
                copy.start()

    spread(2, 0, 8)
    spread(3, 0, 4)
    forward(2)
    for i in range(4):
        c, base = chunk(i)
        gate = None
        for tt in range(4):
            one, two = onehots(tt, base)
            part = jnp.where(one, gates_all[tt, 0:1], jnp.where(two, gates_all[tt, 1:2], 0.0))
            part = jnp.sum(part, axis=1, keepdims=True)
            gate = part if gate is None else gate + part
        kept = (gate * raw[pl.ds(base, pair_rows)].astype(F32)).astype(BF)
        g_out[pl.ds(2 * c, 2)] = kept.reshape(2, QUARTER, kept.shape[1])
    save(4, g_out, g_hbm)

    forward(3, 4)
    for a in (2, 3):
        arrive(near_copies[a])
        arrive(far_copies[a])
    for k in range(4, 8):
        land(k)
    for k in range(1, 8):
        g = lax.rem(d + 8 - k, 8)
        remote(x_buf.at[pl.ds(0, QUARTER)], x_out.at[g], x_s.at[g], x_r.at[g], at_dp(8 - k)).wait_recv()
    for e, copy, keep in sent:

        @pl.when(e == d)
        def _():
            keep.wait()

        @pl.when(e != d)
        def _():
            copy.wait_send()

    for copy in kept_copies:
        copy.wait()
    for copy in cross:
        copy.wait_send()
    for a in range(4):
        direct = sum(dp_copies[a], []) if a == 3 else dp_copies[a]
        for copy in direct + side_copies[a] + near_copies[a] + far_copies[a]:
            copy.wait_send()
    for trio in (cot_pair, sec_pair, gate_pair):
        for copy in trio:
            copy.wait_send()


def gelu_both(x):
    phi = 0.5 * (1.0 + lax.erf(x * (0.5**0.5)))
    slope = phi + x * (jnp.exp(-0.5 * x * x) * 0.3989422804014327)
    return x * phi, slope


def middle_kernel(
    cells,
    x_ref, g_src, expert_all, b_all, vec, cols,
    r_out, q_out, y_out, e_out, e_side_out, msg_out,
    up_bias, dup_out, ddown_out, w_buf, act_buf, pre_buf, x_turned, g_turned, acc, y_acc, y_buf, b_buf, q_buf, g_in, b_in, q_in,
    blocks, core_in, side_buf, side_in, q_blocks, q_core, q_side, q_mid,
    load, store, w_s, w_r, g_s, g_r, a_s, a_r, c_s, c_r, y_s, y_r, e_s, e_r, f_s, f_r, own, core_free, side_free,
):
    d, cell, t = place(cells)
    core, side, far = tensor_peers(t)
    here = d * cells + cell
    width = x_ref.shape[1]
    ff = act_buf.shape[1]
    half = width // 8
    pair_rows = 2 * QUARTER

    def at_dp(k):
        return (lax.rem(d + k, 8) * cells + cell, t)

    twin = d + 1 - 2 * lax.rem(d, 2)
    near_z = d + 2 - 4 * lax.rem(lax.div(d, 2), 2)
    early = (d, twin, near_z, twin + near_z - d)
    late = tuple(lax.rem(p + 4, 8) for p in early)
    loads = [[pltpu.make_async_copy(expert_all.at[t], w_buf.at[t], load.at[0, 0])]]
    for i, tt in enumerate((core, side, far)):
        loads.append(
            [pltpu.make_async_copy(expert_all.at[tt, p], w_buf.at[tt, p], load.at[i + 1, k]) for k, p in enumerate(early)]
        )
    for copy in sum(loads, []):
        copy.start()
    barrier = pltpu.get_barrier_semaphore()
    for k in range(1, 8):
        signal(barrier, at_dp(k))
    signal(barrier, (here, core))
    signal(barrier, (here, side))
    pl.semaphore_wait(barrier, 9)

    plane = lax.div(d, 2)
    near_plane = plane + 1 - 2 * lax.rem(plane, 2)
    planes = (plane, lax.rem(plane + 2, 4), lax.rem(near_plane + 2, 4), near_plane)
    sent = []

    def post(c, src, out, send, recv, keep_sem):
        for h in range(2):
            g = 2 * c + lax.rem(d + h, 2)
            copy = remote(src.at[g], out.at[d], send.at[g], recv.at[d], (g * cells + cell, t))
            keep = pltpu.make_async_copy(src.at[g], out.at[d], keep_sem)
            sent.append((g, copy))

            @pl.when(g == d)
            def _():
                keep.start()

            @pl.when(g != d)
            def _():
                copy.start()

    def landed(g, src, out, send, recv, keep_sem):
        @pl.when(g == d)
        def _():
            pltpu.make_async_copy(src.at[g], out.at[g], keep_sem).wait()

        @pl.when(g != d)
        def _():
            remote(src.at[g], out.at[g], send.at[g], recv.at[g], (g * cells + cell, t)).wait_recv()

    for i in range(4):
        post(planes[3 - i], g_src, g_in, g_s, g_r, own.at[3])
    w_side, w_near, w_far = [], [], []
    for k, p in enumerate(late):
        block = expert_all.at[t, p]
        w_side.append(remote(block, w_buf.at[t, p], w_s.at[0, k], w_r.at[0, k], (here, side)))
        w_near.append(remote(block, w_buf.at[t, p], w_s.at[1, k], w_r.at[1, k], (here, core)))
        w_far.append(remote(w_buf.at[side, p], w_buf.at[side, p], w_s.at[2, k], w_r.at[2, k], (here, core)))
    for copy in w_side + w_near:
        copy.start()
    ff_piece = ff // 8
    for p in range(8):
        for tt in range(4):
            at = (p % 2) * 4 + tt
            up_bias[p // 2, :, at * ff_piece : (at + 1) * ff_piece] = b_all[tt, p, pl.ds(d, 1), 0:ff_piece]
    x_turned[...] = x_ref[...].T
    dup_out[...] = jnp.zeros_like(dup_out)

    def w_in(tt):
        return w_buf[tt, :, 0:half].reshape(width, ff)

    def w_out(tt):
        return w_buf[tt, :, half : 2 * half].reshape(width, ff)

    def held(tt, base):
        return pl.ds(pl.multiple_of(tt * SLOTS + base, pair_rows), pair_rows)

    y_acc[...] = jnp.broadcast_to(vec[pl.ds(15 + d, 1)], y_acc.shape)

    def ahead(tt):
        def rows_step(i, carry):
            base = pl.multiple_of(i * pair_rows, pair_rows)
            span = pl.ds(base, pair_rows)
            pre = nn(x_ref[span], w_in(tt)) + up_bias[tt]
            act, slope = gelu_both(pre)
            act = act.astype(BF)
            act_buf[held(tt, base)] = act
            pre_buf[held(tt, base)] = slope.astype(BF)
            y_acc[span] += nt(act, w_out(tt))
            return carry

        lax.fori_loop(0, 4, rows_step, 0)

    loads[0][0].wait()
    ahead(t)
    for copy in loads[1]:
        copy.wait()
    for copy in w_near:
        copy.wait_recv()
    ahead(core)
    for i in range(4):
        w_side[i].wait_recv()
        w_far[i].start()
    for copy in loads[2]:
        copy.wait()
    ahead(side)
    for copy in loads[3]:
        copy.wait()
    for copy in w_far:
        copy.wait_recv()
    ahead(far)
    for copy in w_far:
        copy.wait_send()
    y_buf[...] = y_acc[...].astype(BF).reshape(y_buf.shape)
    ones = jnp.ones((8, width), BF)
    for i in range(4):
        c = planes[i]
        base = pl.multiple_of(c * pair_rows, pair_rows)
        pair = pl.ds(2 * c, 2)
        for h in range(2):
            landed(2 * c + h, g_src, g_in, g_s, g_r, own.at[3])
        acc[...] = jnp.zeros_like(acc)

        def slice_back(tt, carry):
            grad = nn(g_in[pair].reshape(pair_rows, width), w_out(tt)) * pre_buf[held(tt, base)].astype(F32)
            grad = grad.astype(BF)
            pre_buf[held(tt, base)] = grad
            acc[...] += nt(grad, w_in(tt))
            dup_out[tt] += jnp.sum(grad.astype(F32), axis=0, keepdims=True)
            return carry

        lax.fori_loop(0, 4, slice_back, 0)
        b_buf[pair] = acc[...].astype(BF).reshape(2, QUARTER, width)
        post(c, b_buf, b_in, a_s.at[0], a_r.at[0], own.at[0])
        for h in range(2):
            g = 2 * c + h
            z = y_buf[g].astype(F32) * g_in[g].astype(F32)
            high = z.astype(BF)
            q_buf[g] = nt(ones, high) + nt(ones, (z - high.astype(F32)).astype(BF))
        post(c, q_buf, q_in, a_s.at[2], a_r.at[2], own.at[2])
    for i in range(4):
        post(planes[3 - i], y_buf, y_out, a_s.at[1], a_r.at[1], own.at[1])
    g_rows = g_in[...].reshape(SLOTS, width)
    g_turned[...] = g_rows.T
    ddown_out[...] = jnp.sum(g_rows.astype(F32), axis=0, keepdims=True)

    def grad_slice(tt, carry):
        def grad_rows(n, inner):
            span = pl.ds(pl.multiple_of(n * 2 * half, 2 * half), 2 * half)
            pair = pl.ds(2 * n, 2)
            at = pl.ds(pl.multiple_of(tt * SLOTS, SLOTS), SLOTS)
            w_buf[tt, pair, 0:half] = nn(x_turned[span], pre_buf[at]).astype(BF).reshape(2, half, ff)
            w_buf[tt, pair, half : 2 * half] = nn(g_turned[span], act_buf[at]).astype(BF).reshape(2, half, ff)
            return inner

        lax.fori_loop(0, 4, grad_rows, 0)
        return carry

    lax.fori_loop(0, 4, grad_slice, 0)

    msg_out[...] = jnp.zeros_like(msg_out)
    piece = width // 32
    for n in range(32):
        at = (n % 8) * ff_piece
        msg_out[n, 0:1, 0:ff_piece] = dup_out[n // 8, :, at : at + ff_piece]
        msg_out[n, 1:2, 0:piece] = ddown_out[:, n * piece : (n + 1) * piece]

    pl.semaphore_signal(core_free, inc=1, device_id=(here, core), device_id_type=MESH)
    pl.semaphore_signal(side_free, inc=1, device_id=(here, side), device_id_type=MESH)
    pl.semaphore_wait(core_free, 1)

    def inbox(i, p):
        return pl.ds(pl.multiple_of((i * 8 + p) * 2 * half, 2 * half), 2 * half)

    near = {}
    for i, tt in enumerate((far, core)):
        for k in range(1, 9):
            p = lax.rem(d + k, 8)
            near[i, k] = remote(
                w_buf.at[tt, p], act_buf.at[inbox(i, p)], e_s.at[i, k - 1], e_r.at[i, k - 1], (here, core)
            )
            near[i, k].start()
    pl.semaphore_wait(side_free, 1)
    over = {}
    for k in range(1, 9):
        p = lax.rem(d + k, 8)
        near[0, k].wait_recv()
        total = w_buf[side, p].astype(F32) + act_buf[inbox(0, p)].astype(F32)
        w_buf[side, p] = total.astype(BF)
        if k <= EARLY:
            over[k] = remote(
                w_buf.at[side, p], pre_buf.at[inbox(0, p)], f_s.at[k - 1], f_r.at[k - 1], (here, side)
            )
            over[k].start()
    keep_side = pltpu.make_async_copy(w_buf.at[side], e_side_out, store.at[1])
    keep_side.start()

    def onehots(tt):
        at = lax.broadcasted_iota(jnp.int32, (cols.shape[1], SLOTS), 1)
        col = cols[tt, :, 0:2].astype(jnp.int32)
        return at == col[:, 0:1], at == col[:, 1:2]

    for k in range(1, 9):
        e = lax.rem(d + k, 8)
        landed(e, b_buf, b_in, a_s.at[0], a_r.at[0], own.at[0])
        landed(e, q_buf, q_in, a_s.at[2], a_r.at[2], own.at[2])
    q_line = jnp.concatenate([q_in[e] for e in range(8)], axis=1)
    owner = jnp.concatenate([jnp.full((8, QUARTER), e, jnp.int32) for e in range(8)], axis=1)
    q_line = jnp.where(lax.broadcasted_iota(jnp.int32, q_line.shape, 0) == owner, q_line, 0.0)
    q_high = q_line.astype(BF)
    q_both = jnp.concatenate([q_high, (q_line - q_high.astype(F32)).astype(BF)], axis=0)
    b_rows = b_in[...].reshape(SLOTS, width)

    def back_block(tt):
        one, two = onehots(tt)
        hot = jnp.logical_or(one, two).astype(F32).astype(BF)
        q = nt(q_both, hot)
        return nn(hot, b_rows), q[0:8] + q[8:16]

    def core_send(n, i, src, dst):
        copy = remote(src.at[i], dst.at[i], c_s.at[n, i], c_r.at[n, i], (here, core))
        copy.start()
        return copy

    def side_send(n, src, dst):
        copy = remote(src, dst, y_s.at[n], y_r.at[n], (here, side))
        copy.start()
        return copy

    core_b, core_q = [], []
    for i, tt in enumerate((far, core)):
        total, q = back_block(tt)
        blocks[i] = total.astype(BF)
        q_blocks[i] = q
        core_b.append(core_send(0, i, blocks, core_in))
        core_q.append(core_send(1, i, q_blocks, q_core))
    total, q = back_block(side)
    core_b[0].wait_recv()
    core_q[0].wait_recv()
    side_buf[...] = (total + core_in[0].astype(F32)).astype(BF)
    q_mid[...] = q + q_core[0]
    side_b = side_send(0, side_buf, side_in)
    side_q = side_send(1, q_mid, q_side)
    total, q = back_block(t)
    core_b[1].wait_recv()
    core_q[1].wait_recv()
    r_out[...] = total + core_in[1].astype(F32)
    q_out[...] = q + q_core[1]

    for k in range(1, 9):
        p = lax.rem(d + k, 8)
        near[1, k].wait_recv()
        total = w_buf[t, p].astype(F32) + act_buf[inbox(1, p)].astype(F32)
        if k <= EARLY:
            over[k].wait_recv()
            total = total + pre_buf[inbox(0, p)].astype(F32)
        w_buf[t, p] = total.astype(BF)
    keep_e = pltpu.make_async_copy(w_buf.at[t], e_out, store.at[0])
    keep_e.start()
    side_b.wait_recv()
    side_q.wait_recv()
    r_out[...] += side_in[...].astype(F32)
    q_out[...] += q_side[...]

    for k in range(1, 9):
        landed(lax.rem(d + k, 8), y_buf, y_out, a_s.at[1], a_r.at[1], own.at[1])
    for copy in core_b + core_q + [side_b, side_q] + list(near.values()) + list(over.values()) + w_near:
        copy.wait_send()
    for copy in w_side:
        copy.wait_send()
    for g, copy in sent:

        @pl.when(g != d)
        def _():
            copy.wait_send()

    keep_e.wait()
    keep_side.wait()


def back_kernel(
    cells,
    tok, hid, r_ref, cols, gates, totals, cot, probs, picked_ref, vec, y_hbm, wall_hbm, qkv_hbm, mixed_hbm, e_src, e_side_src,
    bias_msg, out, token_out, e_out, qkv_out, proj_out, line_out, pair_out, router_out, up_out, down_out,
    token_grad, a_out, msg_all, vec_all, n1, vec_grad, vec_msg, a_grad, qv_grad, a_core, a_mid, a_side, a_fin, a_cross, a_in,
    blocks, core_in, side_buf, side_in, e_own, e_in, y_rows, wall, qkv_ref, mixed_ref, fetch,
    c_s, c_r, y_s, y_r, e_s, e_r, f_s, f_r, x_s, x_r, z_s, z_r, o_s, o_r, own, m_s, m_r, v_s, v_r,
):
    d, cell, t = place(cells)
    core, side, far = tensor_peers(t)
    here = d * cells + cell
    fetches = []
    for n, (src, dst) in enumerate(((wall_hbm, wall), (qkv_hbm, qkv_ref), (mixed_hbm, mixed_ref), (y_hbm, y_rows))):
        copy = pltpu.make_async_copy(src, dst, fetch.at[n])
        copy.start()
        fetches.append(copy)
    heads = qkv_ref.shape[2] // 3
    rows = tok.shape[0]
    width = tok.shape[1]
    spot = d * 4 + t
    twin = d + 1 - 2 * lax.rem(d, 2)

    def at_dp(k):
        return (lax.rem(d + k, 8) * cells + cell, t)

    others = [(k, m) for k in range(8) for m in range(4) if k or m]

    def other(k, m):
        return lax.rem(d + k, 8), lax.rem(t + m, 4)

    barrier = pltpu.get_barrier_semaphore()
    for k, m in others:
        dd, tt = other(k, m)
        signal(barrier, (dd * cells + cell, tt))
    pl.semaphore_wait(barrier, 31)

    waits = []
    late = range(EARLY + 1, 9)
    over_e, load_e = {}, {}
    for k in range(1, EARLY + 1):
        copy = remote(e_src.at[lax.rem(d + k, 8)], e_out.at[d], e_s.at[k], e_r.at[k], at_dp(k))
        copy.start()
        waits.append(copy)
    for k in late:
        p = lax.rem(d + k, 8)
        over_e[k] = remote(e_side_src.at[p], e_in.at[p], f_s.at[k - 1], f_r.at[k - 1], (here, side))
        over_e[k].start()
        load_e[k] = pltpu.make_async_copy(e_src.at[p], e_own.at[p], own.at[k])
        load_e[k].start()

    def finish_expert(k):
        p = lax.rem(d + k, 8)
        load_e[k].wait()
        over_e[k].wait_recv()
        e_own[p] = (e_own[p].astype(F32) + e_in[p].astype(F32)).astype(BF)
        if k < 8:
            copy = remote(e_own.at[p], e_out.at[d], e_s.at[k], e_r.at[k], at_dp(k))
            waits.append(copy)
        else:
            copy = pltpu.make_async_copy(e_own.at[p], e_out.at[d], own.at[0])
            load_e[0] = copy
        copy.start()
    for n, (k, m) in enumerate(others):
        dd, tt = other(k, m)
        copy = remote(bias_msg.at[dd * 4 + tt], msg_all.at[spot], m_s.at[n], m_r.at[n], (dd * cells + cell, tt))
        copy.start()
        waits.append(copy)
    msg_own = pltpu.make_async_copy(bias_msg.at[spot], msg_all.at[spot], own.at[1])
    msg_own.start()

    hidden = hid[...]
    picked = picked_ref[...]
    logit = picked - probs[...] * jnp.sum(picked, axis=0, keepdims=True)
    high = logit.astype(BF)
    both = jnp.concatenate([high, (logit - high.astype(F32)).astype(BF)], axis=0)
    unit, inv = unit_norm(hidden)
    gain = vec[2:3]
    second = (unit * gain + vec[3:4]).astype(BF)
    router_grad = nn(both, second)
    vec_grad[...] = jnp.zeros_like(vec_grad)
    vec_grad[8:16] = router_grad[0:8] + router_grad[8:16]
    table = vec[7:15].astype(BF)
    n2 = r_ref[...] + tn(both, jnp.concatenate([table, table], axis=0))
    vec_grad[2:3] = jnp.sum(n2 * unit, axis=0, keepdims=True)
    vec_grad[3:4] = jnp.sum(n2, axis=0, keepdims=True)
    scaled = n2 * gain
    back = inv * (
        scaled
        - jnp.mean(scaled, axis=-1, keepdims=True)
        - unit * jnp.mean(scaled * unit, axis=-1, keepdims=True)
    )
    hidden_grad = cot[...].astype(F32) + back
    token_grad[...] = hidden_grad
    branch = hidden_grad.astype(BF)
    vec_grad[4:5] = jnp.sum(branch.astype(F32), axis=0, keepdims=True)
    unit1, inv1 = unit_norm(tok[...].astype(F32))
    first_norm = (unit1 * vec[0:1] + vec[1:2]).astype(BF)
    n1[...] = jnp.zeros_like(n1)

    def attend_back(tt):
        weights = wall[tt].reshape(width, -1)
        qkv = qkv_ref[tt]
        mixed_grad = nn(branch, weights[:, 3 * heads :]).astype(BF)
        triple = []
        for i in range(rows // SEQ_PAD):
            span = slice(i * SEQ_PAD, (i + 1) * SEQ_PAD)
            part, grad = qkv[span], mixed_grad[span]
            sides = [[], [], []]
            for h in range(heads // HEAD_DIM):
                q, k, v = (part[:, j * heads + h * HEAD_DIM : j * heads + (h + 1) * HEAD_DIM] for j in range(3))
                g = grad[:, h * HEAD_DIM : (h + 1) * HEAD_DIM]
                log_total = totals[tt, i * SEQ_PAD : (i + 1) * SEQ_PAD, h : h + 1]
                w = jnp.exp(masked_scores(q, k) - log_total)
                w_grad = nt(g, v)
                s_grad = (w * (w_grad - jnp.sum(w * w_grad, axis=-1, keepdims=True))).astype(BF)
                sides[0].append((nn(s_grad, k) * (HEAD_DIM**-0.5)).astype(BF))
                sides[1].append((tn(s_grad, q) * (HEAD_DIM**-0.5)).astype(BF))
                sides[2].append(tn(w.astype(BF), g).astype(BF))
            triple.append(jnp.concatenate(sides[0] + sides[1] + sides[2], axis=1))
        triple = jnp.concatenate(triple, axis=0)
        grad = jnp.concatenate([tn(first_norm, triple), tn(branch, mixed_ref[tt])], axis=1).astype(BF)
        a_grad[tt] = grad.reshape(8, width // 8, -1)
        n1[...] += nt(triple, weights[:, : 3 * heads])
        sums = jnp.sum(triple.astype(F32), axis=0, keepdims=True)
        qv_grad[tt] = sums

    def core_a(i, tt):
        copy = remote(a_grad.at[tt], a_core.at[i], c_s.at[i], c_r.at[i], (here, core))
        copy.start()
        return copy

    order = [lax.rem(twin + 2 * m, 8) for m in range(4)] + [lax.rem(d + 2 * m, 8) for m in (1, 2, 3, 0)]
    for copy in fetches:
        copy.wait()
    attend_back(far)
    near_a = core_a(0, far)
    for k in list(late)[:-1][:1]:
        finish_expert(k)
    attend_back(side)
    near_a.wait_recv()
    over_a = []
    for n, p in enumerate(order):
        a_mid[p] = (a_grad[side, p].astype(F32) + a_core[0, p].astype(F32)).astype(BF)
        copy = remote(a_mid.at[p], a_side.at[p], y_s.at[n], y_r.at[n], (here, side))
        copy.start()
        over_a.append(copy)
    for k in list(late)[:-1][1:2]:
        finish_expert(k)
    attend_back(core)
    far_a = core_a(1, core)
    for k in list(late)[2:-1]:
        finish_expert(k)
    attend_back(t)
    finish_expert(8)

    def out_block(tt):
        at = lax.broadcasted_iota(jnp.int32, (rows, SLOTS), 1)
        col = cols[tt, :, 0:2].astype(jnp.int32)
        one, two = at == col[:, 0:1], at == col[:, 1:2]
        hot = jnp.where(one, gates[tt, :, 0:1], jnp.where(two, gates[tt, :, 1:2], 0.0)).astype(BF)
        return nn(hot, y_rows[...])

    out_copies = []
    for i, tt in enumerate((far, core)):
        blocks[i] = out_block(tt).astype(BF)
        copy = remote(blocks.at[i], core_in.at[i], o_s.at[i], o_r.at[i], (here, core))
        copy.start()
        out_copies.append(copy)
    total = out_block(side)
    out_copies[0].wait_recv()
    side_buf[...] = (total + core_in[0].astype(F32)).astype(BF)
    side_out = remote(side_buf, side_in, o_s.at[2], o_r.at[2], (here, side))

    far_a.wait_recv()
    cross = []
    for n, p in enumerate(order):
        over_a[n].wait_recv()
        total = a_grad[t, p].astype(F32) + a_core[1, p].astype(F32) + a_side[p].astype(F32)
        if n < 4:
            a_fin[p] = total.astype(BF)
            copy = remote(a_fin.at[p], a_cross.at[n], x_s.at[n], x_r.at[n], (twin * cells + cell, t))
            copy.start()
            cross.append(copy)
        else:
            m = (n - 3) % 4
            cross[m].wait_recv()
            total = total + a_cross[m].astype(F32)
            if m:
                a_fin[p] = total.astype(BF)
                copy = remote(a_fin.at[p], a_in.at[m], z_s.at[m], z_r.at[m], at_dp(2 * m))
                copy.start()
                waits.append(copy)
            else:
                a_out[...] = total
    side_out.start()

    grad = n1[...]
    vec_grad[0:1] = jnp.sum(grad * unit1, axis=0, keepdims=True)
    vec_grad[1:2] = jnp.sum(grad, axis=0, keepdims=True)
    for j, row in ((0, 5), (2, 6)):
        parts = [qv_grad[tt][:, j * heads : (j + 1) * heads] for tt in range(4)]
        vec_grad[row : row + 1] = jnp.concatenate(parts, axis=1)
    turned = vec_grad[...].T
    vec_msg[...] = turned.reshape(vec_msg.shape)
    for n, (k, m) in enumerate(others):
        dd, tt = other(k, m)
        copy = remote(vec_msg.at[dd * 4 + tt], vec_all.at[spot], v_s.at[n], v_r.at[n], (dd * cells + cell, tt))
        copy.start()
        waits.append(copy)
    vec_all[spot] = vec_msg[spot]
    scaled = grad * vec[0:1]
    token_grad[...] += inv1 * (
        scaled
        - jnp.mean(scaled, axis=-1, keepdims=True)
        - unit1 * jnp.mean(scaled * unit1, axis=-1, keepdims=True)
    )
    for i in range(rows // SEQ_PAD):
        token_out[i * SEQ : (i + 1) * SEQ] = token_grad[i * SEQ_PAD : i * SEQ_PAD + SEQ]
    total = out_block(t)
    out_copies[1].wait_recv()
    total = total + core_in[1].astype(F32)
    side_out.wait_recv()
    total = (hid[...] + (total + side_in[...].astype(F32))).astype(BF)
    for i in range(rows // SEQ_PAD):
        out[i * SEQ : (i + 1) * SEQ] = total[i * SEQ_PAD : i * SEQ_PAD + SEQ]
    for copy in waits:
        copy.wait()
    for m in range(1, 4):
        a_out[...] += a_in[m].astype(F32)
    for j in range(3):
        qkv_out[:, j, :] = a_out[:, j * heads : (j + 1) * heads]
    proj_out[...] = a_out[:, 3 * heads : 4 * heads].T
    load_e[0].wait()
    msg_own.wait()
    vec_sum, msg_sum = vec_all[0], []
    for n in range(1, 32):
        vec_sum = vec_sum + vec_all[n]
    router_out[...] = vec_sum[:, 8:16]
    turned = vec_sum.T
    line_out[...] = turned[0:5]
    pair_out[...] = turned[5:7]
    for e in range(8):
        total = msg_all[4 * e] + msg_all[4 * e + 1] + msg_all[4 * e + 2] + msg_all[4 * e + 3]
        up_out[e : e + 1] = total[0:1, 0 : up_out.shape[1]]
        down_out[e : e + 1] = total[1:2, 0 : down_out.shape[1]]
    for copy in [near_a, far_a, side_out] + out_copies + over_a + cross + list(over_e.values()):
        copy.wait_send()


def finish_kernel(
    out, token, expert, qkv, proj, line, pair, router, up_b, down_b,
    out_o, token_o, up_o, down_o, qkv_o, proj_o, line_0, line_1, line_2, line_3, line_4, pair_o, router_o, up_b_o, down_b_o,
):
    half = up_o.shape[1]
    out_o[...] = out[...]
    token_o[...] = token[...]
    up_o[...] = expert[:, 0:half].astype(F32)
    down_o[...] = expert[:, half : 2 * half].astype(F32)
    qkv_o[...] = qkv[...]
    proj_o[...] = proj[...]
    for i, target in enumerate((line_0, line_1, line_2, line_3, line_4)):
        target[...] = line[i]
    pair_o[...] = pair[...]
    router_o[...] = router[...]
    up_b_o[...] = up_b[...]
    down_b_o[...] = down_b[...]


def pad_images(rows, fill=0):
    images = rows.reshape((-1, SEQ) + rows.shape[1:])
    spare = [(0, 0), (0, SEQ_PAD - SEQ)] + [(0, 0)] * (rows.ndim - 1)
    return jnp.pad(images, spare, constant_values=fill).reshape((-1,) + rows.shape[1:])


def body(
    tokens, ln1_gain, ln1_shift, qkv_weight, qv_bias, out_weight, out_bias, ln2_gain, ln2_shift,
    router_weight, expert_in, expert_in_bias, expert_out, expert_out_bias, expert_ids, expert_slots,
    cotangent,
):
    n_dp = lax.axis_size("dp")
    cells = n_dp // 8
    width = tokens.shape[1]
    experts = expert_in.shape[0]
    head_cols = qkv_weight.shape[2]
    ff_slice = expert_in.shape[2]
    index = lax.axis_index("dp")
    t = lax.axis_index("tensor")
    d, cell = index // cells, index % cells
    peers = [[row * cells + c for c in range(cells)] for row in range(8)]

    expert_pack = [expert_in, jnp.swapaxes(expert_out, 1, 2)]
    vectors = [(line, 0) for line in (ln1_gain, ln1_shift, ln2_gain, ln2_shift, out_bias)]
    vectors += [(qv_bias, 1), (router_weight, 0), (expert_out_bias, 1), (expert_in_bias, 1)]
    if cells > 1:

        def gather(part, axis):
            return lax.all_gather(part, "dp", axis=axis, tiled=True, axis_index_groups=peers)

        def quarter(part, axis):
            part = gather(lax.all_gather(part, "tensor", axis=axis, tiled=True), axis)
            size = part.shape[axis] // 4
            return lax.dynamic_slice_in_dim(part, t * size, size, axis)

        qkv_weight, out_weight = gather(qkv_weight, 0), gather(out_weight, 1)
        expert_pack = [gather(part, 1) for part in expert_pack]
        vectors = [(quarter(part, axis), axis) for part, axis in vectors]
    vectors = [part for part, _ in vectors]
    piece, ff_piece = vectors[0].shape[0], vectors[8].shape[1]
    rows = tokens.shape[0] // SEQ * SEQ_PAD
    routes = pad_images(jnp.concatenate([expert_ids, expert_slots], axis=1), -1).reshape(4, rows, 2 * TOP)
    routes = jnp.swapaxes(routes, 1, 2)
    packed_shape = (width // 8, 4 * head_cols)
    e_block = (experts, 2 * (width // 8), ff_slice)

    dma = pltpu.SemaphoreType.DMA

    def params(identity):
        return pltpu.CompilerParams(
            collective_id=identity, has_side_effects=True, vmem_limit_bytes=VMEM_LIMIT
        )

    def like(shape, dtype=BF):
        return jax.ShapeDtypeStruct(shape, dtype)

    slot_shape = (8, QUARTER, width)
    (
        probs, cols, gates, vec, tok, cot, hidden, qkv, mixed, totals, wall, bias_all, expert_all, x_rows, g_rows,
    ) = pl.pallas_call(
        functools.partial(front_kernel, cells),
        out_shape=[
            like((experts, rows), F32),
            like((4, rows, 8), F32),
            like((4, rows, 8), F32),
            like((32, width), F32),
            like((rows, width)),
            like((rows, width)),
            like((rows, width), F32),
            like((4, rows, 3 * head_cols)),
            like((4, rows, head_cols)),
            like((4, rows, 8), F32),
            like((4, 8) + packed_shape),
            like((4, 8, 8, 128), F32),
            like((4,) + e_block),
            like(slot_shape),
            like(slot_shape),
        ],
        in_specs=[VM] * 11 + [HB] * 2 + [VM] * 3,
        out_specs=[VM] * 4 + [HB] * 11,
        scratch_shapes=[
            pltpu.VMEM((4, rows, 8), F32),
            pltpu.VMEM(packed_shape, BF),
            pltpu.VMEM((piece, 128), F32),
            pltpu.VMEM((8, 128), F32),
            pltpu.VMEM((128, 128), F32),
            pltpu.VMEM((rows, width), BF),
            pltpu.VMEM((4, 8, rows), jnp.int32),
            pltpu.VMEM((4, 8, rows), F32),
            pltpu.VMEM((rows, width), F32),
            pltpu.VMEM((4, rows, 3 * head_cols), BF),
            pltpu.VMEM((4, rows, head_cols), BF),
            pltpu.VMEM((4, 8) + packed_shape, BF),
            pltpu.VMEM(slot_shape, BF),
            pltpu.VMEM((8, 4, piece, 128), F32),
            pltpu.VMEM((4, rows, width), BF),
            pltpu.VMEM((4, rows, width), BF),
            pltpu.VMEM((SLOTS, width), BF),
            pltpu.VMEM((SLOTS, width), BF),
            pltpu.VMEM((rows, width), F32),
            pltpu.VMEM((8, rows), F32),
            pltpu.VMEM((4, 1, 3 * head_cols), F32),
        ]
        + [dma((5, 8))] * 2
        + [dma((4, 8))] * 6
        + [dma((6,)), dma((3, 3)), dma((3, 3)), dma((8,)), dma((8,)), dma((4,)), dma((4,)), dma((8,))],
        compiler_params=params(0),
        name="front",
    )(qkv_weight, out_weight, *vectors, *expert_pack, tokens, cotangent, routes)

    r_rows, picked, y_rows, expert_grad, side_grad, message = pl.pallas_call(
        functools.partial(middle_kernel, cells),
        out_shape=[
            like((rows, width), F32),
            like((8, rows), F32),
            like(slot_shape),
            like(e_block),
            like(e_block),
            like((32, 8, 128), F32),
        ],
        in_specs=[VM, HB, HB, VM, VM, VM],
        out_specs=[VM, VM, HB, HB, HB, VM],
        scratch_shapes=[
            pltpu.VMEM((4, 1, ff_slice), F32),
            pltpu.VMEM((4, 1, ff_slice), F32),
            pltpu.VMEM((1, width), F32),
            pltpu.VMEM(expert_all.shape, BF),
            pltpu.VMEM((4 * SLOTS, ff_slice), BF),
            pltpu.VMEM((4 * SLOTS, ff_slice), BF),
            pltpu.VMEM((width, SLOTS), BF),
            pltpu.VMEM((width, SLOTS), BF),
            pltpu.VMEM((2 * QUARTER, width), F32),
            pltpu.VMEM((SLOTS, width), F32),
            pltpu.VMEM(slot_shape, BF),
            pltpu.VMEM(slot_shape, BF),
            pltpu.VMEM((8, 8, QUARTER), F32),
            pltpu.VMEM(slot_shape, BF),
            pltpu.VMEM(slot_shape, BF),
            pltpu.VMEM((8, 8, QUARTER), F32),
            pltpu.VMEM((2, rows, width), BF),
            pltpu.VMEM((2, rows, width), BF),
            pltpu.VMEM((rows, width), BF),
            pltpu.VMEM((rows, width), BF),
            pltpu.VMEM((2, 8, rows), F32),
            pltpu.VMEM((2, 8, rows), F32),
            pltpu.VMEM((8, rows), F32),
            pltpu.VMEM((8, rows), F32),
            dma((4, 4)), dma((2,)), dma((3, 4)), dma((3, 4)), dma((8,)), dma((8,)), dma((3, 8)), dma((3, 8)), dma((2, 2)), dma((2, 2)),
            dma((2,)), dma((2,)), dma((2, 8)), dma((2, 8)), dma((8,)), dma((8,)), dma((4,)),
            pltpu.SemaphoreType.REGULAR, pltpu.SemaphoreType.REGULAR,
        ],
        compiler_params=params(1),
        name="middle",
    )(x_rows.reshape(SLOTS, width), g_rows, expert_all, bias_all, vec, cols)

    a_block = wall.shape[1:]
    out, token_grad, expert_sum, qkv_sum, proj_sum, line_sum, pair_sum, router_sum, up_sum, down_sum = pl.pallas_call(
        functools.partial(back_kernel, cells),
        out_shape=[
            like(tokens.shape),
            like(tokens.shape, F32),
            like(e_block),
            like((width // 8, 3, head_cols), F32),
            like((head_cols, width // 8), F32),
            like((5, piece), F32),
            like((2, piece), F32),
            like((piece, 8), F32),
            like((8, ff_piece), F32),
            like((8, piece), F32),
        ],
        in_specs=[VM] * 10 + [HB] * 7,
        out_specs=[VM, VM, HB] + [VM] * 7,
        scratch_shapes=[
            pltpu.VMEM((rows, width), F32),
            pltpu.VMEM(a_block[1:], F32),
            pltpu.VMEM(message.shape, F32),
            pltpu.VMEM((32, piece, 128), F32),
            pltpu.VMEM((rows, width), F32),
            pltpu.VMEM((128, width), F32),
            pltpu.VMEM((32, piece, 128), F32),
            pltpu.VMEM(wall.shape, BF),
            pltpu.VMEM((4, 1, 3 * head_cols), F32),
            pltpu.VMEM((2,) + a_block, BF),
            pltpu.VMEM(a_block, BF),
            pltpu.VMEM(a_block, BF),
            pltpu.VMEM(a_block, BF),
            pltpu.VMEM((4,) + a_block[1:], BF),
            pltpu.VMEM((4,) + a_block[1:], BF),
            pltpu.VMEM((2, rows, width), BF),
            pltpu.VMEM((2, rows, width), BF),
            pltpu.VMEM((rows, width), BF),
            pltpu.VMEM((rows, width), BF),
            pltpu.VMEM(e_block, BF),
            pltpu.VMEM(e_block, BF),
            pltpu.VMEM((SLOTS, width), BF),
            pltpu.VMEM(wall.shape, BF),
            pltpu.VMEM(qkv.shape, BF),
            pltpu.VMEM(mixed.shape, BF),
            dma((4,)),
            dma((2,)), dma((2,)), dma((8,)), dma((8,)), dma((8,)), dma((8,)), dma((8,)), dma((8,)),
            dma((4,)), dma((4,)), dma((4,)), dma((4,)), dma((3,)), dma((3,)), dma((9,)), dma((31,)), dma((31,)), dma((31,)), dma((31,)),
        ],
        compiler_params=params(2),
        name="back",
    )(
        tok, hidden, r_rows, cols, gates, totals, cot, probs, picked, vec,
        y_rows.reshape(SLOTS, width), wall, qkv, mixed, expert_grad, side_grad, message,
    )

    if cells > 1:

        def scatter(part, axis):
            return lax.psum_scatter(part, "dp", scatter_dimension=axis, tiled=True, axis_index_groups=peers)

        def share(part, axis):
            part = lax.psum(part, "dp", axis_index_groups=peers)
            part = lax.all_gather(part, "tensor", axis=axis, tiled=True)
            size = part.shape[axis] // (4 * cells)
            return lax.dynamic_slice_in_dim(part, (cell * 4 + t) * size, size, axis)

        expert_sum = scatter(expert_sum.astype(F32).reshape(8, 2, width // 8, -1), 2)
        expert_sum = expert_sum.reshape(8, -1, expert_sum.shape[3])
        qkv_sum, proj_sum = scatter(qkv_sum, 0), scatter(proj_sum, 1)
        line_sum, pair_sum, up_sum, down_sum = (share(part, 1) for part in (line_sum, pair_sum, up_sum, down_sum))
        router_sum = share(router_sum, 0)
    if cells > 1:
        own_rows = expert_in.shape[1]
        up_grad, down_grad = expert_sum[:, :own_rows].astype(F32), expert_sum[:, own_rows:].astype(F32)
        line_sum = [line_sum[i] for i in range(5)]
    else:
        half_block = like((8, width // 8, ff_slice), F32)
        parts = (out, token_grad, expert_sum, qkv_sum, proj_sum, line_sum, pair_sum, router_sum, up_sum, down_sum)
        shapes = [like(part.shape, part.dtype) for part in parts]
        shapes = shapes[:2] + [half_block] * 2 + shapes[3:5] + [like((piece,), F32)] * 5 + shapes[6:]
        out, token_grad, up_grad, down_grad, qkv_sum, proj_sum, *line_sum, pair_sum, router_sum, up_sum, down_sum = (
            pl.pallas_call(
                finish_kernel,
                out_shape=shapes,
                in_specs=[VM] * 10,
                out_specs=[VM] * 15,
                compiler_params=pltpu.CompilerParams(vmem_limit_bytes=VMEM_LIMIT),
                name="finish",
            )(*parts)
        )
    return (
        out,
        token_grad,
        line_sum[0],
        line_sum[1],
        qkv_sum,
        pair_sum,
        proj_sum,
        line_sum[4],
        line_sum[2],
        line_sum[3],
        router_sum,
        up_grad,
        up_sum,
        jnp.swapaxes(down_grad, 1, 2),
        down_sum,
    )


def solution(mesh):
    both = ("dp", "tensor")
    return jax.shard_map(
        body,
        mesh=mesh,
        in_specs=(
            P(both, None),
            P(both),
            P(both),
            P("dp", None, "tensor"),
            P(None, both),
            P("tensor", "dp"),
            P(both),
            P(both),
            P(both),
            P(both, None),
            P(None, "dp", "tensor"),
            P(None, both),
            P(None, "tensor", "dp"),
            P(None, both),
            P("dp", None),
            P("dp", None),
            P(both, None),
        ),
        out_specs=(
            P(both, None),
            P(both, None),
            P(both),
            P(both),
            P("dp", None, "tensor"),
            P(None, both),
            P("tensor", "dp"),
            P(both),
            P(both),
            P(both),
            P(both, None),
            P(None, "dp", "tensor"),
            P(None, both),
            P(None, "tensor", "dp"),
            P(None, both),
        ),
        check_vma=False,
    )
```

```python
import functools

import jax
import jax.numpy as jnp
from jax import lax
from jax.experimental import pallas as pl
from jax.experimental.pallas import tpu as pltpu
from jax.sharding import PartitionSpec as P

HEAD_DIM = 64
SEQ = 197
SEQ_PAD = 208
TOP = 2
QUARTER = 160
SLOTS = 8 * QUARTER
EARLY = 5
EPS = 1e-6
BF = jnp.bfloat16
F32 = jnp.float32
MESH = pl.DeviceIdType.MESH
VMEM_LIMIT = 60 * 1024 * 1024
VM = pl.BlockSpec(memory_space=pltpu.VMEM)
HB = pl.BlockSpec(memory_space=pl.ANY)


def nn(a, b):
    return lax.dot_general(a, b, (((1,), (0,)), ((), ())), preferred_element_type=F32)


def nt(a, b):
    return lax.dot_general(a, b, (((1,), (1,)), ((), ())), preferred_element_type=F32)


def tn(a, b):
    return lax.dot_general(a, b, (((0,), (0,)), ((), ())), preferred_element_type=F32)


def unit_norm(rows):
    centred = rows - jnp.mean(rows, axis=-1, keepdims=True)
    inv = lax.rsqrt(jnp.mean(centred * centred, axis=-1, keepdims=True) + EPS)
    return centred * inv, inv


def place(cells):
    index = lax.axis_index("dp")
    return lax.div(index, cells), lax.rem(index, cells), lax.axis_index("tensor")


def tensor_peers(t):
    core = t + 1 - 2 * lax.rem(t, 2)
    side = lax.rem(t + 2, 4)
    return core, side, lax.rem(core + 2, 4)


def remote(src, dst, send, recv, device):
    return pltpu.make_async_remote_copy(
        src_ref=src, dst_ref=dst, send_sem=send, recv_sem=recv, device_id=device, device_id_type=MESH
    )


def signal(barrier, device):
    pl.semaphore_signal(barrier, inc=1, device_id=device, device_id_type=MESH)


def masked_scores(q, k):
    scores = nt(q, k) * (HEAD_DIM**-0.5)
    lane = lax.broadcasted_iota(jnp.int32, scores.shape, 1)
    return jnp.where(lane < SEQ, scores, -1e30)


def softmax_rows(q, k):
    scores = masked_scores(q, k)
    top = jnp.max(scores, axis=-1, keepdims=True)
    raised = jnp.exp(scores - top)
    total = jnp.sum(raised, axis=-1, keepdims=True)
    return raised * (1.0 / total), top + jnp.log(total)


def front_kernel(
    cells,
    qkv_w, out_w, line_0, line_1, line_2, line_3, line_4, pair_bias, router_w, down_b, up_b, expert_a, expert_b, tokens, cotangent, routes,
    probs_out, cols_out, gates_out, vec_out, tok_hbm, cot_hbm, hidden_hbm, qkv_hbm, mixed_hbm, totals_hbm, wall_hbm, b_all,
    expert_all, x_out, g_hbm,
    totals, packed, small_a, small_b, small_rows, tok, cols, gates_all, hidden_out, qkv_out, mixed_out, wall, g_out, small_all, cot_all, sec_all, x_buf, raw, acc, gates, qkv_bias,
    dp_s, dp_r, y_s, y_r, c_s, c_r, f_s, f_r, own, ag_s, ag_r, x_s, x_r, w_s, w_r, save_s,
):
    d, cell, t = place(cells)
    core, side, far = tensor_peers(t)
    here = d * cells + cell
    twin = d + 1 - 2 * lax.rem(d, 2)
    rows = tok.shape[0]
    srcs = (small_a, packed, small_b)

    def at_dp(k):
        return (lax.rem(d + k, 8) * cells + cell, t)

    def spot(a, tt, s):
        return small_all.at[s, tt] if a == 0 else (None, wall, b_all, expert_all)[a].at[tt, s]

    barrier = pltpu.get_barrier_semaphore()
    for k in range(1, 8):
        signal(barrier, at_dp(k))
    signal(barrier, (here, core))
    signal(barrier, (here, side))
    joined = 3 * qkv_w.shape[2]
    for j in range(3):
        packed[:, j * qkv_w.shape[2] : (j + 1) * qkv_w.shape[2]] = qkv_w[j]
    packed[:, joined : joined + out_w.shape[0]] = out_w[...].astype(F32).T.astype(BF)
    small_rows[...] = jnp.zeros_like(small_rows)
    piece = line_0.shape[0]
    for i, line in enumerate((line_0, line_1, line_2, line_3, line_4)):
        small_rows[i : i + 1, 0:piece] = line[...].astype(F32).reshape(1, piece)
    small_rows[5:7, 0:piece] = pair_bias[...].astype(F32)
    small_rows[7:15, 0:piece] = router_w[...].astype(F32)
    small_rows[15:23, 0:piece] = down_b[...].astype(F32)
    small_a[...] = small_rows[...].T[0:piece]
    small_b[...] = jnp.zeros_like(small_b)
    small_b[:, 0 : up_b.shape[1]] = up_b[...].astype(F32)
    tok[...] = jnp.zeros_like(tok)
    for i in range(rows // SEQ_PAD):
        tok[i * SEQ_PAD : i * SEQ_PAD + SEQ] = tokens[i * SEQ : (i + 1) * SEQ]
    cot_all[t] = jnp.zeros_like(tok)
    for i in range(rows // SEQ_PAD):
        cot_all[t, i * SEQ_PAD : i * SEQ_PAD + SEQ] = cotangent[i * SEQ : (i + 1) * SEQ]
    pl.semaphore_wait(barrier, 9)

    depth = expert_a.shape[1]

    def part_of(ref, h):
        return ref.at[pl.ds(h * depth, depth)]

    mine = [pltpu.make_async_copy(srcs[a], spot(a, t, d), own.at[a]) for a in range(3)]
    mine_w = [
        pltpu.make_async_copy(part.at[d], part_of(spot(3, t, d), h), own.at[3 + 2 * h])
        for h, part in enumerate((expert_a, expert_b))
    ]
    dp_copies = [
        [
            remote(srcs[a], spot(a, t, d), dp_s.at[a, k], dp_r.at[a, k], at_dp(k))
            for k in ((2, 4, 6) if a == 1 else range(1, 8))
        ]
        for a in range(3)
    ]
    dp_copies.append(
        [
            [
                remote(
                    part.at[lax.rem(d + k, 8)],
                    part_of(spot(3, t, d), h),
                    dp_s.at[3 + h, k],
                    dp_r.at[3 + h, d],
                    at_dp(k),
                )
                for h, part in enumerate((expert_a, expert_b))
            ]
            for k in range(1, 8)
        ]
    )

    def land(k):
        block = spot(3, t, source(3, k))
        for h in range(2):
            piece_of = part_of(block, h)
            remote(piece_of, piece_of, dp_s.at[3 + h, k], dp_r.at[3 + h, source(3, k)], at_dp(k)).wait_recv()

    side_copies = [[None] * (4 if a == 3 else 8) for a in range(4)]
    near_copies = [[None] * (4 if a == 3 else 8) for a in range(4)]
    far_copies = [[None] * (4 if a == 3 else 8) for a in range(4)]

    cross = [remote(packed, wall.at[t, d], w_s.at[0], w_r.at[0], (twin * cells + cell, t))]

    def launch(a, part=slice(0, 7)):
        for copy in (mine_w if a == 3 else [mine[a]]) if part.start == 0 else []:
            copy.start()
        for copy in sum(dp_copies[3][part], []) if a == 3 else dp_copies[a]:
            copy.start()
        if a == 1:
            cross[0].start()

    near_z = d + 2 - 4 * lax.rem(lax.div(d, 2), 2)
    near_twin = twin + near_z - d
    by_distance = [d, twin, near_z, near_twin] + [lax.rem(s + 4, 8) for s in (d, twin, near_z, near_twin)]

    def source(a, k):
        if a == 3:
            return by_distance[k]
        if a != 1:
            return lax.rem(d + 8 - k, 8)
        return lax.rem((d if k < 4 else twin) + 8 - 2 * (k % 4), 8)

    def spread(a, first, last):
        for k in range(first, last):
            block = spot(a, t, source(a, k))
            if k == 0:
                for copy in mine_w if a == 3 else [mine[a]]:
                    copy.wait()
            elif a == 3:
                land(k)
            elif a != 1 or k < 4:
                dp_copies[a][k - 1].wait_recv()
            else:
                cross[k - 4].wait_recv()
            if a == 1 and 0 < k < 4:
                cross.append(remote(block, block, w_s.at[k], w_r.at[k], (twin * cells + cell, t)))
                cross[k].start()
            side_copies[a][k] = remote(block, block, y_s.at[a, k], y_r.at[a, k], (here, side))
            side_copies[a][k].start()
            near_copies[a][k] = remote(block, block, c_s.at[a, k], c_r.at[a, k], (here, core))
            near_copies[a][k].start()

    def forward(a, count=8):
        for k in range(count):
            block = spot(a, side, source(a, k))
            side_copies[a][k].wait_recv()
            far_copies[a][k] = remote(block, block, f_s.at[a, k], f_r.at[a, k], (here, core))
            far_copies[a][k].start()

    def arrive(copies):
        for copy in copies:
            copy.wait_recv()

    def exchange(n, src, dst):
        over = remote(src, dst.at[t], ag_s.at[n, 0], ag_r.at[n, 0], (here, side))
        near = remote(src, dst.at[t], ag_s.at[n, 1], ag_r.at[n, 1], (here, core))
        over.start()
        near.start()
        return over, near

    def pass_on(n, pair, dst):
        pair[0].wait_recv()
        along = remote(dst.at[side], dst.at[side], ag_s.at[n, 2], ag_r.at[n, 2], (here, core))
        along.start()
        return pair + (along,)

    launch(0)
    launch(1)
    cot_pair = exchange(0, cot_all.at[t], cot_all)
    for tt in range(4):
        route = routes[tt]
        wanted = route[2:4] - QUARTER * t
        inside = jnp.logical_and(route[2:4] >= 0, jnp.logical_and(wanted >= 0, wanted < QUARTER))
        col = jnp.where(inside, route[0:2] * QUARTER + wanted, -1)
        cols[tt] = jnp.concatenate([col, jnp.full((6, rows), -1, jnp.int32)], axis=0)
        cols_out[tt] = cols[tt].astype(F32).T
    ids = routes[t, 0:2]
    spread(0, 0, 8)
    forward(0)
    arrive(near_copies[0])
    arrive(far_copies[0])
    columns = small_all[...].reshape(-1, 128)
    vec = columns.T[:32]
    vec_out[...] = vec
    heads = qkv_out.shape[2] // 3
    for tt in range(4):
        cut = slice(tt * heads, (tt + 1) * heads)
        qkv_bias[tt] = jnp.concatenate([vec[5:6, cut], jnp.zeros((1, heads), F32), vec[6:7, cut]], axis=1)
    inputs = tok[...].astype(F32)
    unit, _ = unit_norm(inputs)
    first = (unit * vec[0:1] + vec[1:2]).astype(BF)
    acc[...] = inputs + vec[4:5]

    def attend(tt):
        weights = wall[tt].reshape(8 * packed.shape[0], -1)
        qkv = (nn(first, weights[:, : 3 * heads]) + qkv_bias[tt]).astype(BF)
        qkv_out[tt] = qkv
        mixed = []
        for i in range(rows // SEQ_PAD):
            part = qkv[i * SEQ_PAD : (i + 1) * SEQ_PAD]
            sides = []
            for h in range(heads // HEAD_DIM):
                q, k, v = (part[:, j * heads + h * HEAD_DIM : j * heads + (h + 1) * HEAD_DIM] for j in range(3))
                weight, log_total = softmax_rows(q, k)
                totals[tt, i * SEQ_PAD : (i + 1) * SEQ_PAD, h : h + 1] = log_total
                sides.append(nn(weight.astype(BF), v).astype(BF))
            mixed.append(jnp.concatenate(sides, axis=1))
        mixed = jnp.concatenate(mixed, axis=0)
        mixed_out[tt] = mixed
        acc[...] += nt(mixed, weights[:, 3 * heads :])

    spread(1, 0, 4)
    launch(3, slice(1, 7, 2))
    spread(1, 4, 8)
    launch(3, slice(0, 7, 2))
    launch(2)
    cot_pair = pass_on(0, cot_pair, cot_all)
    attend(t)
    forward(1)
    attend(side)
    arrive(near_copies[1])
    attend(core)
    arrive(far_copies[1])
    attend(far)

    kept_copies = []

    def save(n, src, dst):
        copy = pltpu.make_async_copy(src, dst, save_s.at[n])
        copy.start()
        kept_copies.append(copy)

    hidden = acc[...]
    hidden_out[...] = hidden
    unit, _ = unit_norm(hidden)
    second = (unit * vec[2:3] + vec[3:4]).astype(BF)
    sec_all[t] = second
    sec_pair = exchange(1, sec_all.at[t], sec_all)
    logits = nt(vec[7:15].astype(BF), second)
    raised = jnp.exp(logits - jnp.max(logits, axis=0, keepdims=True))
    probs = raised / jnp.sum(raised, axis=0, keepdims=True)
    probs_out[...] = probs
    lane = lax.broadcasted_iota(jnp.int32, probs.shape, 0)
    picked = [jnp.sum(jnp.where(lane == ids[k : k + 1], probs, 0.0), axis=0, keepdims=True) for k in range(2)]
    gates[...] = jnp.concatenate(picked + [jnp.zeros((6, rows), F32)], axis=0)
    gates_all[t] = gates[...]
    gate_pair = exchange(2, gates, gates_all)

    pair_rows = 2 * QUARTER

    def onehots(tt, base):
        at = lax.broadcasted_iota(jnp.int32, (pair_rows, rows), 0) + base
        return at == cols[tt, 0:1], at == cols[tt, 1:2]

    def pick(base, source):
        total = None
        for tt in range(4):
            one, two = onehots(tt, base)
            part = nn(jnp.logical_or(one, two).astype(F32).astype(BF), source[tt])
            total = part if total is None else total + part
        return total.astype(BF)

    def chunk(i):
        c = lax.rem(lax.div(d, 2) + 1 + i, 4)
        return c, pl.multiple_of(c * pair_rows, pair_rows)

    save(0, hidden_out, hidden_hbm)
    save(1, qkv_out, qkv_hbm)
    save(2, mixed_out, mixed_hbm)
    save(7, totals, totals_hbm)
    save(3, wall, wall_hbm)
    save(5, tok, tok_hbm)
    save(6, cot_all.at[t], cot_hbm)
    arrive([cot_pair[1], cot_pair[2]])
    for i in range(4):
        c, base = chunk(i)
        raw[pl.ds(base, pair_rows)] = pick(base, cot_all)
    sec_pair = pass_on(1, sec_pair, sec_all)
    gate_pair = pass_on(2, gate_pair, gates_all)
    arrive([sec_pair[1], sec_pair[2], gate_pair[1], gate_pair[2]])

    for tt in range(4):
        gates_out[tt] = gates_all[tt].T
    sent = []

    for i in range(4):
        c, base = chunk(i)
        x_buf[pl.ds(base, pair_rows)] = pick(base, sec_all)
        for h in range(2):
            half = lax.rem(d + h, 2)
            e = 2 * c + half
            block = x_buf.at[pl.ds(pl.multiple_of(base + half * QUARTER, QUARTER), QUARTER)]
            copy = remote(block, x_out.at[d], x_s.at[e], x_r.at[d], (e * cells + cell, t))
            keep = pltpu.make_async_copy(block, x_out.at[d], own.at[4])
            sent.append((e, copy, keep))

            @pl.when(e == d)
            def _():
                keep.start()

            @pl.when(e != d)
            def _():
                copy.start()

    spread(2, 0, 8)
    spread(3, 0, 4)
    forward(2)
    for i in range(4):
        c, base = chunk(i)
        gate = None
        for tt in range(4):
            one, two = onehots(tt, base)
            part = jnp.where(one, gates_all[tt, 0:1], jnp.where(two, gates_all[tt, 1:2], 0.0))
            part = jnp.sum(part, axis=1, keepdims=True)
            gate = part if gate is None else gate + part
        kept = (gate * raw[pl.ds(base, pair_rows)].astype(F32)).astype(BF)
        g_out[pl.ds(2 * c, 2)] = kept.reshape(2, QUARTER, kept.shape[1])
    save(4, g_out, g_hbm)

    forward(3, 4)
    for a in (2, 3):
        arrive(near_copies[a])
        arrive(far_copies[a])
    for k in range(4, 8):
        land(k)
    for k in range(1, 8):
        g = lax.rem(d + 8 - k, 8)
        remote(x_buf.at[pl.ds(0, QUARTER)], x_out.at[g], x_s.at[g], x_r.at[g], at_dp(8 - k)).wait_recv()
    for e, copy, keep in sent:

        @pl.when(e == d)
        def _():
            keep.wait()

        @pl.when(e != d)
        def _():
            copy.wait_send()

    for copy in kept_copies:
        copy.wait()
    for copy in cross:
        copy.wait_send()
    for a in range(4):
        direct = sum(dp_copies[a], []) if a == 3 else dp_copies[a]
        for copy in direct + side_copies[a] + near_copies[a] + far_copies[a]:
            copy.wait_send()
    for trio in (cot_pair, sec_pair, gate_pair):
        for copy in trio:
            copy.wait_send()


def gelu_both(x):
    phi = 0.5 * (1.0 + lax.erf(x * (0.5**0.5)))
    slope = phi + x * (jnp.exp(-0.5 * x * x) * 0.3989422804014327)
    return x * phi, slope


def middle_kernel(
    cells,
    x_ref, g_src, expert_all, b_all, vec, cols,
    r_out, q_out, y_out, e_out, e_side_out, msg_out,
    up_bias, dup_out, ddown_out, w_buf, act_buf, pre_buf, x_turned, g_turned, acc, y_acc, y_buf, b_buf, q_buf, g_in, b_in, q_in,
    blocks, core_in, side_buf, side_in, q_blocks, q_core, q_side, q_mid,
    load, store, w_s, w_r, g_s, g_r, a_s, a_r, c_s, c_r, y_s, y_r, e_s, e_r, f_s, f_r, own, core_free, side_free,
):
    d, cell, t = place(cells)
    core, side, far = tensor_peers(t)
    here = d * cells + cell
    width = x_ref.shape[1]
    ff = act_buf.shape[1]
    half = width // 8
    pair_rows = 2 * QUARTER

    def at_dp(k):
        return (lax.rem(d + k, 8) * cells + cell, t)

    twin = d + 1 - 2 * lax.rem(d, 2)
    near_z = d + 2 - 4 * lax.rem(lax.div(d, 2), 2)
    early = (d, twin, near_z, twin + near_z - d)
    late = tuple(lax.rem(p + 4, 8) for p in early)
    loads = [[pltpu.make_async_copy(expert_all.at[t], w_buf.at[t], load.at[0, 0])]]
    for i, tt in enumerate((core, side, far)):
        loads.append(
            [pltpu.make_async_copy(expert_all.at[tt, p], w_buf.at[tt, p], load.at[i + 1, k]) for k, p in enumerate(early)]
        )
    for copy in sum(loads, []):
        copy.start()
    barrier = pltpu.get_barrier_semaphore()
    for k in range(1, 8):
        signal(barrier, at_dp(k))
    signal(barrier, (here, core))
    signal(barrier, (here, side))
    pl.semaphore_wait(barrier, 9)

    plane = lax.div(d, 2)
    near_plane = plane + 1 - 2 * lax.rem(plane, 2)
    planes = (plane, lax.rem(plane + 2, 4), lax.rem(near_plane + 2, 4), near_plane)
    sent = []

    def post(c, src, out, send, recv, keep_sem):
        for h in range(2):
            g = 2 * c + lax.rem(d + h, 2)
            copy = remote(src.at[g], out.at[d], send.at[g], recv.at[d], (g * cells + cell, t))
            keep = pltpu.make_async_copy(src.at[g], out.at[d], keep_sem)
            sent.append((g, copy))

            @pl.when(g == d)
            def _():
                keep.start()

            @pl.when(g != d)
            def _():
                copy.start()

    def landed(g, src, out, send, recv, keep_sem):
        @pl.when(g == d)
        def _():
            pltpu.make_async_copy(src.at[g], out.at[g], keep_sem).wait()

        @pl.when(g != d)
        def _():
            remote(src.at[g], out.at[g], send.at[g], recv.at[g], (g * cells + cell, t)).wait_recv()

    for i in range(4):
        post(planes[3 - i], g_src, g_in, g_s, g_r, own.at[3])
    w_side, w_near, w_far = [], [], []
    for k, p in enumerate(late):
        block = expert_all.at[t, p]
        w_side.append(remote(block, w_buf.at[t, p], w_s.at[0, k], w_r.at[0, k], (here, side)))
        w_near.append(remote(block, w_buf.at[t, p], w_s.at[1, k], w_r.at[1, k], (here, core)))
        w_far.append(remote(w_buf.at[side, p], w_buf.at[side, p], w_s.at[2, k], w_r.at[2, k], (here, core)))
    for copy in w_side + w_near:
        copy.start()
    ff_piece = ff // 8
    for p in range(8):
        for tt in range(4):
            at = (p % 2) * 4 + tt
            up_bias[p // 2, :, at * ff_piece : (at + 1) * ff_piece] = b_all[tt, p, pl.ds(d, 1), 0:ff_piece]
    x_turned[...] = x_ref[...].T
    dup_out[...] = jnp.zeros_like(dup_out)

    def w_in(tt):
        return w_buf[tt, :, 0:half].reshape(width, ff)

    def w_out(tt):
        return w_buf[tt, :, half : 2 * half].reshape(width, ff)

    def held(tt, base):
        return pl.ds(pl.multiple_of(tt * SLOTS + base, pair_rows), pair_rows)

    y_acc[...] = jnp.broadcast_to(vec[pl.ds(15 + d, 1)], y_acc.shape)

    def ahead(tt):
        def rows_step(i, carry):
            base = pl.multiple_of(i * pair_rows, pair_rows)
            span = pl.ds(base, pair_rows)
            pre = nn(x_ref[span], w_in(tt)) + up_bias[tt]
            act, slope = gelu_both(pre)
            act = act.astype(BF)
            act_buf[held(tt, base)] = act
            pre_buf[held(tt, base)] = slope.astype(BF)
            y_acc[span] += nt(act, w_out(tt))
            return carry

        lax.fori_loop(0, 4, rows_step, 0)

    loads[0][0].wait()
    ahead(t)
    for copy in loads[1]:
        copy.wait()
    for copy in w_near:
        copy.wait_recv()
    ahead(core)
    for i in range(4):
        w_side[i].wait_recv()
        w_far[i].start()
    for copy in loads[2]:
        copy.wait()
    ahead(side)
    for copy in loads[3]:
        copy.wait()
    for copy in w_far:
        copy.wait_recv()
    ahead(far)
    for copy in w_far:
        copy.wait_send()
    y_buf[...] = y_acc[...].astype(BF).reshape(y_buf.shape)
    ones = jnp.ones((8, width), BF)
    for i in range(4):
        c = planes[i]
        base = pl.multiple_of(c * pair_rows, pair_rows)
        pair = pl.ds(2 * c, 2)
        for h in range(2):
            landed(2 * c + h, g_src, g_in, g_s, g_r, own.at[3])
        acc[...] = jnp.zeros_like(acc)

        def slice_back(tt, carry):
            grad = nn(g_in[pair].reshape(pair_rows, width), w_out(tt)) * pre_buf[held(tt, base)].astype(F32)
            grad = grad.astype(BF)
            pre_buf[held(tt, base)] = grad
            acc[...] += nt(grad, w_in(tt))
            dup_out[tt] += jnp.sum(grad.astype(F32), axis=0, keepdims=True)
            return carry

        lax.fori_loop(0, 4, slice_back, 0)
        b_buf[pair] = acc[...].astype(BF).reshape(2, QUARTER, width)
        post(c, b_buf, b_in, a_s.at[0], a_r.at[0], own.at[0])
        for h in range(2):
            g = 2 * c + h
            z = y_buf[g].astype(F32) * g_in[g].astype(F32)
            high = z.astype(BF)
            q_buf[g] = nt(ones, high) + nt(ones, (z - high.astype(F32)).astype(BF))
        post(c, q_buf, q_in, a_s.at[2], a_r.at[2], own.at[2])
    for i in range(4):
        post(planes[3 - i], y_buf, y_out, a_s.at[1], a_r.at[1], own.at[1])
    g_rows = g_in[...].reshape(SLOTS, width)
    g_turned[...] = g_rows.T
    ddown_out[...] = jnp.sum(g_rows.astype(F32), axis=0, keepdims=True)

    def grad_slice(tt, carry):
        def grad_rows(n, inner):
            span = pl.ds(pl.multiple_of(n * 2 * half, 2 * half), 2 * half)
            pair = pl.ds(2 * n, 2)
            at = pl.ds(pl.multiple_of(tt * SLOTS, SLOTS), SLOTS)
            w_buf[tt, pair, 0:half] = nn(x_turned[span], pre_buf[at]).astype(BF).reshape(2, half, ff)
            w_buf[tt, pair, half : 2 * half] = nn(g_turned[span], act_buf[at]).astype(BF).reshape(2, half, ff)
            return inner

        lax.fori_loop(0, 4, grad_rows, 0)
        return carry

    lax.fori_loop(0, 4, grad_slice, 0)

    msg_out[...] = jnp.zeros_like(msg_out)
    piece = width // 32
    for n in range(32):
        at = (n % 8) * ff_piece
        msg_out[n, 0:1, 0:ff_piece] = dup_out[n // 8, :, at : at + ff_piece]
        msg_out[n, 1:2, 0:piece] = ddown_out[:, n * piece : (n + 1) * piece]

    pl.semaphore_signal(core_free, inc=1, device_id=(here, core), device_id_type=MESH)
    pl.semaphore_signal(side_free, inc=1, device_id=(here, side), device_id_type=MESH)
    pl.semaphore_wait(core_free, 1)

    def inbox(i, p):
        return pl.ds(pl.multiple_of((i * 8 + p) * 2 * half, 2 * half), 2 * half)

    near = {}
    for i, tt in enumerate((far, core)):
        for k in range(1, 9):
            p = lax.rem(d + k, 8)
            near[i, k] = remote(
                w_buf.at[tt, p], act_buf.at[inbox(i, p)], e_s.at[i, k - 1], e_r.at[i, k - 1], (here, core)
            )
            near[i, k].start()
    pl.semaphore_wait(side_free, 1)
    over = {}
    for k in range(1, 9):
        p = lax.rem(d + k, 8)
        near[0, k].wait_recv()
        total = w_buf[side, p].astype(F32) + act_buf[inbox(0, p)].astype(F32)
        w_buf[side, p] = total.astype(BF)
        if k <= EARLY:
            over[k] = remote(
                w_buf.at[side, p], pre_buf.at[inbox(0, p)], f_s.at[k - 1], f_r.at[k - 1], (here, side)
            )
            over[k].start()
    keep_side = pltpu.make_async_copy(w_buf.at[side], e_side_out, store.at[1])
    keep_side.start()

    def onehots(tt):
        at = lax.broadcasted_iota(jnp.int32, (cols.shape[1], SLOTS), 1)
        col = cols[tt, :, 0:2].astype(jnp.int32)
        return at == col[:, 0:1], at == col[:, 1:2]

    for k in range(1, 9):
        e = lax.rem(d + k, 8)
        landed(e, b_buf, b_in, a_s.at[0], a_r.at[0], own.at[0])
        landed(e, q_buf, q_in, a_s.at[2], a_r.at[2], own.at[2])
    q_line = jnp.concatenate([q_in[e] for e in range(8)], axis=1)
    owner = jnp.concatenate([jnp.full((8, QUARTER), e, jnp.int32) for e in range(8)], axis=1)
    q_line = jnp.where(lax.broadcasted_iota(jnp.int32, q_line.shape, 0) == owner, q_line, 0.0)
    q_high = q_line.astype(BF)
    q_both = jnp.concatenate([q_high, (q_line - q_high.astype(F32)).astype(BF)], axis=0)
    b_rows = b_in[...].reshape(SLOTS, width)

    def back_block(tt):
        one, two = onehots(tt)
        hot = jnp.logical_or(one, two).astype(F32).astype(BF)
        q = nt(q_both, hot)
        return nn(hot, b_rows), q[0:8] + q[8:16]

    def core_send(n, i, src, dst):
        copy = remote(src.at[i], dst.at[i], c_s.at[n, i], c_r.at[n, i], (here, core))
        copy.start()
        return copy

    def side_send(n, src, dst):
        copy = remote(src, dst, y_s.at[n], y_r.at[n], (here, side))
        copy.start()
        return copy

    core_b, core_q = [], []
    for i, tt in enumerate((far, core)):
        total, q = back_block(tt)
        blocks[i] = total.astype(BF)
        q_blocks[i] = q
        core_b.append(core_send(0, i, blocks, core_in))
        core_q.append(core_send(1, i, q_blocks, q_core))
    total, q = back_block(side)
    core_b[0].wait_recv()
    core_q[0].wait_recv()
    side_buf[...] = (total + core_in[0].astype(F32)).astype(BF)
    q_mid[...] = q + q_core[0]
    side_b = side_send(0, side_buf, side_in)
    side_q = side_send(1, q_mid, q_side)
    total, q = back_block(t)
    core_b[1].wait_recv()
    core_q[1].wait_recv()
    r_out[...] = total + core_in[1].astype(F32)
    q_out[...] = q + q_core[1]

    for k in range(1, 9):
        p = lax.rem(d + k, 8)
        near[1, k].wait_recv()
        total = w_buf[t, p].astype(F32) + act_buf[inbox(1, p)].astype(F32)
        if k <= EARLY:
            over[k].wait_recv()
            total = total + pre_buf[inbox(0, p)].astype(F32)
        w_buf[t, p] = total.astype(BF)
    keep_e = pltpu.make_async_copy(w_buf.at[t], e_out, store.at[0])
    keep_e.start()
    side_b.wait_recv()
    side_q.wait_recv()
    r_out[...] += side_in[...].astype(F32)
    q_out[...] += q_side[...]

    for k in range(1, 9):
        landed(lax.rem(d + k, 8), y_buf, y_out, a_s.at[1], a_r.at[1], own.at[1])
    for copy in core_b + core_q + [side_b, side_q] + list(near.values()) + list(over.values()) + w_near:
        copy.wait_send()
    for copy in w_side:
        copy.wait_send()
    for g, copy in sent:

        @pl.when(g != d)
        def _():
            copy.wait_send()

    keep_e.wait()
    keep_side.wait()


def back_kernel(
    cells,
    tok, hid, r_ref, cols, gates, totals, cot, probs, picked_ref, vec, y_hbm, wall_hbm, qkv_hbm, mixed_hbm, e_src, e_side_src,
    bias_msg, out, token_out, e_out, qkv_out, proj_out, line_out, pair_out, router_out, up_out, down_out,
    token_grad, a_out, msg_all, vec_all, n1, vec_grad, vec_msg, a_grad, qv_grad, a_core, a_mid, a_side, a_fin, a_cross, a_in,
    blocks, core_in, side_buf, side_in, e_own, e_in, y_rows, wall, qkv_ref, mixed_ref, fetch,
    c_s, c_r, y_s, y_r, e_s, e_r, f_s, f_r, x_s, x_r, z_s, z_r, o_s, o_r, own, m_s, m_r, v_s, v_r,
):
    d, cell, t = place(cells)
    core, side, far = tensor_peers(t)
    here = d * cells + cell
    fetches = []
    for n, (src, dst) in enumerate(((wall_hbm, wall), (qkv_hbm, qkv_ref), (mixed_hbm, mixed_ref), (y_hbm, y_rows))):
        copy = pltpu.make_async_copy(src, dst, fetch.at[n])
        copy.start()
        fetches.append(copy)
    heads = qkv_ref.shape[2] // 3
    rows = tok.shape[0]
    width = tok.shape[1]
    spot = d * 4 + t
    twin = d + 1 - 2 * lax.rem(d, 2)

    def at_dp(k):
        return (lax.rem(d + k, 8) * cells + cell, t)

    others = [(k, m) for k in range(8) for m in range(4) if k or m]

    def other(k, m):
        return lax.rem(d + k, 8), lax.rem(t + m, 4)

    barrier = pltpu.get_barrier_semaphore()
    for k, m in others:
        dd, tt = other(k, m)
        signal(barrier, (dd * cells + cell, tt))
    pl.semaphore_wait(barrier, 31)

    waits = []
    late = range(EARLY + 1, 9)
    over_e, load_e = {}, {}
    for k in range(1, EARLY + 1):
        copy = remote(e_src.at[lax.rem(d + k, 8)], e_out.at[d], e_s.at[k], e_r.at[k], at_dp(k))
        copy.start()
        waits.append(copy)
    for k in late:
        p = lax.rem(d + k, 8)
        over_e[k] = remote(e_side_src.at[p], e_in.at[p], f_s.at[k - 1], f_r.at[k - 1], (here, side))
        over_e[k].start()
        load_e[k] = pltpu.make_async_copy(e_src.at[p], e_own.at[p], own.at[k])
        load_e[k].start()

    def finish_expert(k):
        p = lax.rem(d + k, 8)
        load_e[k].wait()
        over_e[k].wait_recv()
        e_own[p] = (e_own[p].astype(F32) + e_in[p].astype(F32)).astype(BF)
        if k < 8:
            copy = remote(e_own.at[p], e_out.at[d], e_s.at[k], e_r.at[k], at_dp(k))
            waits.append(copy)
        else:
            copy = pltpu.make_async_copy(e_own.at[p], e_out.at[d], own.at[0])
            load_e[0] = copy
        copy.start()
    for n, (k, m) in enumerate(others):
        dd, tt = other(k, m)
        copy = remote(bias_msg.at[dd * 4 + tt], msg_all.at[spot], m_s.at[n], m_r.at[n], (dd * cells + cell, tt))
        copy.start()
        waits.append(copy)
    msg_own = pltpu.make_async_copy(bias_msg.at[spot], msg_all.at[spot], own.at[1])
    msg_own.start()

    hidden = hid[...]
    picked = picked_ref[...]
    logit = picked - probs[...] * jnp.sum(picked, axis=0, keepdims=True)
    high = logit.astype(BF)
    both = jnp.concatenate([high, (logit - high.astype(F32)).astype(BF)], axis=0)
    unit, inv = unit_norm(hidden)
    gain = vec[2:3]
    second = (unit * gain + vec[3:4]).astype(BF)
    router_grad = nn(both, second)
    vec_grad[...] = jnp.zeros_like(vec_grad)
    vec_grad[8:16] = router_grad[0:8] + router_grad[8:16]
    table = vec[7:15].astype(BF)
    n2 = r_ref[...] + tn(both, jnp.concatenate([table, table], axis=0))
    vec_grad[2:3] = jnp.sum(n2 * unit, axis=0, keepdims=True)
    vec_grad[3:4] = jnp.sum(n2, axis=0, keepdims=True)
    scaled = n2 * gain
    back = inv * (
        scaled
        - jnp.mean(scaled, axis=-1, keepdims=True)
        - unit * jnp.mean(scaled * unit, axis=-1, keepdims=True)
    )
    hidden_grad = cot[...].astype(F32) + back
    token_grad[...] = hidden_grad
    branch = hidden_grad.astype(BF)
    vec_grad[4:5] = jnp.sum(branch.astype(F32), axis=0, keepdims=True)
    unit1, inv1 = unit_norm(tok[...].astype(F32))
    first_norm = (unit1 * vec[0:1] + vec[1:2]).astype(BF)
    n1[...] = jnp.zeros_like(n1)

    def attend_back(tt):
        weights = wall[tt].reshape(width, -1)
        qkv = qkv_ref[tt]
        mixed_grad = nn(branch, weights[:, 3 * heads :]).astype(BF)
        triple = []
        for i in range(rows // SEQ_PAD):
            span = slice(i * SEQ_PAD, (i + 1) * SEQ_PAD)
            part, grad = qkv[span], mixed_grad[span]
            sides = [[], [], []]
            for h in range(heads // HEAD_DIM):
                q, k, v = (part[:, j * heads + h * HEAD_DIM : j * heads + (h + 1) * HEAD_DIM] for j in range(3))
                g = grad[:, h * HEAD_DIM : (h + 1) * HEAD_DIM]
                log_total = totals[tt, i * SEQ_PAD : (i + 1) * SEQ_PAD, h : h + 1]
                w = jnp.exp(masked_scores(q, k) - log_total)
                w_grad = nt(g, v)
                s_grad = (w * (w_grad - jnp.sum(w * w_grad, axis=-1, keepdims=True))).astype(BF)
                sides[0].append((nn(s_grad, k) * (HEAD_DIM**-0.5)).astype(BF))
                sides[1].append((tn(s_grad, q) * (HEAD_DIM**-0.5)).astype(BF))
                sides[2].append(tn(w.astype(BF), g).astype(BF))
            triple.append(jnp.concatenate(sides[0] + sides[1] + sides[2], axis=1))
        triple = jnp.concatenate(triple, axis=0)
        grad = jnp.concatenate([tn(first_norm, triple), tn(branch, mixed_ref[tt])], axis=1).astype(BF)
        a_grad[tt] = grad.reshape(8, width // 8, -1)
        n1[...] += nt(triple, weights[:, : 3 * heads])
        sums = jnp.sum(triple.astype(F32), axis=0, keepdims=True)
        qv_grad[tt] = sums

    def core_a(i, tt):
        copy = remote(a_grad.at[tt], a_core.at[i], c_s.at[i], c_r.at[i], (here, core))
        copy.start()
        return copy

    order = [lax.rem(twin + 2 * m, 8) for m in range(4)] + [lax.rem(d + 2 * m, 8) for m in (1, 2, 3, 0)]
    for copy in fetches:
        copy.wait()
    attend_back(far)
    near_a = core_a(0, far)
    for k in list(late)[:-1][:1]:
        finish_expert(k)
    attend_back(side)
    near_a.wait_recv()
    over_a = []
    for n, p in enumerate(order):
        a_mid[p] = (a_grad[side, p].astype(F32) + a_core[0, p].astype(F32)).astype(BF)
        copy = remote(a_mid.at[p], a_side.at[p], y_s.at[n], y_r.at[n], (here, side))
        copy.start()
        over_a.append(copy)
    for k in list(late)[:-1][1:2]:
        finish_expert(k)
    attend_back(core)
    far_a = core_a(1, core)
    for k in list(late)[2:-1]:
        finish_expert(k)
    attend_back(t)
    finish_expert(8)

    def out_block(tt):
        at = lax.broadcasted_iota(jnp.int32, (rows, SLOTS), 1)
        col = cols[tt, :, 0:2].astype(jnp.int32)
        one, two = at == col[:, 0:1], at == col[:, 1:2]
        hot = jnp.where(one, gates[tt, :, 0:1], jnp.where(two, gates[tt, :, 1:2], 0.0)).astype(BF)
        return nn(hot, y_rows[...])

    out_copies = []
    for i, tt in enumerate((far, core)):
        blocks[i] = out_block(tt).astype(BF)
        copy = remote(blocks.at[i], core_in.at[i], o_s.at[i], o_r.at[i], (here, core))
        copy.start()
        out_copies.append(copy)
    total = out_block(side)
    out_copies[0].wait_recv()
    side_buf[...] = (total + core_in[0].astype(F32)).astype(BF)
    side_out = remote(side_buf, side_in, o_s.at[2], o_r.at[2], (here, side))

    far_a.wait_recv()
    cross = []
    for n, p in enumerate(order):
        over_a[n].wait_recv()
        total = a_grad[t, p].astype(F32) + a_core[1, p].astype(F32) + a_side[p].astype(F32)
        if n < 4:
            a_fin[p] = total.astype(BF)
            copy = remote(a_fin.at[p], a_cross.at[n], x_s.at[n], x_r.at[n], (twin * cells + cell, t))
            copy.start()
            cross.append(copy)
        else:
            m = (n - 3) % 4
            cross[m].wait_recv()
            total = total + a_cross[m].astype(F32)
            if m:
                a_fin[p] = total.astype(BF)
                copy = remote(a_fin.at[p], a_in.at[m], z_s.at[m], z_r.at[m], at_dp(2 * m))
                copy.start()
                waits.append(copy)
            else:
                a_out[...] = total
    side_out.start()

    grad = n1[...]
    vec_grad[0:1] = jnp.sum(grad * unit1, axis=0, keepdims=True)
    vec_grad[1:2] = jnp.sum(grad, axis=0, keepdims=True)
    for j, row in ((0, 5), (2, 6)):
        parts = [qv_grad[tt][:, j * heads : (j + 1) * heads] for tt in range(4)]
        vec_grad[row : row + 1] = jnp.concatenate(parts, axis=1)
    turned = vec_grad[...].T
    vec_msg[...] = turned.reshape(vec_msg.shape)
    for n, (k, m) in enumerate(others):
        dd, tt = other(k, m)
        copy = remote(vec_msg.at[dd * 4 + tt], vec_all.at[spot], v_s.at[n], v_r.at[n], (dd * cells + cell, tt))
        copy.start()
        waits.append(copy)
    vec_all[spot] = vec_msg[spot]
    scaled = grad * vec[0:1]
    token_grad[...] += inv1 * (
        scaled
        - jnp.mean(scaled, axis=-1, keepdims=True)
        - unit1 * jnp.mean(scaled * unit1, axis=-1, keepdims=True)
    )
    for i in range(rows // SEQ_PAD):
        token_out[i * SEQ : (i + 1) * SEQ] = token_grad[i * SEQ_PAD : i * SEQ_PAD + SEQ]
    total = out_block(t)
    out_copies[1].wait_recv()
    total = total + core_in[1].astype(F32)
    side_out.wait_recv()
    total = (hid[...] + (total + side_in[...].astype(F32))).astype(BF)
    for i in range(rows // SEQ_PAD):
        out[i * SEQ : (i + 1) * SEQ] = total[i * SEQ_PAD : i * SEQ_PAD + SEQ]
    for copy in waits:
        copy.wait()
    for m in range(1, 4):
        a_out[...] += a_in[m].astype(F32)
    for j in range(3):
        qkv_out[j] = a_out[:, j * heads : (j + 1) * heads]
    proj_out[...] = a_out[:, 3 * heads : 4 * heads].T
    load_e[0].wait()
    msg_own.wait()
    vec_sum, msg_sum = vec_all[0], []
    for n in range(1, 32):
        vec_sum = vec_sum + vec_all[n]
    turned = vec_sum.T
    router_out[...] = turned[8:16]
    line_out[...] = turned[0:5]
    pair_out[...] = turned[5:7]
    for e in range(8):
        total = msg_all[4 * e] + msg_all[4 * e + 1] + msg_all[4 * e + 2] + msg_all[4 * e + 3]
        up_out[e : e + 1] = total[0:1, 0 : up_out.shape[1]]
        down_out[e : e + 1] = total[1:2, 0 : down_out.shape[1]]
    for copy in [near_a, far_a, side_out] + out_copies + over_a + cross + list(over_e.values()):
        copy.wait_send()


def finish_kernel(
    out, token, expert, qkv, proj, line, pair, router, up_b, down_b,
    out_o, token_o, up_o, down_o, qkv_o, proj_o, line_0, line_1, line_2, line_3, line_4, pair_o, router_o, up_b_o, down_b_o,
):
    half = up_o.shape[1]
    out_o[...] = out[...]
    token_o[...] = token[...]
    up_o[...] = expert[:, 0:half].astype(F32)
    down_o[...] = expert[:, half : 2 * half].astype(F32)
    qkv_o[...] = qkv[...]
    proj_o[...] = proj[...]
    for i, target in enumerate((line_0, line_1, line_2, line_3, line_4)):
        target[...] = line[i]
    pair_o[...] = pair[...]
    router_o[...] = router[...]
    up_b_o[...] = up_b[...]
    down_b_o[...] = down_b[...]


def pad_images(rows, fill=0):
    images = rows.reshape((-1, SEQ) + rows.shape[1:])
    spare = [(0, 0), (0, SEQ_PAD - SEQ)] + [(0, 0)] * (rows.ndim - 1)
    return jnp.pad(images, spare, constant_values=fill).reshape((-1,) + rows.shape[1:])


def body(
    tokens, ln1_gain, ln1_shift, qkv_weight, qv_bias, out_weight, out_bias, ln2_gain, ln2_shift,
    router_weight, expert_in, expert_in_bias, expert_out, expert_out_bias, expert_ids, expert_slots,
    cotangent,
):
    n_dp = lax.axis_size("dp")
    cells = n_dp // 8
    width = tokens.shape[1]
    experts = expert_in.shape[0]
    head_cols = qkv_weight.shape[2]
    ff_slice = expert_in.shape[2]
    index = lax.axis_index("dp")
    t = lax.axis_index("tensor")
    d, cell = index // cells, index % cells
    peers = [[row * cells + c for c in range(cells)] for row in range(8)]

    expert_pack = [expert_in, jnp.swapaxes(expert_out, 1, 2)]
    vectors = [(line, 0) for line in (ln1_gain, ln1_shift, ln2_gain, ln2_shift, out_bias)]
    vectors += [(qv_bias, 1), (router_weight.T, 1), (expert_out_bias, 1), (expert_in_bias, 1)]
    if cells > 1:

        def gather(part, axis):
            return lax.all_gather(part, "dp", axis=axis, tiled=True, axis_index_groups=peers)

        def quarter(part, axis):
            part = gather(lax.all_gather(part, "tensor", axis=axis, tiled=True), axis)
            size = part.shape[axis] // 4
            return lax.dynamic_slice_in_dim(part, t * size, size, axis)

        qkv_weight, out_weight = gather(qkv_weight, 0), gather(out_weight, 1)
        expert_pack = [gather(part, 1) for part in expert_pack]
        vectors = [(quarter(part, axis), axis) for part, axis in vectors]
    vectors = [part for part, _ in vectors]
    piece, ff_piece = vectors[0].shape[0], vectors[8].shape[1]
    rows = tokens.shape[0] // SEQ * SEQ_PAD
    routes = pad_images(jnp.concatenate([expert_ids, expert_slots], axis=1), -1).reshape(4, rows, 2 * TOP)
    routes = jnp.swapaxes(routes, 1, 2)
    packed_shape = (width // 8, 4 * head_cols)
    e_block = (experts, 2 * (width // 8), ff_slice)

    dma = pltpu.SemaphoreType.DMA

    def params(identity):
        return pltpu.CompilerParams(
            collective_id=identity, has_side_effects=True, vmem_limit_bytes=VMEM_LIMIT
        )

    def like(shape, dtype=BF):
        return jax.ShapeDtypeStruct(shape, dtype)

    slot_shape = (8, QUARTER, width)
    (
        probs, cols, gates, vec, tok, cot, hidden, qkv, mixed, totals, wall, bias_all, expert_all, x_rows, g_rows,
    ) = pl.pallas_call(
        functools.partial(front_kernel, cells),
        out_shape=[
            like((experts, rows), F32),
            like((4, rows, 8), F32),
            like((4, rows, 8), F32),
            like((32, width), F32),
            like((rows, width)),
            like((rows, width)),
            like((rows, width), F32),
            like((4, rows, 3 * head_cols)),
            like((4, rows, head_cols)),
            like((4, rows, 8), F32),
            like((4, 8) + packed_shape),
            like((4, 8, 8, 128), F32),
            like((4,) + e_block),
            like(slot_shape),
            like(slot_shape),
        ],
        in_specs=[VM] * 11 + [HB] * 2 + [VM] * 3,
        out_specs=[VM] * 4 + [HB] * 11,
        scratch_shapes=[
            pltpu.VMEM((4, rows, 8), F32),
            pltpu.VMEM(packed_shape, BF),
            pltpu.VMEM((piece, 128), F32),
            pltpu.VMEM((8, 128), F32),
            pltpu.VMEM((128, 128), F32),
            pltpu.VMEM((rows, width), BF),
            pltpu.VMEM((4, 8, rows), jnp.int32),
            pltpu.VMEM((4, 8, rows), F32),
            pltpu.VMEM((rows, width), F32),
            pltpu.VMEM((4, rows, 3 * head_cols), BF),
            pltpu.VMEM((4, rows, head_cols), BF),
            pltpu.VMEM((4, 8) + packed_shape, BF),
            pltpu.VMEM(slot_shape, BF),
            pltpu.VMEM((8, 4, piece, 128), F32),
            pltpu.VMEM((4, rows, width), BF),
            pltpu.VMEM((4, rows, width), BF),
            pltpu.VMEM((SLOTS, width), BF),
            pltpu.VMEM((SLOTS, width), BF),
            pltpu.VMEM((rows, width), F32),
            pltpu.VMEM((8, rows), F32),
            pltpu.VMEM((4, 1, 3 * head_cols), F32),
        ]
        + [dma((5, 8))] * 2
        + [dma((4, 8))] * 6
        + [dma((6,)), dma((3, 3)), dma((3, 3)), dma((8,)), dma((8,)), dma((4,)), dma((4,)), dma((8,))],
        compiler_params=params(0),
        name="front",
    )(jnp.swapaxes(qkv_weight, 0, 1), out_weight, *vectors, *expert_pack, tokens, cotangent, routes)

    r_rows, picked, y_rows, expert_grad, side_grad, message = pl.pallas_call(
        functools.partial(middle_kernel, cells),
        out_shape=[
            like((rows, width), F32),
            like((8, rows), F32),
            like(slot_shape),
            like(e_block),
            like(e_block),
            like((32, 8, 128), F32),
        ],
        in_specs=[VM, HB, HB, VM, VM, VM],
        out_specs=[VM, VM, HB, HB, HB, VM],
        scratch_shapes=[
            pltpu.VMEM((4, 1, ff_slice), F32),
            pltpu.VMEM((4, 1, ff_slice), F32),
            pltpu.VMEM((1, width), F32),
            pltpu.VMEM(expert_all.shape, BF),
            pltpu.VMEM((4 * SLOTS, ff_slice), BF),
            pltpu.VMEM((4 * SLOTS, ff_slice), BF),
            pltpu.VMEM((width, SLOTS), BF),
            pltpu.VMEM((width, SLOTS), BF),
            pltpu.VMEM((2 * QUARTER, width), F32),
            pltpu.VMEM((SLOTS, width), F32),
            pltpu.VMEM(slot_shape, BF),
            pltpu.VMEM(slot_shape, BF),
            pltpu.VMEM((8, 8, QUARTER), F32),
            pltpu.VMEM(slot_shape, BF),
            pltpu.VMEM(slot_shape, BF),
            pltpu.VMEM((8, 8, QUARTER), F32),
            pltpu.VMEM((2, rows, width), BF),
            pltpu.VMEM((2, rows, width), BF),
            pltpu.VMEM((rows, width), BF),
            pltpu.VMEM((rows, width), BF),
            pltpu.VMEM((2, 8, rows), F32),
            pltpu.VMEM((2, 8, rows), F32),
            pltpu.VMEM((8, rows), F32),
            pltpu.VMEM((8, rows), F32),
            dma((4, 4)), dma((2,)), dma((3, 4)), dma((3, 4)), dma((8,)), dma((8,)), dma((3, 8)), dma((3, 8)), dma((2, 2)), dma((2, 2)),
            dma((2,)), dma((2,)), dma((2, 8)), dma((2, 8)), dma((8,)), dma((8,)), dma((4,)),
            pltpu.SemaphoreType.REGULAR, pltpu.SemaphoreType.REGULAR,
        ],
        compiler_params=params(1),
        name="middle",
    )(x_rows.reshape(SLOTS, width), g_rows, expert_all, bias_all, vec, cols)

    a_block = wall.shape[1:]
    out, token_grad, expert_sum, qkv_sum, proj_sum, line_sum, pair_sum, router_sum, up_sum, down_sum = pl.pallas_call(
        functools.partial(back_kernel, cells),
        out_shape=[
            like(tokens.shape),
            like(tokens.shape, F32),
            like(e_block),
            like((3, width // 8, head_cols), F32),
            like((head_cols, width // 8), F32),
            like((5, piece), F32),
            like((2, piece), F32),
            like((8, piece), F32),
            like((8, ff_piece), F32),
            like((8, piece), F32),
        ],
        in_specs=[VM] * 10 + [HB] * 7,
        out_specs=[VM, VM, HB] + [VM] * 7,
        scratch_shapes=[
            pltpu.VMEM((rows, width), F32),
            pltpu.VMEM(a_block[1:], F32),
            pltpu.VMEM(message.shape, F32),
            pltpu.VMEM((32, piece, 128), F32),
            pltpu.VMEM((rows, width), F32),
            pltpu.VMEM((128, width), F32),
            pltpu.VMEM((32, piece, 128), F32),
            pltpu.VMEM(wall.shape, BF),
            pltpu.VMEM((4, 1, 3 * head_cols), F32),
            pltpu.VMEM((2,) + a_block, BF),
            pltpu.VMEM(a_block, BF),
            pltpu.VMEM(a_block, BF),
            pltpu.VMEM(a_block, BF),
            pltpu.VMEM((4,) + a_block[1:], BF),
            pltpu.VMEM((4,) + a_block[1:], BF),
            pltpu.VMEM((2, rows, width), BF),
            pltpu.VMEM((2, rows, width), BF),
            pltpu.VMEM((rows, width), BF),
            pltpu.VMEM((rows, width), BF),
            pltpu.VMEM(e_block, BF),
            pltpu.VMEM(e_block, BF),
            pltpu.VMEM((SLOTS, width), BF),
            pltpu.VMEM(wall.shape, BF),
            pltpu.VMEM(qkv.shape, BF),
            pltpu.VMEM(mixed.shape, BF),
            dma((4,)),
            dma((2,)), dma((2,)), dma((8,)), dma((8,)), dma((8,)), dma((8,)), dma((8,)), dma((8,)),
            dma((4,)), dma((4,)), dma((4,)), dma((4,)), dma((3,)), dma((3,)), dma((9,)), dma((31,)), dma((31,)), dma((31,)), dma((31,)),
        ],
        compiler_params=params(2),
        name="back",
    )(
        tok, hidden, r_rows, cols, gates, totals, cot, probs, picked, vec,
        y_rows.reshape(SLOTS, width), wall, qkv, mixed, expert_grad, side_grad, message,
    )

    if cells > 1:

        def scatter(part, axis):
            return lax.psum_scatter(part, "dp", scatter_dimension=axis, tiled=True, axis_index_groups=peers)

        def share(part, axis):
            part = lax.psum(part, "dp", axis_index_groups=peers)
            part = lax.all_gather(part, "tensor", axis=axis, tiled=True)
            size = part.shape[axis] // (4 * cells)
            return lax.dynamic_slice_in_dim(part, (cell * 4 + t) * size, size, axis)

        expert_sum = scatter(expert_sum.astype(F32).reshape(8, 2, width // 8, -1), 2)
        expert_sum = expert_sum.reshape(8, -1, expert_sum.shape[3])
        qkv_sum, proj_sum = scatter(qkv_sum, 1), scatter(proj_sum, 1)
        line_sum, pair_sum, up_sum, down_sum = (share(part, 1) for part in (line_sum, pair_sum, up_sum, down_sum))
        router_sum = share(router_sum, 1)
    if cells > 1:
        own_rows = expert_in.shape[1]
        up_grad, down_grad = expert_sum[:, :own_rows].astype(F32), expert_sum[:, own_rows:].astype(F32)
        line_sum = [line_sum[i] for i in range(5)]
    else:
        half_block = like((8, width // 8, ff_slice), F32)
        parts = (out, token_grad, expert_sum, qkv_sum, proj_sum, line_sum, pair_sum, router_sum, up_sum, down_sum)
        shapes = [like(part.shape, part.dtype) for part in parts]
        shapes = shapes[:2] + [half_block] * 2 + shapes[3:5] + [like((piece,), F32)] * 5 + shapes[6:]
        out, token_grad, up_grad, down_grad, qkv_sum, proj_sum, *line_sum, pair_sum, router_sum, up_sum, down_sum = (
            pl.pallas_call(
                finish_kernel,
                out_shape=shapes,
                in_specs=[VM] * 10,
                out_specs=[VM] * 15,
                compiler_params=pltpu.CompilerParams(vmem_limit_bytes=VMEM_LIMIT),
                name="finish",
            )(*parts)
        )
    return (
        out,
        token_grad,
        line_sum[0],
        line_sum[1],
        jnp.swapaxes(qkv_sum, 0, 1),
        pair_sum,
        proj_sum,
        line_sum[4],
        line_sum[2],
        line_sum[3],
        router_sum.T,
        up_grad,
        up_sum,
        jnp.swapaxes(down_grad, 1, 2),
        down_sum,
    )


def solution(mesh):
    both = ("dp", "tensor")
    return jax.shard_map(
        body,
        mesh=mesh,
        in_specs=(
            P(both, None),
            P(both),
            P(both),
            P("dp", None, "tensor"),
            P(None, both),
            P("tensor", "dp"),
            P(both),
            P(both),
            P(both),
            P(both, None),
            P(None, "dp", "tensor"),
            P(None, both),
            P(None, "tensor", "dp"),
            P(None, both),
            P("dp", None),
            P("dp", None),
            P(both, None),
        ),
        out_specs=(
            P(both, None),
            P(both, None),
            P(both),
            P(both),
            P("dp", None, "tensor"),
            P(None, both),
            P("tensor", "dp"),
            P(both),
            P(both),
            P(both),
            P(both, None),
            P(None, "dp", "tensor"),
            P(None, both),
            P(None, "tensor", "dp"),
            P(None, both),
        ),
        check_vma=False,
    )
```
